32 devices in a mesh: slab: 16 (over z, y, core), mem: 2 (over x).
Axes of the slice: x: 2, y: 2, z: 4, core: 2. Of those that a mesh axis runs over, the one named last changes fastest.
Arguments:
- present_ensemble: float32 [64, 4, 16, 512], P('mem', None, 'slab'), may hold values from -6 to 6
- delayed_ensemble: float32 [64, 2, 4, 16, 512], P('mem', None, None, 'slab'), may hold values from -6 to 6
- spreading_coefficient: float32 [16, 512], P('slab'), may hold values from 0.05 to 0.2
- transport_ratios: float32 [2, 16, 512], P(None, 'slab'), may hold values from -0.3 to 0.3
- obs_value: float32 [2, 256], replicated, may hold values from -6 to 6
- obs_error: float32 [2, 256], replicated, may hold values from 0.4 to 1.2
- obs_noise: float32 [2, 64, 256], replicated, may hold values from -6 to 6
- obs_row: int32 [2, 256], replicated, may hold values from 0 to 15
- obs_col: int32 [2, 256], replicated, may hold values from 1 to 510
- obs_field: int32 [2, 256], replicated, may hold values from 0 to 3
Outputs:
- analysis: float32 [64, 3, 4, 16, 512], P('mem', None, None, 'slab')
The draws below stay inside these ranges and needn't reach their ends.
All inputs are finite; a program needn't handle non-finite values.
Results may differ from the reference program's by a relative error of at most 0.00011.
Values sent between devices are 32-bit elements; how exact they have to be, the bound alone decides.
No kernel may reach another device: no remote copies, remote signals or barrier semaphores. Data moves between devices by JAX's collectives and lax.ppermute only.
A program may use at most 64 MiB of HBM per device.

```python
import math
import jax
import jax.numpy as jnp
from jax import lax

NY = 512
FIELDS = 4
MEMBERS = 64
BATCHES = 2
NOBS = 256
NXG = 16


def plant(array, key, low, largest):
    index_at = [jax.random.randint(jax.random.fold_in(key, axis), (), 0, length) for axis, length in enumerate(array.shape)]
    longest = array.shape.index(max(array.shape))
    next_to = index_at[:longest] + [(index_at[longest] + 1) % array.shape[longest]] + index_at[longest + 1:]
    return array.at[tuple(index_at)].set(low).at[tuple(next_to)].set(largest)


def steps_of(own_key, shape, shards, low, top_value):
    gain, own = 1.0, jax.random.fold_in(own_key, 6)
    for axis_at, parts in shards:
        heights = jnp.exp(jax.random.uniform(jax.random.fold_in(own, axis_at), (parts,), jnp.float32, low / len(shards), top_value / len(shards)))
        gain = gain * jnp.repeat(heights, shape[axis_at] // parts).reshape([-1 if axis == axis_at else 1 for axis in range(len(shape))])
    return gain


def scatter_about(stream_key, extent, deviation, most, shards=(), kind=jnp.bfloat16):
    values = deviation * jax.random.normal(stream_key, extent, jnp.float32)
    if shards:
        values = values * steps_of(stream_key, extent, shards, -0.22, 0.18)
    return jnp.clip(values, -most, most).astype(kind)


def setup_inputs(seed: int = 0) -> dict:
    key_list = jax.random.split(jax.random.key(seed), 11)
    return {
        "present_ensemble": scatter_about(key_list[0], (MEMBERS, FIELDS, NXG, NY), 1.0, 6.0, ((0, 2), (2, 16)), jnp.float32),
        "delayed_ensemble": scatter_about(key_list[1], (MEMBERS, 2, FIELDS, NXG, NY), 1.0, 6.0, ((0, 2), (3, 16)), jnp.float32),
        "spreading_coefficient": jnp.clip(jnp.exp(math.log(0.2) - 1.3862944 * jax.random.uniform(key_list[2], (NXG, NY), jnp.float32) ** steps_of(key_list[2], (NXG, NY), ((0, 16),), -0.2, 0.2)), 0.05, 0.2),
        "transport_ratios": jnp.clip(jax.random.uniform(key_list[3], (2, NXG, NY), jnp.float32, -0.3, 0.3) * steps_of(key_list[3], (2, NXG, NY), ((1, 16),), -0.4, 0.0), -0.3, 0.3),
        "obs_value": scatter_about(key_list[4], (BATCHES, NOBS), 1.5, 6.0, (), jnp.float32),
        "obs_error": jnp.clip(jnp.exp(jax.random.uniform(key_list[5], (BATCHES, NOBS), jnp.float32, math.log(0.4), math.log(1.2))), 0.4, 1.2),
        "obs_noise": scatter_about(key_list[6], (BATCHES, MEMBERS, NOBS), 1.0, 6.0, (), jnp.float32),
        "obs_row": plant(jax.random.randint(key_list[7], (BATCHES, NOBS), 0, NXG), jax.random.fold_in(key_list[7], 1), 0, NXG - 1).astype(jnp.int32),
        "obs_col": plant(jax.random.randint(key_list[8], (BATCHES, NOBS), 1, NY - 1), jax.random.fold_in(key_list[8], 1), 1, (NY - 1) - 1).astype(jnp.int32),
        "obs_field": plant(jax.random.randint(key_list[9], (BATCHES, NOBS), 0, FIELDS), jax.random.fold_in(key_list[9], 1), 0, FIELDS - 1).astype(jnp.int32),
    }


def propagate_ahead(present_ensemble, spreading_coefficient, transport_ratios):
    padded = jnp.pad(present_ensemble, ((0, 0), (0, 0), (1, 1), (1, 1)))
    below = padded[:, :, 2:, 1:-1]
    above = padded[:, :, :-2, 1:-1]
    right = padded[:, :, 1:-1, 2:]
    left = padded[:, :, 1:-1, :-2]
    laplacian_operator = below + above + right + left - 4.0 * present_ensemble
    return present_ensemble + spreading_coefficient * laplacian_operator - transport_ratios[0] * (below - above) * 0.5 - transport_ratios[1] * (right - left) * 0.5

def observe(level_zero, rows, cols, fields, row_start, col_start):
    members, nfield, height, width = level_zero.shape
    flat = level_zero.reshape(members, nfield * height * width)
    total = jnp.zeros((members, rows.shape[0]), jnp.float32)
    for offset, factor in ((-1, 0.25), (0, 0.5), (1, 0.25)):
        row_within = rows - row_start
        column_within = cols + offset - col_start
        valid = (row_within >= 0) & (row_within < height) & (column_within >= 0) & (column_within < width)
        index = ((fields * height + jnp.clip(row_within, 0, height - 1)) * width + jnp.clip(column_within, 0, width - 1)).astype(jnp.int32)
        picked = jnp.take(flat, index, axis=1)
        total = total + factor * jnp.where(valid[None, :], picked, 0.0)
    return total

def transform(observed, values, errors, noise):
    members = observed.shape[0]
    rescaled_values = (observed - jnp.mean(observed, axis=0, keepdims=True)) / errors[None, :]
    innovation = (values[None, :] - observed) / errors[None, :] + noise
    eye = jnp.eye(members, dtype=jnp.float32)
    system = jnp.dot(rescaled_values.astype(jnp.float32), rescaled_values.T.astype(jnp.float32), precision=lax.Precision.HIGHEST, preferred_element_type=jnp.float32) + (members - 1.0) * eye
    right = jnp.dot(rescaled_values.astype(jnp.float32), innovation.T.astype(jnp.float32), precision=lax.Precision.HIGHEST, preferred_element_type=jnp.float32)
    factor = jnp.linalg.cholesky(system)
    middle = lax.linalg.triangular_solve(factor, right, left_side=True, lower=True)
    weights = lax.linalg.triangular_solve(factor, middle, left_side=True, lower=True, transpose_a=True)
    return eye + weights - jnp.mean(weights, axis=0, keepdims=True)

def reference(present_ensemble, delayed_ensemble, spreading_coefficient, transport_ratios, obs_value, obs_error, obs_noise, obs_row, obs_col, obs_field):
    predictive_dynamics = propagate_ahead(present_ensemble, spreading_coefficient, transport_ratios)
    flattened_system_array = jnp.concatenate([predictive_dynamics[:, None], delayed_ensemble], axis=1)
    for batch in range(BATCHES):
        observed = observe(flattened_system_array[:, 0], obs_row[batch], obs_col[batch], obs_field[batch], 0, 0)
        matrix = transform(observed, obs_value[batch], obs_error[batch], obs_noise[batch])
        flattened_system_array = jnp.einsum('jlfrn,jm->mlfrn', flattened_system_array, matrix, precision=lax.Precision.HIGHEST)
    return flattened_system_array
```

```python
import functools

import jax
import jax.numpy as jnp
from jax import lax
from jax.experimental import pallas as pl
from jax.experimental.pallas import tpu as pltpu
from jax.sharding import PartitionSpec as P

LANES = 128
F32 = jnp.float32
BF16 = jnp.bfloat16
HIGHEST = lax.Precision.HIGHEST
VMEM_LIMIT = 48 * 1024 * 1024


def rows_of(array):
    return array.reshape(-1, LANES)


def split_two(x):
    high = x.astype(BF16)
    low = (x - high.astype(F32)).astype(BF16)
    return high, low


def forecast_kernel(
    members,
    fields,
    chunks,
    present_ref,
    above_ref,
    below_ref,
    delayed_ref,
    spread_ref,
    ratio_ref,
    row_ref,
    col_ref,
    field_ref,
    state_ref,
    obs_ref,
):
    width = chunks * LANES
    planes = fields * chunks
    lagged = delayed_ref.shape[0] // members
    levels_planes = planes + lagged

    def plane(ref, start, stride):
        return jnp.concatenate(
            [ref[pl.ds(start + c, members, stride=stride), :] for c in range(chunks)], axis=1
        )

    def line(ref, start):
        return jnp.concatenate([ref[start + c : start + c + 1, :] for c in range(chunks)], axis=1)

    spread = line(spread_ref, 0)
    along_rows = line(ratio_ref, 0)
    along_columns = line(ratio_ref, chunks)
    lane = lax.broadcasted_iota(jnp.int32, (members, width), 1)
    forecasts = []
    for f in range(fields):
        here = plane(present_ref, f * chunks, planes)
        above = plane(above_ref, f * chunks, planes)
        below = plane(below_ref, f * chunks, planes)
        left = jnp.where(lane == 0, 0.0, pltpu.roll(here, 1, 1))
        right = jnp.where(lane == width - 1, 0.0, pltpu.roll(here, width - 1, 1))
        laplacian = below + above + right + left - 4.0 * here
        ahead = (
            here
            + spread * laplacian
            - along_rows * (below - above) * 0.5
            - along_columns * (right - left) * 0.5
        )
        forecasts.append(ahead)
        for c in range(chunks):
            state_ref[pl.ds(f * chunks + c, members, stride=levels_planes), :] = ahead[
                :, c * LANES : (c + 1) * LANES
            ]
    for k in range(lagged):
        state_ref[pl.ds(planes + k, members, stride=levels_planes), :] = delayed_ref[
            pl.ds(k, members, stride=lagged), :
        ]

    own_row = lax.axis_index("slab")
    batches, count = row_ref.shape
    total = batches * count
    flat = lambda ref: jnp.concatenate([ref[b : b + 1, :] for b in range(batches)], axis=1)
    rows, cols, kinds = flat(row_ref), flat(col_ref), flat(field_ref)
    kinds = jnp.where(rows == own_row, kinds, -1)
    at = lax.broadcasted_iota(jnp.int32, (width, total), 0).astype(F32) * 0.25
    taps = jnp.maximum(0.5 - jnp.abs(at - cols.astype(F32) * 0.25), 0.0).astype(BF16)
    stacked = jnp.concatenate(forecasts, axis=0)
    high, rest = stacked.astype(BF16), None
    rest = stacked - high.astype(F32)
    middle = rest.astype(BF16)
    low = (rest - middle.astype(F32)).astype(BF16)
    picked = (
        jnp.dot(low, taps, preferred_element_type=F32)
        + jnp.dot(middle, taps, preferred_element_type=F32)
        + jnp.dot(high, taps, preferred_element_type=F32)
    )
    observed = jnp.zeros((members, total), F32)
    for f in range(fields):
        observed = observed + jnp.where(kinds == f, picked[f * members : (f + 1) * members], 0.0)
    groups = total // LANES
    for g in range(groups):
        obs_ref[pl.ds(g, members, stride=groups), :] = observed[:, g * LANES : (g + 1) * LANES]


def solve_transposed(system, right_t, floor):
    size = system.shape[0]
    eye = (
        lax.broadcasted_iota(jnp.int32, (size, size), 0)
        == lax.broadcasted_iota(jnp.int32, (size, size), 1)
    ).astype(F32)
    top = jnp.max(jnp.sum(jnp.abs(system), axis=0, keepdims=True)) + 1.0
    scale = 2.0 / (top + floor)
    eps = (top - floor) / (top + floor)
    residual = eye - scale * system
    answer = scale * right_t

    def more(carry):
        return carry[0] > 1e-6

    def double(carry):
        eps, residual, answer = carry
        both = jnp.dot(
            jnp.concatenate([residual, answer], axis=0),
            residual,
            precision=HIGHEST,
            preferred_element_type=F32,
        )
        square = eps * eps
        share = 1.0 / (2.0 - square)
        return (
            square * share,
            (2.0 * both[:size] - square * eye) * share,
            (answer + both[size:]) * (2.0 * share),
        )

    return lax.while_loop(more, double, (eps, residual, answer))[2]


def analysis_kernel(
    parts, planes, prior_ref, value_ref, error_ref, noise_ref, *refs
):
    state_refs, out_ref = refs[:parts], refs[parts]
    batches, members, count = noise_ref.shape
    local = members // parts
    groups = count // LANES
    stride = batches * groups
    eye = (
        lax.broadcasted_iota(jnp.int32, (members, members), 0)
        == lax.broadcasted_iota(jnp.int32, (members, members), 1)
    ).astype(F32)
    product_t = None
    nt = (((1,), (1,)), ((), ()))
    for b in range(batches):
        observed = jnp.concatenate(
            [prior_ref[pl.ds(b * groups + g, members, stride=stride), :] for g in range(groups)],
            axis=1,
        )
        if product_t is not None:
            observed = jnp.dot(
                product_t, observed, precision=HIGHEST, preferred_element_type=F32
            )
        errors = error_ref[b : b + 1, :]
        scaled = (observed - jnp.mean(observed, axis=0, keepdims=True)) / errors
        innovation = (value_ref[b : b + 1, :] - observed) / errors + noise_ref[b]
        both = lax.dot_general(
            jnp.concatenate([scaled, innovation], axis=0),
            scaled,
            nt,
            precision=HIGHEST,
            preferred_element_type=F32,
        )
        system = both[:members] + (members - 1.0) * eye
        weights_t = solve_transposed(system, both[members:], members - 1.0)
        matrix_t = eye + weights_t - jnp.mean(weights_t, axis=1, keepdims=True)
        if product_t is None:
            product_t = matrix_t
        else:
            product_t = jnp.dot(
                matrix_t, product_t, precision=HIGHEST, preferred_element_type=F32
            )

    own = lax.axis_index("mem")
    is_own = (
        lax.broadcasted_iota(jnp.int32, (local, members), 0) + own * local
        == lax.broadcasted_iota(jnp.int32, (local, members), 1)
    ).astype(F32)
    mine = jnp.dot(is_own, product_t, precision=HIGHEST, preferred_element_type=F32)
    source = lax.broadcasted_iota(jnp.int32, (members, members), 0)
    target = lax.broadcasted_iota(jnp.int32, (members, members), 1)
    turn = (source == lax.rem(target + own * local, members)).astype(F32)
    mine = jnp.dot(mine, turn, precision=HIGHEST, preferred_element_type=F32)
    high, low = split_two(mine)
    left = jnp.concatenate([high, high, low], axis=1)
    step = 16
    for start in range(0, planes, step):
        held = jnp.concatenate(
            [
                jnp.concatenate(
                    [ref[pl.ds(start + k, local, stride=planes), :] for k in range(step)], axis=1
                )
                for ref in state_refs
            ],
            axis=0,
        )
        held_high, held_low = split_two(held)
        result = jnp.dot(
            left,
            jnp.concatenate([held_high, held_low, held_high], axis=0),
            preferred_element_type=F32,
        )
        for k in range(step):
            out_ref[pl.ds(start + k, local, stride=planes), :] = result[
                :, k * LANES : (k + 1) * LANES
            ]


def shards(
    present_ensemble,
    delayed_ensemble,
    spreading_coefficient,
    transport_ratios,
    obs_value,
    obs_error,
    obs_noise,
    obs_row,
    obs_col,
    obs_field,
):
    members, fields, height, width = present_ensemble.shape
    assert height == 1 and width % LANES == 0
    chunks = width // LANES
    lagged = delayed_ensemble.shape[1]
    slabs, parts = lax.axis_size("slab"), lax.axis_size("mem")
    batches, all_members, count = obs_noise.shape
    total = batches * count
    planes = (1 + lagged) * fields * chunks

    present = rows_of(present_ensemble)
    up = [(i, i + 1) for i in range(slabs - 1)]
    down = [(j, i) for i, j in up]
    above = lax.ppermute(present, "slab", up)
    below = lax.ppermute(present, "slab", down)
    params = pltpu.CompilerParams(vmem_limit_bytes=VMEM_LIMIT)
    state, terms = pl.pallas_call(
        functools.partial(forecast_kernel, members, fields, chunks),
        out_shape=(
            jax.ShapeDtypeStruct((members * planes, LANES), F32),
            jax.ShapeDtypeStruct((members * total // LANES, LANES), F32),
        ),
        compiler_params=params,
        name="forecast",
    )(
        present,
        above,
        below,
        rows_of(delayed_ensemble),
        rows_of(spreading_coefficient),
        rows_of(transport_ratios),
        obs_row,
        obs_col,
        obs_field,
    )
    others = [
        lax.ppermute(state, "mem", [((i + d) % parts, i) for i in range(parts)])
        for d in range(1, parts)
    ]
    if terms.shape[0] % (8 * slabs) == 0:
        pieces = lax.all_to_all(
            terms.reshape(slabs, -1, LANES), "slab", split_axis=0, concat_axis=0
        )
        prior = lax.all_gather(jnp.sum(pieces, axis=0), ("mem", "slab"), axis=0, tiled=True)
    else:
        prior = lax.all_gather(lax.psum(terms, "slab"), "mem", axis=0, tiled=True)
    out = pl.pallas_call(
        functools.partial(analysis_kernel, parts, planes),
        out_shape=jax.ShapeDtypeStruct((members * planes, LANES), F32),
        compiler_params=params,
        name="analysis",
    )(prior, obs_value, obs_error, obs_noise, state, *others)
    return out.reshape(members, 1 + lagged, fields, height, width)


def solution(mesh):
    return jax.shard_map(
        shards,
        mesh=mesh,
        in_specs=(
            P("mem", None, "slab", None),
            P("mem", None, None, "slab", None),
            P("slab", None),
            P(None, "slab", None),
            P(),
            P(),
            P(),
            P(),
            P(),
            P(),
        ),
        out_specs=P("mem", None, None, "slab", None),
        check_vma=False,
    )
```

```python
import functools

import jax
import jax.numpy as jnp
from jax import lax
from jax.experimental import pallas as pl
from jax.experimental.pallas import tpu as pltpu
from jax.sharding import PartitionSpec as P

LANES = 128
F32 = jnp.float32
BF16 = jnp.bfloat16
HIGHEST = lax.Precision.HIGHEST
PARAMS = pltpu.CompilerParams(vmem_limit_bytes=48 * 1024 * 1024)


def rows_of(array):
    return array.reshape(-1, LANES)


def in_hbm(arrays):
    return [pltpu.with_memory_space_constraint(array, pltpu.HBM) for array in arrays]


def shape_of(shape, dtype=F32):
    return jax.ShapeDtypeStruct(shape, dtype)


def split_two(x):
    high = x.astype(BF16)
    low = (x - high.astype(F32)).astype(BF16)
    return high, low


def split_three(x):
    high = x.astype(BF16)
    rest = x - high.astype(F32)
    middle = rest.astype(BF16)
    low = (rest - middle.astype(F32)).astype(BF16)
    return high, middle, low


def line(ref, start, chunks):
    return jnp.concatenate([ref[start + c : start + c + 1, :] for c in range(chunks)], axis=1)


def stacked_planes(ref, members, fields, chunks):
    return jnp.concatenate(
        [
            jnp.concatenate(
                [
                    ref[pl.ds(f * chunks + c, members, stride=fields * chunks), :]
                    for c in range(chunks)
                ],
                axis=1,
            )
            for f in range(fields)
        ],
        axis=0,
    )


def own_row_kernel(members, fields, chunks, *refs):
    sources, (part_ref, here_ref, coefs_ref, taps_ref, kinds_ref), scratch = (
        refs[:6],
        refs[6:11],
        refs[11:17],
    )
    sems = refs[17]
    copies = [
        pltpu.make_async_copy(source, target, sems.at[i])
        for i, (source, target) in enumerate(zip(sources, scratch))
    ]
    for copy in copies:
        copy.start()
    for copy in copies:
        copy.wait()
    present, spread_ref, ratio_ref, row_ref, col_ref, field_ref = scratch
    width = chunks * LANES
    spread = line(spread_ref, 0, chunks)
    along_rows = line(ratio_ref, 0, chunks)
    along_columns = line(ratio_ref, chunks, chunks)
    here = stacked_planes(present, members, fields, chunks)
    here_ref[...] = here
    lane = lax.broadcasted_iota(jnp.int32, here.shape, 1)
    left = jnp.where(lane == 0, 0.0, pltpu.roll(here, 1, 1))
    right = jnp.where(lane == width - 1, 0.0, pltpu.roll(here, width - 1, 1))
    part_ref[...] = (
        here + spread * (right + left - 4.0 * here) - along_columns * (right - left) * 0.5
    )
    coefs_ref[0:1, :] = spread + along_rows * 0.5
    coefs_ref[1:2, :] = spread - along_rows * 0.5

    batches, count = row_ref.shape
    total = batches * count
    flat = lambda ref: jnp.concatenate([ref[b : b + 1, :] for b in range(batches)], axis=1)
    rows, cols, kinds = flat(row_ref), flat(col_ref), flat(field_ref)
    own_row = lax.axis_index("slab")
    kinds_ref[0:1, :] = jnp.where(rows == own_row, kinds, -1)
    kinds_ref[1:2, :] = jnp.where(rows == own_row - 1, kinds, -1)
    at = lax.broadcasted_iota(jnp.int32, (width, total), 0).astype(F32) * 0.25
    taps_ref[...] = jnp.maximum(0.5 - jnp.abs(at - cols.astype(F32) * 0.25), 0.0).astype(BF16)


def observe_kernel(
    members,
    fields,
    chunks,
    above_ref,
    above_spread_ref,
    above_ratio_ref,
    part_ref,
    here_ref,
    coefs_ref,
    taps_ref,
    kinds_ref,
    obs_ref,
    partial_ref,
    present_ref,
):
    above = stacked_planes(above_ref, members, fields, chunks)
    here = here_ref[...]
    partial = part_ref[...] + coefs_ref[0:1, :] * above
    partial_ref[...] = partial
    present_ref[...] = here
    above_coef = line(above_spread_ref, 0, chunks) - line(above_ratio_ref, 0, chunks) * 0.5
    handed = above_coef * here
    taps = taps_ref[...]
    picked = [
        jnp.dot(part, taps, preferred_element_type=F32)
        for part in split_three(jnp.concatenate([partial, handed], axis=0))
    ]
    picked = picked[2] + picked[1] + picked[0]
    observed = None
    for side in range(2):
        kinds = kinds_ref[side : side + 1, :]
        for f in range(fields):
            start = (side * fields + f) * members
            term = jnp.where(kinds == f, picked[start : start + members], 0.0)
            observed = term if observed is None else observed + term
    obs_ref[...] = observed


def complete_kernel(obs_ref, other_ref, partial_ref, below_ref, coefs_ref, sum_ref, forecast_ref):
    sum_ref[...] = obs_ref[...] + other_ref[...]
    forecast_ref[...] = partial_ref[...] + coefs_ref[1:2, :] * below_ref[...]


def solve_transposed(system, right_t, floor):
    size = system.shape[0]
    eye = (
        lax.broadcasted_iota(jnp.int32, (size, size), 0)
        == lax.broadcasted_iota(jnp.int32, (size, size), 1)
    ).astype(F32)
    top = jnp.max(jnp.sum(jnp.abs(system), axis=0, keepdims=True)) + 1.0
    scale = 2.0 / (top + floor)
    eps = (top - floor) / (top + floor)
    residual = eye - scale * system
    answer = scale * right_t

    def more(carry):
        return carry[0] > 1e-6

    def double(carry):
        eps, residual, answer = carry
        both = jnp.dot(
            jnp.concatenate([residual, answer], axis=0),
            residual,
            precision=HIGHEST,
            preferred_element_type=F32,
        )
        square = eps * eps
        share = 1.0 / (2.0 - square)
        return (
            square * share,
            (2.0 * both[:size] - square * eye) * share,
            (answer + both[size:]) * (2.0 * share),
        )

    return lax.while_loop(more, double, (eps, residual, answer))[2]


def analysis_kernel(parts, *refs):
    value_ref, error_ref, noise_ref, delayed_ref = refs[4 + 3 * parts : 8 + 3 * parts]
    prior, sems = refs[8 + 3 * parts :]
    copies = [
        pltpu.make_async_copy(refs[i], refs[4 + 3 * parts + i], sems.at[i]) for i in range(4)
    ]
    for copy in copies:
        copy.start()
    refs = refs[4:]
    prior_refs, forecast_refs = refs[:parts], refs[parts : 2 * parts]
    delayed_refs = (delayed_ref,) + refs[2 * parts : 3 * parts - 1]
    out_ref = refs[3 * parts - 1]
    batches, members, count = noise_ref.shape
    local = members // parts
    own = lax.axis_index("mem")
    for d, ref in enumerate(prior_refs):
        owner = lax.rem(own + d, parts)
        prior[pl.ds(pl.multiple_of(owner * local, local), local), :] = ref[...]
    for copy in copies[:3]:
        copy.wait()
    eye = (
        lax.broadcasted_iota(jnp.int32, (members, members), 0)
        == lax.broadcasted_iota(jnp.int32, (members, members), 1)
    ).astype(F32)
    product_t = None
    nt = (((1,), (1,)), ((), ()))
    for b in range(batches):
        observed = prior[:, b * count : (b + 1) * count]
        if product_t is not None:
            observed = jnp.dot(
                product_t, observed, precision=HIGHEST, preferred_element_type=F32
            )
        errors = error_ref[b : b + 1, :]
        scaled = (observed - jnp.mean(observed, axis=0, keepdims=True)) / errors
        innovation = (value_ref[b : b + 1, :] - observed) / errors + noise_ref[b]
        both = lax.dot_general(
            jnp.concatenate([scaled, innovation], axis=0),
            scaled,
            nt,
            precision=HIGHEST,
            preferred_element_type=F32,
        )
        system = both[:members] + (members - 1.0) * eye
        weights_t = solve_transposed(system, both[members:], members - 1.0)
        matrix_t = eye + weights_t - jnp.mean(weights_t, axis=1, keepdims=True)
        if product_t is None:
            product_t = matrix_t
        else:
            product_t = jnp.dot(
                matrix_t, product_t, precision=HIGHEST, preferred_element_type=F32
            )

    is_own = (
        lax.broadcasted_iota(jnp.int32, (local, members), 0) + own * local
        == lax.broadcasted_iota(jnp.int32, (local, members), 1)
    ).astype(F32)
    mine = jnp.dot(is_own, product_t, precision=HIGHEST, preferred_element_type=F32)
    source = lax.broadcasted_iota(jnp.int32, (members, members), 0)
    target = lax.broadcasted_iota(jnp.int32, (members, members), 1)
    turn = (source == lax.rem(target + own * local, members)).astype(F32)
    mine = jnp.dot(mine, turn, precision=HIGHEST, preferred_element_type=F32)
    high, low = split_two(mine)
    left = jnp.concatenate([high, high, low], axis=1)

    fields = forecast_refs[0].shape[0] // local
    chunks = forecast_refs[0].shape[1] // LANES
    lagged = delayed_ref.shape[0] // local
    planes = fields * chunks + lagged
    copies[3].wait()
    for start in range(0, planes, chunks):
        if start < fields * chunks:
            f = start // chunks
            held = [ref[f * local : (f + 1) * local, :] for ref in forecast_refs]
        else:
            first = start - fields * chunks
            held = [
                jnp.concatenate(
                    [ref[pl.ds(first + c, local, stride=lagged), :] for c in range(chunks)],
                    axis=1,
                )
                for ref in delayed_refs
            ]
        held_high, held_low = split_two(jnp.concatenate(held, axis=0))
        result = jnp.dot(
            left,
            jnp.concatenate([held_high, held_low, held_high], axis=0),
            preferred_element_type=F32,
        )
        for c in range(chunks):
            out_ref[pl.ds(start + c, local, stride=planes), :] = result[
                :, c * LANES : (c + 1) * LANES
            ]


def shards(
    present_ensemble,
    delayed_ensemble,
    spreading_coefficient,
    transport_ratios,
    obs_value,
    obs_error,
    obs_noise,
    obs_row,
    obs_col,
    obs_field,
):
    members, fields, height, width = present_ensemble.shape
    assert height == 1 and width % LANES == 0
    chunks = width // LANES
    lagged = delayed_ensemble.shape[1]
    slabs, parts = lax.axis_size("slab"), lax.axis_size("mem")
    assert slabs & (slabs - 1) == 0
    batches, all_members, count = obs_noise.shape
    total = batches * count
    planes = (1 + lagged) * fields * chunks
    stacked = (fields * members, width)

    def from_partners(array):
        return [
            lax.ppermute(array, "mem", [((i + d) % parts, i) for i in range(parts)])
            for d in range(1, parts)
        ]

    up = [(i, i + 1) for i in range(slabs - 1)]
    down = [(j, i) for i, j in up]
    present, delayed = rows_of(present_ensemble), rows_of(delayed_ensemble)
    spread, ratios = rows_of(spreading_coefficient), rows_of(transport_ratios)
    above = lax.ppermute(present, "slab", up)
    above_spread = lax.ppermute(spread, "slab", up)
    above_ratios = lax.ppermute(ratios, "slab", up)
    sources = (present, spread, ratios, obs_row, obs_col, obs_field)
    part, here, coefs, taps, kinds = pl.pallas_call(
        functools.partial(own_row_kernel, members, fields, chunks),
        out_shape=(
            shape_of(stacked),
            shape_of(stacked),
            shape_of((2, width)),
            shape_of((width, total), BF16),
            shape_of((2, total), jnp.int32),
        ),
        in_specs=[pl.BlockSpec(memory_space=pltpu.HBM)] * len(sources),
        scratch_shapes=[pltpu.VMEM(s.shape, s.dtype) for s in sources]
        + [pltpu.SemaphoreType.DMA((len(sources),))],
        compiler_params=PARAMS,
        name="own_row",
    )(*in_hbm(sources))
    others_delayed = from_partners(delayed)
    terms, partial, present_again = pl.pallas_call(
        functools.partial(observe_kernel, members, fields, chunks),
        out_shape=(shape_of((members, total)), shape_of(stacked), shape_of(stacked)),
        compiler_params=PARAMS,
        name="observe",
    )(above, above_spread, above_ratios, part, here, coefs, taps, kinds)

    def from_slab(array, bit):
        return lax.ppermute(array, "slab", [(i, i ^ bit) for i in range(slabs)])

    other = from_slab(terms, 1)
    below = lax.ppermute(present_again, "slab", down)
    terms, forecast = pl.pallas_call(
        complete_kernel,
        out_shape=(shape_of((members, total)), shape_of(stacked)),
        compiler_params=PARAMS,
        name="complete",
    )(terms, other, partial, below, coefs)
    bit = 2
    while bit < slabs:
        terms = terms + from_slab(terms, bit)
        bit *= 2
    sources = (obs_value, obs_error, obs_noise, delayed)
    in_vmem = pl.BlockSpec(memory_space=pltpu.VMEM)
    out = pl.pallas_call(
        functools.partial(analysis_kernel, parts),
        out_shape=shape_of((members * planes, LANES)),
        in_specs=[pl.BlockSpec(memory_space=pltpu.HBM)] * len(sources)
        + [in_vmem] * (3 * parts - 1),
        scratch_shapes=[pltpu.VMEM(s.shape, s.dtype) for s in sources]
        + [pltpu.VMEM((all_members, total), F32), pltpu.SemaphoreType.DMA((len(sources),))],
        compiler_params=PARAMS,
        name="analysis",
    )(
        *in_hbm(sources),
        terms,
        *from_partners(terms),
        forecast,
        *from_partners(forecast),
        *others_delayed,
    )
    return out.reshape(members, 1 + lagged, fields, height, width)


def solution(mesh):
    return jax.shard_map(
        shards,
        mesh=mesh,
        in_specs=(
            P("mem", None, "slab", None),
            P("mem", None, None, "slab", None),
            P("slab", None),
            P(None, "slab", None),
            P(),
            P(),
            P(),
            P(),
            P(),
            P(),
        ),
        out_specs=P("mem", None, None, "slab", None),
        check_vma=False,
    )
```

```python
import functools

import jax
import jax.numpy as jnp
from jax import lax
from jax.experimental import pallas as pl
from jax.experimental.pallas import tpu as pltpu
from jax.sharding import PartitionSpec as P

LANES = 128
F32 = jnp.float32
BF16 = jnp.bfloat16
HIGHEST = lax.Precision.HIGHEST
PARAMS = pltpu.CompilerParams(vmem_limit_bytes=48 * 1024 * 1024)


def rows_of(array):
    return array.reshape(-1, LANES)


def in_hbm(arrays):
    return [pltpu.with_memory_space_constraint(array, pltpu.HBM) for array in arrays]


def shape_of(shape, dtype=F32):
    return jax.ShapeDtypeStruct(shape, dtype)


def split_two(x):
    high = x.astype(BF16)
    low = (x - high.astype(F32)).astype(BF16)
    return high, low


def split_three(x):
    high = x.astype(BF16)
    rest = x - high.astype(F32)
    middle = rest.astype(BF16)
    low = (rest - middle.astype(F32)).astype(BF16)
    return high, middle, low


def line(ref, start, chunks):
    return jnp.concatenate([ref[start + c : start + c + 1, :] for c in range(chunks)], axis=1)


def stacked_planes(ref, members, fields, chunks):
    return jnp.concatenate(
        [
            jnp.concatenate(
                [
                    ref[pl.ds(f * chunks + c, members, stride=fields * chunks), :]
                    for c in range(chunks)
                ],
                axis=1,
            )
            for f in range(fields)
        ],
        axis=0,
    )


def at_once(sources, targets, sems):
    copies = [
        pltpu.make_async_copy(source, target, sems.at[i])
        for i, (source, target) in enumerate(zip(sources, targets))
    ]
    for copy in copies:
        copy.start()
    return copies


def picked_values(planes, taps):
    high, middle, low = (
        jnp.dot(part, taps, preferred_element_type=F32) for part in split_three(planes)
    )
    return low + middle + high


def coefficient_kernel(chunks, *refs):
    sources, (coefs_ref,), scratch, sems = refs[:2], refs[2:3], refs[3:5], refs[5]
    for copy in at_once(sources, scratch, sems):
        copy.wait()
    spread = line(scratch[0], 0, chunks)
    half = line(scratch[1], 0, chunks) * 0.5
    coefs_ref[0:1, :] = spread + half
    coefs_ref[1:2, :] = spread - half


def own_row_kernel(members, fields, chunks, *refs):
    sources, (part_ref, here_ref, taps_ref, kinds_ref, obs_ref), scratch = (
        refs[:6],
        refs[6:11],
        refs[11:17],
    )
    for copy in at_once(sources, scratch, refs[17]):
        copy.wait()
    present, spread_ref, ratio_ref, row_ref, col_ref, field_ref = scratch
    width = chunks * LANES
    spread = line(spread_ref, 0, chunks)
    along_columns = line(ratio_ref, chunks, chunks)
    here = stacked_planes(present, members, fields, chunks)
    here_ref[...] = here
    lane = lax.broadcasted_iota(jnp.int32, here.shape, 1)
    left = jnp.where(lane == 0, 0.0, pltpu.roll(here, 1, 1))
    right = jnp.where(lane == width - 1, 0.0, pltpu.roll(here, width - 1, 1))
    part = here + spread * (right + left - 4.0 * here) - along_columns * (right - left) * 0.5
    part_ref[...] = part

    batches, count = row_ref.shape
    total = batches * count
    flat = lambda ref: jnp.concatenate([ref[b : b + 1, :] for b in range(batches)], axis=1)
    rows, cols, kinds = flat(row_ref), flat(col_ref), flat(field_ref)
    own_row = lax.axis_index("slab")
    seen = jnp.where(rows == own_row, kinds, -1)
    kinds_ref[0:1, :] = jnp.where(rows == own_row + 1, kinds, -1)
    kinds_ref[1:2, :] = jnp.where(rows == own_row - 1, kinds, -1)
    at = lax.broadcasted_iota(jnp.int32, (width, total), 0).astype(F32) * 0.25
    taps = jnp.maximum(0.5 - jnp.abs(at - cols.astype(F32) * 0.25), 0.0).astype(BF16)
    taps_ref[...] = taps
    picked = picked_values(part, taps)
    observed = jnp.zeros((members, total), F32)
    for f in range(fields):
        observed += jnp.where(seen == f, picked[f * members : (f + 1) * members], 0.0)
    obs_ref[...] = observed


def observe_kernel(
    members,
    fields,
    inner_ref,
    outer_ref,
    part_obs_ref,
    here_ref,
    taps_ref,
    kinds_ref,
    keep_ref,
    send_ref,
    again_ref,
):
    even = lax.rem(lax.axis_index("slab"), 2) == 0
    here = here_ref[...]
    again_ref[...] = here
    below = jnp.where(even, inner_ref[0:1, :], outer_ref[0:1, :])
    above = jnp.where(even, outer_ref[1:2, :], inner_ref[1:2, :])
    picked = picked_values(
        jnp.concatenate([below * here, above * here], axis=0), taps_ref[...]
    )
    observed = part_obs_ref[...]
    for side in range(2):
        kinds = kinds_ref[side : side + 1, :]
        for f in range(fields):
            start = (side * fields + f) * members
            observed += jnp.where(kinds == f, picked[start : start + members], 0.0)
    half = observed.shape[1] // 2
    first, second = observed[:, :half], observed[:, half:]
    keep_ref[...] = jnp.where(even, first, second)
    send_ref[...] = jnp.where(even, second, first)


def complete_kernel(part_ref, inner_ref, outer_ref, coefs_ref, forecast_ref):
    even = lax.rem(lax.axis_index("slab"), 2) == 0
    inner, outer = inner_ref[...], outer_ref[...]
    above, below = coefs_ref[0:1, :], coefs_ref[1:2, :]
    forecast_ref[...] = (
        part_ref[...]
        + jnp.where(even, below, above) * inner
        + jnp.where(even, above, below) * outer
    )


def solve_transposed(system, right_t, floor):
    size = system.shape[0]
    eye = (
        lax.broadcasted_iota(jnp.int32, (size, size), 0)
        == lax.broadcasted_iota(jnp.int32, (size, size), 1)
    ).astype(F32)
    top = jnp.max(jnp.sum(jnp.abs(system), axis=0, keepdims=True)) + 1.0
    scale = 2.0 / (top + floor)
    eps = (top - floor) / (top + floor)
    residual = eye - scale * system
    answer = scale * right_t

    def more(carry):
        return carry[0] > 1e-6

    def double(carry):
        eps, residual, answer = carry
        both = jnp.dot(
            jnp.concatenate([residual, answer], axis=0),
            residual,
            precision=HIGHEST,
            preferred_element_type=F32,
        )
        square = eps * eps
        share = 1.0 / (2.0 - square)
        return (
            square * share,
            (2.0 * both[:size] - square * eye) * share,
            (answer + both[size:]) * (2.0 * share),
        )

    return lax.while_loop(more, double, (eps, residual, answer))[2]


def solve_kernel(parts, *refs):
    sources, priors, mine_ref = refs[:3], refs[3 : 3 + 2 * parts], refs[3 + 2 * parts]
    value_ref, error_ref, noise_ref, prior, sems = refs[4 + 2 * parts :]
    copies = at_once(sources, (value_ref, error_ref, noise_ref), sems)
    batches, members, count = noise_ref.shape
    local = members // parts
    own = lax.axis_index("mem")
    even = lax.rem(lax.axis_index("slab"), 2) == 0
    half = batches * count // 2
    for d in range(parts):
        owner = lax.rem(own + d, parts)
        rows = pl.ds(pl.multiple_of(owner * local, local), local)
        kept, received = priors[d][...], priors[parts + d][...]
        prior[rows, :half] = jnp.where(even, kept, received)
        prior[rows, half:] = jnp.where(even, received, kept)
    for copy in copies:
        copy.wait()
    eye = (
        lax.broadcasted_iota(jnp.int32, (members, members), 0)
        == lax.broadcasted_iota(jnp.int32, (members, members), 1)
    ).astype(F32)
    product_t = None
    nt = (((1,), (1,)), ((), ()))
    for b in range(batches):
        observed = prior[:, b * count : (b + 1) * count]
        if product_t is not None:
            observed = jnp.dot(
                product_t, observed, precision=HIGHEST, preferred_element_type=F32
            )
        errors = error_ref[b : b + 1, :]
        scaled = (observed - jnp.mean(observed, axis=0, keepdims=True)) / errors
        innovation = (value_ref[b : b + 1, :] - observed) / errors + noise_ref[b]
        both = lax.dot_general(
            jnp.concatenate([scaled, innovation], axis=0),
            scaled,
            nt,
            precision=HIGHEST,
            preferred_element_type=F32,
        )
        system = both[:members] + (members - 1.0) * eye
        weights_t = solve_transposed(system, both[members:], members - 1.0)
        matrix_t = eye + weights_t - jnp.mean(weights_t, axis=1, keepdims=True)
        if product_t is None:
            product_t = matrix_t
        else:
            product_t = jnp.dot(
                matrix_t, product_t, precision=HIGHEST, preferred_element_type=F32
            )

    is_own = (
        lax.broadcasted_iota(jnp.int32, (local, members), 0) + own * local
        == lax.broadcasted_iota(jnp.int32, (local, members), 1)
    ).astype(F32)
    mine = jnp.dot(is_own, product_t, precision=HIGHEST, preferred_element_type=F32)
    source = lax.broadcasted_iota(jnp.int32, (members, members), 0)
    target = lax.broadcasted_iota(jnp.int32, (members, members), 1)
    turn = (source == lax.rem(target + own * local, members)).astype(F32)
    mine_ref[...] = jnp.dot(mine, turn, precision=HIGHEST, preferred_element_type=F32)


def combine_kernel(parts, fields, mine_ref, *refs):
    forecast_refs, delayed_refs, out_ref = refs[:parts], refs[parts : 2 * parts], refs[2 * parts]
    local = mine_ref.shape[0]
    high, low = split_two(mine_ref[...])
    left = jnp.concatenate([high, high, low], axis=1)
    chunks = forecast_refs[0].shape[1] // LANES
    lagged = delayed_refs[0].shape[0] // local
    planes = fields * chunks + lagged
    for start in range(0, planes, chunks):
        if start < fields * chunks:
            f = start // chunks
            held = [ref[f * local : (f + 1) * local, :] for ref in forecast_refs]
        else:
            first = start - fields * chunks
            held = [
                jnp.concatenate(
                    [ref[pl.ds(first + c, local, stride=lagged), :] for c in range(chunks)],
                    axis=1,
                )
                for ref in delayed_refs
            ]
        held_high, held_low = split_two(jnp.concatenate(held, axis=0))
        result = jnp.dot(
            left,
            jnp.concatenate([held_high, held_low, held_high], axis=0),
            preferred_element_type=F32,
        )
        for c in range(chunks):
            out_ref[pl.ds(start + c, local, stride=planes), :] = result[
                :, c * LANES : (c + 1) * LANES
            ]


def shards(
    present_ensemble,
    delayed_ensemble,
    spreading_coefficient,
    transport_ratios,
    obs_value,
    obs_error,
    obs_noise,
    obs_row,
    obs_col,
    obs_field,
):
    members, fields, height, width = present_ensemble.shape
    assert height == 1 and width % LANES == 0
    chunks = width // LANES
    lagged = delayed_ensemble.shape[1]
    slabs, parts = lax.axis_size("slab"), lax.axis_size("mem")
    assert slabs & (slabs - 1) == 0
    batches, all_members, count = obs_noise.shape
    total = batches * count
    planes = (1 + lagged) * fields * chunks
    stacked = (fields * members, width)
    hbm = pl.BlockSpec(memory_space=pltpu.HBM)
    vmem = pl.BlockSpec(memory_space=pltpu.VMEM)

    def landing(sources):
        return [pltpu.VMEM(s.shape, s.dtype) for s in sources], pltpu.SemaphoreType.DMA(
            (len(sources),)
        )

    def from_partners(array):
        return [
            lax.ppermute(array, "mem", [((i + d) % parts, i) for i in range(parts)])
            for d in range(1, parts)
        ]

    def from_slab(array, bit):
        return lax.ppermute(array, "slab", [(i, i ^ bit) for i in range(slabs)])

    outer_pairs = [(i, i + 1) for i in range(1, slabs - 1, 2)]
    outer_pairs += [(j, i) for i, j in outer_pairs]

    def from_rows(array):
        outer = lax.ppermute(array, "slab", outer_pairs)
        return from_slab(array, 1), outer

    present, delayed = rows_of(present_ensemble), rows_of(delayed_ensemble)
    spread, ratios = rows_of(spreading_coefficient), rows_of(transport_ratios)
    sources = in_hbm((spread, ratios))
    buffers, sems = landing(sources)
    coefs = pl.pallas_call(
        functools.partial(coefficient_kernel, chunks),
        out_shape=shape_of((2, width)),
        in_specs=[hbm] * len(sources),
        scratch_shapes=[*buffers, sems],
        compiler_params=PARAMS,
        name="coefficients",
    )(*sources)
    inner_coefs, outer_coefs = from_rows(coefs)
    sources = in_hbm((present, spread, ratios, obs_row, obs_col, obs_field))
    buffers, sems = landing(sources)
    part, here, taps, kinds, part_obs = pl.pallas_call(
        functools.partial(own_row_kernel, members, fields, chunks),
        out_shape=(
            shape_of(stacked),
            shape_of(stacked),
            shape_of((width, total), BF16),
            shape_of((2, total), jnp.int32),
            shape_of((members, total)),
        ),
        in_specs=[hbm] * len(sources),
        scratch_shapes=[*buffers, sems],
        compiler_params=PARAMS,
        name="own_row",
    )(*sources)
    others_delayed = from_partners(delayed)
    keep, send, again = pl.pallas_call(
        functools.partial(observe_kernel, members, fields),
        out_shape=(
            shape_of((members, total // 2)),
            shape_of((members, total // 2)),
            shape_of(stacked),
        ),
        compiler_params=PARAMS,
        name="observe",
    )(inner_coefs, outer_coefs, part_obs, here, taps, kinds)

    terms = keep + from_slab(send, 1)
    inner_row, outer_row = from_rows(again)
    forecast = pl.pallas_call(
        complete_kernel,
        out_shape=shape_of(stacked),
        compiler_params=PARAMS,
        name="complete",
    )(part, inner_row, outer_row, coefs)
    bit = 2
    while bit < slabs:
        terms = terms + from_slab(terms, bit)
        bit *= 2
    priors = [terms, *from_partners(terms)]
    if parts == 2:
        gathered = from_slab(jnp.concatenate(priors, axis=0), 1)
        priors += [gathered[d * members : (d + 1) * members] for d in range(parts)]
    else:
        priors += [from_slab(prior, 1) for prior in priors]
    sources = in_hbm((obs_value, obs_error, obs_noise))
    buffers, sems = landing(sources)
    mine = pl.pallas_call(
        functools.partial(solve_kernel, parts),
        out_shape=shape_of((members, all_members)),
        in_specs=[hbm] * len(sources) + [vmem] * len(priors),
        scratch_shapes=[*buffers, pltpu.VMEM((all_members, total), F32), sems],
        compiler_params=PARAMS,
        name="solve",
    )(*sources, *priors)
    out = pl.pallas_call(
        functools.partial(combine_kernel, parts, fields),
        out_shape=shape_of((members * planes, LANES)),
        compiler_params=PARAMS,
        name="combine",
    )(mine, forecast, *from_partners(forecast), delayed, *others_delayed)
    return out.reshape(members, 1 + lagged, fields, height, width)


def solution(mesh):
    return jax.shard_map(
        shards,
        mesh=mesh,
        in_specs=(
            P("mem", None, "slab", None),
            P("mem", None, None, "slab", None),
            P("slab", None),
            P(None, "slab", None),
            P(),
            P(),
            P(),
            P(),
            P(),
            P(),
        ),
        out_specs=P("mem", None, None, "slab", None),
        check_vma=False,
    )
```

```python
import functools

import jax
import jax.numpy as jnp
from jax import lax
from jax.experimental import pallas as pl
from jax.experimental.pallas import tpu as pltpu
from jax.sharding import PartitionSpec as P

LANES = 128
F32 = jnp.float32
BF16 = jnp.bfloat16
HIGHEST = lax.Precision.HIGHEST
PARAMS = pltpu.CompilerParams(vmem_limit_bytes=48 * 1024 * 1024)


OWN_FLOPS, SUM_FLOPS, GATHER_FLOPS, SOLVE_FLOPS = 10**11, 5*10**8, 10**9, 2*10**9


def estimate(flops):
    return pl.CostEstimate(flops=flops, transcendentals=0, bytes_accessed=0)


def rows_of(array):
    return array.reshape(-1, LANES)


def in_hbm(arrays):
    return [pltpu.with_memory_space_constraint(array, pltpu.HBM) for array in arrays]


def shape_of(shape, dtype=F32):
    return jax.ShapeDtypeStruct(shape, dtype)


def split_two(x):
    high = x.astype(BF16)
    low = (x - high.astype(F32)).astype(BF16)
    return high, low


def split_three(x):
    high = x.astype(BF16)
    rest = x - high.astype(F32)
    middle = rest.astype(BF16)
    low = (rest - middle.astype(F32)).astype(BF16)
    return high, middle, low


def line(ref, start, chunks):
    return jnp.concatenate([ref[start + c : start + c + 1, :] for c in range(chunks)], axis=1)


def stacked_planes(ref, members, fields, chunks):
    return jnp.concatenate(
        [
            jnp.concatenate(
                [
                    ref[pl.ds(f * chunks + c, members, stride=fields * chunks), :]
                    for c in range(chunks)
                ],
                axis=1,
            )
            for f in range(fields)
        ],
        axis=0,
    )


def at_once(sources, targets, sems):
    copies = [
        pltpu.make_async_copy(source, target, sems.at[i])
        for i, (source, target) in enumerate(zip(sources, targets))
    ]
    for copy in copies:
        copy.start()
    return copies


def picked_values(planes, taps):
    high, middle, low = (
        jnp.dot(part, taps, preferred_element_type=F32) for part in split_three(planes)
    )
    return low + middle + high


def coefficient_kernel(chunks, *refs):
    sources, (coefs_ref,), scratch, sems = refs[:2], refs[2:3], refs[3:5], refs[5]
    for copy in at_once(sources, scratch, sems):
        copy.wait()
    spread = line(scratch[0], 0, chunks)
    half = line(scratch[1], 0, chunks) * 0.5
    coefs_ref[0:1, :] = spread + half
    coefs_ref[1:2, :] = spread - half


def own_row_kernel(members, fields, chunks, *refs):
    sources, (part_ref, here_ref, taps_ref, kinds_ref, obs_ref), scratch = (
        refs[:6],
        refs[6:11],
        refs[11:17],
    )
    for copy in at_once(sources, scratch, refs[17]):
        copy.wait()
    present, spread_ref, ratio_ref, row_ref, col_ref, field_ref = scratch
    width = chunks * LANES
    spread = line(spread_ref, 0, chunks)
    along_columns = line(ratio_ref, chunks, chunks)
    here = stacked_planes(present, members, fields, chunks)
    here_ref[...] = here
    lane = lax.broadcasted_iota(jnp.int32, here.shape, 1)
    left = jnp.where(lane == 0, 0.0, pltpu.roll(here, 1, 1))
    right = jnp.where(lane == width - 1, 0.0, pltpu.roll(here, width - 1, 1))
    part = here + spread * (right + left - 4.0 * here) - along_columns * (right - left) * 0.5
    part_ref[...] = part

    batches, count = row_ref.shape
    total = batches * count
    flat = lambda ref: jnp.concatenate([ref[b : b + 1, :] for b in range(batches)], axis=1)
    rows, cols, kinds = flat(row_ref), flat(col_ref), flat(field_ref)
    own_row = lax.axis_index("slab")
    seen = jnp.where(rows == own_row, kinds, -1)
    kinds_ref[0:1, :] = jnp.where(rows == own_row + 1, kinds, -1)
    kinds_ref[1:2, :] = jnp.where(rows == own_row - 1, kinds, -1)
    at = lax.broadcasted_iota(jnp.int32, (width, total), 0).astype(F32) * 0.25
    taps = jnp.maximum(0.5 - jnp.abs(at - cols.astype(F32) * 0.25), 0.0).astype(BF16)
    taps_ref[...] = taps
    picked = picked_values(part, taps)
    observed = jnp.zeros((members, total), F32)
    for f in range(fields):
        observed += jnp.where(seen == f, picked[f * members : (f + 1) * members], 0.0)
    obs_ref[...] = observed


def observe_kernel(
    members,
    fields,
    inner_ref,
    outer_ref,
    part_obs_ref,
    here_ref,
    taps_ref,
    kinds_ref,
    keep_ref,
    send_ref,
):
    even = lax.rem(lax.axis_index("slab"), 2) == 0
    here = here_ref[...]
    below = jnp.where(even, inner_ref[0:1, :], outer_ref[0:1, :])
    above = jnp.where(even, outer_ref[1:2, :], inner_ref[1:2, :])
    picked = picked_values(
        jnp.concatenate([below * here, above * here], axis=0), taps_ref[...]
    )
    observed = part_obs_ref[...]
    for side in range(2):
        kinds = kinds_ref[side : side + 1, :]
        for f in range(fields):
            start = (side * fields + f) * members
            observed += jnp.where(kinds == f, picked[start : start + members], 0.0)
    half = observed.shape[1] // 2
    first, second = observed[:, :half], observed[:, half:]
    keep_ref[...] = jnp.where(even, first, second)
    send_ref[...] = jnp.where(even, second, first)


def sum_kernel(terms_ref, other_ref, sum_ref):
    sum_ref[...] = terms_ref[...] + other_ref[...]


def complete_kernel(part_ref, inner_ref, outer_ref, coefs_ref, _, forecast_ref):
    even = lax.rem(lax.axis_index("slab"), 2) == 0
    above, below = coefs_ref[0:1, :], coefs_ref[1:2, :]
    forecast_ref[...] = (
        part_ref[...]
        + jnp.where(even, below, above) * inner_ref[...]
        + jnp.where(even, above, below) * outer_ref[...]
    )


def gather_kernel(*refs):
    local = refs[0].shape[0]
    for d, ref in enumerate(refs[:-1]):
        refs[-1][d * local : (d + 1) * local, :] = ref[...]


def solve_transposed(system, right_t, floor):
    size = system.shape[0]
    eye = (
        lax.broadcasted_iota(jnp.int32, (size, size), 0)
        == lax.broadcasted_iota(jnp.int32, (size, size), 1)
    ).astype(F32)
    top = jnp.max(jnp.sum(jnp.abs(system), axis=0, keepdims=True)) + 1.0
    scale = 2.0 / (top + floor)
    eps = (top - floor) / (top + floor)
    residual = eye - scale * system
    answer = scale * right_t

    def more(carry):
        return carry[0] > 1e-6

    def double(carry):
        eps, residual, answer = carry
        both = jnp.dot(
            jnp.concatenate([residual, answer], axis=0),
            residual,
            precision=HIGHEST,
            preferred_element_type=F32,
        )
        square = eps * eps
        share = 1.0 / (2.0 - square)
        return (
            square * share,
            (2.0 * both[:size] - square * eye) * share,
            (answer + both[size:]) * (2.0 * share),
        )

    return lax.while_loop(more, double, (eps, residual, answer))[2]


def solve_kernel(parts, *refs):
    sources, kept_ref, received_ref, mine_ref = refs[:3], refs[3], refs[4], refs[5]
    value_ref, error_ref, noise_ref, prior, sems = refs[6:]
    copies = at_once(sources, (value_ref, error_ref, noise_ref), sems)
    batches, members, count = noise_ref.shape
    local = members // parts
    own = lax.axis_index("mem")
    even = lax.rem(lax.axis_index("slab"), 2) == 0
    half = batches * count // 2
    for d in range(parts):
        owner = lax.rem(own + d, parts)
        rows = pl.ds(pl.multiple_of(owner * local, local), local)
        kept = kept_ref[d * local : (d + 1) * local, :]
        received = received_ref[d * local : (d + 1) * local, :]
        prior[rows, :half] = jnp.where(even, kept, received)
        prior[rows, half:] = jnp.where(even, received, kept)
    for copy in copies:
        copy.wait()
    eye = (
        lax.broadcasted_iota(jnp.int32, (members, members), 0)
        == lax.broadcasted_iota(jnp.int32, (members, members), 1)
    ).astype(F32)
    product_t = None
    nt = (((1,), (1,)), ((), ()))
    for b in range(batches):
        observed = prior[:, b * count : (b + 1) * count]
        if product_t is not None:
            observed = jnp.dot(
                product_t, observed, precision=HIGHEST, preferred_element_type=F32
            )
        errors = error_ref[b : b + 1, :]
        scaled = (observed - jnp.mean(observed, axis=0, keepdims=True)) / errors
        innovation = (value_ref[b : b + 1, :] - observed) / errors + noise_ref[b]
        both = lax.dot_general(
            jnp.concatenate([scaled, innovation], axis=0),
            scaled,
            nt,
            precision=HIGHEST,
            preferred_element_type=F32,
        )
        system = both[:members] + (members - 1.0) * eye
        weights_t = solve_transposed(system, both[members:], members - 1.0)
        matrix_t = eye + weights_t - jnp.mean(weights_t, axis=1, keepdims=True)
        if product_t is None:
            product_t = matrix_t
        else:
            product_t = jnp.dot(
                matrix_t, product_t, precision=HIGHEST, preferred_element_type=F32
            )

    is_own = (
        lax.broadcasted_iota(jnp.int32, (local, members), 0) + own * local
        == lax.broadcasted_iota(jnp.int32, (local, members), 1)
    ).astype(F32)
    mine = jnp.dot(is_own, product_t, precision=HIGHEST, preferred_element_type=F32)
    source = lax.broadcasted_iota(jnp.int32, (members, members), 0)
    target = lax.broadcasted_iota(jnp.int32, (members, members), 1)
    turn = (source == lax.rem(target + own * local, members)).astype(F32)
    mine_ref[...] = jnp.dot(mine, turn, precision=HIGHEST, preferred_element_type=F32)


def combine_kernel(parts, fields, mine_ref, *refs):
    forecast_refs, delayed_refs, out_ref = refs[:parts], refs[parts : 2 * parts], refs[2 * parts]
    local = mine_ref.shape[0]
    high, low = split_two(mine_ref[...])
    left = jnp.concatenate([high, high, low], axis=1)
    chunks = forecast_refs[0].shape[1] // LANES
    lagged = delayed_refs[0].shape[0] // local
    planes = fields * chunks + lagged
    for start in range(0, planes, chunks):
        if start < fields * chunks:
            f = start // chunks
            held = [ref[f * local : (f + 1) * local, :] for ref in forecast_refs]
        else:
            first = start - fields * chunks
            held = [
                jnp.concatenate(
                    [ref[pl.ds(first + c, local, stride=lagged), :] for c in range(chunks)],
                    axis=1,
                )
                for ref in delayed_refs
            ]
        held_high, held_low = split_two(jnp.concatenate(held, axis=0))
        result = jnp.dot(
            left,
            jnp.concatenate([held_high, held_low, held_high], axis=0),
            preferred_element_type=F32,
        )
        for c in range(chunks):
            out_ref[pl.ds(start + c, local, stride=planes), :] = result[
                :, c * LANES : (c + 1) * LANES
            ]


def shards(
    present_ensemble,
    delayed_ensemble,
    spreading_coefficient,
    transport_ratios,
    obs_value,
    obs_error,
    obs_noise,
    obs_row,
    obs_col,
    obs_field,
):
    members, fields, height, width = present_ensemble.shape
    assert height == 1 and width % LANES == 0
    chunks = width // LANES
    lagged = delayed_ensemble.shape[1]
    slabs, parts = lax.axis_size("slab"), lax.axis_size("mem")
    assert slabs & (slabs - 1) == 0 and slabs >= 8
    batches, all_members, count = obs_noise.shape
    total = batches * count
    planes = (1 + lagged) * fields * chunks
    stacked = (fields * members, width)
    hbm = pl.BlockSpec(memory_space=pltpu.HBM)
    vmem = pl.BlockSpec(memory_space=pltpu.VMEM)

    def landing(sources):
        return [pltpu.VMEM(s.shape, s.dtype) for s in sources], pltpu.SemaphoreType.DMA(
            (len(sources),)
        )

    def from_partners(array):
        return [
            lax.ppermute(array, "mem", [((i + d) % parts, i) for i in range(parts)])
            for d in range(1, parts)
        ]

    def from_slab(array, bit):
        return lax.ppermute(array, "slab", [(i, i ^ bit) for i in range(slabs)])

    outer_pairs = [(i, i + 1) for i in range(1, slabs - 1, 2)]
    outer_pairs += [(j, i) for i, j in outer_pairs]

    present, delayed = rows_of(present_ensemble), rows_of(delayed_ensemble)
    spread, ratios = rows_of(spreading_coefficient), rows_of(transport_ratios)
    sources = in_hbm((spread, ratios))
    buffers, sems = landing(sources)
    coefs = pl.pallas_call(
        functools.partial(coefficient_kernel, chunks),
        out_shape=shape_of((2, width)),
        in_specs=[hbm] * len(sources),
        scratch_shapes=[*buffers, sems],
        compiler_params=PARAMS,
        name="coefficients",
    )(*sources)
    outer_coefs = lax.ppermute(coefs, "slab", outer_pairs)
    inner_coefs = from_slab(coefs, 1)
    sources = in_hbm((present, spread, ratios, obs_row, obs_col, obs_field))
    buffers, sems = landing(sources)
    part, here, taps, kinds, part_obs = pl.pallas_call(
        functools.partial(own_row_kernel, members, fields, chunks),
        out_shape=(
            shape_of(stacked),
            shape_of(stacked),
            shape_of((width, total), BF16),
            shape_of((2, total), jnp.int32),
            shape_of((members, total)),
        ),
        in_specs=[hbm] * len(sources),
        scratch_shapes=[*buffers, sems],
        compiler_params=PARAMS,
        cost_estimate=estimate(OWN_FLOPS),
        name="own_row",
    )(*sources)
    others_delayed = from_partners(lax.optimization_barrier((delayed, coefs))[0])
    keep, send = pl.pallas_call(
        functools.partial(observe_kernel, members, fields),
        out_shape=(
            shape_of((members, total // 2)),
            shape_of((members, total // 2)),
        ),
        compiler_params=PARAMS,
        name="observe",
    )(inner_coefs, outer_coefs, part_obs, here, taps, kinds)

    def summed(terms, bit, flops):
        return pl.pallas_call(
            sum_kernel,
            out_shape=shape_of(terms.shape),
            cost_estimate=estimate(flops),
            compiler_params=PARAMS,
            name="sum",
        )(terms, from_slab(terms, bit))

    terms = keep + from_slab(send, 1)
    here, _ = lax.optimization_barrier((here, terms))
    outer_row = lax.ppermute(here, "slab", outer_pairs)
    inner_row = from_slab(here, 1)
    forecast = pl.pallas_call(
        complete_kernel, out_shape=shape_of(stacked), compiler_params=PARAMS, name="complete"
    )(part, inner_row, outer_row, coefs, others_delayed[0])
    bit = slabs // 2
    while bit > 1:
        terms = summed(terms, bit, SUM_FLOPS)
        bit //= 2
    priors = pl.pallas_call(
        gather_kernel,
        out_shape=shape_of((all_members, total // 2)),
        cost_estimate=estimate(GATHER_FLOPS),
        compiler_params=PARAMS,
        name="gather",
    )(terms, *from_partners(terms))
    priors = [priors, from_slab(priors, 1)]
    sources = in_hbm((obs_value, obs_error, obs_noise))
    buffers, sems = landing(sources)
    mine = pl.pallas_call(
        functools.partial(solve_kernel, parts),
        out_shape=shape_of((members, all_members)),
        in_specs=[hbm] * len(sources) + [vmem] * 2,
        scratch_shapes=[*buffers, pltpu.VMEM((all_members, total), F32), sems],
        compiler_params=PARAMS,
        cost_estimate=estimate(SOLVE_FLOPS),
        name="solve",
    )(*sources, *priors)
    out = pl.pallas_call(
        functools.partial(combine_kernel, parts, fields),
        out_shape=shape_of((members * planes, LANES)),
        compiler_params=PARAMS,
        name="combine",
    )(mine, forecast, *from_partners(forecast), delayed, *others_delayed)
    return out.reshape(members, 1 + lagged, fields, height, width)


def solution(mesh):
    return jax.shard_map(
        shards,
        mesh=mesh,
        in_specs=(
            P("mem", None, "slab", None),
            P("mem", None, None, "slab", None),
            P("slab", None),
            P(None, "slab", None),
            P(),
            P(),
            P(),
            P(),
            P(),
            P(),
        ),
        out_specs=P("mem", None, None, "slab", None),
        check_vma=False,
    )
```

```python
import functools

import jax
import jax.numpy as jnp
from jax import lax
from jax.experimental import pallas as pl
from jax.experimental.pallas import tpu as pltpu
from jax.sharding import PartitionSpec as P

LANES = 128
F32 = jnp.float32
BF16 = jnp.bfloat16
HIGHEST = lax.Precision.HIGHEST
PARAMS = pltpu.CompilerParams(vmem_limit_bytes=48 * 1024 * 1024)


OWN_FLOPS, SUM_FLOPS, GATHER_FLOPS, SOLVE_FLOPS = 10**11, 7*10**8, 10**9, 2*10**9


def estimate(flops):
    return pl.CostEstimate(flops=flops, transcendentals=0, bytes_accessed=0)


def rows_of(array):
    return array.reshape(-1, LANES)


def in_hbm(arrays):
    return [pltpu.with_memory_space_constraint(array, pltpu.HBM) for array in arrays]


def shape_of(shape, dtype=F32):
    return jax.ShapeDtypeStruct(shape, dtype)


def split_two(x):
    high = x.astype(BF16)
    low = (x - high.astype(F32)).astype(BF16)
    return high, low


def split_three(x):
    high = x.astype(BF16)
    rest = x - high.astype(F32)
    middle = rest.astype(BF16)
    low = (rest - middle.astype(F32)).astype(BF16)
    return high, middle, low


def line(ref, start, chunks):
    return jnp.concatenate([ref[start + c : start + c + 1, :] for c in range(chunks)], axis=1)


def stacked_planes(ref, members, fields, chunks):
    return jnp.concatenate(
        [
            jnp.concatenate(
                [
                    ref[pl.ds(f * chunks + c, members, stride=fields * chunks), :]
                    for c in range(chunks)
                ],
                axis=1,
            )
            for f in range(fields)
        ],
        axis=0,
    )


def at_once(sources, targets, sems):
    copies = [
        pltpu.make_async_copy(source, target, sems.at[i])
        for i, (source, target) in enumerate(zip(sources, targets))
    ]
    for copy in copies:
        copy.start()
    return copies


def picked_values(planes, taps):
    high, middle, low = (
        jnp.dot(part, taps, preferred_element_type=F32) for part in split_three(planes)
    )
    return low + middle + high


def load_kernel(chunks, *refs):
    count = (len(refs) - 2) // 2
    sources, held, packed_ref, coefs_ref, sems = refs[:count], refs[count:-3], *refs[-3:]
    rows = sources[0].shape[0]
    copies = at_once(sources, (packed_ref.at[:rows], *held), sems)
    copies[1].wait()
    copies[2].wait()
    spread = held[0][...]
    half = held[1][:chunks, :] * 0.5
    for ref, start in ((packed_ref, rows), (coefs_ref, 0)):
        ref[start : start + chunks, :] = spread + half
        ref[start + chunks : start + 2 * chunks, :] = spread - half
    for copy in (copies[0], *copies[3:]):
        copy.wait()


def own_row_kernel(
    members,
    fields,
    chunks,
    present_ref,
    spread_ref,
    ratio_ref,
    row_ref,
    col_ref,
    field_ref,
    part_ref,
    here_ref,
    taps_ref,
    kinds_ref,
    obs_ref,
):
    width = chunks * LANES
    spread = line(spread_ref, 0, chunks)
    along_columns = line(ratio_ref, chunks, chunks)
    here = stacked_planes(present_ref, members, fields, chunks)
    here_ref[...] = here
    lane = lax.broadcasted_iota(jnp.int32, here.shape, 1)
    left = jnp.where(lane == 0, 0.0, pltpu.roll(here, 1, 1))
    right = jnp.where(lane == width - 1, 0.0, pltpu.roll(here, width - 1, 1))
    part = here + spread * (right + left - 4.0 * here) - along_columns * (right - left) * 0.5
    part_ref[...] = part

    batches, count = row_ref.shape
    total = batches * count
    flat = lambda ref: jnp.concatenate([ref[b : b + 1, :] for b in range(batches)], axis=1)
    rows, cols, kinds = flat(row_ref), flat(col_ref), flat(field_ref)
    own_row = lax.axis_index("slab")
    seen = jnp.where(rows == own_row, kinds, -1)
    kinds_ref[0:1, :] = jnp.where(rows == own_row + 1, kinds, -1)
    kinds_ref[1:2, :] = jnp.where(rows == own_row - 1, kinds, -1)
    at = lax.broadcasted_iota(jnp.int32, (width, total), 0).astype(F32) * 0.25
    taps = jnp.maximum(0.5 - jnp.abs(at - cols.astype(F32) * 0.25), 0.0).astype(BF16)
    taps_ref[...] = taps
    picked = picked_values(part, taps)
    observed = jnp.zeros((members, total), F32)
    for f in range(fields):
        observed += jnp.where(seen == f, picked[f * members : (f + 1) * members], 0.0)
    obs_ref[...] = observed


def observe_kernel(
    members,
    fields,
    chunks,
    inner_ref,
    outer_ref,
    part_obs_ref,
    here_ref,
    taps_ref,
    kinds_ref,
    keep_ref,
    send_ref,
):
    even = lax.rem(lax.axis_index("slab"), 2) == 0
    here = here_ref[...]
    rows = members * fields * chunks
    inner_coefs = [line(inner_ref, rows + k * chunks, chunks) for k in range(2)]
    outer_coefs = [line(outer_ref, k * chunks, chunks) for k in range(2)]
    below = jnp.where(even, inner_coefs[0], outer_coefs[0])
    above = jnp.where(even, outer_coefs[1], inner_coefs[1])
    picked = picked_values(
        jnp.concatenate([below * here, above * here], axis=0), taps_ref[...]
    )
    observed = part_obs_ref[...]
    for side in range(2):
        kinds = kinds_ref[side : side + 1, :]
        for f in range(fields):
            start = (side * fields + f) * members
            observed += jnp.where(kinds == f, picked[start : start + members], 0.0)
    half = observed.shape[1] // 2
    first, second = observed[:, :half], observed[:, half:]
    keep_ref[...] = jnp.where(even, first, second)
    send_ref[...] = jnp.where(even, second, first)


def sum_kernel(terms_ref, other_ref, sum_ref):
    sum_ref[...] = terms_ref[...] + other_ref[...]


def complete_kernel(
    members, fields, chunks, part_ref, inner_ref, outer_ref, coefs_ref, _, forecast_ref
):
    even = lax.rem(lax.axis_index("slab"), 2) == 0
    above, below = line(coefs_ref, 0, chunks), line(coefs_ref, chunks, chunks)
    forecast_ref[...] = (
        part_ref[...]
        + jnp.where(even, below, above) * stacked_planes(inner_ref, members, fields, chunks)
        + jnp.where(even, above, below) * outer_ref[...]
    )


def gather_kernel(*refs):
    local = refs[0].shape[0]
    for d, ref in enumerate(refs[:-1]):
        refs[-1][d * local : (d + 1) * local, :] = ref[...]


def solve_transposed(system, right_t, floor):
    size = system.shape[0]
    eye = identity(size, size)
    top = jnp.max(jnp.sum(jnp.abs(system), axis=0, keepdims=True)) + 1.0
    scale = 2.0 / (top + floor)
    eps = (top - floor) / (top + floor)
    residual = eye - scale * system
    answer = scale * right_t

    def more(carry):
        return carry[0] > 1e-6

    def double(carry):
        eps, residual, answer = carry
        both = jnp.dot(
            jnp.concatenate([residual, answer], axis=0),
            residual,
            precision=HIGHEST,
            preferred_element_type=F32,
        )
        square = eps * eps
        share = 1.0 / (2.0 - square)
        return (
            square * share,
            (2.0 * both[:size] - square * eye) * share,
            (answer + both[size:]) * (2.0 * share),
        )

    return lax.while_loop(more, double, (eps, residual, answer))[2]


def identity(rows, columns, shift=0):
    return (
        lax.broadcasted_iota(jnp.int32, (rows, columns), 0) + shift
        == lax.broadcasted_iota(jnp.int32, (rows, columns), 1)
    ).astype(F32)


def solve_kernel(
    parts, value_ref, error_ref, noise_ref, kept_ref, received_ref, mine_ref, prior, whole
):
    batches, members, count = noise_ref.shape
    local = members // parts
    own = lax.axis_index("mem")
    own_rows = pl.ds(pl.multiple_of(own * local, local), local)
    even = lax.rem(lax.axis_index("slab"), 2) == 0
    half = batches * count // 2
    for d in range(parts):
        owner = lax.rem(own + d, parts)
        rows = pl.ds(pl.multiple_of(owner * local, local), local)
        kept = kept_ref[d * local : (d + 1) * local, :]
        received = received_ref[d * local : (d + 1) * local, :]
        prior[rows, :half] = jnp.where(even, kept, received)
        prior[rows, half:] = jnp.where(even, received, kept)
    source = lax.broadcasted_iota(jnp.int32, (members, members), 0)
    target = lax.broadcasted_iota(jnp.int32, (members, members), 1)
    turn = (source == lax.rem(target + own * local, members)).astype(F32)
    product_t = turned = None
    for b in range(batches):
        last = b == batches - 1
        observed = prior[:, b * count : (b + 1) * count]
        if product_t is not None:
            both = jnp.dot(
                product_t,
                jnp.concatenate([observed, turn], axis=1) if last else observed,
                precision=HIGHEST,
                preferred_element_type=F32,
            )
            observed, turned = both[:, :count], both[:, count:]
        share = 1.0 / error_ref[b : b + 1, :]
        scaled = (observed - jnp.mean(observed, axis=0, keepdims=True)) * share
        if last:
            whole[...] = observed
            innovation = (
                value_ref[b : b + 1, :] * share + noise_ref[b, own_rows, :]
            ) - whole[own_rows, :] * share
            eye = identity(local, members, own * local)
        else:
            innovation = (value_ref[b : b + 1, :] * share + noise_ref[b]) - observed * share
            eye = identity(members, members)
        both = lax.dot_general(
            jnp.concatenate([scaled, innovation], axis=0),
            scaled,
            (((1,), (1,)), ((), ())),
            precision=HIGHEST,
            preferred_element_type=F32,
        )
        system = both[:members] + (members - 1.0) * identity(members, members)
        weights_t = solve_transposed(system, both[members:], members - 1.0)
        matrix_t = eye + weights_t - jnp.mean(weights_t, axis=1, keepdims=True)
        if last:
            mine_ref[...] = jnp.dot(
                matrix_t,
                turn if turned is None else turned,
                precision=HIGHEST,
                preferred_element_type=F32,
            )
        elif product_t is None:
            product_t = matrix_t
        else:
            product_t = jnp.dot(
                matrix_t, product_t, precision=HIGHEST, preferred_element_type=F32
            )


def combine_kernel(parts, fields, mine_ref, *refs):
    forecast_refs, delayed_refs = refs[:parts], refs[parts : 2 * parts]
    out_ref, done_ref, sems = refs[2 * parts :]
    local = mine_ref.shape[0]
    high, low = split_two(mine_ref[...])
    left = jnp.concatenate([high, high, low], axis=1)
    chunks = forecast_refs[0].shape[1] // LANES
    level = fields * chunks
    lagged = delayed_refs[0].shape[0] // local
    planes = level + lagged
    copies = []
    for first in [*range(level, planes, level), 0]:
        for f in range(fields):
            start = first + f * chunks
            if first == 0:
                held = [ref[f * local : (f + 1) * local, :] for ref in forecast_refs]
            else:
                held = [
                    jnp.concatenate(
                        [
                            ref[pl.ds(start - level + c, local, stride=lagged), :]
                            for c in range(chunks)
                        ],
                        axis=1,
                    )
                    for ref in delayed_refs
                ]
            held_high, held_low = split_two(jnp.concatenate(held, axis=0))
            result = jnp.dot(
                left,
                jnp.concatenate([held_high, held_low, held_high], axis=0),
                preferred_element_type=F32,
            )
            for c in range(chunks):
                done_ref[pl.ds(start + c, local, stride=planes), :] = result[
                    :, c * LANES : (c + 1) * LANES
                ]
        copies.append(
            pltpu.make_async_copy(
                done_ref.reshape(local, planes, LANES).at[:, first : first + level, :],
                out_ref.at[:, first : first + level, :],
                sems.at[len(copies)],
            )
        )
        copies[-1].start()
    for copy in copies:
        copy.wait()


def shards(
    present_ensemble,
    delayed_ensemble,
    spreading_coefficient,
    transport_ratios,
    obs_value,
    obs_error,
    obs_noise,
    obs_row,
    obs_col,
    obs_field,
):
    members, fields, height, width = present_ensemble.shape
    assert height == 1 and width % LANES == 0
    chunks = width // LANES
    lagged = delayed_ensemble.shape[1]
    slabs, parts = lax.axis_size("slab"), lax.axis_size("mem")
    assert slabs & (slabs - 1) == 0 and slabs >= 8
    batches, all_members, count = obs_noise.shape
    total = batches * count
    planes = (1 + lagged) * fields * chunks
    stacked = (fields * members, width)
    hbm = pl.BlockSpec(memory_space=pltpu.HBM)

    def from_partners(array):
        return [
            lax.ppermute(array, "mem", [((i + d) % parts, i) for i in range(parts)])
            for d in range(1, parts)
        ]

    def from_slab(array, bit):
        return lax.ppermute(array, "slab", [(i, i ^ bit) for i in range(slabs)])

    outer_pairs = [(i, i + 1) for i in range(1, slabs - 1, 2)]
    outer_pairs += [(j, i) for i, j in outer_pairs]

    present, delayed = rows_of(present_ensemble), rows_of(delayed_ensemble)
    spread, ratios = rows_of(spreading_coefficient), rows_of(transport_ratios)
    sources = in_hbm((present, spread, ratios, obs_row, obs_col, obs_field))
    *held, packed, coefs = pl.pallas_call(
        functools.partial(load_kernel, chunks),
        out_shape=[shape_of(x.shape, x.dtype) for x in sources[1:]]
        + [shape_of((present.shape[0] + 2 * chunks, LANES)), shape_of((2 * chunks, LANES))],
        in_specs=[hbm] * len(sources),
        scratch_shapes=[pltpu.SemaphoreType.DMA((len(sources),))],
        compiler_params=PARAMS,
        name="load",
    )(*sources)
    outer_coefs = lax.ppermute(coefs, "slab", outer_pairs)
    inner = from_slab(packed, 1)
    part, here, taps, kinds, part_obs = pl.pallas_call(
        functools.partial(own_row_kernel, members, fields, chunks),
        out_shape=(
            shape_of(stacked),
            shape_of(stacked),
            shape_of((width, total), BF16),
            shape_of((2, total), jnp.int32),
            shape_of((members, total)),
        ),
        compiler_params=PARAMS,
        cost_estimate=estimate(OWN_FLOPS),
        name="own_row",
    )(packed, *held)
    others_delayed = from_partners(lax.optimization_barrier((delayed, coefs))[0])
    keep, send = pl.pallas_call(
        functools.partial(observe_kernel, members, fields, chunks),
        out_shape=(
            shape_of((members, total // 2)),
            shape_of((members, total // 2)),
        ),
        compiler_params=PARAMS,
        name="observe",
    )(inner, outer_coefs, part_obs, here, taps, kinds)

    def summed(terms, bit, flops):
        return pl.pallas_call(
            sum_kernel,
            out_shape=shape_of(terms.shape),
            cost_estimate=estimate(flops),
            compiler_params=PARAMS,
            name="sum",
        )(terms, from_slab(terms, bit))

    terms = keep + from_slab(send, 1)
    outer_row = lax.ppermute(
        lax.optimization_barrier((here, terms))[0], "slab", outer_pairs
    )
    order = [1 << k for k in reversed(range(1, slabs.bit_length() - 1))]
    for bit in order:
        terms = summed(terms, bit, SUM_FLOPS)
    forecast = pl.pallas_call(
        functools.partial(complete_kernel, members, fields, chunks),
        out_shape=shape_of(stacked),
        compiler_params=PARAMS,
        name="complete",
    )(part, inner, outer_row, coefs, others_delayed[0])
    priors = pl.pallas_call(
        gather_kernel,
        out_shape=shape_of((all_members, total // 2)),
        cost_estimate=estimate(GATHER_FLOPS),
        compiler_params=PARAMS,
        name="gather",
    )(terms, *from_partners(terms))
    priors = [priors, from_slab(priors, 1)]
    mine = pl.pallas_call(
        functools.partial(solve_kernel, parts),
        out_shape=shape_of((members, all_members)),
        scratch_shapes=[
            pltpu.VMEM((all_members, total), F32),
            pltpu.VMEM((all_members, count), F32),
        ],
        compiler_params=PARAMS,
        cost_estimate=estimate(SOLVE_FLOPS),
        name="solve",
    )(obs_value, obs_error, obs_noise, *priors)
    out = pl.pallas_call(
        functools.partial(combine_kernel, parts, fields),
        out_shape=shape_of((members, planes, LANES)),
        out_specs=hbm,
        scratch_shapes=[
            pltpu.VMEM((members * planes, LANES), F32),
            pltpu.SemaphoreType.DMA((1 + lagged,)),
        ],
        compiler_params=PARAMS,
        name="combine",
    )(mine, forecast, *from_partners(forecast), delayed, *others_delayed)
    return out.reshape(members, 1 + lagged, fields, height, width)


def solution(mesh):
    return jax.shard_map(
        shards,
        mesh=mesh,
        in_specs=(
            P("mem", None, "slab", None),
            P("mem", None, None, "slab", None),
            P("slab", None),
            P(None, "slab", None),
            P(),
            P(),
            P(),
            P(),
            P(),
            P(),
        ),
        out_specs=P("mem", None, None, "slab", None),
        check_vma=False,
    )
```

```python
import functools

import jax
import jax.numpy as jnp
from jax import lax
from jax.experimental import pallas as pl
from jax.experimental.pallas import tpu as pltpu
from jax.sharding import PartitionSpec as P

LANES = 128
F32 = jnp.float32
BF16 = jnp.bfloat16
HIGHEST = lax.Precision.HIGHEST
PARAMS = pltpu.CompilerParams(vmem_limit_bytes=16 * 1024 * 1024)


SELECT_FLOPS = 1
OWN_FLOPS, SUM_FLOPS, GATHER_FLOPS, SOLVE_FLOPS = 1, 10**8, 1, 10**9


def estimate(flops):
    return pl.CostEstimate(flops=flops, transcendentals=0, bytes_accessed=0)


def rows_of(array):
    return array.reshape(-1, LANES)


def in_hbm(arrays):
    return [pltpu.with_memory_space_constraint(array, pltpu.HBM) for array in arrays]


def shape_of(shape, dtype=F32):
    return jax.ShapeDtypeStruct(shape, dtype)


def split_two(x):
    high = x.astype(BF16)
    low = (x - high.astype(F32)).astype(BF16)
    return high, low


def split_three(x):
    high = x.astype(BF16)
    rest = x - high.astype(F32)
    middle = rest.astype(BF16)
    low = (rest - middle.astype(F32)).astype(BF16)
    return high, middle, low


def line(ref, start, chunks):
    return jnp.concatenate([ref[start + c : start + c + 1, :] for c in range(chunks)], axis=1)


def stacked_planes(ref, members, fields, chunks):
    return jnp.concatenate(
        [
            jnp.concatenate(
                [
                    ref[pl.ds(f * chunks + c, members, stride=fields * chunks), :]
                    for c in range(chunks)
                ],
                axis=1,
            )
            for f in range(fields)
        ],
        axis=0,
    )


def at_once(sources, targets, sems):
    copies = [
        pltpu.make_async_copy(source, target, sems.at[i])
        for i, (source, target) in enumerate(zip(sources, targets))
    ]
    for copy in copies:
        copy.start()
    return copies


def picked_values(planes, taps):
    high, middle, low = (
        jnp.dot(part, taps, preferred_element_type=F32) for part in split_three(planes)
    )
    return low + middle + high


def load_kernel(chunks, *refs):
    count = (len(refs) - 1) // 2
    sources, packed_ref, held, sems = refs[:count], refs[count], refs[count + 1 : -1], refs[-1]
    rows = sources[0].shape[0]
    copies = at_once(sources, (packed_ref.at[:rows], *held), sems)
    copies[1].wait()
    copies[2].wait()
    spread = held[0][...]
    half = held[1][:chunks, :] * 0.5
    packed_ref[rows : rows + chunks, :] = spread + half
    packed_ref[rows + chunks : rows + 2 * chunks, :] = spread - half
    for copy in (copies[0], *copies[3:]):
        copy.wait()


def weights(packed_ref, chunks):
    rows = packed_ref.shape[0] - 2 * chunks
    return line(packed_ref, rows, chunks), line(packed_ref, rows + chunks, chunks)


def selector_kernel(row_ref, col_ref, field_ref, taps_ref, kinds_ref):
    batches, count = row_ref.shape
    shape = taps_ref.shape
    flat = lambda ref: jnp.concatenate([ref[b : b + 1, :] for b in range(batches)], axis=1)
    rows, cols, kinds = flat(row_ref), flat(col_ref), flat(field_ref)
    own_row = lax.axis_index("slab")
    for k, row in enumerate((own_row, own_row - 1)):
        kinds_ref[k : k + 1, :] = jnp.where(rows == row, kinds, -1)
    at = lax.broadcasted_iota(jnp.int32, shape, 0).astype(F32) * 0.25
    taps_ref[...] = jnp.maximum(0.5 - jnp.abs(at - cols.astype(F32) * 0.25), 0.0).astype(BF16)


def own_row_kernel(
    members,
    fields,
    chunks,
    packed_ref,
    inner_ref,
    spread_ref,
    ratio_ref,
    taps_ref,
    kinds_ref,
    part_ref,
    here_ref,
    obs_ref,
):
    width = chunks * LANES
    spread = line(spread_ref, 0, chunks)
    along_columns = line(ratio_ref, chunks, chunks)
    here = stacked_planes(packed_ref, members, fields, chunks)
    here_ref[...] = here
    lane = lax.broadcasted_iota(jnp.int32, here.shape, 1)
    left = jnp.where(lane == 0, 0.0, pltpu.roll(here, 1, 1))
    right = jnp.where(lane == width - 1, 0.0, pltpu.roll(here, width - 1, 1))
    even = lax.rem(lax.axis_index("slab"), 2) == 0
    above, below = weights(packed_ref, chunks)
    part = (
        here
        + spread * (right + left - 4.0 * here)
        - along_columns * (right - left) * 0.5
        + jnp.where(even, below, above) * stacked_planes(inner_ref, members, fields, chunks)
    )
    part_ref[...] = part
    picked = picked_values(part, taps_ref[...])
    observed = jnp.zeros(obs_ref.shape, F32)
    for f in range(fields):
        observed += jnp.where(
            kinds_ref[0:1, :] == f, picked[f * members : (f + 1) * members], 0.0
        )
    obs_ref[...] = observed


def observe_kernel(
    members,
    fields,
    chunks,
    packed_ref,
    outer_ref,
    part_ref,
    part_obs_ref,
    here_ref,
    taps_ref,
    kinds_ref,
    obs_ref,
    partial_ref,
):
    above, _ = weights(packed_ref, chunks)
    _, below_of_above = weights(outer_ref, chunks)
    taken = above * stacked_planes(outer_ref, members, fields, chunks)
    given = below_of_above * here_ref[...]
    partial_ref[...] = part_ref[...] + taken
    picked = picked_values(jnp.concatenate([taken, given], axis=0), taps_ref[...])
    observed = part_obs_ref[...]
    for side in range(2):
        kinds = kinds_ref[side : side + 1, :]
        for f in range(fields):
            start = (side * fields + f) * members
            observed += jnp.where(kinds == f, picked[start : start + members], 0.0)
    obs_ref[...] = observed


def sum_kernel(terms_ref, other_ref, *refs):
    refs[-1][...] = terms_ref[...] + other_ref[...]


def complete_kernel(members, fields, chunks, partial_ref, outer_ref, packed_ref, forecast_ref):
    _, below = weights(packed_ref, chunks)
    forecast_ref[...] = partial_ref[...] + below * stacked_planes(
        outer_ref, members, fields, chunks
    )


def gather_kernel(*refs):
    local = refs[1].shape[0]
    for d, ref in enumerate(refs[1:-1]):
        refs[-1][d * local : (d + 1) * local, :] = ref[...]


def solve_transposed(system, right_t, floor):
    size = system.shape[0]
    eye = identity(size, size)
    top = jnp.max(jnp.sum(jnp.abs(system), axis=0, keepdims=True)) + 1.0
    scale = 2.0 / (top + floor)
    eps = (top - floor) / (top + floor)
    residual = eye - scale * system
    answer = scale * right_t

    def more(carry):
        return carry[0] > 1e-6

    def double(carry):
        eps, residual, answer = carry
        both = jnp.dot(
            jnp.concatenate([residual, answer], axis=0),
            residual,
            precision=HIGHEST,
            preferred_element_type=F32,
        )
        square = eps * eps
        share = 1.0 / (2.0 - square)
        return (
            square * share,
            (2.0 * both[:size] - square * eye) * share,
            (answer + both[size:]) * (2.0 * share),
        )

    return lax.while_loop(more, double, (eps, residual, answer))[2]


def identity(rows, columns, shift=0):
    return (
        lax.broadcasted_iota(jnp.int32, (rows, columns), 0) + shift
        == lax.broadcasted_iota(jnp.int32, (rows, columns), 1)
    ).astype(F32)


def solve_kernel(
    parts, value_ref, error_ref, noise_ref, kept_ref, received_ref, mine_ref, prior, whole
):
    batches, members, count = noise_ref.shape
    local = members // parts
    own = lax.axis_index("mem")
    own_rows = pl.ds(pl.multiple_of(own * local, local), local)
    even = lax.rem(lax.axis_index("slab"), 2) == 0
    for d in range(parts):
        owner = lax.rem(own + d, parts)
        block = slice(d * local, (d + 1) * local)
        prior[pl.ds(pl.multiple_of(owner * local, local), local), :] = jnp.where(
            even, received_ref[block, :], kept_ref[block, :]
        )
    source = lax.broadcasted_iota(jnp.int32, (members, members), 0)
    target = lax.broadcasted_iota(jnp.int32, (members, members), 1)
    turn = (source == lax.rem(target + own * local, members)).astype(F32)
    product_t = turned = None
    for b in range(batches):
        last = b == batches - 1
        observed = prior[:, b * count : (b + 1) * count]
        if product_t is not None:
            both = jnp.dot(
                product_t,
                jnp.concatenate([observed, turn], axis=1) if last else observed,
                precision=HIGHEST,
                preferred_element_type=F32,
            )
            observed, turned = both[:, :count], both[:, count:]
        share = 1.0 / error_ref[b : b + 1, :]
        scaled = (observed - jnp.mean(observed, axis=0, keepdims=True)) * share
        if last:
            whole[...] = observed
            innovation = (
                value_ref[b : b + 1, :] * share + noise_ref[b, own_rows, :]
            ) - whole[own_rows, :] * share
            eye = identity(local, members, own * local)
        else:
            innovation = (value_ref[b : b + 1, :] * share + noise_ref[b]) - observed * share
            eye = identity(members, members)
        both = lax.dot_general(
            jnp.concatenate([scaled, innovation], axis=0),
            scaled,
            (((1,), (1,)), ((), ())),
            precision=HIGHEST,
            preferred_element_type=F32,
        )
        system = both[:members] + (members - 1.0) * identity(members, members)
        weights_t = solve_transposed(system, both[members:], members - 1.0)
        matrix_t = eye + weights_t - jnp.mean(weights_t, axis=1, keepdims=True)
        if last:
            mine_ref[...] = jnp.dot(
                matrix_t,
                turn if turned is None else turned,
                precision=HIGHEST,
                preferred_element_type=F32,
            )
        elif product_t is None:
            product_t = matrix_t
        else:
            product_t = jnp.dot(
                matrix_t, product_t, precision=HIGHEST, preferred_element_type=F32
            )


def combine_kernel(parts, fields, mine_ref, *refs):
    forecast_refs, delayed_refs = refs[:parts], refs[parts : 2 * parts]
    out_ref, done_ref, sems = refs[2 * parts :]
    local = mine_ref.shape[0]
    high, low = split_two(mine_ref[...])
    left = jnp.concatenate([high, high, low], axis=1)
    chunks = forecast_refs[0].shape[1] // LANES
    level = fields * chunks
    lagged = delayed_refs[0].shape[0] // local
    planes = level + lagged
    copies = []
    for first in [*range(level, planes, level), 0]:
        for f in range(fields):
            start = first + f * chunks
            if first == 0:
                held = [ref[f * local : (f + 1) * local, :] for ref in forecast_refs]
            else:
                held = [
                    jnp.concatenate(
                        [
                            ref[pl.ds(start - level + c, local, stride=lagged), :]
                            for c in range(chunks)
                        ],
                        axis=1,
                    )
                    for ref in delayed_refs
                ]
            held_high, held_low = split_two(jnp.concatenate(held, axis=0))
            result = jnp.dot(
                left,
                jnp.concatenate([held_high, held_low, held_high], axis=0),
                preferred_element_type=F32,
            )
            for c in range(chunks):
                done_ref[pl.ds(start + c, local, stride=planes), :] = result[
                    :, c * LANES : (c + 1) * LANES
                ]
        copies.append(
            pltpu.make_async_copy(
                done_ref.reshape(local, planes, LANES).at[:, first : first + level, :],
                out_ref.at[:, first : first + level, :],
                sems.at[len(copies)],
            )
        )
        copies[-1].start()
    for copy in copies:
        copy.wait()


def shards(
    present_ensemble,
    delayed_ensemble,
    spreading_coefficient,
    transport_ratios,
    obs_value,
    obs_error,
    obs_noise,
    obs_row,
    obs_col,
    obs_field,
):
    members, fields, height, width = present_ensemble.shape
    assert height == 1 and width % LANES == 0
    chunks = width // LANES
    lagged = delayed_ensemble.shape[1]
    slabs, parts = lax.axis_size("slab"), lax.axis_size("mem")
    assert slabs & (slabs - 1) == 0 and slabs >= 8
    batches, all_members, count = obs_noise.shape
    total = batches * count
    planes = (1 + lagged) * fields * chunks
    stacked = (fields * members, width)
    hbm = pl.BlockSpec(memory_space=pltpu.HBM)
    sizes = (members, fields, chunks)

    odd = range(1, slabs, 2)

    def among_odd(array, bit):
        return lax.ppermute(array, "slab", [(i, i ^ bit) for i in odd])

    def from_partners(array, among):
        return [
            lax.ppermute(
                array,
                ("slab", "mem"),
                [(i * parts + (j + d) % parts, i * parts + j) for i in among for j in range(parts)],
            )
            for d in range(1, parts)
        ]

    present, delayed = rows_of(present_ensemble), rows_of(delayed_ensemble)
    spread, ratios = rows_of(spreading_coefficient), rows_of(transport_ratios)
    sources = in_hbm((present, spread, ratios, obs_row, obs_col, obs_field))
    packed, *held = pl.pallas_call(
        functools.partial(load_kernel, chunks),
        out_shape=[shape_of((present.shape[0] + 2 * chunks, LANES))]
        + [shape_of(x.shape, x.dtype) for x in sources[1:]],
        in_specs=[hbm] * len(sources),
        scratch_shapes=[pltpu.SemaphoreType.DMA((len(sources),))],
        compiler_params=PARAMS,
        name="load",
    )(*sources)
    outer_above = lax.ppermute(packed, "slab", [(i, i + 1) for i in odd[:-1]])
    inner = lax.ppermute(packed, "slab", [(i, i ^ 1) for i in range(slabs)])
    others_delayed = from_partners(
        lax.optimization_barrier((in_hbm([delayed])[0], packed))[0], range(slabs)
    )
    outer_below = lax.ppermute(packed, "slab", [(i + 1, i) for i in odd[:-1]])
    taps, kinds = pl.pallas_call(
        selector_kernel,
        out_shape=(shape_of((width, total), BF16), shape_of((2, total), jnp.int32)),
        compiler_params=PARAMS,
        cost_estimate=estimate(SELECT_FLOPS),
        name="selector",
    )(*held[2:])
    part, here, part_obs = pl.pallas_call(
        functools.partial(own_row_kernel, *sizes),
        out_shape=(shape_of(stacked), shape_of(stacked), shape_of((members, total))),
        compiler_params=PARAMS,
        cost_estimate=estimate(OWN_FLOPS),
        name="own_row",
    )(packed, inner, *held[:2], taps, kinds)
    terms, partial = pl.pallas_call(
        functools.partial(observe_kernel, *sizes),
        out_shape=(shape_of((members, total)), shape_of(stacked)),
        compiler_params=PARAMS,
        name="observe",
    )(packed, outer_above, part, part_obs, here, taps, kinds)
    def summed(terms, other, flops, *arrived):
        return pl.pallas_call(
            sum_kernel,
            out_shape=shape_of(terms.shape),
            cost_estimate=estimate(flops),
            compiler_params=PARAMS,
            name="sum",
        )(terms, other, *arrived)

    terms = summed(terms, lax.ppermute(terms, "slab", [(i - 1, i) for i in odd]), 1)
    for bit in [1 << k for k in reversed(range(1, slabs.bit_length() - 1))]:
        terms = summed(
            terms, among_odd(terms, bit), SUM_FLOPS, *([outer_below] if bit == 4 else [])
        )
    forecast = pl.pallas_call(
        functools.partial(complete_kernel, *sizes),
        out_shape=shape_of(stacked),
        compiler_params=PARAMS,
        name="complete",
    )(lax.optimization_barrier((partial, terms))[0], outer_below, packed)

    prior = pl.pallas_call(
        gather_kernel,
        out_shape=shape_of((all_members, total)),
        cost_estimate=estimate(GATHER_FLOPS),
        compiler_params=PARAMS,
        name="gather",
    )(others_delayed[0], terms, *from_partners(terms, odd))
    received = lax.ppermute(prior, "slab", [(i, i - 1) for i in odd])
    mine = pl.pallas_call(
        functools.partial(solve_kernel, parts),
        out_shape=shape_of((members, all_members)),
        scratch_shapes=[
            pltpu.VMEM((all_members, total), F32),
            pltpu.VMEM((all_members, count), F32),
        ],
        compiler_params=PARAMS,
        cost_estimate=estimate(SOLVE_FLOPS),
        name="solve",
    )(obs_value, obs_error, obs_noise, prior, received)
    out = pl.pallas_call(
        functools.partial(combine_kernel, parts, fields),
        out_shape=shape_of((members, planes, LANES)),
        out_specs=hbm,
        scratch_shapes=[
            pltpu.VMEM((members * planes, LANES), F32),
            pltpu.SemaphoreType.DMA((1 + lagged,)),
        ],
        compiler_params=PARAMS,
        name="combine",
    )(mine, forecast, *from_partners(forecast, range(slabs)), delayed, *others_delayed)
    return out.reshape(members, 1 + lagged, fields, height, width)


def solution(mesh):
    return jax.shard_map(
        shards,
        mesh=mesh,
        in_specs=(
            P("mem", None, "slab", None),
            P("mem", None, None, "slab", None),
            P("slab", None),
            P(None, "slab", None),
            P(),
            P(),
            P(),
            P(),
            P(),
            P(),
        ),
        out_specs=P("mem", None, None, "slab", None),
        check_vma=False,
    )
```

```python
import functools

import jax
import jax.numpy as jnp
from jax import lax
from jax.experimental import pallas as pl
from jax.experimental.pallas import tpu as pltpu
from jax.sharding import PartitionSpec as P

LANES = 128
F32 = jnp.float32
BF16 = jnp.bfloat16
HIGHEST = lax.Precision.HIGHEST
PARAMS = pltpu.CompilerParams(vmem_limit_bytes=48 * 1024 * 1024)


SELECT_FLOPS = 1
OWN_FLOPS, SUM_FLOPS, GATHER_FLOPS, SOLVE_FLOPS = 1, 5*10**8, 10**9, 2*10**9


def estimate(flops):
    return pl.CostEstimate(flops=flops, transcendentals=0, bytes_accessed=0)


def rows_of(array):
    return array.reshape(-1, LANES)


def in_hbm(arrays):
    return [pltpu.with_memory_space_constraint(array, pltpu.HBM) for array in arrays]


def shape_of(shape, dtype=F32):
    return jax.ShapeDtypeStruct(shape, dtype)


def split_two(x):
    high = x.astype(BF16)
    low = (x - high.astype(F32)).astype(BF16)
    return high, low


def split_three(x):
    high = x.astype(BF16)
    rest = x - high.astype(F32)
    middle = rest.astype(BF16)
    low = (rest - middle.astype(F32)).astype(BF16)
    return high, middle, low


def line(ref, start, chunks):
    return jnp.concatenate([ref[start + c : start + c + 1, :] for c in range(chunks)], axis=1)


def stacked_planes(ref, members, fields, chunks):
    return jnp.concatenate(
        [
            jnp.concatenate(
                [
                    ref[pl.ds(f * chunks + c, members, stride=fields * chunks), :]
                    for c in range(chunks)
                ],
                axis=1,
            )
            for f in range(fields)
        ],
        axis=0,
    )


def at_once(sources, targets, sems):
    copies = [
        pltpu.make_async_copy(source, target, sems.at[i])
        for i, (source, target) in enumerate(zip(sources, targets))
    ]
    for copy in copies:
        copy.start()
    return copies


def picked_values(planes, taps):
    high, middle, low = (
        jnp.dot(part, taps, preferred_element_type=F32) for part in split_three(planes)
    )
    return low + middle + high


def load_kernel(chunks, *refs):
    count = (len(refs) - 1) // 2
    sources, packed_ref, held, sems = refs[:count], refs[count], refs[count + 1 : -1], refs[-1]
    rows = sources[0].shape[0]
    copies = at_once(sources, (packed_ref.at[:rows], *held), sems)
    copies[1].wait()
    copies[2].wait()
    spread = held[0][...]
    half = held[1][:chunks, :] * 0.5
    packed_ref[rows : rows + chunks, :] = spread + half
    packed_ref[rows + chunks : rows + 2 * chunks, :] = spread - half
    for copy in (copies[0], *copies[3:]):
        copy.wait()


def weights(packed_ref, chunks):
    rows = packed_ref.shape[0] - 2 * chunks
    return line(packed_ref, rows, chunks), line(packed_ref, rows + chunks, chunks)


def selector_kernel(row_ref, col_ref, field_ref, taps_ref, kinds_ref):
    batches, count = row_ref.shape
    shape = taps_ref.shape
    flat = lambda ref: jnp.concatenate([ref[b : b + 1, :] for b in range(batches)], axis=1)
    rows, cols, kinds = flat(row_ref), flat(col_ref), flat(field_ref)
    own_row = lax.axis_index("slab")
    for k, row in enumerate((own_row, own_row - 1)):
        kinds_ref[k : k + 1, :] = jnp.where(rows == row, kinds, -1)
    at = lax.broadcasted_iota(jnp.int32, shape, 0).astype(F32) * 0.25
    taps_ref[...] = jnp.maximum(0.5 - jnp.abs(at - cols.astype(F32) * 0.25), 0.0).astype(BF16)


def own_row_kernel(
    members,
    fields,
    chunks,
    packed_ref,
    inner_ref,
    spread_ref,
    ratio_ref,
    taps_ref,
    kinds_ref,
    part_ref,
    here_ref,
    obs_ref,
):
    width = chunks * LANES
    spread = line(spread_ref, 0, chunks)
    along_columns = line(ratio_ref, chunks, chunks)
    here = stacked_planes(packed_ref, members, fields, chunks)
    here_ref[...] = here
    lane = lax.broadcasted_iota(jnp.int32, here.shape, 1)
    left = jnp.where(lane == 0, 0.0, pltpu.roll(here, 1, 1))
    right = jnp.where(lane == width - 1, 0.0, pltpu.roll(here, width - 1, 1))
    even = lax.rem(lax.axis_index("slab"), 2) == 0
    above, below = weights(packed_ref, chunks)
    part = (
        here
        + spread * (right + left - 4.0 * here)
        - along_columns * (right - left) * 0.5
        + jnp.where(even, below, above) * stacked_planes(inner_ref, members, fields, chunks)
    )
    part_ref[...] = part
    picked = picked_values(part, taps_ref[...])
    observed = jnp.zeros(obs_ref.shape, F32)
    for f in range(fields):
        observed += jnp.where(
            kinds_ref[0:1, :] == f, picked[f * members : (f + 1) * members], 0.0
        )
    obs_ref[...] = observed


def observe_kernel(
    members,
    fields,
    chunks,
    packed_ref,
    outer_ref,
    part_ref,
    part_obs_ref,
    here_ref,
    taps_ref,
    kinds_ref,
    keep_ref,
    send_ref,
    partial_ref,
):
    above, _ = weights(packed_ref, chunks)
    _, below_of_above = weights(outer_ref, chunks)
    taken = above * stacked_planes(outer_ref, members, fields, chunks)
    given = below_of_above * here_ref[...]
    partial_ref[...] = part_ref[...] + taken
    picked = picked_values(jnp.concatenate([taken, given], axis=0), taps_ref[...])
    observed = part_obs_ref[...]
    for side in range(2):
        kinds = kinds_ref[side : side + 1, :]
        for f in range(fields):
            start = (side * fields + f) * members
            observed += jnp.where(kinds == f, picked[start : start + members], 0.0)
    even = lax.rem(lax.axis_index("slab"), 2) == 0
    half = observed.shape[1] // 2
    first, second = observed[:, :half], observed[:, half:]
    keep_ref[...] = jnp.where(even, first, second)
    send_ref[...] = jnp.where(even, second, first)


def sum_kernel(terms_ref, other_ref, *refs):
    refs[-1][...] = terms_ref[...] + other_ref[...]


def complete_kernel(members, fields, chunks, partial_ref, outer_ref, packed_ref, _, forecast_ref):
    _, below = weights(packed_ref, chunks)
    forecast_ref[...] = partial_ref[...] + below * stacked_planes(
        outer_ref, members, fields, chunks
    )


def gather_kernel(*refs):
    local = refs[0].shape[0]
    for d, ref in enumerate(refs[:-1]):
        refs[-1][d * local : (d + 1) * local, :] = ref[...]


def solve_transposed(system, right_t, floor):
    size = system.shape[0]
    eye = identity(size, size)
    top = jnp.max(jnp.sum(jnp.abs(system), axis=0, keepdims=True)) + 1.0
    scale = 2.0 / (top + floor)
    eps = (top - floor) / (top + floor)
    residual = eye - scale * system
    answer = scale * right_t

    def more(carry):
        return carry[0] > 1e-6

    def double(carry):
        eps, residual, answer = carry
        both = jnp.dot(
            jnp.concatenate([residual, answer], axis=0),
            residual,
            precision=HIGHEST,
            preferred_element_type=F32,
        )
        square = eps * eps
        share = 1.0 / (2.0 - square)
        return (
            square * share,
            (2.0 * both[:size] - square * eye) * share,
            (answer + both[size:]) * (2.0 * share),
        )

    return lax.while_loop(more, double, (eps, residual, answer))[2]


def identity(rows, columns, shift=0):
    return (
        lax.broadcasted_iota(jnp.int32, (rows, columns), 0) + shift
        == lax.broadcasted_iota(jnp.int32, (rows, columns), 1)
    ).astype(F32)


def solve_kernel(
    parts, value_ref, error_ref, noise_ref, kept_ref, received_ref, mine_ref, prior, whole
):
    batches, members, count = noise_ref.shape
    local = members // parts
    own = lax.axis_index("mem")
    own_rows = pl.ds(pl.multiple_of(own * local, local), local)
    even = lax.rem(lax.axis_index("slab"), 2) == 0
    half = batches * count // 2
    for d in range(parts):
        owner = lax.rem(own + d, parts)
        rows = pl.ds(pl.multiple_of(owner * local, local), local)
        kept = kept_ref[d * local : (d + 1) * local, :]
        received = received_ref[d * local : (d + 1) * local, :]
        prior[rows, :half] = jnp.where(even, kept, received)
        prior[rows, half:] = jnp.where(even, received, kept)
    source = lax.broadcasted_iota(jnp.int32, (members, members), 0)
    target = lax.broadcasted_iota(jnp.int32, (members, members), 1)
    turn = (source == lax.rem(target + own * local, members)).astype(F32)
    product_t = turned = None
    for b in range(batches):
        last = b == batches - 1
        observed = prior[:, b * count : (b + 1) * count]
        if product_t is not None:
            both = jnp.dot(
                product_t,
                jnp.concatenate([observed, turn], axis=1) if last else observed,
                precision=HIGHEST,
                preferred_element_type=F32,
            )
            observed, turned = both[:, :count], both[:, count:]
        share = 1.0 / error_ref[b : b + 1, :]
        scaled = (observed - jnp.mean(observed, axis=0, keepdims=True)) * share
        if last:
            whole[...] = observed
            innovation = (
                value_ref[b : b + 1, :] * share + noise_ref[b, own_rows, :]
            ) - whole[own_rows, :] * share
            eye = identity(local, members, own * local)
        else:
            innovation = (value_ref[b : b + 1, :] * share + noise_ref[b]) - observed * share
            eye = identity(members, members)
        both = lax.dot_general(
            jnp.concatenate([scaled, innovation], axis=0),
            scaled,
            (((1,), (1,)), ((), ())),
            precision=HIGHEST,
            preferred_element_type=F32,
        )
        system = both[:members] + (members - 1.0) * identity(members, members)
        weights_t = solve_transposed(system, both[members:], members - 1.0)
        matrix_t = eye + weights_t - jnp.mean(weights_t, axis=1, keepdims=True)
        if last:
            mine_ref[...] = jnp.dot(
                matrix_t,
                turn if turned is None else turned,
                precision=HIGHEST,
                preferred_element_type=F32,
            )
        elif product_t is None:
            product_t = matrix_t
        else:
            product_t = jnp.dot(
                matrix_t, product_t, precision=HIGHEST, preferred_element_type=F32
            )


def combine_kernel(parts, fields, mine_ref, *refs):
    forecast_refs, delayed_refs = refs[:parts], refs[parts : 2 * parts]
    out_ref, done_ref, sems = refs[2 * parts :]
    local = mine_ref.shape[0]
    high, low = split_two(mine_ref[...])
    left = jnp.concatenate([high, high, low], axis=1)
    chunks = forecast_refs[0].shape[1] // LANES
    level = fields * chunks
    lagged = delayed_refs[0].shape[0] // local
    planes = level + lagged
    copies = []
    for first in [*range(level, planes, level), 0]:
        for f in range(fields):
            start = first + f * chunks
            if first == 0:
                held = [ref[f * local : (f + 1) * local, :] for ref in forecast_refs]
            else:
                held = [
                    jnp.concatenate(
                        [
                            ref[pl.ds(start - level + c, local, stride=lagged), :]
                            for c in range(chunks)
                        ],
                        axis=1,
                    )
                    for ref in delayed_refs
                ]
            held_high, held_low = split_two(jnp.concatenate(held, axis=0))
            result = jnp.dot(
                left,
                jnp.concatenate([held_high, held_low, held_high], axis=0),
                preferred_element_type=F32,
            )
            for c in range(chunks):
                done_ref[pl.ds(start + c, local, stride=planes), :] = result[
                    :, c * LANES : (c + 1) * LANES
                ]
        copies.append(
            pltpu.make_async_copy(
                done_ref.reshape(local, planes, LANES).at[:, first : first + level, :],
                out_ref.at[:, first : first + level, :],
                sems.at[len(copies)],
            )
        )
        copies[-1].start()
    for copy in copies:
        copy.wait()


def shards(
    present_ensemble,
    delayed_ensemble,
    spreading_coefficient,
    transport_ratios,
    obs_value,
    obs_error,
    obs_noise,
    obs_row,
    obs_col,
    obs_field,
):
    members, fields, height, width = present_ensemble.shape
    assert height == 1 and width % LANES == 0
    chunks = width // LANES
    lagged = delayed_ensemble.shape[1]
    slabs, parts = lax.axis_size("slab"), lax.axis_size("mem")
    assert slabs & (slabs - 1) == 0 and slabs >= 8
    batches, all_members, count = obs_noise.shape
    total = batches * count
    planes = (1 + lagged) * fields * chunks
    stacked = (fields * members, width)
    hbm = pl.BlockSpec(memory_space=pltpu.HBM)
    sizes = (members, fields, chunks)

    odd = range(1, slabs, 2)

    def from_slab(array, bit):
        return lax.ppermute(array, "slab", [(i, i ^ bit) for i in range(slabs)])

    def from_partners(array):
        return [
            lax.ppermute(array, "mem", [((i + d) % parts, i) for i in range(parts)])
            for d in range(1, parts)
        ]

    present, delayed = rows_of(present_ensemble), rows_of(delayed_ensemble)
    spread, ratios = rows_of(spreading_coefficient), rows_of(transport_ratios)
    sources = in_hbm((present, spread, ratios, obs_row, obs_col, obs_field))
    packed, *held = pl.pallas_call(
        functools.partial(load_kernel, chunks),
        out_shape=[shape_of((present.shape[0] + 2 * chunks, LANES))]
        + [shape_of(x.shape, x.dtype) for x in sources[1:]],
        in_specs=[hbm] * len(sources),
        scratch_shapes=[pltpu.SemaphoreType.DMA((len(sources),))],
        compiler_params=PARAMS,
        name="load",
    )(*sources)
    outer_above = lax.ppermute(packed, "slab", [(i, i + 1) for i in odd[:-1]])
    inner = from_slab(packed, 1)
    others_delayed = from_partners(
        lax.optimization_barrier((delayed, packed))[0]
    )
    outer_below = lax.ppermute(packed, "slab", [(i + 1, i) for i in odd[:-1]])
    taps, kinds = pl.pallas_call(
        selector_kernel,
        out_shape=(shape_of((width, total), BF16), shape_of((2, total), jnp.int32)),
        compiler_params=PARAMS,
        cost_estimate=estimate(SELECT_FLOPS),
        name="selector",
    )(*held[2:])
    part, here, part_obs = pl.pallas_call(
        functools.partial(own_row_kernel, *sizes),
        out_shape=(shape_of(stacked), shape_of(stacked), shape_of((members, total))),
        compiler_params=PARAMS,
        cost_estimate=estimate(OWN_FLOPS),
        name="own_row",
    )(packed, inner, *held[:2], taps, kinds)
    keep, send, partial = pl.pallas_call(
        functools.partial(observe_kernel, *sizes),
        out_shape=(
            shape_of((members, total // 2)),
            shape_of((members, total // 2)),
            shape_of(stacked),
        ),
        compiler_params=PARAMS,
        name="observe",
    )(packed, outer_above, part, part_obs, here, taps, kinds)
    def summed(terms, other, flops, *arrived):
        return pl.pallas_call(
            sum_kernel,
            out_shape=shape_of(terms.shape),
            cost_estimate=estimate(flops),
            compiler_params=PARAMS,
            name="sum",
        )(terms, other, *arrived)

    terms = keep + from_slab(send, 1)
    for bit in [1 << k for k in reversed(range(1, slabs.bit_length() - 1))]:
        terms = summed(
            terms, from_slab(terms, bit), SUM_FLOPS, *([outer_below] if bit == 4 else [])
        )
    forecast = pl.pallas_call(
        functools.partial(complete_kernel, *sizes),
        out_shape=shape_of(stacked),
        compiler_params=PARAMS,
        name="complete",
    )(
        lax.optimization_barrier((partial, terms))[0], outer_below, packed, others_delayed[0]
    )

    prior = pl.pallas_call(
        gather_kernel,
        out_shape=shape_of((all_members, total // 2)),
        cost_estimate=estimate(GATHER_FLOPS),
        compiler_params=PARAMS,
        name="gather",
    )(terms, *from_partners(terms))
    mine = pl.pallas_call(
        functools.partial(solve_kernel, parts),
        out_shape=shape_of((members, all_members)),
        scratch_shapes=[
            pltpu.VMEM((all_members, total), F32),
            pltpu.VMEM((all_members, count), F32),
        ],
        compiler_params=PARAMS,
        cost_estimate=estimate(SOLVE_FLOPS),
        name="solve",
    )(obs_value, obs_error, obs_noise, prior, from_slab(prior, 1))
    out = pl.pallas_call(
        functools.partial(combine_kernel, parts, fields),
        out_shape=shape_of((members, planes, LANES)),
        out_specs=hbm,
        scratch_shapes=[
            pltpu.VMEM((members * planes, LANES), F32),
            pltpu.SemaphoreType.DMA((1 + lagged,)),
        ],
        compiler_params=PARAMS,
        name="combine",
    )(mine, forecast, *from_partners(forecast), delayed, *others_delayed)
    return out.reshape(members, 1 + lagged, fields, height, width)


def solution(mesh):
    return jax.shard_map(
        shards,
        mesh=mesh,
        in_specs=(
            P("mem", None, "slab", None),
            P("mem", None, None, "slab", None),
            P("slab", None),
            P(None, "slab", None),
            P(),
            P(),
            P(),
            P(),
            P(),
            P(),
        ),
        out_specs=P("mem", None, None, "slab", None),
        check_vma=False,
    )
```

```python
import functools

import jax
import jax.numpy as jnp
from jax import lax
from jax.experimental import pallas as pl
from jax.experimental.pallas import tpu as pltpu
from jax.sharding import PartitionSpec as P

LANES = 128
F32 = jnp.float32
BF16 = jnp.bfloat16
HIGHEST = lax.Precision.HIGHEST
PARAMS = pltpu.CompilerParams(vmem_limit_bytes=48 * 1024 * 1024)


SELECT_FLOPS = 1
OWN_FLOPS, SUM_FLOPS, GATHER_FLOPS, SOLVE_FLOPS = 1, 5*10**8, 10**9, 2*10**9


def estimate(flops):
    return pl.CostEstimate(flops=flops, transcendentals=0, bytes_accessed=0)


def rows_of(array):
    return array.reshape(-1, LANES)


def in_hbm(arrays):
    return [pltpu.with_memory_space_constraint(array, pltpu.HBM) for array in arrays]


def shape_of(shape, dtype=F32):
    return jax.ShapeDtypeStruct(shape, dtype)


def split_two(x):
    high = x.astype(BF16)
    low = (x - high.astype(F32)).astype(BF16)
    return high, low


def split_three(x):
    high = x.astype(BF16)
    rest = x - high.astype(F32)
    middle = rest.astype(BF16)
    low = (rest - middle.astype(F32)).astype(BF16)
    return high, middle, low


def line(ref, start, chunks):
    return jnp.concatenate([ref[start + c : start + c + 1, :] for c in range(chunks)], axis=1)


def stacked_planes(ref, members, fields, chunks):
    return jnp.concatenate(
        [
            jnp.concatenate(
                [
                    ref[pl.ds(f * chunks + c, members, stride=fields * chunks), :]
                    for c in range(chunks)
                ],
                axis=1,
            )
            for f in range(fields)
        ],
        axis=0,
    )


def at_once(sources, targets, sems):
    copies = [
        pltpu.make_async_copy(source, target, sems.at[i])
        for i, (source, target) in enumerate(zip(sources, targets))
    ]
    for copy in copies:
        copy.start()
    return copies


def picked_values(planes, taps):
    high, middle, low = (
        jnp.dot(part, taps, preferred_element_type=F32) for part in split_three(planes)
    )
    return low + middle + high


def load_kernel(chunks, *refs):
    count = (len(refs) - 1) // 2
    sources, packed_ref, held, sems = refs[:count], refs[count], refs[count + 1 : -1], refs[-1]
    rows = sources[0].shape[0]
    copies = at_once(sources, (packed_ref.at[:rows], *held), sems)
    copies[1].wait()
    copies[2].wait()
    spread = held[0][...]
    half = held[1][:chunks, :] * 0.5
    packed_ref[rows : rows + chunks, :] = spread + half
    packed_ref[rows + chunks : rows + 2 * chunks, :] = spread - half
    for copy in (copies[0], *copies[3:]):
        copy.wait()


def keeps_first(parts):
    rest = lax.axis_index("slab")
    ones = lax.axis_index("mem") if parts == 2 else 0
    for _ in range(lax.axis_size("slab").bit_length() - 1):
        ones = ones + lax.rem(rest, 2)
        rest = rest // 2
    return lax.rem(ones, 2) == 0


def weights(packed_ref, chunks):
    rows = packed_ref.shape[0] - 2 * chunks
    return line(packed_ref, rows, chunks), line(packed_ref, rows + chunks, chunks)


def selector_kernel(row_ref, col_ref, field_ref, taps_ref, kinds_ref):
    batches, count = row_ref.shape
    shape = taps_ref.shape
    flat = lambda ref: jnp.concatenate([ref[b : b + 1, :] for b in range(batches)], axis=1)
    rows, cols, kinds = flat(row_ref), flat(col_ref), flat(field_ref)
    own_row = lax.axis_index("slab")
    for k, row in enumerate((own_row, own_row - 1)):
        kinds_ref[k : k + 1, :] = jnp.where(rows == row, kinds, -1)
    at = lax.broadcasted_iota(jnp.int32, shape, 0).astype(F32) * 0.25
    taps_ref[...] = jnp.maximum(0.5 - jnp.abs(at - cols.astype(F32) * 0.25), 0.0).astype(BF16)


def own_row_kernel(
    members,
    fields,
    chunks,
    packed_ref,
    inner_ref,
    spread_ref,
    ratio_ref,
    taps_ref,
    kinds_ref,
    part_ref,
    here_ref,
    obs_ref,
):
    width = chunks * LANES
    spread = line(spread_ref, 0, chunks)
    along_columns = line(ratio_ref, chunks, chunks)
    here = stacked_planes(packed_ref, members, fields, chunks)
    here_ref[...] = here
    lane = lax.broadcasted_iota(jnp.int32, here.shape, 1)
    left = jnp.where(lane == 0, 0.0, pltpu.roll(here, 1, 1))
    right = jnp.where(lane == width - 1, 0.0, pltpu.roll(here, width - 1, 1))
    even = lax.rem(lax.axis_index("slab"), 2) == 0
    above, below = weights(packed_ref, chunks)
    part = (
        here
        + spread * (right + left - 4.0 * here)
        - along_columns * (right - left) * 0.5
        + jnp.where(even, below, above) * stacked_planes(inner_ref, members, fields, chunks)
    )
    part_ref[...] = part
    picked = picked_values(part, taps_ref[...])
    observed = jnp.zeros(obs_ref.shape, F32)
    for f in range(fields):
        observed += jnp.where(
            kinds_ref[0:1, :] == f, picked[f * members : (f + 1) * members], 0.0
        )
    obs_ref[...] = observed


def observe_kernel(
    parts,
    members,
    fields,
    chunks,
    packed_ref,
    outer_ref,
    part_ref,
    part_obs_ref,
    here_ref,
    taps_ref,
    kinds_ref,
    keep_ref,
    send_ref,
    partial_ref,
):
    above, _ = weights(packed_ref, chunks)
    _, below_of_above = weights(outer_ref, chunks)
    taken = above * stacked_planes(outer_ref, members, fields, chunks)
    given = below_of_above * here_ref[...]
    partial_ref[...] = part_ref[...] + taken
    picked = picked_values(jnp.concatenate([taken, given], axis=0), taps_ref[...])
    observed = part_obs_ref[...]
    for side in range(2):
        kinds = kinds_ref[side : side + 1, :]
        for f in range(fields):
            start = (side * fields + f) * members
            observed += jnp.where(kinds == f, picked[start : start + members], 0.0)
    first_here = keeps_first(parts)
    half = observed.shape[1] // 2
    first, second = observed[:, :half], observed[:, half:]
    keep_ref[...] = jnp.where(first_here, first, second)
    send_ref[...] = jnp.where(first_here, second, first)


def sum_kernel(terms_ref, other_ref, *refs):
    refs[-1][...] = terms_ref[...] + other_ref[...]


def complete_kernel(members, fields, chunks, partial_ref, outer_ref, packed_ref, _, forecast_ref):
    _, below = weights(packed_ref, chunks)
    forecast_ref[...] = partial_ref[...] + below * stacked_planes(
        outer_ref, members, fields, chunks
    )


def gather_kernel(*refs):
    local = refs[0].shape[0]
    for d, ref in enumerate(refs[:-1]):
        refs[-1][d * local : (d + 1) * local, :] = ref[...]


def solve_transposed(system, right_t, floor):
    size = system.shape[0]
    eye = identity(size, size)
    top = jnp.max(jnp.sum(jnp.abs(system), axis=0, keepdims=True)) + 1.0
    scale = 2.0 / (top + floor)
    eps = (top - floor) / (top + floor)
    residual = eye - scale * system
    answer = scale * right_t

    def more(carry):
        return carry[0] > 1e-6

    def double(carry):
        eps, residual, answer = carry
        both = jnp.dot(
            jnp.concatenate([residual, answer], axis=0),
            residual,
            precision=HIGHEST,
            preferred_element_type=F32,
        )
        square = eps * eps
        share = 1.0 / (2.0 - square)
        return (
            square * share,
            (2.0 * both[:size] - square * eye) * share,
            (answer + both[size:]) * (2.0 * share),
        )

    return lax.while_loop(more, double, (eps, residual, answer))[2]


def identity(rows, columns, shift=0):
    return (
        lax.broadcasted_iota(jnp.int32, (rows, columns), 0) + shift
        == lax.broadcasted_iota(jnp.int32, (rows, columns), 1)
    ).astype(F32)


def solve_kernel(
    parts, value_ref, error_ref, noise_ref, kept_ref, received_ref, mine_ref, prior, whole
):
    batches, members, count = noise_ref.shape
    local = members // parts
    own = lax.axis_index("mem")
    own_rows = pl.ds(pl.multiple_of(own * local, local), local)
    first_here = keeps_first(parts)
    half = batches * count // 2
    for d in range(parts):
        owner = lax.rem(own + d, parts)
        rows = pl.ds(pl.multiple_of(owner * local, local), local)
        kept = kept_ref[d * local : (d + 1) * local, :]
        received = received_ref[d * local : (d + 1) * local, :]
        prior[rows, :half] = jnp.where(first_here, kept, received)
        prior[rows, half:] = jnp.where(first_here, received, kept)
    source = lax.broadcasted_iota(jnp.int32, (members, members), 0)
    target = lax.broadcasted_iota(jnp.int32, (members, members), 1)
    turn = (source == lax.rem(target + own * local, members)).astype(F32)
    product_t = turned = None
    for b in range(batches):
        last = b == batches - 1
        observed = prior[:, b * count : (b + 1) * count]
        if product_t is not None:
            both = jnp.dot(
                product_t,
                jnp.concatenate([observed, turn], axis=1) if last else observed,
                precision=HIGHEST,
                preferred_element_type=F32,
            )
            observed, turned = both[:, :count], both[:, count:]
        share = 1.0 / error_ref[b : b + 1, :]
        scaled = (observed - jnp.mean(observed, axis=0, keepdims=True)) * share
        if last:
            whole[...] = observed
            innovation = (
                value_ref[b : b + 1, :] * share + noise_ref[b, own_rows, :]
            ) - whole[own_rows, :] * share
            eye = identity(local, members, own * local)
        else:
            innovation = (value_ref[b : b + 1, :] * share + noise_ref[b]) - observed * share
            eye = identity(members, members)
        both = lax.dot_general(
            jnp.concatenate([scaled, innovation], axis=0),
            scaled,
            (((1,), (1,)), ((), ())),
            precision=HIGHEST,
            preferred_element_type=F32,
        )
        system = both[:members] + (members - 1.0) * identity(members, members)
        weights_t = solve_transposed(system, both[members:], members - 1.0)
        matrix_t = eye + weights_t - jnp.mean(weights_t, axis=1, keepdims=True)
        if last:
            mine_ref[...] = jnp.dot(
                matrix_t,
                turn if turned is None else turned,
                precision=HIGHEST,
                preferred_element_type=F32,
            )
        elif product_t is None:
            product_t = matrix_t
        else:
            product_t = jnp.dot(
                matrix_t, product_t, precision=HIGHEST, preferred_element_type=F32
            )


def combine_kernel(parts, fields, mine_ref, *refs):
    forecast_refs, delayed_refs = refs[:parts], refs[parts : 2 * parts]
    out_ref, done_ref, sems = refs[2 * parts :]
    local = mine_ref.shape[0]
    high, low = split_two(mine_ref[...])
    left = jnp.concatenate([high, high, low], axis=1)
    chunks = forecast_refs[0].shape[1] // LANES
    level = fields * chunks
    lagged = delayed_refs[0].shape[0] // local
    planes = level + lagged
    copies = []
    for first in [*range(level, planes, level), 0]:
        for f in range(fields):
            start = first + f * chunks
            if first == 0:
                held = [ref[f * local : (f + 1) * local, :] for ref in forecast_refs]
            else:
                held = [
                    jnp.concatenate(
                        [
                            ref[pl.ds(start - level + c, local, stride=lagged), :]
                            for c in range(chunks)
                        ],
                        axis=1,
                    )
                    for ref in delayed_refs
                ]
            held_high, held_low = split_two(jnp.concatenate(held, axis=0))
            result = jnp.dot(
                left,
                jnp.concatenate([held_high, held_low, held_high], axis=0),
                preferred_element_type=F32,
            )
            for c in range(chunks):
                done_ref[pl.ds(start + c, local, stride=planes), :] = result[
                    :, c * LANES : (c + 1) * LANES
                ]
        copies.append(
            pltpu.make_async_copy(
                done_ref.reshape(local, planes, LANES).at[:, first : first + level, :],
                out_ref.at[:, first : first + level, :],
                sems.at[len(copies)],
            )
        )
        copies[-1].start()
    for copy in copies:
        copy.wait()


def shards(
    present_ensemble,
    delayed_ensemble,
    spreading_coefficient,
    transport_ratios,
    obs_value,
    obs_error,
    obs_noise,
    obs_row,
    obs_col,
    obs_field,
):
    members, fields, height, width = present_ensemble.shape
    assert height == 1 and width % LANES == 0
    chunks = width // LANES
    lagged = delayed_ensemble.shape[1]
    slabs, parts = lax.axis_size("slab"), lax.axis_size("mem")
    assert slabs & (slabs - 1) == 0 and slabs >= 8
    batches, all_members, count = obs_noise.shape
    total = batches * count
    planes = (1 + lagged) * fields * chunks
    stacked = (fields * members, width)
    hbm = pl.BlockSpec(memory_space=pltpu.HBM)
    sizes = (members, fields, chunks)

    odd = range(1, slabs, 2)

    def from_slab(array, bit):
        return lax.ppermute(array, "slab", [(i, i ^ bit) for i in range(slabs)])

    def from_other_pair(array, bit):
        return from_slab(array, bit ^ 1)

    def from_other_mem(array):
        if parts != 2:
            return from_partners(array)
        return [
            lax.ppermute(
                array, ("slab", "mem"), [(i ^ 3, i) for i in range(slabs * parts)]
            )
        ]

    def from_partners(array):
        return [
            lax.ppermute(array, "mem", [((i + d) % parts, i) for i in range(parts)])
            for d in range(1, parts)
        ]

    present, delayed = rows_of(present_ensemble), rows_of(delayed_ensemble)
    spread, ratios = rows_of(spreading_coefficient), rows_of(transport_ratios)
    sources = in_hbm((present, spread, ratios, obs_row, obs_col, obs_field))
    packed, *held = pl.pallas_call(
        functools.partial(load_kernel, chunks),
        out_shape=[shape_of((present.shape[0] + 2 * chunks, LANES))]
        + [shape_of(x.shape, x.dtype) for x in sources[1:]],
        in_specs=[hbm] * len(sources),
        scratch_shapes=[pltpu.SemaphoreType.DMA((len(sources),))],
        compiler_params=PARAMS,
        name="load",
    )(*sources)
    outer_above = lax.ppermute(packed, "slab", [(i, i + 1) for i in odd[:-1]])
    inner = from_slab(packed, 1)
    others_delayed = from_partners(
        lax.optimization_barrier((delayed, packed))[0]
    )
    outer_below = lax.ppermute(packed, "slab", [(i + 1, i) for i in odd[:-1]])
    taps, kinds = pl.pallas_call(
        selector_kernel,
        out_shape=(shape_of((width, total), BF16), shape_of((2, total), jnp.int32)),
        compiler_params=PARAMS,
        cost_estimate=estimate(SELECT_FLOPS),
        name="selector",
    )(*held[2:])
    part, here, part_obs = pl.pallas_call(
        functools.partial(own_row_kernel, *sizes),
        out_shape=(shape_of(stacked), shape_of(stacked), shape_of((members, total))),
        compiler_params=PARAMS,
        cost_estimate=estimate(OWN_FLOPS),
        name="own_row",
    )(packed, inner, *held[:2], taps, kinds)
    keep, send, partial = pl.pallas_call(
        functools.partial(observe_kernel, parts, *sizes),
        out_shape=(
            shape_of((members, total // 2)),
            shape_of((members, total // 2)),
            shape_of(stacked),
        ),
        compiler_params=PARAMS,
        name="observe",
    )(packed, outer_above, part, part_obs, here, taps, kinds)
    def summed(terms, other, flops, *arrived):
        return pl.pallas_call(
            sum_kernel,
            out_shape=shape_of(terms.shape),
            cost_estimate=estimate(flops),
            compiler_params=PARAMS,
            name="sum",
        )(terms, other, *arrived)

    terms = keep + from_slab(send, 1)
    for bit in [1 << k for k in reversed(range(1, slabs.bit_length() - 1))]:
        terms = summed(
            terms, from_other_pair(terms, bit), SUM_FLOPS, *([outer_below] if bit == 4 else [])
        )
    forecast = pl.pallas_call(
        functools.partial(complete_kernel, *sizes),
        out_shape=shape_of(stacked),
        compiler_params=PARAMS,
        name="complete",
    )(
        lax.optimization_barrier((partial, terms))[0], outer_below, packed, others_delayed[0]
    )

    prior = pl.pallas_call(
        gather_kernel,
        out_shape=shape_of((all_members, total // 2)),
        cost_estimate=estimate(GATHER_FLOPS),
        compiler_params=PARAMS,
        name="gather",
    )(terms, *from_other_mem(terms))
    mine = pl.pallas_call(
        functools.partial(solve_kernel, parts),
        out_shape=shape_of((members, all_members)),
        scratch_shapes=[
            pltpu.VMEM((all_members, total), F32),
            pltpu.VMEM((all_members, count), F32),
        ],
        compiler_params=PARAMS,
        cost_estimate=estimate(SOLVE_FLOPS),
        name="solve",
    )(obs_value, obs_error, obs_noise, prior, from_slab(prior, 1))
    out = pl.pallas_call(
        functools.partial(combine_kernel, parts, fields),
        out_shape=shape_of((members, planes, LANES)),
        out_specs=hbm,
        scratch_shapes=[
            pltpu.VMEM((members * planes, LANES), F32),
            pltpu.SemaphoreType.DMA((1 + lagged,)),
        ],
        compiler_params=PARAMS,
        name="combine",
    )(mine, forecast, *from_partners(forecast), delayed, *others_delayed)
    return out.reshape(members, 1 + lagged, fields, height, width)


def solution(mesh):
    return jax.shard_map(
        shards,
        mesh=mesh,
        in_specs=(
            P("mem", None, "slab", None),
            P("mem", None, None, "slab", None),
            P("slab", None),
            P(None, "slab", None),
            P(),
            P(),
            P(),
            P(),
            P(),
            P(),
        ),
        out_specs=P("mem", None, None, "slab", None),
        check_vma=False,
    )
```

```python
import functools

import jax
import jax.numpy as jnp
from jax import lax
from jax.experimental import pallas as pl
from jax.experimental.pallas import tpu as pltpu
from jax.sharding import PartitionSpec as P

LANES = 128
F32 = jnp.float32
BF16 = jnp.bfloat16
HIGHEST = lax.Precision.HIGHEST
PARAMS = pltpu.CompilerParams(vmem_limit_bytes=48 * 1024 * 1024)


SELECT_FLOPS = 1
OWN_FLOPS, SUM_FLOPS, GATHER_FLOPS, SOLVE_FLOPS = 1, (8*10**8,8*10**8,1), 10**8, 5*10**8


def estimate(flops):
    return pl.CostEstimate(flops=flops, transcendentals=0, bytes_accessed=0)


def rows_of(array):
    return array.reshape(-1, LANES)


def in_hbm(arrays):
    return [pltpu.with_memory_space_constraint(array, pltpu.HBM) for array in arrays]


def shape_of(shape, dtype=F32):
    return jax.ShapeDtypeStruct(shape, dtype)


def split_two(x):
    high = x.astype(BF16)
    low = (x - high.astype(F32)).astype(BF16)
    return high, low


def split_three(x):
    high = x.astype(BF16)
    rest = x - high.astype(F32)
    middle = rest.astype(BF16)
    low = (rest - middle.astype(F32)).astype(BF16)
    return high, middle, low


def line(ref, start, chunks):
    return jnp.concatenate([ref[start + c : start + c + 1, :] for c in range(chunks)], axis=1)


def stacked_planes(ref, members, fields, chunks):
    return jnp.concatenate(
        [
            jnp.concatenate(
                [
                    ref[pl.ds(f * chunks + c, members, stride=fields * chunks), :]
                    for c in range(chunks)
                ],
                axis=1,
            )
            for f in range(fields)
        ],
        axis=0,
    )


def at_once(sources, targets, sems):
    copies = [
        pltpu.make_async_copy(source, target, sems.at[i])
        for i, (source, target) in enumerate(zip(sources, targets))
    ]
    for copy in copies:
        copy.start()
    return copies


def picked_values(planes, taps):
    high, middle, low = (
        jnp.dot(part, taps, preferred_element_type=F32) for part in split_three(planes)
    )
    return low + middle + high


def load_kernel(chunks, *refs):
    count = (len(refs) - 1) // 2
    sources, packed_ref, held, sems = refs[:count], refs[count], refs[count + 1 : -1], refs[-1]
    rows = sources[0].shape[0]
    copies = at_once(sources, (packed_ref.at[:rows], *held), sems)
    copies[1].wait()
    copies[2].wait()
    spread = held[0][...]
    half = held[1][:chunks, :] * 0.5
    packed_ref[rows : rows + chunks, :] = spread + half
    packed_ref[rows + chunks : rows + 2 * chunks, :] = spread - half
    for copy in (copies[0], *copies[3:]):
        copy.wait()


def keeps_first(parts):
    rest = lax.axis_index("slab")
    ones = lax.axis_index("mem") if parts == 2 else 0
    for _ in range(lax.axis_size("slab").bit_length() - 1):
        ones = ones + lax.rem(rest, 2)
        rest = rest // 2
    return lax.rem(ones, 2) == 0


def weights(packed_ref, chunks):
    rows = packed_ref.shape[0] - 2 * chunks
    return line(packed_ref, rows, chunks), line(packed_ref, rows + chunks, chunks)


def selector_kernel(row_ref, col_ref, field_ref, taps_ref, kinds_ref):
    batches, count = row_ref.shape
    shape = taps_ref.shape
    flat = lambda ref: jnp.concatenate([ref[b : b + 1, :] for b in range(batches)], axis=1)
    rows, cols, kinds = flat(row_ref), flat(col_ref), flat(field_ref)
    own_row = lax.axis_index("slab")
    for k, row in enumerate((own_row, own_row - 1)):
        kinds_ref[k : k + 1, :] = jnp.where(rows == row, kinds, -1)
    at = lax.broadcasted_iota(jnp.int32, shape, 0).astype(F32) * 0.25
    taps_ref[...] = jnp.maximum(0.5 - jnp.abs(at - cols.astype(F32) * 0.25), 0.0).astype(BF16)


def own_row_kernel(
    members,
    fields,
    chunks,
    packed_ref,
    spread_ref,
    ratio_ref,
    taps_ref,
    kinds_ref,
    part_ref,
    here_ref,
    obs_ref,
):
    width = chunks * LANES
    spread = line(spread_ref, 0, chunks)
    along_columns = line(ratio_ref, chunks, chunks)
    here = stacked_planes(packed_ref, members, fields, chunks)
    here_ref[...] = here
    lane = lax.broadcasted_iota(jnp.int32, here.shape, 1)
    left = jnp.where(lane == 0, 0.0, pltpu.roll(here, 1, 1))
    right = jnp.where(lane == width - 1, 0.0, pltpu.roll(here, width - 1, 1))
    part = (
        here
        + spread * (right + left - 4.0 * here)
        - along_columns * (right - left) * 0.5
    )
    part_ref[...] = part
    picked = picked_values(part, taps_ref[...])
    observed = jnp.zeros(obs_ref.shape, F32)
    for f in range(fields):
        observed += jnp.where(
            kinds_ref[0:1, :] == f, picked[f * members : (f + 1) * members], 0.0
        )
    obs_ref[...] = observed


def observe_kernel(
    parts,
    members,
    fields,
    chunks,
    packed_ref,
    inner_ref,
    outer_ref,
    part_ref,
    part_obs_ref,
    here_ref,
    taps_ref,
    kinds_ref,
    keep_ref,
    send_ref,
    partial_ref,
):
    even = lax.rem(lax.axis_index("slab"), 2) == 0
    above, below = weights(packed_ref, chunks)
    _, below_of_above = weights(outer_ref, chunks)
    taken = jnp.where(even, below, above) * stacked_planes(
        inner_ref, members, fields, chunks
    ) + above * stacked_planes(outer_ref, members, fields, chunks)
    given = below_of_above * here_ref[...]
    partial_ref[...] = part_ref[...] + taken
    picked = picked_values(jnp.concatenate([taken, given], axis=0), taps_ref[...])
    observed = part_obs_ref[...]
    for side in range(2):
        kinds = kinds_ref[side : side + 1, :]
        for f in range(fields):
            start = (side * fields + f) * members
            observed += jnp.where(kinds == f, picked[start : start + members], 0.0)
    first_here = keeps_first(parts)
    half = observed.shape[1] // 2
    first, second = observed[:, :half], observed[:, half:]
    keep_ref[...] = jnp.where(first_here, first, second)
    send_ref[...] = jnp.where(first_here, second, first)


def sum_kernel(terms_ref, other_ref, *refs):
    refs[-1][...] = terms_ref[...] + other_ref[...]


def complete_kernel(members, fields, chunks, partial_ref, outer_ref, packed_ref, forecast_ref):
    _, below = weights(packed_ref, chunks)
    forecast_ref[...] = partial_ref[...] + below * stacked_planes(
        outer_ref, members, fields, chunks
    )


def gather_kernel(*refs):
    local = refs[0].shape[0]
    for d, ref in enumerate(refs[:-1]):
        refs[-1][d * local : (d + 1) * local, :] = ref[...]


def solve_transposed(system, right_t, floor):
    size = system.shape[0]
    eye = identity(size, size)
    top = jnp.max(jnp.sum(jnp.abs(system), axis=0, keepdims=True)) + 1.0
    scale = 2.0 / (top + floor)
    eps = (top - floor) / (top + floor)
    residual = eye - scale * system
    answer = scale * right_t

    def more(carry):
        return carry[0] > 1e-6

    def double(carry):
        eps, residual, answer = carry
        both = jnp.dot(
            jnp.concatenate([residual, answer], axis=0),
            residual,
            precision=HIGHEST,
            preferred_element_type=F32,
        )
        square = eps * eps
        share = 1.0 / (2.0 - square)
        return (
            square * share,
            (2.0 * both[:size] - square * eye) * share,
            (answer + both[size:]) * (2.0 * share),
        )

    return lax.while_loop(more, double, (eps, residual, answer))[2]


def identity(rows, columns, shift=0):
    return (
        lax.broadcasted_iota(jnp.int32, (rows, columns), 0) + shift
        == lax.broadcasted_iota(jnp.int32, (rows, columns), 1)
    ).astype(F32)


def solve_kernel(
    parts, value_ref, error_ref, noise_ref, kept_ref, received_ref, mine_ref, prior, whole
):
    batches, members, count = noise_ref.shape
    local = members // parts
    own = lax.axis_index("mem")
    own_rows = pl.ds(pl.multiple_of(own * local, local), local)
    first_here = keeps_first(parts)
    half = batches * count // 2
    for d in range(parts):
        owner = lax.rem(own + d, parts)
        rows = pl.ds(pl.multiple_of(owner * local, local), local)
        kept = kept_ref[d * local : (d + 1) * local, :]
        received = received_ref[d * local : (d + 1) * local, :]
        prior[rows, :half] = jnp.where(first_here, kept, received)
        prior[rows, half:] = jnp.where(first_here, received, kept)
    source = lax.broadcasted_iota(jnp.int32, (members, members), 0)
    target = lax.broadcasted_iota(jnp.int32, (members, members), 1)
    turn = (source == lax.rem(target + own * local, members)).astype(F32)
    product_t = turned = None
    for b in range(batches):
        last = b == batches - 1
        observed = prior[:, b * count : (b + 1) * count]
        if product_t is not None:
            both = jnp.dot(
                product_t,
                jnp.concatenate([observed, turn], axis=1) if last else observed,
                precision=HIGHEST,
                preferred_element_type=F32,
            )
            observed, turned = both[:, :count], both[:, count:]
        share = 1.0 / error_ref[b : b + 1, :]
        scaled = (observed - jnp.mean(observed, axis=0, keepdims=True)) * share
        if last:
            whole[...] = observed
            innovation = (
                value_ref[b : b + 1, :] * share + noise_ref[b, own_rows, :]
            ) - whole[own_rows, :] * share
            eye = identity(local, members, own * local)
        else:
            innovation = (value_ref[b : b + 1, :] * share + noise_ref[b]) - observed * share
            eye = identity(members, members)
        both = lax.dot_general(
            jnp.concatenate([scaled, innovation], axis=0),
            scaled,
            (((1,), (1,)), ((), ())),
            precision=HIGHEST,
            preferred_element_type=F32,
        )
        system = both[:members] + (members - 1.0) * identity(members, members)
        weights_t = solve_transposed(system, both[members:], members - 1.0)
        matrix_t = eye + weights_t - jnp.mean(weights_t, axis=1, keepdims=True)
        if last:
            mine_ref[...] = jnp.dot(
                matrix_t,
                turn if turned is None else turned,
                precision=HIGHEST,
                preferred_element_type=F32,
            )
        elif product_t is None:
            product_t = matrix_t
        else:
            product_t = jnp.dot(
                matrix_t, product_t, precision=HIGHEST, preferred_element_type=F32
            )


def combine_kernel(parts, fields, mine_ref, *refs):
    forecast_refs, delayed_refs = refs[:parts], refs[parts : 2 * parts]
    out_ref, done_ref, sems = refs[2 * parts :]
    local = mine_ref.shape[0]
    high, low = split_two(mine_ref[...])
    left = jnp.concatenate([high, high, low], axis=1)
    chunks = forecast_refs[0].shape[1] // LANES
    level = fields * chunks
    lagged = delayed_refs[0].shape[0] // local
    planes = level + lagged
    copies = []
    for first in [*range(level, planes, level), 0]:
        for f in range(fields):
            start = first + f * chunks
            if first == 0:
                held = [ref[f * local : (f + 1) * local, :] for ref in forecast_refs]
            else:
                held = [
                    jnp.concatenate(
                        [
                            ref[pl.ds(start - level + c, local, stride=lagged), :]
                            for c in range(chunks)
                        ],
                        axis=1,
                    )
                    for ref in delayed_refs
                ]
            held_high, held_low = split_two(jnp.concatenate(held, axis=0))
            result = jnp.dot(
                left,
                jnp.concatenate([held_high, held_low, held_high], axis=0),
                preferred_element_type=F32,
            )
            for c in range(chunks):
                done_ref[pl.ds(start + c, local, stride=planes), :] = result[
                    :, c * LANES : (c + 1) * LANES
                ]
        copies.append(
            pltpu.make_async_copy(
                done_ref.reshape(local, planes, LANES).at[:, first : first + level, :],
                out_ref.at[:, first : first + level, :],
                sems.at[len(copies)],
            )
        )
        copies[-1].start()
    for copy in copies:
        copy.wait()


def shards(
    present_ensemble,
    delayed_ensemble,
    spreading_coefficient,
    transport_ratios,
    obs_value,
    obs_error,
    obs_noise,
    obs_row,
    obs_col,
    obs_field,
):
    members, fields, height, width = present_ensemble.shape
    assert height == 1 and width % LANES == 0
    chunks = width // LANES
    lagged = delayed_ensemble.shape[1]
    slabs, parts = lax.axis_size("slab"), lax.axis_size("mem")
    assert slabs & (slabs - 1) == 0 and slabs >= 8
    batches, all_members, count = obs_noise.shape
    total = batches * count
    planes = (1 + lagged) * fields * chunks
    stacked = (fields * members, width)
    hbm = pl.BlockSpec(memory_space=pltpu.HBM)
    sizes = (members, fields, chunks)

    odd = range(1, slabs, 2)

    def from_slab(array, bit):
        return lax.ppermute(array, "slab", [(i, i ^ bit) for i in range(slabs)])

    def from_other_pair(array, bit):
        return from_slab(array, bit ^ 1)

    def from_other_mem(array):
        if parts != 2:
            return from_partners(array)
        return [
            lax.ppermute(
                array, ("slab", "mem"), [(i ^ 3, i) for i in range(slabs * parts)]
            )
        ]

    def from_partners(array):
        return [
            lax.ppermute(array, "mem", [((i + d) % parts, i) for i in range(parts)])
            for d in range(1, parts)
        ]

    present, delayed = rows_of(present_ensemble), rows_of(delayed_ensemble)
    spread, ratios = rows_of(spreading_coefficient), rows_of(transport_ratios)
    sources = in_hbm((present, spread, ratios, obs_row, obs_col, obs_field))
    packed, *held = pl.pallas_call(
        functools.partial(load_kernel, chunks),
        out_shape=[shape_of((present.shape[0] + 2 * chunks, LANES))]
        + [shape_of(x.shape, x.dtype) for x in sources[1:]],
        in_specs=[hbm] * len(sources),
        scratch_shapes=[pltpu.SemaphoreType.DMA((len(sources),))],
        compiler_params=PARAMS,
        name="load",
    )(*sources)
    outer_above = lax.ppermute(packed, "slab", [(i, i + 1) for i in odd[:-1]])
    others_delayed = from_partners(
        lax.optimization_barrier((delayed, packed))[0]
    )
    outer_below = lax.ppermute(packed, "slab", [(i + 1, i) for i in odd[:-1]])
    taps, kinds = pl.pallas_call(
        selector_kernel,
        out_shape=(shape_of((width, total), BF16), shape_of((2, total), jnp.int32)),
        compiler_params=PARAMS,
        cost_estimate=estimate(SELECT_FLOPS),
        name="selector",
    )(*held[2:])
    part, here, part_obs = pl.pallas_call(
        functools.partial(own_row_kernel, *sizes),
        out_shape=(shape_of(stacked), shape_of(stacked), shape_of((members, total))),
        compiler_params=PARAMS,
        cost_estimate=estimate(OWN_FLOPS),
        name="own_row",
    )(packed, *held[:2], taps, kinds)
    inner = from_slab(packed, 1)
    keep, send, partial = pl.pallas_call(
        functools.partial(observe_kernel, parts, *sizes),
        out_shape=(
            shape_of((members, total // 2)),
            shape_of((members, total // 2)),
            shape_of(stacked),
        ),
        compiler_params=PARAMS,
        name="observe",
    )(packed, inner, outer_above, part, part_obs, here, taps, kinds)
    def summed(terms, other, flops, *arrived):
        return pl.pallas_call(
            sum_kernel,
            out_shape=shape_of(terms.shape),
            cost_estimate=estimate(flops),
            compiler_params=PARAMS,
            name="sum",
        )(terms, other, *arrived)

    terms = keep + from_slab(send, 1)
    for bit in [1 << k for k in reversed(range(1, slabs.bit_length() - 1))]:
        terms = summed(
            terms,
            from_other_pair(terms, bit),
            SUM_FLOPS[min(slabs // 2 // bit, 4) // 2],
            *([others_delayed[0]] if bit == 2 else []),
        )
        if bit == slabs // 2:
            after_far = terms
    forecast = pl.pallas_call(
        functools.partial(complete_kernel, *sizes),
        out_shape=shape_of(stacked),
        compiler_params=PARAMS,
        name="complete",
    )(
        lax.optimization_barrier((partial, after_far))[0], outer_below, packed
    )

    prior = pl.pallas_call(
        gather_kernel,
        out_shape=shape_of((all_members, total // 2)),
        cost_estimate=estimate(GATHER_FLOPS),
        compiler_params=PARAMS,
        name="gather",
    )(terms, *from_other_mem(terms))
    mine = pl.pallas_call(
        functools.partial(solve_kernel, parts),
        out_shape=shape_of((members, all_members)),
        scratch_shapes=[
            pltpu.VMEM((all_members, total), F32),
            pltpu.VMEM((all_members, count), F32),
        ],
        compiler_params=PARAMS,
        cost_estimate=estimate(SOLVE_FLOPS),
        name="solve",
    )(obs_value, obs_error, obs_noise, prior, from_slab(prior, 1))
    out = pl.pallas_call(
        functools.partial(combine_kernel, parts, fields),
        out_shape=shape_of((members, planes, LANES)),
        out_specs=hbm,
        scratch_shapes=[
            pltpu.VMEM((members * planes, LANES), F32),
            pltpu.SemaphoreType.DMA((1 + lagged,)),
        ],
        compiler_params=PARAMS,
        name="combine",
    )(mine, forecast, *from_partners(forecast), delayed, *others_delayed)
    return out.reshape(members, 1 + lagged, fields, height, width)


def solution(mesh):
    return jax.shard_map(
        shards,
        mesh=mesh,
        in_specs=(
            P("mem", None, "slab", None),
            P("mem", None, None, "slab", None),
            P("slab", None),
            P(None, "slab", None),
            P(),
            P(),
            P(),
            P(),
            P(),
            P(),
        ),
        out_specs=P("mem", None, None, "slab", None),
        check_vma=False,
    )
```

```python
import functools

import jax
import jax.numpy as jnp
from jax import lax
from jax.experimental import pallas as pl
from jax.experimental.pallas import tpu as pltpu
from jax.sharding import PartitionSpec as P

LANES = 128
F32 = jnp.float32
BF16 = jnp.bfloat16
HIGHEST = lax.Precision.HIGHEST
PARAMS = pltpu.CompilerParams(vmem_limit_bytes=48 * 1024 * 1024)


SELECT_FLOPS = 1
STEPS = 5
OWN_FLOPS, SUM_FLOPS, GATHER_FLOPS, SOLVE_FLOPS = 1, (7*10**8,7*10**8,1), 10**8, 5*10**8


def estimate(flops):
    return pl.CostEstimate(flops=flops, transcendentals=0, bytes_accessed=0)


def rows_of(array):
    return array.reshape(-1, LANES)


def in_hbm(arrays):
    return [pltpu.with_memory_space_constraint(array, pltpu.HBM) for array in arrays]


def shape_of(shape, dtype=F32):
    return jax.ShapeDtypeStruct(shape, dtype)


def split_two(x):
    high = x.astype(BF16)
    low = (x - high.astype(F32)).astype(BF16)
    return high, low


def split_three(x):
    high = x.astype(BF16)
    rest = x - high.astype(F32)
    middle = rest.astype(BF16)
    low = (rest - middle.astype(F32)).astype(BF16)
    return high, middle, low


def line(ref, start, chunks):
    return jnp.concatenate([ref[start + c : start + c + 1, :] for c in range(chunks)], axis=1)


def stacked_planes(ref, members, fields, chunks):
    return jnp.concatenate(
        [
            jnp.concatenate(
                [
                    ref[pl.ds(f * chunks + c, members, stride=fields * chunks), :]
                    for c in range(chunks)
                ],
                axis=1,
            )
            for f in range(fields)
        ],
        axis=0,
    )


def at_once(sources, targets, sems):
    copies = [
        pltpu.make_async_copy(source, target, sems.at[i])
        for i, (source, target) in enumerate(zip(sources, targets))
    ]
    for copy in copies:
        copy.start()
    return copies


def picked_values(planes, taps):
    high, middle, low = (
        jnp.dot(part, taps, preferred_element_type=F32) for part in split_three(planes)
    )
    return low + middle + high


def load_kernel(chunks, *refs):
    count = (len(refs) - 1) // 2
    sources, packed_ref, held, sems = refs[:count], refs[count], refs[count + 1 : -1], refs[-1]
    rows = sources[0].shape[0]
    copies = at_once(sources, (packed_ref.at[:rows], *held), sems)
    copies[1].wait()
    copies[2].wait()
    spread = held[0][...]
    half = held[1][:chunks, :] * 0.5
    packed_ref[rows : rows + chunks, :] = spread + half
    packed_ref[rows + chunks : rows + 2 * chunks, :] = spread - half
    for copy in (copies[0], *copies[3:]):
        copy.wait()


def keeps_first(parts):
    rest = lax.axis_index("slab")
    ones = lax.axis_index("mem") if parts == 2 else 0
    for _ in range(lax.axis_size("slab").bit_length() - 1):
        ones = ones + lax.rem(rest, 2)
        rest = rest // 2
    return lax.rem(ones, 2) == 0


def weights(packed_ref, chunks):
    rows = packed_ref.shape[0] - 2 * chunks
    return line(packed_ref, rows, chunks), line(packed_ref, rows + chunks, chunks)


def selector_kernel(row_ref, col_ref, field_ref, taps_ref, kinds_ref):
    batches, count = row_ref.shape
    shape = taps_ref.shape
    flat = lambda ref: jnp.concatenate([ref[b : b + 1, :] for b in range(batches)], axis=1)
    rows, cols, kinds = flat(row_ref), flat(col_ref), flat(field_ref)
    own_row = lax.axis_index("slab")
    for k, row in enumerate((own_row, own_row - 1)):
        kinds_ref[k : k + 1, :] = jnp.where(rows == row, kinds, -1)
    at = lax.broadcasted_iota(jnp.int32, shape, 0).astype(F32) * 0.25
    taps_ref[...] = jnp.maximum(0.5 - jnp.abs(at - cols.astype(F32) * 0.25), 0.0).astype(BF16)


def own_row_kernel(
    members,
    fields,
    chunks,
    packed_ref,
    spread_ref,
    ratio_ref,
    taps_ref,
    kinds_ref,
    part_ref,
    here_ref,
    obs_ref,
):
    width = chunks * LANES
    spread = line(spread_ref, 0, chunks)
    along_columns = line(ratio_ref, chunks, chunks)
    here = stacked_planes(packed_ref, members, fields, chunks)
    here_ref[...] = here
    lane = lax.broadcasted_iota(jnp.int32, here.shape, 1)
    left = jnp.where(lane == 0, 0.0, pltpu.roll(here, 1, 1))
    right = jnp.where(lane == width - 1, 0.0, pltpu.roll(here, width - 1, 1))
    part = (
        here
        + spread * (right + left - 4.0 * here)
        - along_columns * (right - left) * 0.5
    )
    part_ref[...] = part
    picked = picked_values(part, taps_ref[...])
    observed = jnp.zeros(obs_ref.shape, F32)
    for f in range(fields):
        observed += jnp.where(
            kinds_ref[0:1, :] == f, picked[f * members : (f + 1) * members], 0.0
        )
    obs_ref[...] = observed


def observe_kernel(
    parts,
    members,
    fields,
    chunks,
    packed_ref,
    inner_ref,
    outer_ref,
    part_ref,
    part_obs_ref,
    here_ref,
    taps_ref,
    kinds_ref,
    keep_ref,
    send_ref,
    partial_ref,
):
    even = lax.rem(lax.axis_index("slab"), 2) == 0
    above, below = weights(packed_ref, chunks)
    _, below_of_above = weights(outer_ref, chunks)
    taken = jnp.where(even, below, above) * stacked_planes(
        inner_ref, members, fields, chunks
    ) + above * stacked_planes(outer_ref, members, fields, chunks)
    given = below_of_above * here_ref[...]
    partial_ref[...] = part_ref[...] + taken
    picked = picked_values(jnp.concatenate([taken, given], axis=0), taps_ref[...])
    observed = part_obs_ref[...]
    for side in range(2):
        kinds = kinds_ref[side : side + 1, :]
        for f in range(fields):
            start = (side * fields + f) * members
            observed += jnp.where(kinds == f, picked[start : start + members], 0.0)
    first_here = keeps_first(parts)
    half = observed.shape[1] // 2
    first, second = observed[:, :half], observed[:, half:]
    keep_ref[...] = jnp.where(first_here, first, second)
    send_ref[...] = jnp.where(first_here, second, first)


def sum_kernel(terms_ref, other_ref, *refs):
    refs[-1][...] = terms_ref[...] + other_ref[...]


def complete_kernel(members, fields, chunks, partial_ref, outer_ref, packed_ref, forecast_ref):
    _, below = weights(packed_ref, chunks)
    forecast_ref[...] = partial_ref[...] + below * stacked_planes(
        outer_ref, members, fields, chunks
    )


def gather_kernel(*refs):
    local = refs[0].shape[0]
    for d, ref in enumerate(refs[:-1]):
        refs[-1][d * local : (d + 1) * local, :] = ref[...]


def identity(rows, columns):
    return (
        lax.broadcasted_iota(jnp.int32, (rows, columns), 0)
        == lax.broadcasted_iota(jnp.int32, (rows, columns), 1)
    ).astype(F32)


def precise(x, y):
    return jnp.dot(x, y, precision=HIGHEST, preferred_element_type=F32)


def three_pass(x, y):
    x_high, x_low = split_two(x)
    y_high, y_low = split_two(y)
    dot = functools.partial(jnp.dot, preferred_element_type=F32)
    return dot(x_low, y_high) + dot(x_high, y_low) + dot(x_high, y_high)


def solve_transposed(system, right_t, floor):
    size = system.shape[0]
    eye = identity(size, size)
    top = jnp.max(jnp.sum(jnp.abs(system), axis=0, keepdims=True)) + 1.0
    scale = 2.0 / (top + floor)
    start = ((top - floor) / (top + floor), eye - scale * system, scale * right_t)

    def double(product, carry):
        eps, residual, answer = carry
        both = product(jnp.concatenate([residual, answer], axis=0), residual)
        square = eps * eps
        share = 1.0 / (2.0 - square)
        return (
            square * share,
            (2.0 * both[:size] - square * eye) * share,
            (answer + both[size:]) * (2.0 * share),
        )

    def more(carry):
        return carry[0] > 1e-6

    def well_conditioned():
        carry = start
        for _ in range(STEPS):
            carry = double(three_pass, carry)
        return lax.while_loop(more, functools.partial(double, three_pass), carry)[2]

    def otherwise():
        return lax.while_loop(more, functools.partial(double, precise), start)[2]

    return lax.cond(top < 32.0 * floor, well_conditioned, otherwise)


def solve_kernel(
    parts, value_ref, error_ref, noise_ref, kept_ref, received_ref, mine_ref
):
    batches, members, count = noise_ref.shape
    local = members // parts
    own = lax.axis_index("mem")
    first_here = keeps_first(parts)
    halves = [
        jnp.where(first_here, kept_ref[...], received_ref[...]),
        jnp.where(first_here, received_ref[...], kept_ref[...]),
    ]
    prior = jnp.concatenate(halves, axis=1)
    product_t = None
    for b in range(batches):
        last = b == batches - 1
        wanted = local if last else members
        observed = prior[:, b * count : (b + 1) * count]
        if product_t is not None:
            observed = precise(product_t, observed)
        share = 1.0 / error_ref[b : b + 1, :]
        scaled = (observed - jnp.mean(observed, axis=0, keepdims=True)) * share
        blocks = []
        for d in range(wanted // local):
            owner = lax.rem(own + d, parts)
            blocks.append(
                noise_ref[b, pl.ds(pl.multiple_of(owner * local, local), local), :]
            )
        noise = jnp.concatenate(blocks, axis=0)
        innovation = (value_ref[b : b + 1, :] * share + noise) - observed[:wanted] * share
        both = lax.dot_general(
            jnp.concatenate([scaled, innovation], axis=0),
            scaled,
            (((1,), (1,)), ((), ())),
            precision=HIGHEST,
            preferred_element_type=F32,
        )
        system = both[:members] + (members - 1.0) * identity(members, members)
        weights_t = solve_transposed(system, both[members:], members - 1.0)
        matrix_t = (
            identity(wanted, members) + weights_t - jnp.mean(weights_t, axis=1, keepdims=True)
        )
        product_t = matrix_t if product_t is None else precise(matrix_t, product_t)
    mine_ref[...] = product_t


def prepare_kernel(parts, *refs):
    sources, high_ref, low_ref = refs[:parts], refs[parts], refs[parts + 1]
    lagged = high_ref.shape[1] // LANES
    local = high_ref.shape[0] // parts
    for k in range(lagged):
        held = jnp.concatenate(
            [ref[pl.ds(k, local, stride=lagged), :] for ref in sources], axis=0
        )
        high, low = split_two(held)
        high_ref[:, k * LANES : (k + 1) * LANES] = high
        low_ref[:, k * LANES : (k + 1) * LANES] = low


def combine_kernel(parts, fields, mine_ref, *refs):
    forecast_refs = refs[:parts]
    lagged_high_ref, lagged_low_ref, out_ref, done_ref, sems = refs[parts:]
    local = mine_ref.shape[0]
    high, low = split_two(mine_ref[...])
    left = jnp.concatenate([high, high, low], axis=1)
    width = forecast_refs[0].shape[1]
    chunks = width // LANES
    level = fields * chunks
    planes = level + lagged_high_ref.shape[1] // LANES
    copies = []
    for first in [*range(level, planes, level), 0]:
        for f in range(fields):
            start = first + f * chunks
            if first == 0:
                held_high, held_low = split_two(
                    jnp.concatenate(
                        [ref[f * local : (f + 1) * local, :] for ref in forecast_refs], axis=0
                    )
                )
            else:
                lanes = slice((start - level) * LANES, (start - level) * LANES + width)
                held_high, held_low = lagged_high_ref[:, lanes], lagged_low_ref[:, lanes]
            result = jnp.dot(
                left,
                jnp.concatenate([held_high, held_low, held_high], axis=0),
                preferred_element_type=F32,
            )
            for c in range(chunks):
                done_ref[pl.ds(start + c, local, stride=planes), :] = result[
                    :, c * LANES : (c + 1) * LANES
                ]
        copies.append(
            pltpu.make_async_copy(
                done_ref.reshape(local, planes, LANES).at[:, first : first + level, :],
                out_ref.at[:, first : first + level, :],
                sems.at[len(copies)],
            )
        )
        copies[-1].start()
    for copy in copies:
        copy.wait()


def shards(
    present_ensemble,
    delayed_ensemble,
    spreading_coefficient,
    transport_ratios,
    obs_value,
    obs_error,
    obs_noise,
    obs_row,
    obs_col,
    obs_field,
):
    members, fields, height, width = present_ensemble.shape
    assert height == 1 and width % LANES == 0
    chunks = width // LANES
    lagged = delayed_ensemble.shape[1]
    slabs, parts = lax.axis_size("slab"), lax.axis_size("mem")
    assert slabs & (slabs - 1) == 0 and slabs >= 8
    batches, all_members, count = obs_noise.shape
    total = batches * count
    planes = (1 + lagged) * fields * chunks
    stacked = (fields * members, width)
    hbm = pl.BlockSpec(memory_space=pltpu.HBM)
    sizes = (members, fields, chunks)

    odd = range(1, slabs, 2)

    def from_slab(array, bit):
        return lax.ppermute(array, "slab", [(i, i ^ bit) for i in range(slabs)])

    def from_other_pair(array, bit):
        return from_slab(array, bit ^ 1)

    def from_other_mem(array):
        if parts != 2:
            return from_partners(array)
        return [
            lax.ppermute(
                array, ("slab", "mem"), [(i ^ 3, i) for i in range(slabs * parts)]
            )
        ]

    def from_partners(array):
        return [
            lax.ppermute(array, "mem", [((i + d) % parts, i) for i in range(parts)])
            for d in range(1, parts)
        ]

    present, delayed = rows_of(present_ensemble), rows_of(delayed_ensemble)
    spread, ratios = rows_of(spreading_coefficient), rows_of(transport_ratios)
    sources = in_hbm((present, spread, ratios, obs_row, obs_col, obs_field))
    packed, *held = pl.pallas_call(
        functools.partial(load_kernel, chunks),
        out_shape=[shape_of((present.shape[0] + 2 * chunks, LANES))]
        + [shape_of(x.shape, x.dtype) for x in sources[1:]],
        in_specs=[hbm] * len(sources),
        scratch_shapes=[pltpu.SemaphoreType.DMA((len(sources),))],
        compiler_params=PARAMS,
        name="load",
    )(*sources)
    outer_above = lax.ppermute(packed, "slab", [(i, i + 1) for i in odd[:-1]])
    others_delayed = from_partners(
        lax.optimization_barrier((delayed, packed))[0]
    )
    outer_below = lax.ppermute(packed, "slab", [(i + 1, i) for i in odd[:-1]])
    taps, kinds = pl.pallas_call(
        selector_kernel,
        out_shape=(shape_of((width, total), BF16), shape_of((2, total), jnp.int32)),
        compiler_params=PARAMS,
        cost_estimate=estimate(SELECT_FLOPS),
        name="selector",
    )(*held[2:])
    part, here, part_obs = pl.pallas_call(
        functools.partial(own_row_kernel, *sizes),
        out_shape=(shape_of(stacked), shape_of(stacked), shape_of((members, total))),
        compiler_params=PARAMS,
        cost_estimate=estimate(OWN_FLOPS),
        name="own_row",
    )(packed, *held[:2], taps, kinds)
    inner = from_slab(packed, 1)
    keep, send, partial = pl.pallas_call(
        functools.partial(observe_kernel, parts, *sizes),
        out_shape=(
            shape_of((members, total // 2)),
            shape_of((members, total // 2)),
            shape_of(stacked),
        ),
        compiler_params=PARAMS,
        name="observe",
    )(packed, inner, outer_above, part, part_obs, here, taps, kinds)
    def summed(terms, other, flops, *arrived):
        return pl.pallas_call(
            sum_kernel,
            out_shape=shape_of(terms.shape),
            cost_estimate=estimate(flops),
            compiler_params=PARAMS,
            name="sum",
        )(terms, other, *arrived)

    terms = keep + from_slab(send, 1)
    for bit in [1 << k for k in reversed(range(1, slabs.bit_length() - 1))]:
        terms = summed(
            terms,
            from_other_pair(terms, bit),
            SUM_FLOPS[min(slabs // 2 // bit, 4) // 2],
            *([others_delayed[0]] if bit == 2 else []),
        )
        if bit == slabs // 2:
            after_far = terms
    forecast = pl.pallas_call(
        functools.partial(complete_kernel, *sizes),
        out_shape=shape_of(stacked),
        compiler_params=PARAMS,
        name="complete",
    )(
        lax.optimization_barrier((partial, after_far))[0], outer_below, packed
    )

    prior = pl.pallas_call(
        gather_kernel,
        out_shape=shape_of((all_members, total // 2)),
        cost_estimate=estimate(GATHER_FLOPS),
        compiler_params=PARAMS,
        name="gather",
    )(terms, *from_other_mem(terms))
    mine = pl.pallas_call(
        functools.partial(solve_kernel, parts),
        out_shape=shape_of((members, all_members)),
        compiler_params=PARAMS,
        cost_estimate=estimate(SOLVE_FLOPS),
        name="solve",
    )(obs_value, obs_error, obs_noise, prior, from_slab(prior, 1))
    lagged_parts = pl.pallas_call(
        functools.partial(prepare_kernel, parts),
        out_shape=[shape_of((all_members, delayed.size // members), BF16)] * 2,
        compiler_params=PARAMS,
        name="prepare",
    )(delayed, *others_delayed)
    out = pl.pallas_call(
        functools.partial(combine_kernel, parts, fields),
        out_shape=shape_of((members, planes, LANES)),
        out_specs=hbm,
        scratch_shapes=[
            pltpu.VMEM((members * planes, LANES), F32),
            pltpu.SemaphoreType.DMA((1 + lagged,)),
        ],
        compiler_params=PARAMS,
        name="combine",
    )(mine, forecast, *from_partners(forecast), *lagged_parts)
    return out.reshape(members, 1 + lagged, fields, height, width)


def solution(mesh):
    return jax.shard_map(
        shards,
        mesh=mesh,
        in_specs=(
            P("mem", None, "slab", None),
            P("mem", None, None, "slab", None),
            P("slab", None),
            P(None, "slab", None),
            P(),
            P(),
            P(),
            P(),
            P(),
            P(),
        ),
        out_specs=P("mem", None, None, "slab", None),
        check_vma=False,
    )
```

```python
import functools

import jax
import jax.numpy as jnp
from jax import lax
from jax.experimental import pallas as pl
from jax.experimental.pallas import tpu as pltpu
from jax.sharding import PartitionSpec as P

LANES = 128
F32 = jnp.float32
BF16 = jnp.bfloat16
HIGHEST = lax.Precision.HIGHEST
PARAMS = pltpu.CompilerParams(vmem_limit_bytes=48 * 1024 * 1024)


SELECT_FLOPS = 1
OWN_FLOPS, SUM_FLOPS, GATHER_FLOPS, SOLVE_FLOPS = 1, (7*10**8,7*10**8,1), 10**8, 5*10**8


def estimate(flops):
    return pl.CostEstimate(flops=flops, transcendentals=0, bytes_accessed=0)


def rows_of(array):
    return array.reshape(-1, LANES)


def in_hbm(arrays):
    return [pltpu.with_memory_space_constraint(array, pltpu.HBM) for array in arrays]


def shape_of(shape, dtype=F32):
    return jax.ShapeDtypeStruct(shape, dtype)


def split_two(x):
    high = x.astype(BF16)
    low = (x - high.astype(F32)).astype(BF16)
    return high, low


def split_three(x):
    high = x.astype(BF16)
    rest = x - high.astype(F32)
    middle = rest.astype(BF16)
    low = (rest - middle.astype(F32)).astype(BF16)
    return high, middle, low


def line(ref, start, chunks):
    return jnp.concatenate([ref[start + c : start + c + 1, :] for c in range(chunks)], axis=1)


def stacked_planes(ref, members, fields, chunks):
    return jnp.concatenate(
        [
            jnp.concatenate(
                [
                    ref[pl.ds(f * chunks + c, members, stride=fields * chunks), :]
                    for c in range(chunks)
                ],
                axis=1,
            )
            for f in range(fields)
        ],
        axis=0,
    )


def at_once(sources, targets, sems):
    copies = [
        pltpu.make_async_copy(source, target, sems.at[i])
        for i, (source, target) in enumerate(zip(sources, targets))
    ]
    for copy in copies:
        copy.start()
    return copies


def picked_values(planes, taps):
    high, middle, low = (
        jnp.dot(part, taps, preferred_element_type=F32) for part in split_three(planes)
    )
    return low + middle + high


def load_kernel(chunks, *refs):
    count = (len(refs) - 1) // 2
    sources, packed_ref, held, sems = refs[:count], refs[count], refs[count + 1 : -1], refs[-1]
    rows = sources[0].shape[0]
    copies = at_once(sources, (packed_ref.at[:rows], *held), sems)
    copies[1].wait()
    copies[2].wait()
    spread = held[0][...]
    half = held[1][:chunks, :] * 0.5
    packed_ref[rows : rows + chunks, :] = spread + half
    packed_ref[rows + chunks : rows + 2 * chunks, :] = spread - half
    for copy in (copies[0], *copies[3:]):
        copy.wait()


def keeps_first(parts):
    rest = lax.axis_index("slab")
    ones = lax.axis_index("mem") if parts == 2 else 0
    for _ in range(lax.axis_size("slab").bit_length() - 1):
        ones = ones + lax.rem(rest, 2)
        rest = rest // 2
    return lax.rem(ones, 2) == 0


def weights(packed_ref, chunks):
    rows = packed_ref.shape[0] - 2 * chunks
    return line(packed_ref, rows, chunks), line(packed_ref, rows + chunks, chunks)


def selector_kernel(row_ref, col_ref, field_ref, taps_ref, kinds_ref):
    batches, count = row_ref.shape
    shape = taps_ref.shape
    flat = lambda ref: jnp.concatenate([ref[b : b + 1, :] for b in range(batches)], axis=1)
    rows, cols, kinds = flat(row_ref), flat(col_ref), flat(field_ref)
    own_row = lax.axis_index("slab")
    for k, row in enumerate((own_row, own_row - 1)):
        kinds_ref[k : k + 1, :] = jnp.where(rows == row, kinds, -1)
    at = lax.broadcasted_iota(jnp.int32, shape, 0).astype(F32) * 0.25
    taps_ref[...] = jnp.maximum(0.5 - jnp.abs(at - cols.astype(F32) * 0.25), 0.0).astype(BF16)


def own_row_kernel(
    members,
    fields,
    chunks,
    packed_ref,
    spread_ref,
    ratio_ref,
    taps_ref,
    kinds_ref,
    part_ref,
    here_ref,
    obs_ref,
):
    width = chunks * LANES
    spread = line(spread_ref, 0, chunks)
    along_columns = line(ratio_ref, chunks, chunks)
    here = stacked_planes(packed_ref, members, fields, chunks)
    here_ref[...] = here
    lane = lax.broadcasted_iota(jnp.int32, here.shape, 1)
    left = jnp.where(lane == 0, 0.0, pltpu.roll(here, 1, 1))
    right = jnp.where(lane == width - 1, 0.0, pltpu.roll(here, width - 1, 1))
    part = (
        here
        + spread * (right + left - 4.0 * here)
        - along_columns * (right - left) * 0.5
    )
    part_ref[...] = part
    picked = picked_values(part, taps_ref[...])
    observed = jnp.zeros(obs_ref.shape, F32)
    for f in range(fields):
        observed += jnp.where(
            kinds_ref[0:1, :] == f, picked[f * members : (f + 1) * members], 0.0
        )
    obs_ref[...] = observed


def observe_kernel(
    parts,
    members,
    fields,
    chunks,
    packed_ref,
    inner_ref,
    outer_ref,
    part_ref,
    part_obs_ref,
    here_ref,
    taps_ref,
    kinds_ref,
    keep_ref,
    send_ref,
    partial_ref,
):
    even = lax.rem(lax.axis_index("slab"), 2) == 0
    above, below = weights(packed_ref, chunks)
    _, below_of_above = weights(outer_ref, chunks)
    taken = jnp.where(even, below, above) * stacked_planes(
        inner_ref, members, fields, chunks
    ) + above * stacked_planes(outer_ref, members, fields, chunks)
    given = below_of_above * here_ref[...]
    partial_ref[...] = part_ref[...] + taken
    picked = picked_values(jnp.concatenate([taken, given], axis=0), taps_ref[...])
    observed = part_obs_ref[...]
    for side in range(2):
        kinds = kinds_ref[side : side + 1, :]
        for f in range(fields):
            start = (side * fields + f) * members
            observed += jnp.where(kinds == f, picked[start : start + members], 0.0)
    first_here = keeps_first(parts)
    half = observed.shape[1] // 2
    first, second = observed[:, :half], observed[:, half:]
    keep_ref[...] = jnp.where(first_here, first, second)
    send_ref[...] = jnp.where(first_here, second, first)


def sum_kernel(terms_ref, other_ref, *refs):
    refs[-1][...] = terms_ref[...] + other_ref[...]


def complete_kernel(members, fields, chunks, partial_ref, outer_ref, packed_ref, forecast_ref):
    _, below = weights(packed_ref, chunks)
    forecast_ref[...] = partial_ref[...] + below * stacked_planes(
        outer_ref, members, fields, chunks
    )


def gather_kernel(*refs):
    local = refs[0].shape[0]
    for d, ref in enumerate(refs[:-1]):
        refs[-1][d * local : (d + 1) * local, :] = ref[...]


def identity(rows, columns):
    return (
        lax.broadcasted_iota(jnp.int32, (rows, columns), 0)
        == lax.broadcasted_iota(jnp.int32, (rows, columns), 1)
    ).astype(F32)


def precise(x, y):
    return jnp.dot(x, y, precision=HIGHEST, preferred_element_type=F32)


def three_pass(x, y):
    x_high, x_low = split_two(x)
    y_high, y_low = split_two(y)
    dot = functools.partial(jnp.dot, preferred_element_type=F32)
    return dot(x_low, y_high) + dot(x_high, y_low) + dot(x_high, y_high)


def solve_transposed(system, right_t, floor):
    size = system.shape[0]
    eye = identity(size, size)
    sums = jnp.sum(jnp.abs(system), axis=0, keepdims=True)
    top = jnp.max(sums, axis=1, keepdims=True) + 1.0
    scale = 2.0 / (top + floor)
    start = (1.0 - floor * scale, eye - scale * system, scale * right_t)

    def double(product, carry):
        eps, residual, answer = carry
        both = product(jnp.concatenate([residual, answer], axis=0), residual)
        square = eps * eps
        share = 1.0 / (2.0 - square)
        return (
            square * share,
            (2.0 * both[:size] - square * eye) * share,
            (answer + both[size:]) * (2.0 * share),
        )

    def steps(count):
        carry = start
        for _ in range(count):
            carry = double(three_pass, carry)
        return carry[2]

    def loop():
        return lax.while_loop(
            lambda carry: jnp.max(carry[0]) > 1e-6, functools.partial(double, precise), start
        )[2]

    condition = jnp.max(top) / floor
    return lax.cond(
        condition < 20.0,
        lambda: steps(5),
        lambda: lax.cond(condition < 78.0, lambda: steps(6), loop),
    )


def precise_nt(x, y):
    return lax.dot_general(
        x, y, (((1,), (1,)), ((), ())), precision=HIGHEST, preferred_element_type=F32
    )


def solve_kernel(parts, value_ref, error_ref, noise_ref, kept_ref, received_ref, mine_ref):
    batches, members, count = noise_ref.shape
    local = members // parts
    own = lax.axis_index("mem")
    first_here = keeps_first(parts)
    halves = [
        jnp.where(first_here, kept_ref[...], received_ref[...]),
        jnp.where(first_here, received_ref[...], kept_ref[...]),
    ]
    prior = jnp.concatenate(halves, axis=1)
    grams = []
    for b in range(batches):
        wanted = local if b == batches - 1 else members
        observed = prior[:, b * count : (b + 1) * count]
        share = 1.0 / error_ref[b : b + 1, :]
        mean = jnp.mean(observed, axis=0, keepdims=True)
        anomalies = (observed - mean) * share
        blocks = []
        for d in range(wanted // local):
            owner = lax.rem(own + d, parts)
            blocks.append(
                noise_ref[b, pl.ds(pl.multiple_of(owner * local, local), local), :]
            )
        innovation = (value_ref[b : b + 1, :] - mean) * share + jnp.concatenate(blocks, axis=0)
        both = precise_nt(jnp.concatenate([anomalies, innovation], axis=0), anomalies)
        grams.append((both[:members], both[members:]))
    diagonal = (members - 1.0) * identity(members, members)
    product_t = None
    for b, (gram, cross) in enumerate(grams):
        wanted = cross.shape[0]
        if product_t is None:
            system, right_t = gram, cross - gram[:wanted]
        else:
            centred = product_t - jnp.mean(product_t, axis=0, keepdims=True)
            both = precise(jnp.concatenate([centred, product_t[:wanted]], axis=0), gram)
            both = precise_nt(
                jnp.concatenate([both[:members], cross - both[members:]], axis=0), centred
            )
            system, right_t = both[:members], both[members:]
        weights_t = solve_transposed(system + diagonal, right_t, members - 1.0)
        matrix_t = (
            identity(wanted, members) + weights_t - jnp.mean(weights_t, axis=1, keepdims=True)
        )
        product_t = matrix_t if product_t is None else precise(matrix_t, product_t)
    mine_ref[...] = product_t


def prepare_kernel(parts, *refs):
    sources, high_ref, low_ref = refs[:parts], refs[parts], refs[parts + 1]
    lagged = high_ref.shape[1] // LANES
    local = high_ref.shape[0] // parts
    for k in range(lagged):
        held = jnp.concatenate(
            [ref[pl.ds(k, local, stride=lagged), :] for ref in sources], axis=0
        )
        high, low = split_two(held)
        high_ref[:, k * LANES : (k + 1) * LANES] = high
        low_ref[:, k * LANES : (k + 1) * LANES] = low


def combine_kernel(parts, fields, mine_ref, *refs):
    forecast_refs = refs[:parts]
    lagged_high_ref, lagged_low_ref, out_ref, done_ref, sems = refs[parts:]
    local = mine_ref.shape[0]
    high, low = split_two(mine_ref[...])
    left = jnp.concatenate([high, high, low], axis=1)
    width = forecast_refs[0].shape[1]
    chunks = width // LANES
    level = fields * chunks
    planes = level + lagged_high_ref.shape[1] // LANES
    copies = []
    for first in [*range(level, planes, level), 0]:
        for f in range(fields):
            start = first + f * chunks
            if first == 0:
                held_high, held_low = split_two(
                    jnp.concatenate(
                        [ref[f * local : (f + 1) * local, :] for ref in forecast_refs], axis=0
                    )
                )
            else:
                lanes = slice((start - level) * LANES, (start - level) * LANES + width)
                held_high, held_low = lagged_high_ref[:, lanes], lagged_low_ref[:, lanes]
            result = jnp.dot(
                left,
                jnp.concatenate([held_high, held_low, held_high], axis=0),
                preferred_element_type=F32,
            )
            for c in range(chunks):
                done_ref[pl.ds(start + c, local, stride=planes), :] = result[
                    :, c * LANES : (c + 1) * LANES
                ]
        copies.append(
            pltpu.make_async_copy(
                done_ref.reshape(local, planes, LANES).at[:, first : first + level, :],
                out_ref.at[:, first : first + level, :],
                sems.at[len(copies)],
            )
        )
        copies[-1].start()
    for copy in copies:
        copy.wait()


def shards(
    present_ensemble,
    delayed_ensemble,
    spreading_coefficient,
    transport_ratios,
    obs_value,
    obs_error,
    obs_noise,
    obs_row,
    obs_col,
    obs_field,
):
    members, fields, height, width = present_ensemble.shape
    assert height == 1 and width % LANES == 0
    chunks = width // LANES
    lagged = delayed_ensemble.shape[1]
    slabs, parts = lax.axis_size("slab"), lax.axis_size("mem")
    assert slabs & (slabs - 1) == 0 and slabs >= 8
    batches, all_members, count = obs_noise.shape
    total = batches * count
    planes = (1 + lagged) * fields * chunks
    stacked = (fields * members, width)
    hbm = pl.BlockSpec(memory_space=pltpu.HBM)
    sizes = (members, fields, chunks)

    odd = range(1, slabs, 2)

    def from_slab(array, bit):
        return lax.ppermute(array, "slab", [(i, i ^ bit) for i in range(slabs)])

    def from_other_pair(array, bit):
        return from_slab(array, bit ^ 1)

    def from_other_mem(array):
        if parts != 2:
            return from_partners(array)
        return [
            lax.ppermute(
                array, ("slab", "mem"), [(i ^ 3, i) for i in range(slabs * parts)]
            )
        ]

    def from_partners(array):
        return [
            lax.ppermute(array, "mem", [((i + d) % parts, i) for i in range(parts)])
            for d in range(1, parts)
        ]

    present, delayed = rows_of(present_ensemble), rows_of(delayed_ensemble)
    spread, ratios = rows_of(spreading_coefficient), rows_of(transport_ratios)
    sources = in_hbm((present, spread, ratios, obs_row, obs_col, obs_field))
    packed, *held = pl.pallas_call(
        functools.partial(load_kernel, chunks),
        out_shape=[shape_of((present.shape[0] + 2 * chunks, LANES))]
        + [shape_of(x.shape, x.dtype) for x in sources[1:]],
        in_specs=[hbm] * len(sources),
        scratch_shapes=[pltpu.SemaphoreType.DMA((len(sources),))],
        compiler_params=PARAMS,
        name="load",
    )(*sources)
    outer_above = lax.ppermute(packed, "slab", [(i, i + 1) for i in odd[:-1]])
    others_delayed = from_partners(
        lax.optimization_barrier((delayed, packed))[0]
    )
    outer_below = lax.ppermute(packed, "slab", [(i + 1, i) for i in odd[:-1]])
    taps, kinds = pl.pallas_call(
        selector_kernel,
        out_shape=(shape_of((width, total), BF16), shape_of((2, total), jnp.int32)),
        compiler_params=PARAMS,
        cost_estimate=estimate(SELECT_FLOPS),
        name="selector",
    )(*held[2:])
    part, here, part_obs = pl.pallas_call(
        functools.partial(own_row_kernel, *sizes),
        out_shape=(shape_of(stacked), shape_of(stacked), shape_of((members, total))),
        compiler_params=PARAMS,
        cost_estimate=estimate(OWN_FLOPS),
        name="own_row",
    )(packed, *held[:2], taps, kinds)
    inner = from_slab(packed, 1)
    keep, send, partial = pl.pallas_call(
        functools.partial(observe_kernel, parts, *sizes),
        out_shape=(
            shape_of((members, total // 2)),
            shape_of((members, total // 2)),
            shape_of(stacked),
        ),
        compiler_params=PARAMS,
        name="observe",
    )(packed, inner, outer_above, part, part_obs, here, taps, kinds)
    def summed(terms, other, flops, *arrived):
        return pl.pallas_call(
            sum_kernel,
            out_shape=shape_of(terms.shape),
            cost_estimate=estimate(flops),
            compiler_params=PARAMS,
            name="sum",
        )(terms, other, *arrived)

    terms = keep + from_slab(send, 1)
    for bit in [1 << k for k in reversed(range(1, slabs.bit_length() - 1))]:
        terms = summed(
            terms,
            from_other_pair(terms, bit),
            SUM_FLOPS[min(slabs // 2 // bit, 4) // 2],
            *([others_delayed[0]] if bit == 2 else []),
        )
        if bit == slabs // 2:
            after_far = terms
    forecast = pl.pallas_call(
        functools.partial(complete_kernel, *sizes),
        out_shape=shape_of(stacked),
        compiler_params=PARAMS,
        name="complete",
    )(
        lax.optimization_barrier((partial, after_far))[0], outer_below, packed
    )

    prior = pl.pallas_call(
        gather_kernel,
        out_shape=shape_of((all_members, total // 2)),
        cost_estimate=estimate(GATHER_FLOPS),
        compiler_params=PARAMS,
        name="gather",
    )(terms, *from_other_mem(terms))
    mine = pl.pallas_call(
        functools.partial(solve_kernel, parts),
        out_shape=shape_of((members, all_members)),
        compiler_params=PARAMS,
        cost_estimate=estimate(SOLVE_FLOPS),
        name="solve",
    )(obs_value, obs_error, obs_noise, prior, from_slab(prior, 1))
    lagged_parts = pl.pallas_call(
        functools.partial(prepare_kernel, parts),
        out_shape=[shape_of((all_members, delayed.size // members), BF16)] * 2,
        compiler_params=PARAMS,
        name="prepare",
    )(delayed, *others_delayed)
    out = pl.pallas_call(
        functools.partial(combine_kernel, parts, fields),
        out_shape=shape_of((members, planes, LANES)),
        out_specs=hbm,
        scratch_shapes=[
            pltpu.VMEM((members * planes, LANES), F32),
            pltpu.SemaphoreType.DMA((1 + lagged,)),
        ],
        compiler_params=PARAMS,
        name="combine",
    )(mine, forecast, *from_partners(forecast), *lagged_parts)
    return out.reshape(members, 1 + lagged, fields, height, width)


def solution(mesh):
    return jax.shard_map(
        shards,
        mesh=mesh,
        in_specs=(
            P("mem", None, "slab", None),
            P("mem", None, None, "slab", None),
            P("slab", None),
            P(None, "slab", None),
            P(),
            P(),
            P(),
            P(),
            P(),
            P(),
        ),
        out_specs=P("mem", None, None, "slab", None),
        check_vma=False,
    )
```

```python
import functools

import jax
import jax.numpy as jnp
from jax import lax
from jax.experimental import pallas as pl
from jax.experimental.pallas import tpu as pltpu
from jax.sharding import PartitionSpec as P

LANES = 128
F32 = jnp.float32
BF16 = jnp.bfloat16
HIGHEST = lax.Precision.HIGHEST
PARAMS = pltpu.CompilerParams(vmem_limit_bytes=48 * 1024 * 1024)


SELECT_FLOPS = 1
OWN_FLOPS, SUM_FLOPS, GATHER_FLOPS, SOLVE_FLOPS = 1, (7*10**8,7*10**8,1), 10**8, 5*10**8


def estimate(flops):
    return pl.CostEstimate(flops=flops, transcendentals=0, bytes_accessed=0)


def rows_of(array):
    return array.reshape(-1, LANES)


def in_hbm(arrays):
    return [pltpu.with_memory_space_constraint(array, pltpu.HBM) for array in arrays]


def shape_of(shape, dtype=F32):
    return jax.ShapeDtypeStruct(shape, dtype)


def split_two(x):
    high = x.astype(BF16)
    low = (x - high.astype(F32)).astype(BF16)
    return high, low


def split_three(x):
    high = x.astype(BF16)
    rest = x - high.astype(F32)
    middle = rest.astype(BF16)
    low = (rest - middle.astype(F32)).astype(BF16)
    return high, middle, low


def line(ref, start, chunks):
    return jnp.concatenate([ref[start + c : start + c + 1, :] for c in range(chunks)], axis=1)


def stacked_planes(ref, members, fields, chunks):
    return jnp.concatenate(
        [
            jnp.concatenate(
                [
                    ref[pl.ds(f * chunks + c, members, stride=fields * chunks), :]
                    for c in range(chunks)
                ],
                axis=1,
            )
            for f in range(fields)
        ],
        axis=0,
    )


def at_once(sources, targets, sems):
    copies = [
        pltpu.make_async_copy(source, target, sems.at[i])
        for i, (source, target) in enumerate(zip(sources, targets))
    ]
    for copy in copies:
        copy.start()
    return copies


def picked_values(planes, taps):
    high, middle, low = (
        jnp.dot(part, taps, preferred_element_type=F32) for part in split_three(planes)
    )
    return low + middle + high


def load_kernel(chunks, *refs):
    count = (len(refs) - 1) // 2
    sources, packed_ref, held, sems = refs[:count], refs[count], refs[count + 1 : -1], refs[-1]
    rows = sources[0].shape[0]
    copies = at_once(sources, (packed_ref.at[:rows], *held), sems)
    copies[1].wait()
    copies[2].wait()
    spread = held[0][...]
    half = held[1][:chunks, :] * 0.5
    packed_ref[rows : rows + chunks, :] = spread + half
    packed_ref[rows + chunks : rows + 2 * chunks, :] = spread - half
    for copy in (copies[0], *copies[3:]):
        copy.wait()


def keeps_first(parts):
    rest = lax.axis_index("slab")
    ones = lax.axis_index("mem") if parts == 2 else 0
    for _ in range(lax.axis_size("slab").bit_length() - 1):
        ones = ones + lax.rem(rest, 2)
        rest = rest // 2
    return lax.rem(ones, 2) == 0


def weights(packed_ref, chunks):
    rows = packed_ref.shape[0] - 2 * chunks
    return line(packed_ref, rows, chunks), line(packed_ref, rows + chunks, chunks)


def selector_kernel(row_ref, col_ref, field_ref, taps_ref, kinds_ref):
    batches, count = row_ref.shape
    shape = taps_ref.shape
    flat = lambda ref: jnp.concatenate([ref[b : b + 1, :] for b in range(batches)], axis=1)
    rows, cols, kinds = flat(row_ref), flat(col_ref), flat(field_ref)
    own_row = lax.axis_index("slab")
    for k, row in enumerate((own_row, own_row - 1)):
        kinds_ref[k : k + 1, :] = jnp.where(rows == row, kinds, -1)
    at = lax.broadcasted_iota(jnp.int32, shape, 0).astype(F32) * 0.25
    taps_ref[...] = jnp.maximum(0.5 - jnp.abs(at - cols.astype(F32) * 0.25), 0.0).astype(BF16)


def own_row_kernel(
    members,
    fields,
    chunks,
    packed_ref,
    spread_ref,
    ratio_ref,
    taps_ref,
    kinds_ref,
    part_ref,
    here_ref,
    obs_ref,
):
    width = chunks * LANES
    spread = line(spread_ref, 0, chunks)
    along_columns = line(ratio_ref, chunks, chunks)
    here = stacked_planes(packed_ref, members, fields, chunks)
    here_ref[...] = here
    lane = lax.broadcasted_iota(jnp.int32, here.shape, 1)
    left = jnp.where(lane == 0, 0.0, pltpu.roll(here, 1, 1))
    right = jnp.where(lane == width - 1, 0.0, pltpu.roll(here, width - 1, 1))
    part = (
        here
        + spread * (right + left - 4.0 * here)
        - along_columns * (right - left) * 0.5
    )
    part_ref[...] = part
    picked = picked_values(part, taps_ref[...])
    observed = jnp.zeros(obs_ref.shape, F32)
    for f in range(fields):
        observed += jnp.where(
            kinds_ref[0:1, :] == f, picked[f * members : (f + 1) * members], 0.0
        )
    obs_ref[...] = observed


def observe_kernel(
    parts,
    members,
    fields,
    chunks,
    packed_ref,
    up_ref,
    part_ref,
    part_obs_ref,
    here_ref,
    taps_ref,
    kinds_ref,
    keep_ref,
    send_ref,
    partial_ref,
):
    above, _ = weights(packed_ref, chunks)
    _, below_of_above = weights(up_ref, chunks)
    taken = above * stacked_planes(up_ref, members, fields, chunks)
    given = below_of_above * here_ref[...]
    partial_ref[...] = part_ref[...] + taken
    picked = picked_values(jnp.concatenate([taken, given], axis=0), taps_ref[...])
    observed = part_obs_ref[...]
    for side in range(2):
        kinds = kinds_ref[side : side + 1, :]
        for f in range(fields):
            start = (side * fields + f) * members
            observed += jnp.where(kinds == f, picked[start : start + members], 0.0)
    first_here = keeps_first(parts)
    half = observed.shape[1] // 2
    first, second = observed[:, :half], observed[:, half:]
    keep_ref[...] = jnp.where(first_here, first, second)
    send_ref[...] = jnp.where(first_here, second, first)


def sum_kernel(terms_ref, other_ref, *refs):
    refs[-1][...] = terms_ref[...] + other_ref[...]


def complete_kernel(members, fields, chunks, partial_ref, down_ref, packed_ref, forecast_ref):
    _, below = weights(packed_ref, chunks)
    forecast_ref[...] = partial_ref[...] + below * stacked_planes(
        down_ref, members, fields, chunks
    )


def gather_kernel(*refs):
    local = refs[0].shape[0]
    for d, ref in enumerate(refs[:-1]):
        refs[-1][d * local : (d + 1) * local, :] = ref[...]


def identity(rows, columns):
    return (
        lax.broadcasted_iota(jnp.int32, (rows, columns), 0)
        == lax.broadcasted_iota(jnp.int32, (rows, columns), 1)
    ).astype(F32)


def precise(x, y):
    return jnp.dot(x, y, precision=HIGHEST, preferred_element_type=F32)


def three_pass(x, y):
    x_high, x_low = split_two(x)
    y_high, y_low = split_two(y)
    dot = functools.partial(jnp.dot, preferred_element_type=F32)
    return dot(x_low, y_high) + dot(x_high, y_low) + dot(x_high, y_high)


def solve_transposed(system, right_t, floor):
    size = system.shape[0]
    eye = identity(size, size)
    sums = jnp.sum(jnp.abs(system), axis=0, keepdims=True)
    top = jnp.max(sums, axis=1, keepdims=True) + 1.0
    scale = 2.0 / (top + floor)
    start = (1.0 - floor * scale, eye - scale * system, scale * right_t)

    def double(product, carry):
        eps, residual, answer = carry
        both = product(jnp.concatenate([residual, answer], axis=0), residual)
        square = eps * eps
        share = 1.0 / (2.0 - square)
        return (
            square * share,
            (2.0 * both[:size] - square * eye) * share,
            (answer + both[size:]) * (2.0 * share),
        )

    def steps(count):
        carry = start
        for _ in range(count):
            carry = double(three_pass, carry)
        return carry[2]

    def loop():
        return lax.while_loop(
            lambda carry: jnp.max(carry[0]) > 1e-6, functools.partial(double, precise), start
        )[2]

    condition = jnp.max(top) / floor
    return lax.cond(
        condition < 20.0,
        lambda: steps(5),
        lambda: lax.cond(condition < 78.0, lambda: steps(6), loop),
    )


def precise_nt(x, y):
    return lax.dot_general(
        x, y, (((1,), (1,)), ((), ())), precision=HIGHEST, preferred_element_type=F32
    )


def solve_kernel(parts, value_ref, error_ref, noise_ref, kept_ref, received_ref, mine_ref):
    batches, members, count = noise_ref.shape
    local = members // parts
    own = lax.axis_index("mem")
    first_here = keeps_first(parts)
    halves = [
        jnp.where(first_here, kept_ref[...], received_ref[...]),
        jnp.where(first_here, received_ref[...], kept_ref[...]),
    ]
    prior = jnp.concatenate(halves, axis=1)
    grams = []
    for b in range(batches):
        wanted = local if b == batches - 1 else members
        observed = prior[:, b * count : (b + 1) * count]
        share = 1.0 / error_ref[b : b + 1, :]
        mean = jnp.mean(observed, axis=0, keepdims=True)
        anomalies = (observed - mean) * share
        blocks = []
        for d in range(wanted // local):
            owner = lax.rem(own + d, parts)
            blocks.append(
                noise_ref[b, pl.ds(pl.multiple_of(owner * local, local), local), :]
            )
        innovation = (value_ref[b : b + 1, :] - mean) * share + jnp.concatenate(blocks, axis=0)
        both = precise_nt(jnp.concatenate([anomalies, innovation], axis=0), anomalies)
        grams.append((both[:members], both[members:]))
    diagonal = (members - 1.0) * identity(members, members)
    product_t = None
    for b, (gram, cross) in enumerate(grams):
        wanted = cross.shape[0]
        if product_t is None:
            system, right_t = gram, cross - gram[:wanted]
        else:
            centred = product_t - jnp.mean(product_t, axis=0, keepdims=True)
            both = precise(jnp.concatenate([centred, product_t[:wanted]], axis=0), gram)
            both = precise_nt(
                jnp.concatenate([both[:members], cross - both[members:]], axis=0), centred
            )
            system, right_t = both[:members], both[members:]
        weights_t = solve_transposed(system + diagonal, right_t, members - 1.0)
        matrix_t = (
            identity(wanted, members) + weights_t - jnp.mean(weights_t, axis=1, keepdims=True)
        )
        product_t = matrix_t if product_t is None else precise(matrix_t, product_t)
    mine_ref[...] = product_t


def prepare_kernel(parts, *refs):
    sources, high_ref, low_ref = refs[:parts], refs[parts], refs[parts + 1]
    lagged = high_ref.shape[1] // LANES
    local = high_ref.shape[0] // parts
    for k in range(lagged):
        held = jnp.concatenate(
            [ref[pl.ds(k, local, stride=lagged), :] for ref in sources], axis=0
        )
        high, low = split_two(held)
        high_ref[:, k * LANES : (k + 1) * LANES] = high
        low_ref[:, k * LANES : (k + 1) * LANES] = low


def combine_kernel(parts, fields, mine_ref, *refs):
    forecast_refs = refs[:parts]
    lagged_high_ref, lagged_low_ref, out_ref, done_ref, sems = refs[parts:]
    local = mine_ref.shape[0]
    high, low = split_two(mine_ref[...])
    left = jnp.concatenate([high, high, low], axis=1)
    width = forecast_refs[0].shape[1]
    chunks = width // LANES
    level = fields * chunks
    planes = level + lagged_high_ref.shape[1] // LANES
    copies = []
    for first in [*range(level, planes, level), 0]:
        for f in range(fields):
            start = first + f * chunks
            if first == 0:
                held_high, held_low = split_two(
                    jnp.concatenate(
                        [ref[f * local : (f + 1) * local, :] for ref in forecast_refs], axis=0
                    )
                )
            else:
                lanes = slice((start - level) * LANES, (start - level) * LANES + width)
                held_high, held_low = lagged_high_ref[:, lanes], lagged_low_ref[:, lanes]
            result = jnp.dot(
                left,
                jnp.concatenate([held_high, held_low, held_high], axis=0),
                preferred_element_type=F32,
            )
            for c in range(chunks):
                done_ref[pl.ds(start + c, local, stride=planes), :] = result[
                    :, c * LANES : (c + 1) * LANES
                ]
        copies.append(
            pltpu.make_async_copy(
                done_ref.reshape(local, planes, LANES).at[:, first : first + level, :],
                out_ref.at[:, first : first + level, :],
                sems.at[len(copies)],
            )
        )
        copies[-1].start()
    for copy in copies:
        copy.wait()


def shards(
    present_ensemble,
    delayed_ensemble,
    spreading_coefficient,
    transport_ratios,
    obs_value,
    obs_error,
    obs_noise,
    obs_row,
    obs_col,
    obs_field,
):
    members, fields, height, width = present_ensemble.shape
    assert height == 1 and width % LANES == 0
    chunks = width // LANES
    lagged = delayed_ensemble.shape[1]
    slabs, parts = lax.axis_size("slab"), lax.axis_size("mem")
    assert slabs & (slabs - 1) == 0 and slabs >= 8
    batches, all_members, count = obs_noise.shape
    total = batches * count
    planes = (1 + lagged) * fields * chunks
    stacked = (fields * members, width)
    hbm = pl.BlockSpec(memory_space=pltpu.HBM)
    sizes = (members, fields, chunks)

    def from_slab(array, bit):
        return lax.ppermute(array, "slab", [(i, i ^ bit) for i in range(slabs)])

    def from_other_pair(array, bit):
        return from_slab(array, bit ^ 1)

    def from_other_mem(array):
        if parts != 2:
            return from_partners(array)
        return [
            lax.ppermute(
                array, ("slab", "mem"), [(i ^ 3, i) for i in range(slabs * parts)]
            )
        ]

    def from_partners(array):
        return [
            lax.ppermute(array, "mem", [((i + d) % parts, i) for i in range(parts)])
            for d in range(1, parts)
        ]

    present, delayed = rows_of(present_ensemble), rows_of(delayed_ensemble)
    spread, ratios = rows_of(spreading_coefficient), rows_of(transport_ratios)
    sources = in_hbm((present, spread, ratios, obs_row, obs_col, obs_field))
    packed, *held = pl.pallas_call(
        functools.partial(load_kernel, chunks),
        out_shape=[shape_of((present.shape[0] + 2 * chunks, LANES))]
        + [shape_of(x.shape, x.dtype) for x in sources[1:]],
        in_specs=[hbm] * len(sources),
        scratch_shapes=[pltpu.SemaphoreType.DMA((len(sources),))],
        compiler_params=PARAMS,
        name="load",
    )(*sources)
    up = [(i, i + 1) for i in range(slabs - 1)]
    from_above = lax.ppermute(packed, "slab", up)
    others_delayed = from_partners(
        lax.optimization_barrier((delayed, packed))[0]
    )
    from_below = lax.ppermute(packed, "slab", [(j, i) for i, j in up])
    taps, kinds = pl.pallas_call(
        selector_kernel,
        out_shape=(shape_of((width, total), BF16), shape_of((2, total), jnp.int32)),
        compiler_params=PARAMS,
        cost_estimate=estimate(SELECT_FLOPS),
        name="selector",
    )(*held[2:])
    part, here, part_obs = pl.pallas_call(
        functools.partial(own_row_kernel, *sizes),
        out_shape=(shape_of(stacked), shape_of(stacked), shape_of((members, total))),
        compiler_params=PARAMS,
        cost_estimate=estimate(OWN_FLOPS),
        name="own_row",
    )(packed, *held[:2], taps, kinds)
    keep, send, partial = pl.pallas_call(
        functools.partial(observe_kernel, parts, *sizes),
        out_shape=(
            shape_of((members, total // 2)),
            shape_of((members, total // 2)),
            shape_of(stacked),
        ),
        compiler_params=PARAMS,
        name="observe",
    )(packed, from_above, part, part_obs, here, taps, kinds)
    def summed(terms, other, flops, *arrived):
        return pl.pallas_call(
            sum_kernel,
            out_shape=shape_of(terms.shape),
            cost_estimate=estimate(flops),
            compiler_params=PARAMS,
            name="sum",
        )(terms, other, *arrived)

    terms = keep + from_slab(send, 1)
    for bit in [1 << k for k in reversed(range(1, slabs.bit_length() - 1))]:
        terms = summed(
            terms,
            from_other_pair(terms, bit),
            SUM_FLOPS[min(slabs // 2 // bit, 4) // 2],
            *([others_delayed[0]] if bit == 2 else []),
        )
        if bit == slabs // 2:
            after_far = terms
    forecast = pl.pallas_call(
        functools.partial(complete_kernel, *sizes),
        out_shape=shape_of(stacked),
        compiler_params=PARAMS,
        name="complete",
    )(
        lax.optimization_barrier((partial, after_far))[0], from_below, packed
    )

    prior = pl.pallas_call(
        gather_kernel,
        out_shape=shape_of((all_members, total // 2)),
        cost_estimate=estimate(GATHER_FLOPS),
        compiler_params=PARAMS,
        name="gather",
    )(terms, *from_other_mem(terms))
    mine = pl.pallas_call(
        functools.partial(solve_kernel, parts),
        out_shape=shape_of((members, all_members)),
        compiler_params=PARAMS,
        cost_estimate=estimate(SOLVE_FLOPS),
        name="solve",
    )(obs_value, obs_error, obs_noise, prior, from_slab(prior, 1))
    lagged_parts = pl.pallas_call(
        functools.partial(prepare_kernel, parts),
        out_shape=[shape_of((all_members, delayed.size // members), BF16)] * 2,
        compiler_params=PARAMS,
        name="prepare",
    )(delayed, *others_delayed)
    out = pl.pallas_call(
        functools.partial(combine_kernel, parts, fields),
        out_shape=shape_of((members, planes, LANES)),
        out_specs=hbm,
        scratch_shapes=[
            pltpu.VMEM((members * planes, LANES), F32),
            pltpu.SemaphoreType.DMA((1 + lagged,)),
        ],
        compiler_params=PARAMS,
        name="combine",
    )(mine, forecast, *from_partners(forecast), *lagged_parts)
    return out.reshape(members, 1 + lagged, fields, height, width)


def solution(mesh):
    return jax.shard_map(
        shards,
        mesh=mesh,
        in_specs=(
            P("mem", None, "slab", None),
            P("mem", None, None, "slab", None),
            P("slab", None),
            P(None, "slab", None),
            P(),
            P(),
            P(),
            P(),
            P(),
            P(),
        ),
        out_specs=P("mem", None, None, "slab", None),
        check_vma=False,
    )
```

```python
import functools

import jax
import jax.numpy as jnp
from jax import lax
from jax.experimental import pallas as pl
from jax.experimental.pallas import tpu as pltpu
from jax.sharding import PartitionSpec as P

LANES = 128
F32 = jnp.float32
BF16 = jnp.bfloat16
HIGHEST = lax.Precision.HIGHEST
PARAMS = pltpu.CompilerParams(vmem_limit_bytes=48 * 1024 * 1024)


SELECT_FLOPS = 1
OWN_FLOPS, SUM_FLOPS, GATHER_FLOPS, SOLVE_FLOPS = 10**11, (2*10**9,7*10**8,1), 10**8, 5*10**8


def estimate(flops):
    return pl.CostEstimate(flops=flops, transcendentals=0, bytes_accessed=0)


def rows_of(array):
    return array.reshape(-1, LANES)


def in_hbm(arrays):
    return [pltpu.with_memory_space_constraint(array, pltpu.HBM) for array in arrays]


def shape_of(shape, dtype=F32):
    return jax.ShapeDtypeStruct(shape, dtype)


def split_two(x):
    high = x.astype(BF16)
    low = (x - high.astype(F32)).astype(BF16)
    return high, low


def split_three(x):
    high = x.astype(BF16)
    rest = x - high.astype(F32)
    middle = rest.astype(BF16)
    low = (rest - middle.astype(F32)).astype(BF16)
    return high, middle, low


def line(ref, start, chunks):
    return jnp.concatenate([ref[start + c : start + c + 1, :] for c in range(chunks)], axis=1)


def stacked_planes(ref, members, fields, chunks):
    return jnp.concatenate(
        [
            jnp.concatenate(
                [
                    ref[pl.ds(f * chunks + c, members, stride=fields * chunks), :]
                    for c in range(chunks)
                ],
                axis=1,
            )
            for f in range(fields)
        ],
        axis=0,
    )


def at_once(sources, targets, sems):
    copies = [
        pltpu.make_async_copy(source, target, sems.at[i])
        for i, (source, target) in enumerate(zip(sources, targets))
    ]
    for copy in copies:
        copy.start()
    return copies


def picked_values(planes, taps):
    high, middle, low = (
        jnp.dot(part, taps, preferred_element_type=F32) for part in split_three(planes)
    )
    return low + middle + high


def load_kernel(chunks, *refs):
    count = (len(refs) - 2) // 2
    sources, held, packed_ref, coefs_ref, sems = refs[:count], refs[count:-3], *refs[-3:]
    rows = sources[0].shape[0]
    copies = at_once(sources, (packed_ref.at[:rows], *held), sems)
    copies[1].wait()
    copies[2].wait()
    spread = held[0][...]
    half = held[1][:chunks, :] * 0.5
    for ref, start in ((packed_ref, rows), (coefs_ref, 0)):
        ref[start : start + chunks, :] = spread + half
        ref[start + chunks : start + 2 * chunks, :] = spread - half
    for copy in (copies[0], *copies[3:]):
        copy.wait()


def keeps_first(parts):
    rest = lax.axis_index("slab")
    ones = lax.axis_index("mem") if parts == 2 else 0
    for _ in range(lax.axis_size("slab").bit_length() - 1):
        ones = ones + lax.rem(rest, 2)
        rest = rest // 2
    return lax.rem(ones, 2) == 0


def weights(packed_ref, chunks):
    rows = packed_ref.shape[0] - 2 * chunks
    return line(packed_ref, rows, chunks), line(packed_ref, rows + chunks, chunks)


def selector_kernel(row_ref, col_ref, field_ref, taps_ref, kinds_ref):
    batches, count = row_ref.shape
    shape = taps_ref.shape
    flat = lambda ref: jnp.concatenate([ref[b : b + 1, :] for b in range(batches)], axis=1)
    rows, cols, kinds = flat(row_ref), flat(col_ref), flat(field_ref)
    own_row = lax.axis_index("slab")
    for k, row in enumerate((own_row, own_row + 1, own_row - 1)):
        kinds_ref[k : k + 1, :] = jnp.where(rows == row, kinds, -1)
    at = lax.broadcasted_iota(jnp.int32, shape, 0).astype(F32) * 0.25
    taps_ref[...] = jnp.maximum(0.5 - jnp.abs(at - cols.astype(F32) * 0.25), 0.0).astype(BF16)


def own_row_kernel(
    members,
    fields,
    chunks,
    packed_ref,
    spread_ref,
    ratio_ref,
    taps_ref,
    kinds_ref,
    part_ref,
    here_ref,
    obs_ref,
):
    width = chunks * LANES
    spread = line(spread_ref, 0, chunks)
    along_columns = line(ratio_ref, chunks, chunks)
    here = stacked_planes(packed_ref, members, fields, chunks)
    here_ref[...] = here
    lane = lax.broadcasted_iota(jnp.int32, here.shape, 1)
    left = jnp.where(lane == 0, 0.0, pltpu.roll(here, 1, 1))
    right = jnp.where(lane == width - 1, 0.0, pltpu.roll(here, width - 1, 1))
    part = (
        here
        + spread * (right + left - 4.0 * here)
        - along_columns * (right - left) * 0.5
    )
    part_ref[...] = part
    picked = picked_values(part, taps_ref[...])
    observed = jnp.zeros(obs_ref.shape, F32)
    for f in range(fields):
        observed += jnp.where(
            kinds_ref[0:1, :] == f, picked[f * members : (f + 1) * members], 0.0
        )
    obs_ref[...] = observed


def observe_kernel(
    parts,
    members,
    fields,
    chunks,
    inner_ref,
    outer_ref,
    part_obs_ref,
    here_ref,
    taps_ref,
    kinds_ref,
    keep_ref,
    send_ref,
):
    even = lax.rem(lax.axis_index("slab"), 2) == 0
    here = here_ref[...]
    inner, outer = weights(inner_ref, chunks), weights(outer_ref, chunks)
    to_below = jnp.where(even, inner[0], outer[0])
    to_above = jnp.where(even, outer[1], inner[1])
    picked = picked_values(
        jnp.concatenate([to_below * here, to_above * here], axis=0), taps_ref[...]
    )
    observed = part_obs_ref[...]
    for side in range(2):
        kinds = kinds_ref[1 + side : 2 + side, :]
        for f in range(fields):
            start = (side * fields + f) * members
            observed += jnp.where(kinds == f, picked[start : start + members], 0.0)
    first_here = keeps_first(parts)
    half = observed.shape[1] // 2
    first, second = observed[:, :half], observed[:, half:]
    keep_ref[...] = jnp.where(first_here, first, second)
    send_ref[...] = jnp.where(first_here, second, first)


def sum_kernel(terms_ref, other_ref, *refs):
    refs[-1][...] = terms_ref[...] + other_ref[...]


def complete_kernel(members, fields, chunks, part_ref, packed_ref, inner_ref, outer_ref, forecast_ref):
    even = lax.rem(lax.axis_index("slab"), 2) == 0
    above, below = weights(packed_ref, chunks)
    forecast_ref[...] = (
        part_ref[...]
        + jnp.where(even, below, above) * stacked_planes(inner_ref, members, fields, chunks)
        + jnp.where(even, above, below) * stacked_planes(outer_ref, members, fields, chunks)
    )


def gather_kernel(*refs):
    local = refs[0].shape[0]
    for d, ref in enumerate(refs[:-1]):
        refs[-1][d * local : (d + 1) * local, :] = ref[...]


def identity(rows, columns):
    return (
        lax.broadcasted_iota(jnp.int32, (rows, columns), 0)
        == lax.broadcasted_iota(jnp.int32, (rows, columns), 1)
    ).astype(F32)


def precise(x, y):
    return jnp.dot(x, y, precision=HIGHEST, preferred_element_type=F32)


def three_pass(x, y):
    x_high, x_low = split_two(x)
    y_high, y_low = split_two(y)
    dot = functools.partial(jnp.dot, preferred_element_type=F32)
    return dot(x_low, y_high) + dot(x_high, y_low) + dot(x_high, y_high)


def solve_transposed(system, right_t, floor):
    size = system.shape[0]
    eye = identity(size, size)
    sums = jnp.sum(jnp.abs(system), axis=0, keepdims=True)
    top = jnp.max(sums, axis=1, keepdims=True) + 1.0
    scale = 2.0 / (top + floor)
    start = (1.0 - floor * scale, eye - scale * system, scale * right_t)

    def double(product, carry):
        eps, residual, answer = carry
        both = product(jnp.concatenate([residual, answer], axis=0), residual)
        square = eps * eps
        share = 1.0 / (2.0 - square)
        return (
            square * share,
            (2.0 * both[:size] - square * eye) * share,
            (answer + both[size:]) * (2.0 * share),
        )

    def steps(count):
        carry = start
        for _ in range(count):
            carry = double(three_pass, carry)
        return carry[2]

    def loop():
        return lax.while_loop(
            lambda carry: jnp.max(carry[0]) > 1e-6, functools.partial(double, precise), start
        )[2]

    condition = jnp.max(top) / floor
    return lax.cond(
        condition < 20.0,
        lambda: steps(5),
        lambda: lax.cond(condition < 78.0, lambda: steps(6), loop),
    )


def precise_nt(x, y):
    return lax.dot_general(
        x, y, (((1,), (1,)), ((), ())), precision=HIGHEST, preferred_element_type=F32
    )


def solve_kernel(parts, value_ref, error_ref, noise_ref, kept_ref, received_ref, mine_ref):
    batches, members, count = noise_ref.shape
    local = members // parts
    own = lax.axis_index("mem")
    first_here = keeps_first(parts)
    halves = [
        jnp.where(first_here, kept_ref[...], received_ref[...]),
        jnp.where(first_here, received_ref[...], kept_ref[...]),
    ]
    prior = jnp.concatenate(halves, axis=1)
    grams = []
    for b in range(batches):
        wanted = local if b == batches - 1 else members
        observed = prior[:, b * count : (b + 1) * count]
        share = 1.0 / error_ref[b : b + 1, :]
        mean = jnp.mean(observed, axis=0, keepdims=True)
        anomalies = (observed - mean) * share
        blocks = []
        for d in range(wanted // local):
            owner = lax.rem(own + d, parts)
            blocks.append(
                noise_ref[b, pl.ds(pl.multiple_of(owner * local, local), local), :]
            )
        innovation = (value_ref[b : b + 1, :] - mean) * share + jnp.concatenate(blocks, axis=0)
        both = precise_nt(jnp.concatenate([anomalies, innovation], axis=0), anomalies)
        grams.append((both[:members], both[members:]))
    diagonal = (members - 1.0) * identity(members, members)
    product_t = None
    for b, (gram, cross) in enumerate(grams):
        wanted = cross.shape[0]
        if product_t is None:
            system, right_t = gram, cross - gram[:wanted]
        else:
            centred = product_t - jnp.mean(product_t, axis=0, keepdims=True)
            both = precise(jnp.concatenate([centred, product_t[:wanted]], axis=0), gram)
            both = precise_nt(
                jnp.concatenate([both[:members], cross - both[members:]], axis=0), centred
            )
            system, right_t = both[:members], both[members:]
        weights_t = solve_transposed(system + diagonal, right_t, members - 1.0)
        matrix_t = (
            identity(wanted, members) + weights_t - jnp.mean(weights_t, axis=1, keepdims=True)
        )
        product_t = matrix_t if product_t is None else precise(matrix_t, product_t)
    mine_ref[...] = product_t


def prepare_kernel(parts, *refs):
    sources, high_ref, low_ref = refs[:parts], refs[parts], refs[parts + 1]
    lagged = high_ref.shape[1] // LANES
    local = high_ref.shape[0] // parts
    for k in range(lagged):
        held = jnp.concatenate(
            [ref[pl.ds(k, local, stride=lagged), :] for ref in sources], axis=0
        )
        high, low = split_two(held)
        high_ref[:, k * LANES : (k + 1) * LANES] = high
        low_ref[:, k * LANES : (k + 1) * LANES] = low


def combine_kernel(parts, fields, mine_ref, *refs):
    forecast_refs = refs[:parts]
    lagged_high_ref, lagged_low_ref, out_ref, done_ref, sems = refs[parts:]
    local = mine_ref.shape[0]
    high, low = split_two(mine_ref[...])
    left = jnp.concatenate([high, high, low], axis=1)
    width = forecast_refs[0].shape[1]
    chunks = width // LANES
    level = fields * chunks
    planes = level + lagged_high_ref.shape[1] // LANES
    copies = []
    for first in [*range(level, planes, level), 0]:
        for f in range(fields):
            start = first + f * chunks
            if first == 0:
                held_high, held_low = split_two(
                    jnp.concatenate(
                        [ref[f * local : (f + 1) * local, :] for ref in forecast_refs], axis=0
                    )
                )
            else:
                lanes = slice((start - level) * LANES, (start - level) * LANES + width)
                held_high, held_low = lagged_high_ref[:, lanes], lagged_low_ref[:, lanes]
            result = jnp.dot(
                left,
                jnp.concatenate([held_high, held_low, held_high], axis=0),
                preferred_element_type=F32,
            )
            for c in range(chunks):
                done_ref[pl.ds(start + c, local, stride=planes), :] = result[
                    :, c * LANES : (c + 1) * LANES
                ]
        copies.append(
            pltpu.make_async_copy(
                done_ref.reshape(local, planes, LANES).at[:, first : first + level, :],
                out_ref.at[:, first : first + level, :],
                sems.at[len(copies)],
            )
        )
        copies[-1].start()
    for copy in copies:
        copy.wait()


def shards(
    present_ensemble,
    delayed_ensemble,
    spreading_coefficient,
    transport_ratios,
    obs_value,
    obs_error,
    obs_noise,
    obs_row,
    obs_col,
    obs_field,
):
    members, fields, height, width = present_ensemble.shape
    assert height == 1 and width % LANES == 0
    chunks = width // LANES
    lagged = delayed_ensemble.shape[1]
    slabs, parts = lax.axis_size("slab"), lax.axis_size("mem")
    assert slabs & (slabs - 1) == 0 and slabs >= 8
    batches, all_members, count = obs_noise.shape
    total = batches * count
    planes = (1 + lagged) * fields * chunks
    stacked = (fields * members, width)
    hbm = pl.BlockSpec(memory_space=pltpu.HBM)
    sizes = (members, fields, chunks)

    def from_slab(array, bit):
        return lax.ppermute(array, "slab", [(i, i ^ bit) for i in range(slabs)])

    def from_other_pair(array, bit):
        return from_slab(array, bit ^ 1)

    def from_other_mem(array):
        if parts != 2:
            return from_partners(array)
        return [
            lax.ppermute(
                array, ("slab", "mem"), [(i ^ 3, i) for i in range(slabs * parts)]
            )
        ]

    def from_partners(array):
        return [
            lax.ppermute(array, "mem", [((i + d) % parts, i) for i in range(parts)])
            for d in range(1, parts)
        ]

    present, delayed = rows_of(present_ensemble), rows_of(delayed_ensemble)
    spread, ratios = rows_of(spreading_coefficient), rows_of(transport_ratios)
    sources = in_hbm((present, spread, ratios, obs_row, obs_col, obs_field))
    *held, packed, coefs = pl.pallas_call(
        functools.partial(load_kernel, chunks),
        out_shape=[shape_of(x.shape, x.dtype) for x in sources[1:]]
        + [shape_of((present.shape[0] + 2 * chunks, LANES)), shape_of((2 * chunks, LANES))],
        in_specs=[hbm] * len(sources),
        scratch_shapes=[pltpu.SemaphoreType.DMA((len(sources),))],
        compiler_params=PARAMS,
        name="load",
    )(*sources)
    outer_pairs = [(i, i + 1) for i in range(1, slabs - 1, 2)]
    outer_pairs += [(j, i) for i, j in outer_pairs]
    outer_coefs = lax.ppermute(coefs, "slab", outer_pairs)
    inner = from_slab(packed, 1)
    others_delayed = from_partners(
        lax.optimization_barrier((delayed, packed))[0]
    )
    taps, kinds = pl.pallas_call(
        selector_kernel,
        out_shape=(shape_of((width, total), BF16), shape_of((3, total), jnp.int32)),
        compiler_params=PARAMS,
        cost_estimate=estimate(SELECT_FLOPS),
        name="selector",
    )(*held[2:])
    part, here, part_obs = pl.pallas_call(
        functools.partial(own_row_kernel, *sizes),
        out_shape=(shape_of(stacked), shape_of(stacked), shape_of((members, total))),
        compiler_params=PARAMS,
        cost_estimate=estimate(OWN_FLOPS),
        name="own_row",
    )(packed, *held[:2], taps, kinds)
    keep, send = pl.pallas_call(
        functools.partial(observe_kernel, parts, *sizes),
        out_shape=[shape_of((members, total // 2))] * 2,
        compiler_params=PARAMS,
        name="observe",
    )(inner, outer_coefs, part_obs, here, taps, kinds)

    def summed(terms, other, flops, *arrived):
        return pl.pallas_call(
            sum_kernel,
            out_shape=shape_of(terms.shape),
            cost_estimate=estimate(flops),
            compiler_params=PARAMS,
            name="sum",
        )(terms, other, *arrived)

    terms = keep + from_slab(send, 1)
    outer_row = lax.ppermute(
        lax.optimization_barrier((packed, terms))[0], "slab", outer_pairs
    )
    far = slabs // 2
    terms = summed(terms, from_other_pair(terms, far), SUM_FLOPS[0])
    terms = pl.pallas_call(
        gather_kernel,
        out_shape=shape_of((all_members, total // 2)),
        cost_estimate=estimate(GATHER_FLOPS),
        compiler_params=PARAMS,
        name="gather",
    )(terms, *from_other_mem(terms))
    forecast = pl.pallas_call(
        functools.partial(complete_kernel, *sizes),
        out_shape=shape_of(stacked),
        compiler_params=PARAMS,
        name="complete",
    )(lax.optimization_barrier((part, terms))[0], packed, inner, outer_row)
    bit = far // 2
    while bit > 1:
        last = bit == 2
        terms = summed(
            terms,
            from_other_pair(terms, bit),
            SUM_FLOPS[1 + last],
            *([others_delayed[0]] if last else []),
        )
        bit //= 2
    priors = [terms, from_slab(terms, 1)]
    mine = pl.pallas_call(
        functools.partial(solve_kernel, parts),
        out_shape=shape_of((members, all_members)),
        compiler_params=PARAMS,
        cost_estimate=estimate(SOLVE_FLOPS),
        name="solve",
    )(obs_value, obs_error, obs_noise, *priors)
    lagged_parts = pl.pallas_call(
        functools.partial(prepare_kernel, parts),
        out_shape=[shape_of((all_members, delayed.size // members), BF16)] * 2,
        compiler_params=PARAMS,
        name="prepare",
    )(delayed, *others_delayed)
    out = pl.pallas_call(
        functools.partial(combine_kernel, parts, fields),
        out_shape=shape_of((members, planes, LANES)),
        out_specs=hbm,
        scratch_shapes=[
            pltpu.VMEM((members * planes, LANES), F32),
            pltpu.SemaphoreType.DMA((1 + lagged,)),
        ],
        compiler_params=PARAMS,
        name="combine",
    )(mine, forecast, *from_partners(forecast), *lagged_parts)
    return out.reshape(members, 1 + lagged, fields, height, width)


def solution(mesh):
    return jax.shard_map(
        shards,
        mesh=mesh,
        in_specs=(
            P("mem", None, "slab", None),
            P("mem", None, None, "slab", None),
            P("slab", None),
            P(None, "slab", None),
            P(),
            P(),
            P(),
            P(),
            P(),
            P(),
        ),
        out_specs=P("mem", None, None, "slab", None),
        check_vma=False,
    )
```

```python
import functools

import jax
import jax.numpy as jnp
from jax import lax
from jax.experimental import pallas as pl
from jax.experimental.pallas import tpu as pltpu
from jax.sharding import PartitionSpec as P

LANES = 128
F32 = jnp.float32
BF16 = jnp.bfloat16
HIGHEST = lax.Precision.HIGHEST
PARAMS = pltpu.CompilerParams(vmem_limit_bytes=48 * 1024 * 1024)


SELECT_FLOPS = 1
OWN_FLOPS, SUM_FLOPS, GATHER_FLOPS, SOLVE_FLOPS = 10**11, (10**9,7*10**8,1), 10**9, 5*10**8


def estimate(flops):
    return pl.CostEstimate(flops=flops, transcendentals=0, bytes_accessed=0)


def rows_of(array):
    return array.reshape(-1, LANES)


def in_hbm(arrays):
    return [pltpu.with_memory_space_constraint(array, pltpu.HBM) for array in arrays]


def shape_of(shape, dtype=F32):
    return jax.ShapeDtypeStruct(shape, dtype)


def split_two(x):
    high = x.astype(BF16)
    low = (x - high.astype(F32)).astype(BF16)
    return high, low


def split_three(x):
    high = x.astype(BF16)
    rest = x - high.astype(F32)
    middle = rest.astype(BF16)
    low = (rest - middle.astype(F32)).astype(BF16)
    return high, middle, low


def line(ref, start, chunks):
    return jnp.concatenate([ref[start + c : start + c + 1, :] for c in range(chunks)], axis=1)


def stacked_planes(ref, members, fields, chunks):
    return jnp.concatenate(
        [
            jnp.concatenate(
                [
                    ref[pl.ds(f * chunks + c, members, stride=fields * chunks), :]
                    for c in range(chunks)
                ],
                axis=1,
            )
            for f in range(fields)
        ],
        axis=0,
    )


def at_once(sources, targets, sems):
    copies = [
        pltpu.make_async_copy(source, target, sems.at[i])
        for i, (source, target) in enumerate(zip(sources, targets))
    ]
    for copy in copies:
        copy.start()
    return copies


def picked_values(planes, taps):
    high, middle, low = (
        jnp.dot(part, taps, preferred_element_type=F32) for part in split_three(planes)
    )
    return low + middle + high


def load_kernel(chunks, *refs):
    sources, (*held, first_ref, second_ref, packed_ref, coefs_ref), sems = (
        refs[:7],
        refs[7:-1],
        refs[-1],
    )
    present, delayed, *others = sources
    rows, half = present.shape[0], first_ref.shape[0]
    copies = at_once(
        [present, delayed.at[:half], delayed.at[half:], *others],
        [packed_ref.at[:rows], first_ref, second_ref, *held],
        sems,
    )
    copies[3].wait()
    copies[4].wait()
    spread = held[0][...]
    along_rows = held[1][:chunks, :] * 0.5
    for ref, start in ((packed_ref, rows), (coefs_ref, 0)):
        ref[start : start + chunks, :] = spread + along_rows
        ref[start + chunks : start + 2 * chunks, :] = spread - along_rows
    for copy in (*copies[:3], *copies[5:]):
        copy.wait()


def keeps_first(parts):
    rest = lax.axis_index("slab")
    ones = lax.axis_index("mem") if parts == 2 else 0
    for _ in range(lax.axis_size("slab").bit_length() - 1):
        ones = ones + lax.rem(rest, 2)
        rest = rest // 2
    return lax.rem(ones, 2) == 0


def weights(packed_ref, chunks):
    rows = packed_ref.shape[0] - 2 * chunks
    return line(packed_ref, rows, chunks), line(packed_ref, rows + chunks, chunks)


def selector_kernel(row_ref, col_ref, field_ref, taps_ref, kinds_ref):
    batches, count = row_ref.shape
    shape = taps_ref.shape
    flat = lambda ref: jnp.concatenate([ref[b : b + 1, :] for b in range(batches)], axis=1)
    rows, cols, kinds = flat(row_ref), flat(col_ref), flat(field_ref)
    own_row = lax.axis_index("slab")
    for k, row in enumerate((own_row, own_row + 1, own_row - 1)):
        kinds_ref[k : k + 1, :] = jnp.where(rows == row, kinds, -1)
    at = lax.broadcasted_iota(jnp.int32, shape, 0).astype(F32) * 0.25
    taps_ref[...] = jnp.maximum(0.5 - jnp.abs(at - cols.astype(F32) * 0.25), 0.0).astype(BF16)


def own_row_kernel(
    members,
    fields,
    chunks,
    packed_ref,
    spread_ref,
    ratio_ref,
    taps_ref,
    kinds_ref,
    part_ref,
    here_ref,
    obs_ref,
):
    width = chunks * LANES
    spread = line(spread_ref, 0, chunks)
    along_columns = line(ratio_ref, chunks, chunks)
    here = stacked_planes(packed_ref, members, fields, chunks)
    here_ref[...] = here
    lane = lax.broadcasted_iota(jnp.int32, here.shape, 1)
    left = jnp.where(lane == 0, 0.0, pltpu.roll(here, 1, 1))
    right = jnp.where(lane == width - 1, 0.0, pltpu.roll(here, width - 1, 1))
    part = (
        here
        + spread * (right + left - 4.0 * here)
        - along_columns * (right - left) * 0.5
    )
    part_ref[...] = part
    picked = picked_values(part, taps_ref[...])
    observed = jnp.zeros(obs_ref.shape, F32)
    for f in range(fields):
        observed += jnp.where(
            kinds_ref[0:1, :] == f, picked[f * members : (f + 1) * members], 0.0
        )
    obs_ref[...] = observed


def observe_kernel(
    parts,
    members,
    fields,
    chunks,
    inner_ref,
    outer_ref,
    part_obs_ref,
    here_ref,
    taps_ref,
    kinds_ref,
    keep_ref,
    send_ref,
):
    even = lax.rem(lax.axis_index("slab"), 2) == 0
    here = here_ref[...]
    inner, outer = weights(inner_ref, chunks), weights(outer_ref, chunks)
    to_below = jnp.where(even, inner[0], outer[0])
    to_above = jnp.where(even, outer[1], inner[1])
    picked = picked_values(
        jnp.concatenate([to_below * here, to_above * here], axis=0), taps_ref[...]
    )
    observed = part_obs_ref[...]
    for side in range(2):
        kinds = kinds_ref[1 + side : 2 + side, :]
        for f in range(fields):
            start = (side * fields + f) * members
            observed += jnp.where(kinds == f, picked[start : start + members], 0.0)
    first_here = keeps_first(parts)
    half = observed.shape[1] // 2
    first, second = observed[:, :half], observed[:, half:]
    keep_ref[...] = jnp.where(first_here, first, second)
    send_ref[...] = jnp.where(first_here, second, first)


def sum_kernel(terms_ref, other_ref, *refs):
    refs[-1][...] = terms_ref[...] + other_ref[...]


def complete_kernel(members, fields, chunks, part_ref, packed_ref, inner_ref, outer_ref, forecast_ref):
    even = lax.rem(lax.axis_index("slab"), 2) == 0
    above, below = weights(packed_ref, chunks)
    forecast_ref[...] = (
        part_ref[...]
        + jnp.where(even, below, above) * stacked_planes(inner_ref, members, fields, chunks)
        + jnp.where(even, above, below) * stacked_planes(outer_ref, members, fields, chunks)
    )


def gather_kernel(*refs):
    local = refs[0].shape[0]
    for d, ref in enumerate(refs[:-1]):
        refs[-1][d * local : (d + 1) * local, :] = ref[...]


def identity(rows, columns):
    return (
        lax.broadcasted_iota(jnp.int32, (rows, columns), 0)
        == lax.broadcasted_iota(jnp.int32, (rows, columns), 1)
    ).astype(F32)


def precise(x, y):
    return jnp.dot(x, y, precision=HIGHEST, preferred_element_type=F32)


def three_pass(x, y):
    x_high, x_low = split_two(x)
    y_high, y_low = split_two(y)
    dot = functools.partial(jnp.dot, preferred_element_type=F32)
    return dot(x_low, y_high) + dot(x_high, y_low) + dot(x_high, y_high)


def solve_transposed(system, right_t, floor):
    size = system.shape[0]
    eye = identity(size, size)
    sums = jnp.sum(jnp.abs(system), axis=0, keepdims=True)
    top = jnp.max(sums, axis=1, keepdims=True) + 1.0
    scale = 2.0 / (top + floor)
    start = (1.0 - floor * scale, eye - scale * system, scale * right_t)

    def double(product, carry):
        eps, residual, answer = carry
        both = product(jnp.concatenate([residual, answer], axis=0), residual)
        square = eps * eps
        share = 1.0 / (2.0 - square)
        return (
            square * share,
            (2.0 * both[:size] - square * eye) * share,
            (answer + both[size:]) * (2.0 * share),
        )

    def steps(count):
        carry = start
        for _ in range(count):
            carry = double(three_pass, carry)
        return carry[2]

    def loop():
        return lax.while_loop(
            lambda carry: jnp.max(carry[0]) > 1e-6, functools.partial(double, precise), start
        )[2]

    condition = jnp.max(top) / floor
    return lax.cond(
        condition < 20.0,
        lambda: steps(5),
        lambda: lax.cond(condition < 78.0, lambda: steps(6), loop),
    )


def precise_nt(x, y):
    return lax.dot_general(
        x, y, (((1,), (1,)), ((), ())), precision=HIGHEST, preferred_element_type=F32
    )


def solve_kernel(parts, value_ref, error_ref, noise_ref, kept_ref, received_ref, mine_ref):
    batches, members, count = noise_ref.shape
    local = members // parts
    own = lax.axis_index("mem")
    first_here = keeps_first(parts)
    halves = [
        jnp.where(first_here, kept_ref[...], received_ref[...]),
        jnp.where(first_here, received_ref[...], kept_ref[...]),
    ]
    prior = jnp.concatenate(halves, axis=1)
    grams = []
    for b in range(batches):
        wanted = local if b == batches - 1 else members
        observed = prior[:, b * count : (b + 1) * count]
        share = 1.0 / error_ref[b : b + 1, :]
        mean = jnp.mean(observed, axis=0, keepdims=True)
        anomalies = (observed - mean) * share
        blocks = []
        for d in range(wanted // local):
            owner = lax.rem(own + d, parts)
            blocks.append(
                noise_ref[b, pl.ds(pl.multiple_of(owner * local, local), local), :]
            )
        innovation = (value_ref[b : b + 1, :] - mean) * share + jnp.concatenate(blocks, axis=0)
        both = precise_nt(jnp.concatenate([anomalies, innovation], axis=0), anomalies)
        grams.append((both[:members], both[members:]))
    diagonal = (members - 1.0) * identity(members, members)
    product_t = None
    for b, (gram, cross) in enumerate(grams):
        wanted = cross.shape[0]
        if product_t is None:
            system, right_t = gram, cross - gram[:wanted]
        else:
            centred = product_t - jnp.mean(product_t, axis=0, keepdims=True)
            both = precise(jnp.concatenate([centred, product_t[:wanted]], axis=0), gram)
            both = precise_nt(
                jnp.concatenate([both[:members], cross - both[members:]], axis=0), centred
            )
            system, right_t = both[:members], both[members:]
        weights_t = solve_transposed(system + diagonal, right_t, members - 1.0)
        matrix_t = (
            identity(wanted, members) + weights_t - jnp.mean(weights_t, axis=1, keepdims=True)
        )
        product_t = matrix_t if product_t is None else precise(matrix_t, product_t)
    mine_ref[...] = product_t


def prepare_kernel(parts, *refs):
    sources, high_ref, low_ref = refs[: 2 * parts], refs[2 * parts], refs[2 * parts + 1]
    lagged = high_ref.shape[1] // LANES
    count = high_ref.shape[0] // (2 * parts)
    for k in range(lagged):
        held = jnp.concatenate(
            [ref[pl.ds(k, count, stride=lagged), :] for ref in sources], axis=0
        )
        high, low = split_two(held)
        high_ref[:, k * LANES : (k + 1) * LANES] = high
        low_ref[:, k * LANES : (k + 1) * LANES] = low


def combine_kernel(parts, fields, mine_ref, *refs):
    forecast_refs = refs[:parts]
    lagged_high_ref, lagged_low_ref, out_ref, done_ref, sems = refs[parts:]
    local = mine_ref.shape[0]
    high, low = split_two(mine_ref[...])
    left = jnp.concatenate([high, high, low], axis=1)
    width = forecast_refs[0].shape[1]
    chunks = width // LANES
    level = fields * chunks
    planes = level + lagged_high_ref.shape[1] // LANES
    copies = []
    for first in [*range(level, planes, level), 0]:
        for f in range(fields):
            start = first + f * chunks
            if first == 0:
                held_high, held_low = split_two(
                    jnp.concatenate(
                        [ref[f * local : (f + 1) * local, :] for ref in forecast_refs], axis=0
                    )
                )
            else:
                lanes = slice((start - level) * LANES, (start - level) * LANES + width)
                held_high, held_low = lagged_high_ref[:, lanes], lagged_low_ref[:, lanes]
            result = jnp.dot(
                left,
                jnp.concatenate([held_high, held_low, held_high], axis=0),
                preferred_element_type=F32,
            )
            for c in range(chunks):
                done_ref[pl.ds(start + c, local, stride=planes), :] = result[
                    :, c * LANES : (c + 1) * LANES
                ]
        copies.append(
            pltpu.make_async_copy(
                done_ref.reshape(local, planes, LANES).at[:, first : first + level, :],
                out_ref.at[:, first : first + level, :],
                sems.at[len(copies)],
            )
        )
        copies[-1].start()
    for copy in copies:
        copy.wait()


def shards(
    present_ensemble,
    delayed_ensemble,
    spreading_coefficient,
    transport_ratios,
    obs_value,
    obs_error,
    obs_noise,
    obs_row,
    obs_col,
    obs_field,
):
    members, fields, height, width = present_ensemble.shape
    assert height == 1 and width % LANES == 0
    chunks = width // LANES
    lagged = delayed_ensemble.shape[1]
    slabs, parts = lax.axis_size("slab"), lax.axis_size("mem")
    assert slabs & (slabs - 1) == 0 and slabs >= 8
    batches, all_members, count = obs_noise.shape
    total = batches * count
    planes = (1 + lagged) * fields * chunks
    stacked = (fields * members, width)
    hbm = pl.BlockSpec(memory_space=pltpu.HBM)
    sizes = (members, fields, chunks)

    def from_slab(array, bit):
        return lax.ppermute(array, "slab", [(i, i ^ bit) for i in range(slabs)])

    def from_other_pair(array, bit):
        return from_slab(array, bit ^ 1)

    def from_other_mem(array):
        if parts != 2:
            return from_partners(array)
        return [
            lax.ppermute(
                array, ("slab", "mem"), [(i ^ 3, i) for i in range(slabs * parts)]
            )
        ]

    def from_partners(array):
        return [
            lax.ppermute(array, "mem", [((i + d) % parts, i) for i in range(parts)])
            for d in range(1, parts)
        ]

    present, delayed = rows_of(present_ensemble), rows_of(delayed_ensemble)
    spread, ratios = rows_of(spreading_coefficient), rows_of(transport_ratios)
    sources = in_hbm((present, delayed, spread, ratios, obs_row, obs_col, obs_field))
    half_shape = (delayed.shape[0] // 2, LANES)
    *held, first_half, second_half, packed, coefs = pl.pallas_call(
        functools.partial(load_kernel, chunks),
        out_shape=[shape_of(x.shape, x.dtype) for x in sources[2:]]
        + [shape_of(half_shape)] * 2
        + [shape_of((present.shape[0] + 2 * chunks, LANES)), shape_of((2 * chunks, LANES))],
        in_specs=[hbm] * len(sources),
        scratch_shapes=[pltpu.SemaphoreType.DMA((len(sources) + 1,))],
        compiler_params=PARAMS,
        name="load",
    )(*sources)
    outer_pairs = [(i, i + 1) for i in range(1, slabs - 1, 2)]
    outer_pairs += [(j, i) for i, j in outer_pairs]
    outer_coefs = lax.ppermute(coefs, "slab", outer_pairs)
    inner = from_slab(packed, 1)
    others_first = from_partners(first_half)
    taps, kinds = pl.pallas_call(
        selector_kernel,
        out_shape=(shape_of((width, total), BF16), shape_of((3, total), jnp.int32)),
        compiler_params=PARAMS,
        cost_estimate=estimate(SELECT_FLOPS),
        name="selector",
    )(*held[2:])
    part, here, part_obs = pl.pallas_call(
        functools.partial(own_row_kernel, *sizes),
        out_shape=(shape_of(stacked), shape_of(stacked), shape_of((members, total))),
        compiler_params=PARAMS,
        cost_estimate=estimate(OWN_FLOPS),
        name="own_row",
    )(packed, *held[:2], taps, kinds)
    keep, send = pl.pallas_call(
        functools.partial(observe_kernel, parts, *sizes),
        out_shape=[shape_of((members, total // 2))] * 2,
        compiler_params=PARAMS,
        name="observe",
    )(inner, outer_coefs, part_obs, here, taps, kinds)

    def summed(terms, other, flops, *arrived):
        return pl.pallas_call(
            sum_kernel,
            out_shape=shape_of(terms.shape),
            cost_estimate=estimate(flops),
            compiler_params=PARAMS,
            name="sum",
        )(terms, other, *arrived)

    terms = keep + from_slab(send, 1)
    outer_row = lax.ppermute(
        lax.optimization_barrier((packed, terms))[0], "slab", outer_pairs
    )
    far = slabs // 2
    terms = summed(terms, from_other_pair(terms, far), SUM_FLOPS[0], others_first[0])
    others_second = from_partners(lax.optimization_barrier((second_half, terms))[0])
    terms = pl.pallas_call(
        gather_kernel,
        out_shape=shape_of((all_members, total // 2)),
        cost_estimate=estimate(GATHER_FLOPS),
        compiler_params=PARAMS,
        name="gather",
    )(terms, *from_other_mem(terms))
    forecast = pl.pallas_call(
        functools.partial(complete_kernel, *sizes),
        out_shape=shape_of(stacked),
        compiler_params=PARAMS,
        name="complete",
    )(lax.optimization_barrier((part, terms))[0], packed, inner, outer_row)
    bit = far // 2
    while bit > 1:
        last = bit == 2
        terms = summed(
            terms,
            from_other_pair(terms, bit),
            SUM_FLOPS[1 + last],
            *([others_second[0]] if last else []),
        )
        bit //= 2
    priors = [terms, from_slab(terms, 1)]
    mine = pl.pallas_call(
        functools.partial(solve_kernel, parts),
        out_shape=shape_of((members, all_members)),
        compiler_params=PARAMS,
        cost_estimate=estimate(SOLVE_FLOPS),
        name="solve",
    )(obs_value, obs_error, obs_noise, *priors)
    lagged_parts = pl.pallas_call(
        functools.partial(prepare_kernel, parts),
        out_shape=[shape_of((all_members, delayed.size // members), BF16)] * 2,
        compiler_params=PARAMS,
        name="prepare",
    )(
        first_half,
        second_half,
        *[half for both in zip(others_first, others_second) for half in both],
    )
    out = pl.pallas_call(
        functools.partial(combine_kernel, parts, fields),
        out_shape=shape_of((members, planes, LANES)),
        out_specs=hbm,
        scratch_shapes=[
            pltpu.VMEM((members * planes, LANES), F32),
            pltpu.SemaphoreType.DMA((1 + lagged,)),
        ],
        compiler_params=PARAMS,
        name="combine",
    )(mine, forecast, *from_partners(forecast), *lagged_parts)
    return out.reshape(members, 1 + lagged, fields, height, width)


def solution(mesh):
    return jax.shard_map(
        shards,
        mesh=mesh,
        in_specs=(
            P("mem", None, "slab", None),
            P("mem", None, None, "slab", None),
            P("slab", None),
            P(None, "slab", None),
            P(),
            P(),
            P(),
            P(),
            P(),
            P(),
        ),
        out_specs=P("mem", None, None, "slab", None),
        check_vma=False,
    )
```

```python
import functools

import jax
import jax.numpy as jnp
from jax import lax
from jax.experimental import pallas as pl
from jax.experimental.pallas import tpu as pltpu
from jax.sharding import PartitionSpec as P

LANES = 128
F32 = jnp.float32
BF16 = jnp.bfloat16
HIGHEST = lax.Precision.HIGHEST
PARAMS = pltpu.CompilerParams(vmem_limit_bytes=48 * 1024 * 1024)


SELECT_FLOPS = 1
OWN_FLOPS, SUM_FLOPS, GATHER_FLOPS, SOLVE_FLOPS = 10**11, (3*10**9,1,5*10**8), 1, 10**9


def estimate(flops):
    return pl.CostEstimate(flops=flops, transcendentals=0, bytes_accessed=0)


def rows_of(array):
    return array.reshape(-1, LANES)


def in_hbm(arrays):
    return [pltpu.with_memory_space_constraint(array, pltpu.HBM) for array in arrays]


def shape_of(shape, dtype=F32):
    return jax.ShapeDtypeStruct(shape, dtype)


def split_two(x):
    high = x.astype(BF16)
    low = (x - high.astype(F32)).astype(BF16)
    return high, low


def split_three(x):
    high = x.astype(BF16)
    rest = x - high.astype(F32)
    middle = rest.astype(BF16)
    low = (rest - middle.astype(F32)).astype(BF16)
    return high, middle, low


def line(ref, start, chunks):
    return jnp.concatenate([ref[start + c : start + c + 1, :] for c in range(chunks)], axis=1)


def stacked_planes(ref, members, fields, chunks):
    return jnp.concatenate(
        [
            jnp.concatenate(
                [
                    ref[pl.ds(f * chunks + c, members, stride=fields * chunks), :]
                    for c in range(chunks)
                ],
                axis=1,
            )
            for f in range(fields)
        ],
        axis=0,
    )


def at_once(sources, targets, sems):
    copies = [
        pltpu.make_async_copy(source, target, sems.at[i])
        for i, (source, target) in enumerate(zip(sources, targets))
    ]
    for copy in copies:
        copy.start()
    return copies


def picked_values(planes, taps):
    high, middle, low = (
        jnp.dot(part, taps, preferred_element_type=F32) for part in split_three(planes)
    )
    return low + middle + high


def load_kernel(chunks, *refs):
    sources, (*held, first_ref, second_ref, packed_ref, coefs_ref), sems = (
        refs[:7],
        refs[7:-1],
        refs[-1],
    )
    present, delayed, *others = sources
    rows, half = present.shape[0], first_ref.shape[0]
    copies = at_once(
        [present, delayed.at[:half], delayed.at[half:], *others],
        [packed_ref.at[:rows], first_ref, second_ref, *held],
        sems,
    )
    copies[3].wait()
    copies[4].wait()
    spread = held[0][...]
    along_rows = held[1][:chunks, :] * 0.5
    for ref, start in ((packed_ref, rows), (coefs_ref, 0)):
        ref[start : start + chunks, :] = spread + along_rows
        ref[start + chunks : start + 2 * chunks, :] = spread - along_rows
    for copy in (*copies[:3], *copies[5:]):
        copy.wait()


def keeps_first(parts):
    rest = lax.axis_index("slab")
    ones = lax.axis_index("mem") if parts == 2 else 0
    for _ in range(lax.axis_size("slab").bit_length() - 1):
        ones = ones + lax.rem(rest, 2)
        rest = rest // 2
    return lax.rem(ones, 2) == 0


def weights(packed_ref, chunks):
    rows = packed_ref.shape[0] - 2 * chunks
    return line(packed_ref, rows, chunks), line(packed_ref, rows + chunks, chunks)


def selector_kernel(row_ref, col_ref, field_ref, taps_ref, kinds_ref):
    batches, count = row_ref.shape
    shape = taps_ref.shape
    flat = lambda ref: jnp.concatenate([ref[b : b + 1, :] for b in range(batches)], axis=1)
    rows, cols, kinds = flat(row_ref), flat(col_ref), flat(field_ref)
    own_row = lax.axis_index("slab")
    for k, row in enumerate((own_row, own_row + 1, own_row - 1)):
        kinds_ref[k : k + 1, :] = jnp.where(rows == row, kinds, -1)
    at = lax.broadcasted_iota(jnp.int32, shape, 0).astype(F32) * 0.25
    taps_ref[...] = jnp.maximum(0.5 - jnp.abs(at - cols.astype(F32) * 0.25), 0.0).astype(BF16)


def own_row_kernel(
    members,
    fields,
    chunks,
    packed_ref,
    spread_ref,
    ratio_ref,
    taps_ref,
    kinds_ref,
    part_ref,
    here_ref,
    obs_ref,
):
    width = chunks * LANES
    spread = line(spread_ref, 0, chunks)
    along_columns = line(ratio_ref, chunks, chunks)
    here = stacked_planes(packed_ref, members, fields, chunks)
    here_ref[...] = here
    lane = lax.broadcasted_iota(jnp.int32, here.shape, 1)
    left = jnp.where(lane == 0, 0.0, pltpu.roll(here, 1, 1))
    right = jnp.where(lane == width - 1, 0.0, pltpu.roll(here, width - 1, 1))
    part = (
        here
        + spread * (right + left - 4.0 * here)
        - along_columns * (right - left) * 0.5
    )
    part_ref[...] = part
    picked = picked_values(part, taps_ref[...])
    observed = jnp.zeros(obs_ref.shape, F32)
    for f in range(fields):
        observed += jnp.where(
            kinds_ref[0:1, :] == f, picked[f * members : (f + 1) * members], 0.0
        )
    obs_ref[...] = observed


def observe_kernel(
    parts,
    members,
    fields,
    chunks,
    inner_ref,
    outer_ref,
    part_obs_ref,
    here_ref,
    taps_ref,
    kinds_ref,
    keep_ref,
    send_ref,
):
    even = lax.rem(lax.axis_index("slab"), 2) == 0
    here = here_ref[...]
    inner, outer = weights(inner_ref, chunks), weights(outer_ref, chunks)
    to_below = jnp.where(even, inner[0], outer[0])
    to_above = jnp.where(even, outer[1], inner[1])
    picked = picked_values(
        jnp.concatenate([to_below * here, to_above * here], axis=0), taps_ref[...]
    )
    observed = part_obs_ref[...]
    for side in range(2):
        kinds = kinds_ref[1 + side : 2 + side, :]
        for f in range(fields):
            start = (side * fields + f) * members
            observed += jnp.where(kinds == f, picked[start : start + members], 0.0)
    first_here = keeps_first(parts)
    half = observed.shape[1] // 2
    first, second = observed[:, :half], observed[:, half:]
    keep_ref[...] = jnp.where(first_here, first, second)
    send_ref[...] = jnp.where(first_here, second, first)


def sum_kernel(terms_ref, other_ref, *refs):
    refs[-1][...] = terms_ref[...] + other_ref[...]


def complete_kernel(members, fields, chunks, part_ref, packed_ref, inner_ref, outer_ref, forecast_ref):
    even = lax.rem(lax.axis_index("slab"), 2) == 0
    above, below = weights(packed_ref, chunks)
    forecast_ref[...] = (
        part_ref[...]
        + jnp.where(even, below, above) * stacked_planes(inner_ref, members, fields, chunks)
        + jnp.where(even, above, below) * stacked_planes(outer_ref, members, fields, chunks)
    )


def gather_kernel(*refs):
    local = refs[0].shape[0]
    for d, ref in enumerate(refs[:-1]):
        refs[-1][d * local : (d + 1) * local, :] = ref[...]


def identity(rows, columns):
    return (
        lax.broadcasted_iota(jnp.int32, (rows, columns), 0)
        == lax.broadcasted_iota(jnp.int32, (rows, columns), 1)
    ).astype(F32)


def precise(x, y):
    return jnp.dot(x, y, precision=HIGHEST, preferred_element_type=F32)


def three_pass(x, y):
    x_high, x_low = split_two(x)
    y_high, y_low = split_two(y)
    dot = functools.partial(jnp.dot, preferred_element_type=F32)
    return dot(x_low, y_high) + dot(x_high, y_low) + dot(x_high, y_high)


def solve_transposed(system, right_t, floor):
    size = system.shape[0]
    eye = identity(size, size)
    sums = jnp.sum(jnp.abs(system), axis=0, keepdims=True)
    top = jnp.max(sums, axis=1, keepdims=True) + 1.0
    scale = 2.0 / (top + floor)
    start = (1.0 - floor * scale, eye - scale * system, scale * right_t)

    def double(product, carry):
        eps, residual, answer = carry
        both = product(jnp.concatenate([residual, answer], axis=0), residual)
        square = eps * eps
        share = 1.0 / (2.0 - square)
        return (
            square * share,
            (2.0 * both[:size] - square * eye) * share,
            (answer + both[size:]) * (2.0 * share),
        )

    def steps(count):
        carry = start
        for _ in range(count):
            carry = double(three_pass, carry)
        return carry[2]

    def loop():
        return lax.while_loop(
            lambda carry: jnp.max(carry[0]) > 1e-6, functools.partial(double, precise), start
        )[2]

    condition = jnp.max(top) / floor
    return lax.cond(
        condition < 20.0,
        lambda: steps(5),
        lambda: lax.cond(condition < 78.0, lambda: steps(6), loop),
    )


def precise_nt(x, y):
    return lax.dot_general(
        x, y, (((1,), (1,)), ((), ())), precision=HIGHEST, preferred_element_type=F32
    )


def solve_kernel(
    parts, value_ref, error_ref, noise_ref, kept_ref, received_ref, _high, _low, mine_ref
):
    batches, members, count = noise_ref.shape
    local = members // parts
    own = lax.axis_index("mem")
    first_here = keeps_first(parts)
    halves = [
        jnp.where(first_here, kept_ref[...], received_ref[...]),
        jnp.where(first_here, received_ref[...], kept_ref[...]),
    ]
    prior = jnp.concatenate(halves, axis=1)
    grams = []
    for b in range(batches):
        wanted = local if b == batches - 1 else members
        observed = prior[:, b * count : (b + 1) * count]
        share = 1.0 / error_ref[b : b + 1, :]
        mean = jnp.mean(observed, axis=0, keepdims=True)
        anomalies = (observed - mean) * share
        blocks = []
        for d in range(wanted // local):
            owner = lax.rem(own + d, parts)
            blocks.append(
                noise_ref[b, pl.ds(pl.multiple_of(owner * local, local), local), :]
            )
        innovation = (value_ref[b : b + 1, :] - mean) * share + jnp.concatenate(blocks, axis=0)
        both = precise_nt(jnp.concatenate([anomalies, innovation], axis=0), anomalies)
        grams.append((both[:members], both[members:]))
    diagonal = (members - 1.0) * identity(members, members)
    product_t = None
    for b, (gram, cross) in enumerate(grams):
        wanted = cross.shape[0]
        if product_t is None:
            system, right_t = gram, cross - gram[:wanted]
        else:
            centred = product_t - jnp.mean(product_t, axis=0, keepdims=True)
            both = precise(jnp.concatenate([centred, product_t[:wanted]], axis=0), gram)
            both = precise_nt(
                jnp.concatenate([both[:members], cross - both[members:]], axis=0), centred
            )
            system, right_t = both[:members], both[members:]
        weights_t = solve_transposed(system + diagonal, right_t, members - 1.0)
        matrix_t = (
            identity(wanted, members) + weights_t - jnp.mean(weights_t, axis=1, keepdims=True)
        )
        product_t = matrix_t if product_t is None else precise(matrix_t, product_t)
    mine_ref[...] = product_t


def prepare_kernel(parts, *refs):
    sources, high_ref, low_ref = refs[: 2 * parts], refs[2 * parts], refs[2 * parts + 1]
    lagged = high_ref.shape[1] // LANES
    count = high_ref.shape[0] // (2 * parts)
    for k in range(lagged):
        held = jnp.concatenate(
            [ref[pl.ds(k, count, stride=lagged), :] for ref in sources], axis=0
        )
        high, low = split_two(held)
        high_ref[:, k * LANES : (k + 1) * LANES] = high
        low_ref[:, k * LANES : (k + 1) * LANES] = low


def write_level(mine, parts_of, first, fields, chunks, done_ref, out_ref, sem):
    local, planes = out_ref.shape[:2]
    high, low = split_two(mine)
    left = jnp.concatenate([high, high, low], axis=1)
    level = fields * chunks
    for f in range(fields):
        held_high, held_low = parts_of(f)
        result = jnp.dot(
            left,
            jnp.concatenate([held_high, held_low, held_high], axis=0),
            preferred_element_type=F32,
        )
        for c in range(chunks):
            done_ref[pl.ds(f * chunks + c, local, stride=level), :] = result[
                :, c * LANES : (c + 1) * LANES
            ]
    copy = pltpu.make_async_copy(
        done_ref.reshape(local, level, LANES), out_ref.at[:, first : first + level, :], sem
    )
    copy.start()
    return copy


def combine_lagged_kernel(fields, chunks, mine_ref, high_ref, low_ref, out_ref, done_ref, sems):
    level = fields * chunks
    copies = []
    for k in range(done_ref.shape[0]):

        def parts_of(f):
            start = (k * level + f * chunks) * LANES
            lanes = slice(start, start + chunks * LANES)
            return high_ref[:, lanes], low_ref[:, lanes]

        copies.append(
            write_level(
                mine_ref[...],
                parts_of,
                (1 + k) * level,
                fields,
                chunks,
                done_ref.at[k],
                out_ref,
                sems.at[k],
            )
        )
    for copy in copies:
        copy.wait()


def combine_forecast_kernel(parts, fields, chunks, mine_ref, *refs):
    forecast_refs = refs[:parts]
    _, out_ref, done_ref, sem = refs[parts:]
    local = mine_ref.shape[0]

    def parts_of(f):
        return split_two(
            jnp.concatenate(
                [ref[f * local : (f + 1) * local, :] for ref in forecast_refs], axis=0
            )
        )

    write_level(mine_ref[...], parts_of, 0, fields, chunks, done_ref, out_ref, sem).wait()


def shards(
    present_ensemble,
    delayed_ensemble,
    spreading_coefficient,
    transport_ratios,
    obs_value,
    obs_error,
    obs_noise,
    obs_row,
    obs_col,
    obs_field,
):
    members, fields, height, width = present_ensemble.shape
    assert height == 1 and width % LANES == 0
    chunks = width // LANES
    lagged = delayed_ensemble.shape[1]
    slabs, parts = lax.axis_size("slab"), lax.axis_size("mem")
    assert slabs & (slabs - 1) == 0 and slabs >= 8
    batches, all_members, count = obs_noise.shape
    total = batches * count
    planes = (1 + lagged) * fields * chunks
    stacked = (fields * members, width)
    hbm = pl.BlockSpec(memory_space=pltpu.HBM)
    sizes = (members, fields, chunks)

    def from_slab(array, bit):
        return lax.ppermute(array, "slab", [(i, i ^ bit) for i in range(slabs)])

    def from_other_pair(array, bit):
        return from_slab(array, bit ^ 1)

    def from_other_mem(array):
        if parts != 2:
            return from_partners(array)
        return [
            lax.ppermute(
                array, ("slab", "mem"), [(i ^ 3, i) for i in range(slabs * parts)]
            )
        ]

    def from_partners(array):
        return [
            lax.ppermute(array, "mem", [((i + d) % parts, i) for i in range(parts)])
            for d in range(1, parts)
        ]

    present, delayed = rows_of(present_ensemble), rows_of(delayed_ensemble)
    spread, ratios = rows_of(spreading_coefficient), rows_of(transport_ratios)
    sources = in_hbm((present, delayed, spread, ratios, obs_row, obs_col, obs_field))
    half_shape = (delayed.shape[0] // 2, LANES)
    *held, first_half, second_half, packed, coefs = pl.pallas_call(
        functools.partial(load_kernel, chunks),
        out_shape=[shape_of(x.shape, x.dtype) for x in sources[2:]]
        + [shape_of(half_shape)] * 2
        + [shape_of((present.shape[0] + 2 * chunks, LANES)), shape_of((2 * chunks, LANES))],
        in_specs=[hbm] * len(sources),
        scratch_shapes=[pltpu.SemaphoreType.DMA((len(sources) + 1,))],
        compiler_params=PARAMS,
        name="load",
    )(*sources)
    outer_pairs = [(i, i + 1) for i in range(1, slabs - 1, 2)]
    outer_pairs += [(j, i) for i, j in outer_pairs]
    outer_coefs = lax.ppermute(coefs, "slab", outer_pairs)
    inner = from_slab(packed, 1)
    others_first = from_partners(first_half)
    taps, kinds = pl.pallas_call(
        selector_kernel,
        out_shape=(shape_of((width, total), BF16), shape_of((3, total), jnp.int32)),
        compiler_params=PARAMS,
        cost_estimate=estimate(SELECT_FLOPS),
        name="selector",
    )(*held[2:])
    part, here, part_obs = pl.pallas_call(
        functools.partial(own_row_kernel, *sizes),
        out_shape=(shape_of(stacked), shape_of(stacked), shape_of((members, total))),
        compiler_params=PARAMS,
        cost_estimate=estimate(OWN_FLOPS),
        name="own_row",
    )(packed, *held[:2], taps, kinds)
    keep, send = pl.pallas_call(
        functools.partial(observe_kernel, parts, *sizes),
        out_shape=[shape_of((members, total // 2))] * 2,
        compiler_params=PARAMS,
        name="observe",
    )(inner, outer_coefs, part_obs, here, taps, kinds)

    def summed(terms, other, flops, *arrived):
        return pl.pallas_call(
            sum_kernel,
            out_shape=shape_of(terms.shape),
            cost_estimate=estimate(flops),
            compiler_params=PARAMS,
            name="sum",
        )(terms, other, *arrived)

    terms = keep + from_slab(send, 1)
    outer_row = lax.ppermute(
        lax.optimization_barrier((packed, terms))[0], "slab", outer_pairs
    )
    far = slabs // 2
    terms = summed(terms, from_other_pair(terms, far), SUM_FLOPS[0], others_first[0])
    others_second = from_partners(lax.optimization_barrier((second_half, terms))[0])
    terms = pl.pallas_call(
        gather_kernel,
        out_shape=shape_of((all_members, total // 2)),
        cost_estimate=estimate(GATHER_FLOPS),
        compiler_params=PARAMS,
        name="gather",
    )(terms, *from_other_mem(terms))
    bit = far // 2
    while bit > 1:
        last = bit == 2
        before_last = terms
        terms = summed(
            terms,
            from_other_pair(terms, bit),
            SUM_FLOPS[1 + last],
        )
        bit //= 2
    forecast = pl.pallas_call(
        functools.partial(complete_kernel, *sizes),
        out_shape=shape_of(stacked),
        compiler_params=PARAMS,
        name="complete",
    )(lax.optimization_barrier((part, before_last))[0], packed, inner, outer_row)
    priors = [terms, from_slab(terms, 1)]
    lagged_parts = pl.pallas_call(
        functools.partial(prepare_kernel, parts),
        out_shape=[shape_of((all_members, delayed.size // members), BF16)] * 2,
        compiler_params=PARAMS,
        name="prepare",
    )(
        first_half,
        second_half,
        *[half for both in zip(others_first, others_second) for half in both],
    )
    mine = pl.pallas_call(
        functools.partial(solve_kernel, parts),
        out_shape=shape_of((members, all_members)),
        compiler_params=PARAMS,
        cost_estimate=estimate(SOLVE_FLOPS),
        name="solve",
    )(obs_value, obs_error, obs_noise, *priors, *lagged_parts)
    level = fields * chunks
    out = pl.pallas_call(
        functools.partial(combine_lagged_kernel, fields, chunks),
        out_shape=shape_of((members, planes, LANES)),
        out_specs=hbm,
        scratch_shapes=[
            pltpu.VMEM((lagged, members * level, LANES), F32),
            pltpu.SemaphoreType.DMA((lagged,)),
        ],
        compiler_params=PARAMS,
        name="combine_lagged",
    )(mine, *lagged_parts)
    out = pl.pallas_call(
        functools.partial(combine_forecast_kernel, parts, fields, chunks),
        out_shape=shape_of((members, planes, LANES)),
        in_specs=[pl.BlockSpec(memory_space=pltpu.VMEM)] * (1 + parts) + [hbm],
        out_specs=hbm,
        input_output_aliases={1 + parts: 0},
        scratch_shapes=[pltpu.VMEM((members * level, LANES), F32), pltpu.SemaphoreType.DMA],
        compiler_params=PARAMS,
        name="combine_forecast",
    )(mine, forecast, *from_partners(forecast), out)
    return out.reshape(members, 1 + lagged, fields, height, width)


def solution(mesh):
    return jax.shard_map(
        shards,
        mesh=mesh,
        in_specs=(
            P("mem", None, "slab", None),
            P("mem", None, None, "slab", None),
            P("slab", None),
            P(None, "slab", None),
            P(),
            P(),
            P(),
            P(),
            P(),
            P(),
        ),
        out_specs=P("mem", None, None, "slab", None),
        check_vma=False,
    )
```

```python
import functools

import jax
import jax.numpy as jnp
from jax import lax
from jax.experimental import pallas as pl
from jax.experimental.pallas import tpu as pltpu
from jax.sharding import PartitionSpec as P

LANES = 128
F32 = jnp.float32
BF16 = jnp.bfloat16
HIGHEST = lax.Precision.HIGHEST
PARAMS = pltpu.CompilerParams(vmem_limit_bytes=48 * 1024 * 1024)


SELECT_FLOPS = 1
OWN_FLOPS, SUM_FLOPS, GATHER_FLOPS, SOLVE_FLOPS = 1, (7*10**8,7*10**8,1), 10**8, 5*10**8


def estimate(flops):
    return pl.CostEstimate(flops=flops, transcendentals=0, bytes_accessed=0)


def rows_of(array):
    return array.reshape(-1, LANES)


def in_hbm(arrays):
    return [pltpu.with_memory_space_constraint(array, pltpu.HBM) for array in arrays]


def shape_of(shape, dtype=F32):
    return jax.ShapeDtypeStruct(shape, dtype)


def split_two(x):
    high = x.astype(BF16)
    low = (x - high.astype(F32)).astype(BF16)
    return high, low


def split_three(x):
    high = x.astype(BF16)
    rest = x - high.astype(F32)
    middle = rest.astype(BF16)
    low = (rest - middle.astype(F32)).astype(BF16)
    return high, middle, low


def line(ref, start, chunks):
    return jnp.concatenate([ref[start + c : start + c + 1, :] for c in range(chunks)], axis=1)


def stacked_planes(ref, members, fields, chunks):
    return jnp.concatenate(
        [
            jnp.concatenate(
                [
                    ref[pl.ds(f * chunks + c, members, stride=fields * chunks), :]
                    for c in range(chunks)
                ],
                axis=1,
            )
            for f in range(fields)
        ],
        axis=0,
    )


def at_once(sources, targets, sems):
    copies = [
        pltpu.make_async_copy(source, target, sems.at[i])
        for i, (source, target) in enumerate(zip(sources, targets))
    ]
    for copy in copies:
        copy.start()
    return copies


def picked_values(planes, taps):
    high, middle, low = (
        jnp.dot(part, taps, preferred_element_type=F32) for part in split_three(planes)
    )
    return low + middle + high


def load_kernel(chunks, *refs):
    count = (len(refs) - 1) // 2
    sources, packed_ref, held, sems = refs[:count], refs[count], refs[count + 1 : -1], refs[-1]
    rows = sources[0].shape[0]
    copies = at_once(sources, (packed_ref.at[:rows], *held), sems)
    copies[1].wait()
    copies[2].wait()
    spread = held[0][...]
    half = held[1][:chunks, :] * 0.5
    packed_ref[rows : rows + chunks, :] = spread + half
    packed_ref[rows + chunks : rows + 2 * chunks, :] = spread - half
    for copy in (copies[0], *copies[3:]):
        copy.wait()


def keeps_first(parts):
    rest = lax.axis_index("slab")
    ones = lax.axis_index("mem") if parts == 2 else 0
    for _ in range(lax.axis_size("slab").bit_length() - 1):
        ones = ones + lax.rem(rest, 2)
        rest = rest // 2
    return lax.rem(ones, 2) == 0


def weights(packed_ref, chunks):
    rows = packed_ref.shape[0] - 2 * chunks
    return line(packed_ref, rows, chunks), line(packed_ref, rows + chunks, chunks)


def selector_kernel(row_ref, col_ref, field_ref, taps_ref, kinds_ref):
    batches, count = row_ref.shape
    shape = taps_ref.shape
    flat = lambda ref: jnp.concatenate([ref[b : b + 1, :] for b in range(batches)], axis=1)
    rows, cols, kinds = flat(row_ref), flat(col_ref), flat(field_ref)
    own_row = lax.axis_index("slab")
    for k, row in enumerate((own_row, own_row + 1)):
        kinds_ref[k : k + 1, :] = jnp.where(rows == row, kinds, -1)
    at = lax.broadcasted_iota(jnp.int32, shape, 0).astype(F32) * 0.25
    taps_ref[...] = jnp.maximum(0.5 - jnp.abs(at - cols.astype(F32) * 0.25), 0.0).astype(BF16)


def own_row_kernel(
    members,
    fields,
    chunks,
    packed_ref,
    spread_ref,
    ratio_ref,
    taps_ref,
    kinds_ref,
    part_ref,
    here_ref,
    obs_ref,
):
    width = chunks * LANES
    spread = line(spread_ref, 0, chunks)
    along_columns = line(ratio_ref, chunks, chunks)
    here = stacked_planes(packed_ref, members, fields, chunks)
    here_ref[...] = here
    lane = lax.broadcasted_iota(jnp.int32, here.shape, 1)
    left = jnp.where(lane == 0, 0.0, pltpu.roll(here, 1, 1))
    right = jnp.where(lane == width - 1, 0.0, pltpu.roll(here, width - 1, 1))
    part = (
        here
        + spread * (right + left - 4.0 * here)
        - along_columns * (right - left) * 0.5
    )
    part_ref[...] = part
    picked = picked_values(part, taps_ref[...])
    observed = jnp.zeros(obs_ref.shape, F32)
    for f in range(fields):
        observed += jnp.where(
            kinds_ref[0:1, :] == f, picked[f * members : (f + 1) * members], 0.0
        )
    obs_ref[...] = observed


def observe_kernel(
    parts,
    members,
    fields,
    chunks,
    packed_ref,
    next_ref,
    part_ref,
    part_obs_ref,
    here_ref,
    taps_ref,
    kinds_ref,
    keep_ref,
    send_ref,
    partial_ref,
):
    _, below = weights(packed_ref, chunks)
    above_of_below, _ = weights(next_ref, chunks)
    taken = below * stacked_planes(next_ref, members, fields, chunks)
    given = above_of_below * here_ref[...]
    partial_ref[...] = part_ref[...] + taken
    picked = sum(
        jnp.dot(part, taps_ref[...], preferred_element_type=F32)
        for part in reversed(split_two(jnp.concatenate([taken, given], axis=0)))
    )
    observed = part_obs_ref[...]
    for side in range(2):
        kinds = kinds_ref[side : side + 1, :]
        for f in range(fields):
            start = (side * fields + f) * members
            observed += jnp.where(kinds == f, picked[start : start + members], 0.0)
    first_here = keeps_first(parts)
    half = observed.shape[1] // 2
    first, second = observed[:, :half], observed[:, half:]
    keep_ref[...] = jnp.where(first_here, first, second)
    send_ref[...] = jnp.where(first_here, second, first)


def sum_kernel(terms_ref, other_ref, *refs):
    refs[-1][...] = terms_ref[...] + other_ref[...]


def complete_kernel(members, fields, chunks, partial_ref, previous_ref, packed_ref, forecast_ref):
    above, _ = weights(packed_ref, chunks)
    forecast_ref[...] = partial_ref[...] + above * stacked_planes(
        previous_ref, members, fields, chunks
    )


def gather_kernel(*refs):
    local = refs[0].shape[0]
    for d, ref in enumerate(refs[:-1]):
        refs[-1][d * local : (d + 1) * local, :] = ref[...]


def identity(rows, columns):
    return (
        lax.broadcasted_iota(jnp.int32, (rows, columns), 0)
        == lax.broadcasted_iota(jnp.int32, (rows, columns), 1)
    ).astype(F32)


def precise(x, y):
    return jnp.dot(x, y, precision=HIGHEST, preferred_element_type=F32)


def three_pass(x, y):
    x_high, x_low = split_two(x)
    y_high, y_low = split_two(y)
    dot = functools.partial(jnp.dot, preferred_element_type=F32)
    return dot(x_low, y_high) + dot(x_high, y_low) + dot(x_high, y_high)


def solve_transposed(system, right_t, floor):
    size = system.shape[0]
    eye = identity(size, size)
    sums = jnp.sum(jnp.abs(system), axis=0, keepdims=True)
    top = jnp.max(sums, axis=1, keepdims=True) + 1.0
    scale = 2.0 / (top + floor)
    start = (1.0 - floor * scale, eye - scale * system, scale * right_t)

    def double(product, carry):
        eps, residual, answer = carry
        both = product(jnp.concatenate([residual, answer], axis=0), residual)
        square = eps * eps
        share = 1.0 / (2.0 - square)
        return (
            square * share,
            (2.0 * both[:size] - square * eye) * share,
            (answer + both[size:]) * (2.0 * share),
        )

    def steps(count):
        carry = start
        for _ in range(count):
            carry = double(three_pass, carry)
        return carry[2]

    def loop():
        return lax.while_loop(
            lambda carry: jnp.max(carry[0]) > 1e-6, functools.partial(double, precise), start
        )[2]

    condition = jnp.max(top) / floor
    return lax.cond(
        condition < 20.0,
        lambda: steps(5),
        lambda: lax.cond(condition < 78.0, lambda: steps(6), loop),
    )


def precise_nt(x, y):
    return lax.dot_general(
        x, y, (((1,), (1,)), ((), ())), precision=HIGHEST, preferred_element_type=F32
    )


def solve_kernel(parts, value_ref, error_ref, noise_ref, kept_ref, received_ref, mine_ref):
    batches, members, count = noise_ref.shape
    local = members // parts
    own = lax.axis_index("mem")
    first_here = keeps_first(parts)
    halves = [
        jnp.where(first_here, kept_ref[...], received_ref[...]),
        jnp.where(first_here, received_ref[...], kept_ref[...]),
    ]
    prior = jnp.concatenate(halves, axis=1)
    grams = []
    for b in range(batches):
        wanted = local if b == batches - 1 else members
        observed = prior[:, b * count : (b + 1) * count]
        share = 1.0 / error_ref[b : b + 1, :]
        mean = jnp.mean(observed, axis=0, keepdims=True)
        anomalies = (observed - mean) * share
        blocks = []
        for d in range(wanted // local):
            owner = lax.rem(own + d, parts)
            blocks.append(
                noise_ref[b, pl.ds(pl.multiple_of(owner * local, local), local), :]
            )
        innovation = (value_ref[b : b + 1, :] - mean) * share + jnp.concatenate(blocks, axis=0)
        both = precise_nt(jnp.concatenate([anomalies, innovation], axis=0), anomalies)
        grams.append((both[:members], both[members:]))
    diagonal = (members - 1.0) * identity(members, members)
    product_t = None
    for b, (gram, cross) in enumerate(grams):
        wanted = cross.shape[0]
        if product_t is None:
            system, right_t = gram, cross - gram[:wanted]
        else:
            centred = product_t - jnp.mean(product_t, axis=0, keepdims=True)
            both = precise(jnp.concatenate([centred, product_t[:wanted]], axis=0), gram)
            both = precise_nt(
                jnp.concatenate([both[:members], cross - both[members:]], axis=0), centred
            )
            system, right_t = both[:members], both[members:]
        weights_t = solve_transposed(system + diagonal, right_t, members - 1.0)
        matrix_t = (
            identity(wanted, members) + weights_t - jnp.mean(weights_t, axis=1, keepdims=True)
        )
        product_t = matrix_t if product_t is None else precise(matrix_t, product_t)
    mine_ref[...] = product_t


def prepare_kernel(parts, *refs):
    sources, high_ref, low_ref = refs[:parts], refs[parts], refs[parts + 1]
    lagged = high_ref.shape[1] // LANES
    local = high_ref.shape[0] // parts
    for k in range(lagged):
        held = jnp.concatenate(
            [ref[pl.ds(k, local, stride=lagged), :] for ref in sources], axis=0
        )
        high, low = split_two(held)
        high_ref[:, k * LANES : (k + 1) * LANES] = high
        low_ref[:, k * LANES : (k + 1) * LANES] = low


def combine_kernel(parts, fields, mine_ref, *refs):
    forecast_refs = refs[:parts]
    lagged_high_ref, lagged_low_ref, out_ref, done_ref, sems = refs[parts:]
    local = mine_ref.shape[0]
    high, low = split_two(mine_ref[...])
    left = jnp.concatenate([high, high, low], axis=1)
    width = forecast_refs[0].shape[1]
    chunks = width // LANES
    level = fields * chunks
    planes = level + lagged_high_ref.shape[1] // LANES
    copies = []
    for first in [*range(level, planes, level), 0]:
        for f in range(fields):
            start = first + f * chunks
            if first == 0:
                held_high, held_low = split_two(
                    jnp.concatenate(
                        [ref[f * local : (f + 1) * local, :] for ref in forecast_refs], axis=0
                    )
                )
            else:
                lanes = slice((start - level) * LANES, (start - level) * LANES + width)
                held_high, held_low = lagged_high_ref[:, lanes], lagged_low_ref[:, lanes]
            result = jnp.dot(
                left,
                jnp.concatenate([held_high, held_low, held_high], axis=0),
                preferred_element_type=F32,
            )
            for c in range(chunks):
                done_ref[pl.ds(start + c, local, stride=planes), :] = result[
                    :, c * LANES : (c + 1) * LANES
                ]
        copies.append(
            pltpu.make_async_copy(
                done_ref.reshape(local, planes, LANES).at[:, first : first + level, :],
                out_ref.at[:, first : first + level, :],
                sems.at[len(copies)],
            )
        )
        copies[-1].start()
    for copy in copies:
        copy.wait()


def shards(
    present_ensemble,
    delayed_ensemble,
    spreading_coefficient,
    transport_ratios,
    obs_value,
    obs_error,
    obs_noise,
    obs_row,
    obs_col,
    obs_field,
):
    members, fields, height, width = present_ensemble.shape
    assert height == 1 and width % LANES == 0
    chunks = width // LANES
    lagged = delayed_ensemble.shape[1]
    slabs, parts = lax.axis_size("slab"), lax.axis_size("mem")
    assert slabs & (slabs - 1) == 0 and slabs >= 8
    batches, all_members, count = obs_noise.shape
    total = batches * count
    planes = (1 + lagged) * fields * chunks
    stacked = (fields * members, width)
    hbm = pl.BlockSpec(memory_space=pltpu.HBM)
    sizes = (members, fields, chunks)

    def from_slab(array, bit):
        return lax.ppermute(array, "slab", [(i, i ^ bit) for i in range(slabs)])

    def from_other_pair(array, bit):
        return from_slab(array, bit ^ 1)

    def from_other_mem(array):
        if parts != 2:
            return from_partners(array)
        return [
            lax.ppermute(
                array, ("slab", "mem"), [(i ^ 3, i) for i in range(slabs * parts)]
            )
        ]

    def from_partners(array):
        return [
            lax.ppermute(array, "mem", [((i + d) % parts, i) for i in range(parts)])
            for d in range(1, parts)
        ]

    present, delayed = rows_of(present_ensemble), rows_of(delayed_ensemble)
    spread, ratios = rows_of(spreading_coefficient), rows_of(transport_ratios)
    sources = in_hbm((present, spread, ratios, obs_row, obs_col, obs_field))
    packed, *held = pl.pallas_call(
        functools.partial(load_kernel, chunks),
        out_shape=[shape_of((present.shape[0] + 2 * chunks, LANES))]
        + [shape_of(x.shape, x.dtype) for x in sources[1:]],
        in_specs=[hbm] * len(sources),
        scratch_shapes=[pltpu.SemaphoreType.DMA((len(sources),))],
        compiler_params=PARAMS,
        name="load",
    )(*sources)
    up = [(i, i + 1) for i in range(slabs - 1)]
    from_below = lax.ppermute(packed, "slab", [(j, i) for i, j in up])
    others_delayed = from_partners(
        lax.optimization_barrier((delayed, packed))[0]
    )
    taps, kinds = pl.pallas_call(
        selector_kernel,
        out_shape=(shape_of((width, total), BF16), shape_of((2, total), jnp.int32)),
        compiler_params=PARAMS,
        cost_estimate=estimate(SELECT_FLOPS),
        name="selector",
    )(*held[2:])
    part, here, part_obs = pl.pallas_call(
        functools.partial(own_row_kernel, *sizes),
        out_shape=(shape_of(stacked), shape_of(stacked), shape_of((members, total))),
        compiler_params=PARAMS,
        cost_estimate=estimate(OWN_FLOPS),
        name="own_row",
    )(packed, *held[:2], taps, kinds)
    from_above = lax.ppermute(lax.optimization_barrier((packed, part))[0], "slab", up)
    keep, send, partial = pl.pallas_call(
        functools.partial(observe_kernel, parts, *sizes),
        out_shape=(
            shape_of((members, total // 2)),
            shape_of((members, total // 2)),
            shape_of(stacked),
        ),
        compiler_params=PARAMS,
        name="observe",
    )(packed, from_below, part, part_obs, here, taps, kinds)
    def summed(terms, other, flops, *arrived):
        return pl.pallas_call(
            sum_kernel,
            out_shape=shape_of(terms.shape),
            cost_estimate=estimate(flops),
            compiler_params=PARAMS,
            name="sum",
        )(terms, other, *arrived)

    terms = keep + from_slab(send, 1)
    for bit in [1 << k for k in reversed(range(1, slabs.bit_length() - 1))]:
        terms = summed(
            terms,
            from_other_pair(terms, bit),
            SUM_FLOPS[min(slabs // 2 // bit, 4) // 2],
            *([others_delayed[0]] if bit == 2 else []),
        )
        if bit == slabs // 2:
            after_far = terms
    forecast = pl.pallas_call(
        functools.partial(complete_kernel, *sizes),
        out_shape=shape_of(stacked),
        compiler_params=PARAMS,
        name="complete",
    )(
        lax.optimization_barrier((partial, after_far))[0], from_above, packed
    )

    prior = pl.pallas_call(
        gather_kernel,
        out_shape=shape_of((all_members, total // 2)),
        cost_estimate=estimate(GATHER_FLOPS),
        compiler_params=PARAMS,
        name="gather",
    )(terms, *from_other_mem(terms))
    mine = pl.pallas_call(
        functools.partial(solve_kernel, parts),
        out_shape=shape_of((members, all_members)),
        compiler_params=PARAMS,
        cost_estimate=estimate(SOLVE_FLOPS),
        name="solve",
    )(obs_value, obs_error, obs_noise, prior, from_slab(prior, 1))
    lagged_parts = pl.pallas_call(
        functools.partial(prepare_kernel, parts),
        out_shape=[shape_of((all_members, delayed.size // members), BF16)] * 2,
        compiler_params=PARAMS,
        name="prepare",
    )(delayed, *others_delayed)
    out = pl.pallas_call(
        functools.partial(combine_kernel, parts, fields),
        out_shape=shape_of((members, planes, LANES)),
        out_specs=hbm,
        scratch_shapes=[
            pltpu.VMEM((members * planes, LANES), F32),
            pltpu.SemaphoreType.DMA((1 + lagged,)),
        ],
        compiler_params=PARAMS,
        name="combine",
    )(mine, forecast, *from_partners(forecast), *lagged_parts)
    return out.reshape(members, 1 + lagged, fields, height, width)


def solution(mesh):
    return jax.shard_map(
        shards,
        mesh=mesh,
        in_specs=(
            P("mem", None, "slab", None),
            P("mem", None, None, "slab", None),
            P("slab", None),
            P(None, "slab", None),
            P(),
            P(),
            P(),
            P(),
            P(),
            P(),
        ),
        out_specs=P("mem", None, None, "slab", None),
        check_vma=False,
    )
```

```python
import functools

import jax
import jax.numpy as jnp
from jax import lax
from jax.experimental import pallas as pl
from jax.experimental.pallas import tpu as pltpu
from jax.sharding import PartitionSpec as P

LANES = 128
F32 = jnp.float32
BF16 = jnp.bfloat16
HIGHEST = lax.Precision.HIGHEST
PARAMS = pltpu.CompilerParams(vmem_limit_bytes=48 * 1024 * 1024)


SELECT_FLOPS = 1
OWN_FLOPS, SUM_FLOPS, GATHER_FLOPS, SOLVE_FLOPS = 1, (7*10**8,7*10**8,1), 10**8, 5*10**8


def estimate(flops):
    return pl.CostEstimate(flops=flops, transcendentals=0, bytes_accessed=0)


def rows_of(array):
    return array.reshape(-1, LANES)


def in_hbm(arrays):
    return [pltpu.with_memory_space_constraint(array, pltpu.HBM) for array in arrays]


def shape_of(shape, dtype=F32):
    return jax.ShapeDtypeStruct(shape, dtype)


def split_two(x):
    high = x.astype(BF16)
    low = (x - high.astype(F32)).astype(BF16)
    return high, low


def split_three(x):
    high = x.astype(BF16)
    rest = x - high.astype(F32)
    middle = rest.astype(BF16)
    low = (rest - middle.astype(F32)).astype(BF16)
    return high, middle, low


def line(ref, start, chunks):
    return jnp.concatenate([ref[start + c : start + c + 1, :] for c in range(chunks)], axis=1)


def stacked_planes(ref, members, fields, chunks):
    return jnp.concatenate(
        [
            jnp.concatenate(
                [
                    ref[pl.ds(f * chunks + c, members, stride=fields * chunks), :]
                    for c in range(chunks)
                ],
                axis=1,
            )
            for f in range(fields)
        ],
        axis=0,
    )


def at_once(sources, targets, sems):
    copies = [
        pltpu.make_async_copy(source, target, sems.at[i])
        for i, (source, target) in enumerate(zip(sources, targets))
    ]
    for copy in copies:
        copy.start()
    return copies


def picked_values(planes, taps):
    high, middle, low = (
        jnp.dot(part, taps, preferred_element_type=F32) for part in split_three(planes)
    )
    return low + middle + high


def load_kernel(chunks, *refs):
    count = (len(refs) - 1) // 2
    sources, packed_ref, held, sems = refs[:count], refs[count], refs[count + 1 : -1], refs[-1]
    rows = sources[0].shape[0]
    copies = at_once(sources, (packed_ref.at[:rows], *held), sems)
    copies[1].wait()
    copies[2].wait()
    spread = held[0][...]
    half = held[1][:chunks, :] * 0.5
    packed_ref[rows : rows + chunks, :] = spread + half
    packed_ref[rows + chunks : rows + 2 * chunks, :] = spread - half
    for copy in (copies[0], *copies[3:]):
        copy.wait()


def keeps_first(parts):
    rest = lax.axis_index("slab")
    ones = lax.axis_index("mem") if parts == 2 else 0
    for _ in range(lax.axis_size("slab").bit_length() - 1):
        ones = ones + lax.rem(rest, 2)
        rest = rest // 2
    return lax.rem(ones, 2) == 0


def weights(packed_ref, chunks):
    rows = packed_ref.shape[0] - 2 * chunks
    return line(packed_ref, rows, chunks), line(packed_ref, rows + chunks, chunks)


def selector_kernel(row_ref, col_ref, field_ref, taps_ref, kinds_ref):
    batches, count = row_ref.shape
    shape = taps_ref.shape
    flat = lambda ref: jnp.concatenate([ref[b : b + 1, :] for b in range(batches)], axis=1)
    rows, cols, kinds = flat(row_ref), flat(col_ref), flat(field_ref)
    own_row = lax.axis_index("slab")
    for k, row in enumerate((own_row, own_row + 1)):
        kinds_ref[k : k + 1, :] = jnp.where(rows == row, kinds, -1)
    at = lax.broadcasted_iota(jnp.int32, shape, 0).astype(F32) * 0.25
    taps_ref[...] = jnp.maximum(0.5 - jnp.abs(at - cols.astype(F32) * 0.25), 0.0).astype(BF16)


def own_row_kernel(
    members,
    fields,
    chunks,
    packed_ref,
    spread_ref,
    ratio_ref,
    taps_ref,
    kinds_ref,
    part_ref,
    here_ref,
    obs_ref,
):
    width = chunks * LANES
    spread = line(spread_ref, 0, chunks)
    along_columns = line(ratio_ref, chunks, chunks)
    here = stacked_planes(packed_ref, members, fields, chunks)
    here_ref[...] = here
    lane = lax.broadcasted_iota(jnp.int32, here.shape, 1)
    left = jnp.where(lane == 0, 0.0, pltpu.roll(here, 1, 1))
    right = jnp.where(lane == width - 1, 0.0, pltpu.roll(here, width - 1, 1))
    part = (
        here
        + spread * (right + left - 4.0 * here)
        - along_columns * (right - left) * 0.5
    )
    part_ref[...] = part
    picked = picked_values(part, taps_ref[...])
    observed = jnp.zeros(obs_ref.shape, F32)
    for f in range(fields):
        observed += jnp.where(
            kinds_ref[0:1, :] == f, picked[f * members : (f + 1) * members], 0.0
        )
    obs_ref[...] = observed


def observe_kernel(
    parts,
    members,
    fields,
    chunks,
    packed_ref,
    next_ref,
    part_ref,
    part_obs_ref,
    here_ref,
    taps_ref,
    kinds_ref,
    keep_ref,
    send_ref,
    partial_ref,
):
    _, below = weights(packed_ref, chunks)
    above_of_below, _ = weights(next_ref, chunks)
    taken = below * stacked_planes(next_ref, members, fields, chunks)
    given = above_of_below * here_ref[...]
    partial_ref[...] = part_ref[...] + taken
    picked = sum(
        jnp.dot(part, taps_ref[...], preferred_element_type=F32)
        for part in reversed(split_two(jnp.concatenate([taken, given], axis=0)))
    )
    observed = part_obs_ref[...]
    for side in range(2):
        kinds = kinds_ref[side : side + 1, :]
        for f in range(fields):
            start = (side * fields + f) * members
            observed += jnp.where(kinds == f, picked[start : start + members], 0.0)
    first_here = keeps_first(parts)
    half = observed.shape[1] // 2
    first, second = observed[:, :half], observed[:, half:]
    keep_ref[...] = jnp.where(first_here, first, second)
    send_ref[...] = jnp.where(first_here, second, first)


def sum_kernel(terms_ref, other_ref, *refs):
    refs[-1][...] = terms_ref[...] + other_ref[...]


def complete_kernel(members, fields, chunks, partial_ref, previous_ref, packed_ref, forecast_ref):
    above, _ = weights(packed_ref, chunks)
    forecast_ref[...] = partial_ref[...] + above * stacked_planes(
        previous_ref, members, fields, chunks
    )


def gather_kernel(*refs):
    local = refs[0].shape[0]
    for d, ref in enumerate(refs[:-1]):
        refs[-1][d * local : (d + 1) * local, :] = ref[...]


def identity(rows, columns):
    return (
        lax.broadcasted_iota(jnp.int32, (rows, columns), 0)
        == lax.broadcasted_iota(jnp.int32, (rows, columns), 1)
    ).astype(F32)


def precise(x, y):
    return jnp.dot(x, y, precision=HIGHEST, preferred_element_type=F32)


def three_pass(x, y):
    x_high, x_low = split_two(x)
    y_high, y_low = split_two(y)
    dot = functools.partial(jnp.dot, preferred_element_type=F32)
    return dot(x_low, y_high) + dot(x_high, y_low) + dot(x_high, y_high)


def solve_transposed(system, right_t, floor):
    size = system.shape[0]
    eye = identity(size, size)
    sums = jnp.sum(jnp.abs(system), axis=0, keepdims=True)
    top = jnp.max(sums, axis=1, keepdims=True) + 1.0
    scale = 2.0 / (top + floor)
    start = (1.0 - floor * scale, eye - scale * system, scale * right_t)

    def double(product, carry):
        eps, residual, answer = carry
        both = product(jnp.concatenate([residual, answer], axis=0), residual)
        square = eps * eps
        share = 1.0 / (2.0 - square)
        return (
            square * share,
            (2.0 * both[:size] - square * eye) * share,
            (answer + both[size:]) * (2.0 * share),
        )

    def steps(count):
        carry = start
        for _ in range(count):
            carry = double(three_pass, carry)
        return carry[2]

    def loop():
        return lax.while_loop(
            lambda carry: jnp.max(carry[0]) > 1e-6, functools.partial(double, precise), start
        )[2]

    condition = jnp.max(top) / floor
    return lax.cond(
        condition < 20.0,
        lambda: steps(5),
        lambda: lax.cond(condition < 78.0, lambda: steps(6), loop),
    )


def precise_nt(x, y):
    return lax.dot_general(
        x, y, (((1,), (1,)), ((), ())), precision=HIGHEST, preferred_element_type=F32
    )


def solve_kernel(parts, value_ref, error_ref, noise_ref, kept_ref, received_ref, mine_ref):
    batches, members, count = noise_ref.shape
    local = members // parts
    own = lax.axis_index("mem")
    first_here = keeps_first(parts)
    halves = [
        jnp.where(first_here, kept_ref[...], received_ref[...]),
        jnp.where(first_here, received_ref[...], kept_ref[...]),
    ]
    prior = jnp.concatenate(halves, axis=1)
    grams = []
    for b in range(batches):
        wanted = local if b == batches - 1 else members
        observed = prior[:, b * count : (b + 1) * count]
        share = 1.0 / error_ref[b : b + 1, :]
        mean = jnp.mean(observed, axis=0, keepdims=True)
        anomalies = (observed - mean) * share
        blocks = []
        for d in range(wanted // local):
            owner = lax.rem(own + d, parts)
            blocks.append(
                noise_ref[b, pl.ds(pl.multiple_of(owner * local, local), local), :]
            )
        innovation = (value_ref[b : b + 1, :] - mean) * share + jnp.concatenate(blocks, axis=0)
        both = precise_nt(jnp.concatenate([anomalies, innovation], axis=0), anomalies)
        grams.append((both[:members], both[members:]))
    diagonal = (members - 1.0) * identity(members, members)
    product_t = None
    for b, (gram, cross) in enumerate(grams):
        wanted = cross.shape[0]
        if product_t is None:
            system, right_t = gram, cross - gram[:wanted]
        else:
            centred = product_t - jnp.mean(product_t, axis=0, keepdims=True)
            both = precise(jnp.concatenate([centred, product_t[:wanted]], axis=0), gram)
            both = precise_nt(
                jnp.concatenate([both[:members], cross - both[members:]], axis=0), centred
            )
            system, right_t = both[:members], both[members:]
        weights_t = solve_transposed(system + diagonal, right_t, members - 1.0)
        matrix_t = (
            identity(wanted, members) + weights_t - jnp.mean(weights_t, axis=1, keepdims=True)
        )
        product_t = matrix_t if product_t is None else precise(matrix_t, product_t)
    mine_ref[...] = product_t


def prepare_kernel(parts, *refs):
    sources, high_ref, low_ref = refs[:parts], refs[parts], refs[parts + 1]
    lagged = high_ref.shape[1] // LANES
    local = high_ref.shape[0] // parts
    for k in range(lagged):
        held = jnp.concatenate(
            [ref[pl.ds(k, local, stride=lagged), :] for ref in sources], axis=0
        )
        high, low = split_two(held)
        high_ref[:, k * LANES : (k + 1) * LANES] = high
        low_ref[:, k * LANES : (k + 1) * LANES] = low


def combine_kernel(parts, fields, mine_ref, *refs):
    forecast_refs = refs[:parts]
    lagged_high_ref, lagged_low_ref, out_ref, done_ref, sems = refs[parts:]
    local = mine_ref.shape[0]
    high, low = split_two(mine_ref[...])
    left = jnp.concatenate([high, high, low], axis=1)
    width = forecast_refs[0].shape[1]
    chunks = width // LANES
    level = fields * chunks
    planes = level + lagged_high_ref.shape[1] // LANES
    copies = []
    for first in [*range(level, planes, level), 0]:
        for f in range(fields):
            start = first + f * chunks
            if first == 0:
                held_high, held_low = split_two(
                    jnp.concatenate(
                        [ref[f * local : (f + 1) * local, :] for ref in forecast_refs], axis=0
                    )
                )
            else:
                lanes = slice((start - level) * LANES, (start - level) * LANES + width)
                held_high, held_low = lagged_high_ref[:, lanes], lagged_low_ref[:, lanes]
            result = jnp.dot(
                left,
                jnp.concatenate([held_high, held_low, held_high], axis=0),
                preferred_element_type=F32,
            )
            for c in range(chunks):
                done_ref[pl.ds(start + c, local, stride=planes), :] = result[
                    :, c * LANES : (c + 1) * LANES
                ]
        copies.append(
            pltpu.make_async_copy(
                done_ref.reshape(local, planes, LANES).at[:, first : first + level, :],
                out_ref.at[:, first : first + level, :],
                sems.at[len(copies)],
            )
        )
        copies[-1].start()
    for copy in copies:
        copy.wait()


def shards(
    present_ensemble,
    delayed_ensemble,
    spreading_coefficient,
    transport_ratios,
    obs_value,
    obs_error,
    obs_noise,
    obs_row,
    obs_col,
    obs_field,
):
    members, fields, height, width = present_ensemble.shape
    assert height == 1 and width % LANES == 0
    chunks = width // LANES
    lagged = delayed_ensemble.shape[1]
    slabs, parts = lax.axis_size("slab"), lax.axis_size("mem")
    assert slabs & (slabs - 1) == 0 and slabs >= 8
    batches, all_members, count = obs_noise.shape
    total = batches * count
    planes = (1 + lagged) * fields * chunks
    stacked = (fields * members, width)
    hbm = pl.BlockSpec(memory_space=pltpu.HBM)
    sizes = (members, fields, chunks)

    def from_slab(array, bit):
        return lax.ppermute(array, "slab", [(i, i ^ bit) for i in range(slabs)])

    def from_other_pair(array, bit):
        return from_slab(array, bit ^ 1)

    def from_other_mem(array):
        if parts != 2:
            return from_partners(array)
        return [
            lax.ppermute(
                array, ("slab", "mem"), [(i ^ 3, i) for i in range(slabs * parts)]
            )
        ]

    def from_partners(array):
        return [
            lax.ppermute(array, "mem", [((i + d) % parts, i) for i in range(parts)])
            for d in range(1, parts)
        ]

    present, delayed = rows_of(present_ensemble), rows_of(delayed_ensemble)
    spread, ratios = rows_of(spreading_coefficient), rows_of(transport_ratios)
    sources = in_hbm((present, spread, ratios, obs_row, obs_col, obs_field))
    packed, *held = pl.pallas_call(
        functools.partial(load_kernel, chunks),
        out_shape=[shape_of((present.shape[0] + 2 * chunks, LANES))]
        + [shape_of(x.shape, x.dtype) for x in sources[1:]],
        in_specs=[hbm] * len(sources),
        scratch_shapes=[pltpu.SemaphoreType.DMA((len(sources),))],
        compiler_params=PARAMS,
        name="load",
    )(*sources)
    up = [(i, i + 1) for i in range(slabs - 1)]
    from_below = lax.ppermute(packed, "slab", [(j, i) for i, j in up])
    taps, kinds = pl.pallas_call(
        selector_kernel,
        out_shape=(shape_of((width, total), BF16), shape_of((2, total), jnp.int32)),
        compiler_params=PARAMS,
        cost_estimate=estimate(SELECT_FLOPS),
        name="selector",
    )(*held[2:])
    part, here, part_obs = pl.pallas_call(
        functools.partial(own_row_kernel, *sizes),
        out_shape=(shape_of(stacked), shape_of(stacked), shape_of((members, total))),
        compiler_params=PARAMS,
        cost_estimate=estimate(OWN_FLOPS),
        name="own_row",
    )(packed, *held[:2], taps, kinds)
    others_delayed = from_partners(lax.optimization_barrier((delayed, part))[0])
    from_above = lax.ppermute(lax.optimization_barrier((packed, part))[0], "slab", up)
    keep, send, partial = pl.pallas_call(
        functools.partial(observe_kernel, parts, *sizes),
        out_shape=(
            shape_of((members, total // 2)),
            shape_of((members, total // 2)),
            shape_of(stacked),
        ),
        compiler_params=PARAMS,
        name="observe",
    )(packed, from_below, part, part_obs, here, taps, kinds)
    def summed(terms, other, flops, *arrived):
        return pl.pallas_call(
            sum_kernel,
            out_shape=shape_of(terms.shape),
            cost_estimate=estimate(flops),
            compiler_params=PARAMS,
            name="sum",
        )(terms, other, *arrived)

    terms = keep + from_slab(send, 1)
    for bit in [1 << k for k in reversed(range(1, slabs.bit_length() - 1))]:
        terms = summed(
            terms,
            from_other_pair(terms, bit),
            SUM_FLOPS[min(slabs // 2 // bit, 4) // 2],
            *([others_delayed[0]] if bit == 2 else []),
        )
        if bit == slabs // 2:
            after_far = terms
    forecast = pl.pallas_call(
        functools.partial(complete_kernel, *sizes),
        out_shape=shape_of(stacked),
        compiler_params=PARAMS,
        name="complete",
    )(
        lax.optimization_barrier((partial, after_far))[0], from_above, packed
    )

    prior = pl.pallas_call(
        gather_kernel,
        out_shape=shape_of((all_members, total // 2)),
        cost_estimate=estimate(GATHER_FLOPS),
        compiler_params=PARAMS,
        name="gather",
    )(terms, *from_other_mem(terms))
    mine = pl.pallas_call(
        functools.partial(solve_kernel, parts),
        out_shape=shape_of((members, all_members)),
        compiler_params=PARAMS,
        cost_estimate=estimate(SOLVE_FLOPS),
        name="solve",
    )(obs_value, obs_error, obs_noise, prior, from_slab(prior, 1))
    lagged_parts = pl.pallas_call(
        functools.partial(prepare_kernel, parts),
        out_shape=[shape_of((all_members, delayed.size // members), BF16)] * 2,
        compiler_params=PARAMS,
        name="prepare",
    )(delayed, *others_delayed)
    out = pl.pallas_call(
        functools.partial(combine_kernel, parts, fields),
        out_shape=shape_of((members, planes, LANES)),
        out_specs=hbm,
        scratch_shapes=[
            pltpu.VMEM((members * planes, LANES), F32),
            pltpu.SemaphoreType.DMA((1 + lagged,)),
        ],
        compiler_params=PARAMS,
        name="combine",
    )(mine, forecast, *from_partners(forecast), *lagged_parts)
    return out.reshape(members, 1 + lagged, fields, height, width)


def solution(mesh):
    return jax.shard_map(
        shards,
        mesh=mesh,
        in_specs=(
            P("mem", None, "slab", None),
            P("mem", None, None, "slab", None),
            P("slab", None),
            P(None, "slab", None),
            P(),
            P(),
            P(),
            P(),
            P(),
            P(),
        ),
        out_specs=P("mem", None, None, "slab", None),
        check_vma=False,
    )
```

```python
import functools

import jax
import jax.numpy as jnp
from jax import lax
from jax.experimental import pallas as pl
from jax.experimental.pallas import tpu as pltpu
from jax.sharding import PartitionSpec as P

LANES = 128
F32 = jnp.float32
BF16 = jnp.bfloat16
HIGHEST = lax.Precision.HIGHEST
PARAMS = pltpu.CompilerParams(vmem_limit_bytes=48 * 1024 * 1024)


SELECT_FLOPS = 1
OWN_FLOPS, SUM_FLOPS, GATHER_FLOPS, SOLVE_FLOPS = 1, (7*10**8,7*10**8,1), 10**8, 8*10**8


def estimate(flops):
    return pl.CostEstimate(flops=flops, transcendentals=0, bytes_accessed=0)


def rows_of(array):
    return array.reshape(-1, LANES)


def in_hbm(arrays):
    return [pltpu.with_memory_space_constraint(array, pltpu.HBM) for array in arrays]


def shape_of(shape, dtype=F32):
    return jax.ShapeDtypeStruct(shape, dtype)


def split_two(x):
    high = x.astype(BF16)
    low = (x - high.astype(F32)).astype(BF16)
    return high, low


def split_three(x):
    high = x.astype(BF16)
    rest = x - high.astype(F32)
    middle = rest.astype(BF16)
    low = (rest - middle.astype(F32)).astype(BF16)
    return high, middle, low


def line(ref, start, chunks):
    return jnp.concatenate([ref[start + c : start + c + 1, :] for c in range(chunks)], axis=1)


def stacked_planes(ref, members, fields, chunks):
    return jnp.concatenate(
        [
            jnp.concatenate(
                [
                    ref[pl.ds(f * chunks + c, members, stride=fields * chunks), :]
                    for c in range(chunks)
                ],
                axis=1,
            )
            for f in range(fields)
        ],
        axis=0,
    )


def at_once(sources, targets, sems):
    copies = [
        pltpu.make_async_copy(source, target, sems.at[i])
        for i, (source, target) in enumerate(zip(sources, targets))
    ]
    for copy in copies:
        copy.start()
    return copies


def picked_values(planes, taps):
    high, middle, low = (
        jnp.dot(part, taps, preferred_element_type=F32) for part in split_three(planes)
    )
    return low + middle + high


def load_kernel(chunks, *refs):
    count = (len(refs) - 1) // 2
    sources, packed_ref, held, sems = refs[:count], refs[count], refs[count + 1 : -1], refs[-1]
    rows = sources[0].shape[0]
    copies = at_once(sources, (packed_ref.at[:rows], *held), sems)
    copies[1].wait()
    copies[2].wait()
    spread = held[0][...]
    half = held[1][:chunks, :] * 0.5
    packed_ref[rows : rows + chunks, :] = spread + half
    packed_ref[rows + chunks : rows + 2 * chunks, :] = spread - half
    for copy in (copies[0], *copies[3:]):
        copy.wait()


def keeps_first(parts):
    rest = lax.axis_index("slab")
    ones = lax.axis_index("mem") if parts == 2 else 0
    for _ in range(lax.axis_size("slab").bit_length() - 1):
        ones = ones + lax.rem(rest, 2)
        rest = rest // 2
    return lax.rem(ones, 2) == 0


def weights(packed_ref, chunks):
    rows = packed_ref.shape[0] - 2 * chunks
    return line(packed_ref, rows, chunks), line(packed_ref, rows + chunks, chunks)


def selector_kernel(row_ref, col_ref, field_ref, taps_ref, kinds_ref):
    batches, count = row_ref.shape
    shape = taps_ref.shape
    flat = lambda ref: jnp.concatenate([ref[b : b + 1, :] for b in range(batches)], axis=1)
    rows, cols, kinds = flat(row_ref), flat(col_ref), flat(field_ref)
    own_row = lax.axis_index("slab")
    for k, row in enumerate((own_row, own_row + 1)):
        kinds_ref[k : k + 1, :] = jnp.where(rows == row, kinds, -1)
    at = lax.broadcasted_iota(jnp.int32, shape, 0).astype(F32) * 0.25
    taps_ref[...] = jnp.maximum(0.5 - jnp.abs(at - cols.astype(F32) * 0.25), 0.0).astype(BF16)


def own_row_kernel(
    members,
    fields,
    chunks,
    packed_ref,
    spread_ref,
    ratio_ref,
    taps_ref,
    kinds_ref,
    part_ref,
    here_ref,
    obs_ref,
):
    width = chunks * LANES
    spread = line(spread_ref, 0, chunks)
    along_columns = line(ratio_ref, chunks, chunks)
    here = stacked_planes(packed_ref, members, fields, chunks)
    here_ref[...] = here
    lane = lax.broadcasted_iota(jnp.int32, here.shape, 1)
    left = jnp.where(lane == 0, 0.0, pltpu.roll(here, 1, 1))
    right = jnp.where(lane == width - 1, 0.0, pltpu.roll(here, width - 1, 1))
    part = (
        here
        + spread * (right + left - 4.0 * here)
        - along_columns * (right - left) * 0.5
    )
    part_ref[...] = part
    picked = picked_values(part, taps_ref[...])
    observed = jnp.zeros(obs_ref.shape, F32)
    for f in range(fields):
        observed += jnp.where(
            kinds_ref[0:1, :] == f, picked[f * members : (f + 1) * members], 0.0
        )
    obs_ref[...] = observed


def observe_kernel(
    parts,
    members,
    fields,
    chunks,
    packed_ref,
    next_ref,
    part_ref,
    part_obs_ref,
    here_ref,
    taps_ref,
    kinds_ref,
    keep_ref,
    send_ref,
    partial_ref,
):
    _, below = weights(packed_ref, chunks)
    above_of_below, _ = weights(next_ref, chunks)
    taken = below * stacked_planes(next_ref, members, fields, chunks)
    given = above_of_below * here_ref[...]
    partial_ref[...] = part_ref[...] + taken
    picked = sum(
        jnp.dot(part, taps_ref[...], preferred_element_type=F32)
        for part in reversed(split_two(jnp.concatenate([taken, given], axis=0)))
    )
    observed = part_obs_ref[...]
    for side in range(2):
        kinds = kinds_ref[side : side + 1, :]
        for f in range(fields):
            start = (side * fields + f) * members
            observed += jnp.where(kinds == f, picked[start : start + members], 0.0)
    first_here = keeps_first(parts)
    half = observed.shape[1] // 2
    first, second = observed[:, :half], observed[:, half:]
    keep_ref[...] = jnp.where(first_here, first, second)
    send_ref[...] = jnp.where(first_here, second, first)


def sum_kernel(terms_ref, other_ref, *refs):
    refs[-1][...] = terms_ref[...] + other_ref[...]


def complete_kernel(members, fields, chunks, partial_ref, previous_ref, packed_ref, forecast_ref):
    above, _ = weights(packed_ref, chunks)
    forecast_ref[...] = partial_ref[...] + above * stacked_planes(
        previous_ref, members, fields, chunks
    )


def identity(rows, columns):
    return (
        lax.broadcasted_iota(jnp.int32, (rows, columns), 0)
        == lax.broadcasted_iota(jnp.int32, (rows, columns), 1)
    ).astype(F32)


def precise(x, y):
    return jnp.dot(x, y, precision=HIGHEST, preferred_element_type=F32)


def three_pass(x, y):
    x_high, x_low = split_two(x)
    y_high, y_low = split_two(y)
    dot = functools.partial(jnp.dot, preferred_element_type=F32)
    return dot(x_low, y_high) + dot(x_high, y_low) + dot(x_high, y_high)


def precise_nt(x, y):
    return lax.dot_general(
        x, y, (((1,), (1,)), ((), ())), precision=HIGHEST, preferred_element_type=F32
    )


def gram_kernel(parts, value_ref, error_ref, noise_ref, *refs):
    term_refs, grams_ref = refs[:parts], refs[parts]
    members, count = noise_ref.shape[1:]
    local = members // parts
    own = lax.axis_index("mem")
    batch = 1 - keeps_first(parts).astype(jnp.int32)
    observed = jnp.concatenate([ref[...] for ref in term_refs], axis=0)
    share = 1.0 / error_ref[pl.ds(batch, 1), :]
    mean = jnp.mean(observed, axis=0, keepdims=True)
    anomalies = (observed - mean) * share
    noise = jnp.concatenate(
        [
            noise_ref[batch, pl.ds(pl.multiple_of(lax.rem(own + d, parts) * local, local), local), :]
            for d in range(parts)
        ],
        axis=0,
    )
    innovation = (value_ref[pl.ds(batch, 1), :] - mean) * share + noise
    grams_ref[...] = precise_nt(jnp.concatenate([anomalies, innovation], axis=0), anomalies)


def solve_transposed(system, right_t, floor):
    size = system.shape[0]
    eye = identity(size, size)
    sums = jnp.sum(jnp.abs(system), axis=0, keepdims=True)
    top = jnp.max(sums, axis=1, keepdims=True) + 1.0
    scale = 2.0 / (top + floor)
    start = (1.0 - floor * scale, eye - scale * system, scale * right_t)

    def double(product, carry):
        eps, residual, answer = carry
        both = product(jnp.concatenate([residual, answer], axis=0), residual)
        square = eps * eps
        share = 1.0 / (2.0 - square)
        return (
            square * share,
            (2.0 * both[:size] - square * eye) * share,
            (answer + both[size:]) * (2.0 * share),
        )

    def steps(count):
        carry = start
        for _ in range(count):
            carry = double(three_pass, carry)
        return carry[2]

    def loop():
        return lax.while_loop(
            lambda carry: jnp.max(carry[0]) > 1e-6, functools.partial(double, precise), start
        )[2]

    condition = jnp.max(top) / floor
    return lax.cond(
        condition < 20.0,
        lambda: steps(5),
        lambda: lax.cond(condition < 78.0, lambda: steps(6), loop),
    )


def solve_kernel(parts, batches, kept_ref, received_ref, mine_ref):
    members = kept_ref.shape[1]
    local = members // parts
    first_here = keeps_first(parts)
    kept, received = kept_ref[...], received_ref[...]
    grams = [
        jnp.where(first_here, kept, received),
        jnp.where(first_here, received, kept),
    ]
    diagonal = (members - 1.0) * identity(members, members)
    product_t = None
    for b, both in enumerate(grams):
        wanted = local if b == batches - 1 else members
        gram, cross = both[:members], both[members : members + wanted]
        if product_t is None:
            system, right_t = gram, cross - gram[:wanted]
        else:
            centred = product_t - jnp.mean(product_t, axis=0, keepdims=True)
            both = precise(jnp.concatenate([centred, product_t[:wanted]], axis=0), gram)
            both = precise_nt(
                jnp.concatenate([both[:members], cross - both[members:]], axis=0), centred
            )
            system, right_t = both[:members], both[members:]
        weights_t = solve_transposed(system + diagonal, right_t, members - 1.0)
        matrix_t = (
            identity(wanted, members) + weights_t - jnp.mean(weights_t, axis=1, keepdims=True)
        )
        product_t = matrix_t if product_t is None else precise(matrix_t, product_t)
    mine_ref[...] = product_t


def prepare_kernel(parts, *refs):
    sources, high_ref, low_ref = refs[:parts], refs[parts], refs[parts + 1]
    lagged = high_ref.shape[1] // LANES
    local = high_ref.shape[0] // parts
    for k in range(lagged):
        held = jnp.concatenate(
            [ref[pl.ds(k, local, stride=lagged), :] for ref in sources], axis=0
        )
        high, low = split_two(held)
        high_ref[:, k * LANES : (k + 1) * LANES] = high
        low_ref[:, k * LANES : (k + 1) * LANES] = low


def combine_kernel(parts, fields, mine_ref, *refs):
    forecast_refs = refs[:parts]
    lagged_high_ref, lagged_low_ref, out_ref, done_ref, sems = refs[parts:]
    local = mine_ref.shape[0]
    high, low = split_two(mine_ref[...])
    left = jnp.concatenate([high, high, low], axis=1)
    width = forecast_refs[0].shape[1]
    chunks = width // LANES
    level = fields * chunks
    planes = level + lagged_high_ref.shape[1] // LANES
    copies = []
    for first in [*range(level, planes, level), 0]:
        for f in range(fields):
            start = first + f * chunks
            if first == 0:
                held_high, held_low = split_two(
                    jnp.concatenate(
                        [ref[f * local : (f + 1) * local, :] for ref in forecast_refs], axis=0
                    )
                )
            else:
                lanes = slice((start - level) * LANES, (start - level) * LANES + width)
                held_high, held_low = lagged_high_ref[:, lanes], lagged_low_ref[:, lanes]
            result = jnp.dot(
                left,
                jnp.concatenate([held_high, held_low, held_high], axis=0),
                preferred_element_type=F32,
            )
            for c in range(chunks):
                done_ref[pl.ds(start + c, local, stride=planes), :] = result[
                    :, c * LANES : (c + 1) * LANES
                ]
        copies.append(
            pltpu.make_async_copy(
                done_ref.reshape(local, planes, LANES).at[:, first : first + level, :],
                out_ref.at[:, first : first + level, :],
                sems.at[len(copies)],
            )
        )
        copies[-1].start()
    for copy in copies:
        copy.wait()


def shards(
    present_ensemble,
    delayed_ensemble,
    spreading_coefficient,
    transport_ratios,
    obs_value,
    obs_error,
    obs_noise,
    obs_row,
    obs_col,
    obs_field,
):
    members, fields, height, width = present_ensemble.shape
    assert height == 1 and width % LANES == 0
    chunks = width // LANES
    lagged = delayed_ensemble.shape[1]
    slabs, parts = lax.axis_size("slab"), lax.axis_size("mem")
    assert slabs & (slabs - 1) == 0 and slabs >= 8
    batches, all_members, count = obs_noise.shape
    total = batches * count
    planes = (1 + lagged) * fields * chunks
    stacked = (fields * members, width)
    hbm = pl.BlockSpec(memory_space=pltpu.HBM)
    sizes = (members, fields, chunks)

    def from_slab(array, bit):
        return lax.ppermute(array, "slab", [(i, i ^ bit) for i in range(slabs)])

    def from_other_pair(array, bit):
        return from_slab(array, bit ^ 1)

    def from_other_mem(array):
        if parts != 2:
            return from_partners(array)
        return [
            lax.ppermute(
                array, ("slab", "mem"), [(i ^ 3, i) for i in range(slabs * parts)]
            )
        ]

    def from_partners(array):
        return [
            lax.ppermute(array, "mem", [((i + d) % parts, i) for i in range(parts)])
            for d in range(1, parts)
        ]

    present, delayed = rows_of(present_ensemble), rows_of(delayed_ensemble)
    spread, ratios = rows_of(spreading_coefficient), rows_of(transport_ratios)
    sources = in_hbm((present, spread, ratios, obs_row, obs_col, obs_field))
    packed, *held = pl.pallas_call(
        functools.partial(load_kernel, chunks),
        out_shape=[shape_of((present.shape[0] + 2 * chunks, LANES))]
        + [shape_of(x.shape, x.dtype) for x in sources[1:]],
        in_specs=[hbm] * len(sources),
        scratch_shapes=[pltpu.SemaphoreType.DMA((len(sources),))],
        compiler_params=PARAMS,
        name="load",
    )(*sources)
    up = [(i, i + 1) for i in range(slabs - 1)]
    from_below = lax.ppermute(packed, "slab", [(j, i) for i, j in up])
    others_delayed = from_partners(
        lax.optimization_barrier((delayed, packed))[0]
    )
    taps, kinds = pl.pallas_call(
        selector_kernel,
        out_shape=(shape_of((width, total), BF16), shape_of((2, total), jnp.int32)),
        compiler_params=PARAMS,
        cost_estimate=estimate(SELECT_FLOPS),
        name="selector",
    )(*held[2:])
    part, here, part_obs = pl.pallas_call(
        functools.partial(own_row_kernel, *sizes),
        out_shape=(shape_of(stacked), shape_of(stacked), shape_of((members, total))),
        compiler_params=PARAMS,
        cost_estimate=estimate(OWN_FLOPS),
        name="own_row",
    )(packed, *held[:2], taps, kinds)
    from_above = lax.ppermute(lax.optimization_barrier((packed, part))[0], "slab", up)
    keep, send, partial = pl.pallas_call(
        functools.partial(observe_kernel, parts, *sizes),
        out_shape=(
            shape_of((members, total // 2)),
            shape_of((members, total // 2)),
            shape_of(stacked),
        ),
        compiler_params=PARAMS,
        name="observe",
    )(packed, from_below, part, part_obs, here, taps, kinds)
    def summed(terms, other, flops, *arrived):
        return pl.pallas_call(
            sum_kernel,
            out_shape=shape_of(terms.shape),
            cost_estimate=estimate(flops),
            compiler_params=PARAMS,
            name="sum",
        )(terms, other, *arrived)

    terms = keep + from_slab(send, 1)
    for bit in [1 << k for k in reversed(range(1, slabs.bit_length() - 1))]:
        terms = summed(
            terms,
            from_other_pair(terms, bit),
            SUM_FLOPS[min(slabs // 2 // bit, 4) // 2],
            *([others_delayed[0]] if bit == 2 else []),
        )
        if bit == slabs // 2:
            after_far = terms
    forecast = pl.pallas_call(
        functools.partial(complete_kernel, *sizes),
        out_shape=shape_of(stacked),
        compiler_params=PARAMS,
        name="complete",
    )(
        lax.optimization_barrier((partial, after_far))[0], from_above, packed
    )

    assert batches == 2
    grams = pl.pallas_call(
        functools.partial(gram_kernel, parts),
        out_shape=shape_of((2 * all_members, all_members)),
        cost_estimate=estimate(GATHER_FLOPS),
        compiler_params=PARAMS,
        name="gram",
    )(obs_value, obs_error, obs_noise, terms, *from_other_mem(terms))
    mine = pl.pallas_call(
        functools.partial(solve_kernel, parts, batches),
        out_shape=shape_of((members, all_members)),
        compiler_params=PARAMS,
        cost_estimate=estimate(SOLVE_FLOPS),
        name="solve",
    )(grams, from_slab(grams, 1))
    lagged_parts = pl.pallas_call(
        functools.partial(prepare_kernel, parts),
        out_shape=[shape_of((all_members, delayed.size // members), BF16)] * 2,
        compiler_params=PARAMS,
        name="prepare",
    )(delayed, *others_delayed)
    out = pl.pallas_call(
        functools.partial(combine_kernel, parts, fields),
        out_shape=shape_of((members, planes, LANES)),
        out_specs=hbm,
        scratch_shapes=[
            pltpu.VMEM((members * planes, LANES), F32),
            pltpu.SemaphoreType.DMA((1 + lagged,)),
        ],
        compiler_params=PARAMS,
        name="combine",
    )(mine, forecast, *from_partners(forecast), *lagged_parts)
    return out.reshape(members, 1 + lagged, fields, height, width)


def solution(mesh):
    return jax.shard_map(
        shards,
        mesh=mesh,
        in_specs=(
            P("mem", None, "slab", None),
            P("mem", None, None, "slab", None),
            P("slab", None),
            P(None, "slab", None),
            P(),
            P(),
            P(),
            P(),
            P(),
            P(),
        ),
        out_specs=P("mem", None, None, "slab", None),
        check_vma=False,
    )
```

```python
import functools

import jax
import jax.numpy as jnp
from jax import lax
from jax.experimental import pallas as pl
from jax.experimental.pallas import tpu as pltpu
from jax.sharding import PartitionSpec as P

LANES = 128
F32 = jnp.float32
BF16 = jnp.bfloat16
HIGHEST = lax.Precision.HIGHEST
PARAMS = pltpu.CompilerParams(vmem_limit_bytes=48 * 1024 * 1024)


SELECT_FLOPS = 1
OWN_FLOPS, SUM_FLOPS, GATHER_FLOPS, SOLVE_FLOPS = 1, (7*10**8,7*10**8,1), 10**8, 5*10**8


def estimate(flops):
    return pl.CostEstimate(flops=flops, transcendentals=0, bytes_accessed=0)


def rows_of(array):
    return array.reshape(-1, LANES)


def in_hbm(arrays):
    return [pltpu.with_memory_space_constraint(array, pltpu.HBM) for array in arrays]


def shape_of(shape, dtype=F32):
    return jax.ShapeDtypeStruct(shape, dtype)


def split_two(x):
    high = x.astype(BF16)
    low = (x - high.astype(F32)).astype(BF16)
    return high, low


def split_three(x):
    high = x.astype(BF16)
    rest = x - high.astype(F32)
    middle = rest.astype(BF16)
    low = (rest - middle.astype(F32)).astype(BF16)
    return high, middle, low


def line(ref, start, chunks):
    return jnp.concatenate([ref[start + c : start + c + 1, :] for c in range(chunks)], axis=1)


def stacked_planes(ref, members, fields, chunks):
    return jnp.concatenate(
        [
            jnp.concatenate(
                [
                    ref[pl.ds(f * chunks + c, members, stride=fields * chunks), :]
                    for c in range(chunks)
                ],
                axis=1,
            )
            for f in range(fields)
        ],
        axis=0,
    )


def at_once(sources, targets, sems):
    copies = [
        pltpu.make_async_copy(source, target, sems.at[i])
        for i, (source, target) in enumerate(zip(sources, targets))
    ]
    for copy in copies:
        copy.start()
    return copies


def picked_values(planes, taps):
    high, middle, low = (
        jnp.dot(part, taps, preferred_element_type=F32) for part in split_three(planes)
    )
    return low + middle + high


def load_kernel(chunks, *refs):
    count = (len(refs) - 1) // 2
    sources, packed_ref, held, sems = refs[:count], refs[count], refs[count + 1 : -1], refs[-1]
    rows = sources[0].shape[0]
    copies = at_once(sources, (packed_ref.at[:rows], *held), sems)
    copies[1].wait()
    copies[2].wait()
    spread = held[0][...]
    half = held[1][:chunks, :] * 0.5
    packed_ref[rows : rows + chunks, :] = spread + half
    packed_ref[rows + chunks : rows + 2 * chunks, :] = spread - half
    for copy in (copies[0], *copies[3:]):
        copy.wait()


def keeps_first(parts):
    rest = lax.axis_index("slab")
    ones = lax.axis_index("mem") if parts == 2 else 0
    for _ in range(lax.axis_size("slab").bit_length() - 1):
        ones = ones + lax.rem(rest, 2)
        rest = rest // 2
    return lax.rem(ones, 2) == 0


def weights(packed_ref, chunks):
    rows = packed_ref.shape[0] - 2 * chunks
    return line(packed_ref, rows, chunks), line(packed_ref, rows + chunks, chunks)


def selector_kernel(row_ref, col_ref, field_ref, taps_ref, kinds_ref):
    batches, count = row_ref.shape
    shape = taps_ref.shape
    flat = lambda ref: jnp.concatenate([ref[b : b + 1, :] for b in range(batches)], axis=1)
    rows, cols, kinds = flat(row_ref), flat(col_ref), flat(field_ref)
    own_row = lax.axis_index("slab")
    for k, row in enumerate((own_row, own_row + 1)):
        kinds_ref[k : k + 1, :] = jnp.where(rows == row, kinds, -1)
    at = lax.broadcasted_iota(jnp.int32, shape, 0).astype(F32) * 0.25
    taps_ref[...] = jnp.maximum(0.5 - jnp.abs(at - cols.astype(F32) * 0.25), 0.0).astype(BF16)


def own_row_kernel(
    members,
    fields,
    chunks,
    packed_ref,
    spread_ref,
    ratio_ref,
    taps_ref,
    kinds_ref,
    part_ref,
    here_ref,
    obs_ref,
):
    width = chunks * LANES
    spread = line(spread_ref, 0, chunks)
    along_columns = line(ratio_ref, chunks, chunks)
    here = stacked_planes(packed_ref, members, fields, chunks)
    here_ref[...] = here
    lane = lax.broadcasted_iota(jnp.int32, here.shape, 1)
    left = jnp.where(lane == 0, 0.0, pltpu.roll(here, 1, 1))
    right = jnp.where(lane == width - 1, 0.0, pltpu.roll(here, width - 1, 1))
    part = (
        here
        + spread * (right + left - 4.0 * here)
        - along_columns * (right - left) * 0.5
    )
    part_ref[...] = part
    picked = picked_values(part, taps_ref[...])
    observed = jnp.zeros(obs_ref.shape, F32)
    for f in range(fields):
        observed += jnp.where(
            kinds_ref[0:1, :] == f, picked[f * members : (f + 1) * members], 0.0
        )
    obs_ref[...] = observed


def observe_kernel(
    parts,
    members,
    fields,
    chunks,
    packed_ref,
    next_ref,
    part_ref,
    part_obs_ref,
    here_ref,
    taps_ref,
    kinds_ref,
    keep_ref,
    send_ref,
    partial_ref,
):
    _, below = weights(packed_ref, chunks)
    above_of_below, _ = weights(next_ref, chunks)
    taken = below * stacked_planes(next_ref, members, fields, chunks)
    given = above_of_below * here_ref[...]
    partial_ref[...] = part_ref[...] + taken
    picked = sum(
        jnp.dot(part, taps_ref[...], preferred_element_type=F32)
        for part in reversed(split_two(jnp.concatenate([taken, given], axis=0)))
    )
    observed = part_obs_ref[...]
    for side in range(2):
        kinds = kinds_ref[side : side + 1, :]
        for f in range(fields):
            start = (side * fields + f) * members
            observed += jnp.where(kinds == f, picked[start : start + members], 0.0)
    first_here = keeps_first(parts)
    half = observed.shape[1] // 2
    first, second = observed[:, :half], observed[:, half:]
    keep_ref[...] = jnp.where(first_here, first, second)
    send_ref[...] = jnp.where(first_here, second, first)


def sum_kernel(terms_ref, other_ref, *refs):
    refs[-1][...] = terms_ref[...] + other_ref[...]


def complete_kernel(members, fields, chunks, partial_ref, previous_ref, packed_ref, forecast_ref):
    above, _ = weights(packed_ref, chunks)
    forecast_ref[...] = partial_ref[...] + above * stacked_planes(
        previous_ref, members, fields, chunks
    )


def gather_kernel(*refs):
    local = refs[0].shape[0]
    for d, ref in enumerate(refs[:-1]):
        refs[-1][d * local : (d + 1) * local, :] = ref[...]


def identity(rows, columns):
    return (
        lax.broadcasted_iota(jnp.int32, (rows, columns), 0)
        == lax.broadcasted_iota(jnp.int32, (rows, columns), 1)
    ).astype(F32)


def precise(x, y):
    return jnp.dot(x, y, precision=HIGHEST, preferred_element_type=F32)


def three_pass(x, y):
    x_high, x_low = split_two(x)
    y_high, y_low = split_two(y)
    dot = functools.partial(jnp.dot, preferred_element_type=F32)
    return dot(x_low, y_high) + dot(x_high, y_low) + dot(x_high, y_high)


def solve_transposed(system, right_t, floor):
    size = system.shape[0]
    eye = identity(size, size)
    sums = jnp.sum(jnp.abs(system), axis=0, keepdims=True)
    top = jnp.max(sums, axis=1, keepdims=True) + 1.0
    scale = 2.0 / (top + floor)
    start = (1.0 - floor * scale, eye - scale * system, scale * right_t)

    def double(product, carry):
        eps, residual, answer = carry
        both = product(jnp.concatenate([residual, answer], axis=0), residual)
        square = eps * eps
        share = 1.0 / (2.0 - square)
        return (
            square * share,
            (2.0 * both[:size] - square * eye) * share,
            (answer + both[size:]) * (2.0 * share),
        )

    def steps(count):
        carry = start
        for _ in range(count):
            carry = double(three_pass, carry)
        return carry[2]

    def loop():
        return lax.while_loop(
            lambda carry: jnp.max(carry[0]) > 1e-6, functools.partial(double, precise), start
        )[2]

    condition = jnp.max(top) / floor
    return lax.cond(
        condition < 20.0,
        lambda: steps(5),
        lambda: lax.cond(condition < 78.0, lambda: steps(6), loop),
    )


def precise_nt(x, y):
    return lax.dot_general(
        x, y, (((1,), (1,)), ((), ())), precision=HIGHEST, preferred_element_type=F32
    )


def solve_kernel(parts, value_ref, error_ref, noise_ref, kept_ref, received_ref, mine_ref):
    batches, members, count = noise_ref.shape
    local = members // parts
    own = lax.axis_index("mem")
    first_here = keeps_first(parts)
    halves = [
        jnp.where(first_here, kept_ref[...], received_ref[...]),
        jnp.where(first_here, received_ref[...], kept_ref[...]),
    ]
    prior = jnp.concatenate(halves, axis=1)
    grams = []
    for b in range(batches):
        wanted = local if b == batches - 1 else members
        observed = prior[:, b * count : (b + 1) * count]
        share = 1.0 / error_ref[b : b + 1, :]
        mean = jnp.mean(observed, axis=0, keepdims=True)
        anomalies = (observed - mean) * share
        blocks = []
        for d in range(wanted // local):
            owner = lax.rem(own + d, parts)
            blocks.append(
                noise_ref[b, pl.ds(pl.multiple_of(owner * local, local), local), :]
            )
        innovation = (value_ref[b : b + 1, :] - mean) * share + jnp.concatenate(blocks, axis=0)
        both = precise_nt(jnp.concatenate([anomalies, innovation], axis=0), anomalies)
        grams.append((both[:members], both[members:]))
    diagonal = (members - 1.0) * identity(members, members)
    product_t = None
    for b, (gram, cross) in enumerate(grams):
        wanted = cross.shape[0]
        if product_t is None:
            system, right_t = gram, cross - gram[:wanted]
        else:
            centred = product_t - jnp.mean(product_t, axis=0, keepdims=True)
            both = precise(jnp.concatenate([centred, product_t[:wanted]], axis=0), gram)
            both = precise_nt(
                jnp.concatenate([both[:members], cross - both[members:]], axis=0), centred
            )
            system, right_t = both[:members], both[members:]
        weights_t = solve_transposed(system + diagonal, right_t, members - 1.0)
        matrix_t = (
            identity(wanted, members) + weights_t - jnp.mean(weights_t, axis=1, keepdims=True)
        )
        product_t = matrix_t if product_t is None else precise(matrix_t, product_t)
    mine_ref[...] = product_t


def prepare_kernel(parts, *refs):
    sources, high_ref, low_ref = refs[:parts], refs[parts], refs[parts + 1]
    lagged = high_ref.shape[1] // LANES
    local = high_ref.shape[0] // parts
    for k in range(lagged):
        held = jnp.concatenate(
            [ref[pl.ds(k, local, stride=lagged), :] for ref in sources], axis=0
        )
        high, low = split_two(held)
        high_ref[:, k * LANES : (k + 1) * LANES] = high
        low_ref[:, k * LANES : (k + 1) * LANES] = low


def combine_kernel(parts, fields, mine_ref, *refs):
    forecast_refs = refs[:parts]
    lagged_high_ref, lagged_low_ref, out_ref, done_ref, sems = refs[parts:]
    local = mine_ref.shape[0]
    high, low = split_two(mine_ref[...])
    left = jnp.concatenate([high, high, low], axis=1)
    width = forecast_refs[0].shape[1]
    chunks = width // LANES
    level = fields * chunks
    planes = level + lagged_high_ref.shape[1] // LANES
    copies = []
    for first in [*range(level, planes, level), 0]:
        for f in range(fields):
            start = first + f * chunks
            if first == 0:
                held_high, held_low = split_two(
                    jnp.concatenate(
                        [ref[f * local : (f + 1) * local, :] for ref in forecast_refs], axis=0
                    )
                )
            else:
                lanes = slice((start - level) * LANES, (start - level) * LANES + width)
                held_high, held_low = lagged_high_ref[:, lanes], lagged_low_ref[:, lanes]
            result = jnp.dot(
                left,
                jnp.concatenate([held_high, held_low, held_high], axis=0),
                preferred_element_type=F32,
            )
            for c in range(chunks):
                done_ref[pl.ds(start + c, local, stride=planes), :] = result[
                    :, c * LANES : (c + 1) * LANES
                ]
        copies.append(
            pltpu.make_async_copy(
                done_ref.reshape(local, planes, LANES).at[:, first : first + level, :],
                out_ref.at[:, first : first + level, :],
                sems.at[len(copies)],
            )
        )
        copies[-1].start()
    for copy in copies:
        copy.wait()


def shards(
    present_ensemble,
    delayed_ensemble,
    spreading_coefficient,
    transport_ratios,
    obs_value,
    obs_error,
    obs_noise,
    obs_row,
    obs_col,
    obs_field,
):
    members, fields, height, width = present_ensemble.shape
    assert height == 1 and width % LANES == 0
    chunks = width // LANES
    lagged = delayed_ensemble.shape[1]
    slabs, parts = lax.axis_size("slab"), lax.axis_size("mem")
    assert slabs & (slabs - 1) == 0 and slabs >= 8
    batches, all_members, count = obs_noise.shape
    total = batches * count
    planes = (1 + lagged) * fields * chunks
    stacked = (fields * members, width)
    hbm = pl.BlockSpec(memory_space=pltpu.HBM)
    sizes = (members, fields, chunks)

    def from_slab(array, bit):
        return lax.ppermute(array, "slab", [(i, i ^ bit) for i in range(slabs)])

    def from_other_pair(array, bit):
        return from_slab(array, bit ^ 1)

    def from_other_mem(array):
        if parts != 2:
            return from_partners(array)
        return [
            lax.ppermute(
                array, ("slab", "mem"), [(i ^ 3, i) for i in range(slabs * parts)]
            )
        ]

    def from_partners(array):
        return [
            lax.ppermute(array, "mem", [((i + d) % parts, i) for i in range(parts)])
            for d in range(1, parts)
        ]

    present, delayed = rows_of(present_ensemble), rows_of(delayed_ensemble)
    spread, ratios = rows_of(spreading_coefficient), rows_of(transport_ratios)
    sources = in_hbm((present, spread, ratios, obs_row, obs_col, obs_field))
    packed, *held = pl.pallas_call(
        functools.partial(load_kernel, chunks),
        out_shape=[shape_of((present.shape[0] + 2 * chunks, LANES))]
        + [shape_of(x.shape, x.dtype) for x in sources[1:]],
        in_specs=[hbm] * len(sources),
        scratch_shapes=[pltpu.SemaphoreType.DMA((len(sources),))],
        compiler_params=PARAMS,
        name="load",
    )(*sources)
    up = [(i, i + 1) for i in range(slabs - 1)]
    from_below = lax.ppermute(packed, "slab", [(j, i) for i, j in up])
    others_delayed = from_partners(
        lax.optimization_barrier((delayed, packed))[0]
    )
    taps, kinds = pl.pallas_call(
        selector_kernel,
        out_shape=(shape_of((width, total), BF16), shape_of((2, total), jnp.int32)),
        compiler_params=PARAMS,
        cost_estimate=estimate(SELECT_FLOPS),
        name="selector",
    )(*held[2:])
    part, here, part_obs = pl.pallas_call(
        functools.partial(own_row_kernel, *sizes),
        out_shape=(shape_of(stacked), shape_of(stacked), shape_of((members, total))),
        compiler_params=PARAMS,
        cost_estimate=estimate(OWN_FLOPS),
        name="own_row",
    )(packed, *held[:2], taps, kinds)
    from_above = lax.ppermute(lax.optimization_barrier((packed, part))[0], "slab", up)
    keep, send, partial = pl.pallas_call(
        functools.partial(observe_kernel, parts, *sizes),
        out_shape=(
            shape_of((members, total // 2)),
            shape_of((members, total // 2)),
            shape_of(stacked),
        ),
        compiler_params=PARAMS,
        name="observe",
    )(packed, from_below, part, part_obs, here, taps, kinds)
    def summed(terms, other, flops, *arrived):
        return pl.pallas_call(
            sum_kernel,
            out_shape=shape_of(terms.shape),
            cost_estimate=estimate(flops),
            compiler_params=PARAMS,
            name="sum",
        )(terms, other, *arrived)

    terms = keep + from_slab(send, 1)
    bits = [1 << k for k in reversed(range(1, slabs.bit_length() - 1))]
    bits[:2] = bits[1::-1]
    for k, bit in enumerate(bits):
        terms = summed(
            terms,
            from_other_pair(terms, bit),
            SUM_FLOPS[min(k, 2)],
            *([others_delayed[0]] if bit == bits[-1] else []),
        )
        if k == 0:
            after_first = terms
    forecast = pl.pallas_call(
        functools.partial(complete_kernel, *sizes),
        out_shape=shape_of(stacked),
        compiler_params=PARAMS,
        name="complete",
    )(
        lax.optimization_barrier((partial, after_first))[0], from_above, packed
    )

    prior = pl.pallas_call(
        gather_kernel,
        out_shape=shape_of((all_members, total // 2)),
        cost_estimate=estimate(GATHER_FLOPS),
        compiler_params=PARAMS,
        name="gather",
    )(terms, *from_other_mem(terms))
    mine = pl.pallas_call(
        functools.partial(solve_kernel, parts),
        out_shape=shape_of((members, all_members)),
        compiler_params=PARAMS,
        cost_estimate=estimate(SOLVE_FLOPS),
        name="solve",
    )(obs_value, obs_error, obs_noise, prior, from_slab(prior, 1))
    lagged_parts = pl.pallas_call(
        functools.partial(prepare_kernel, parts),
        out_shape=[shape_of((all_members, delayed.size // members), BF16)] * 2,
        compiler_params=PARAMS,
        name="prepare",
    )(delayed, *others_delayed)
    out = pl.pallas_call(
        functools.partial(combine_kernel, parts, fields),
        out_shape=shape_of((members, planes, LANES)),
        out_specs=hbm,
        scratch_shapes=[
            pltpu.VMEM((members * planes, LANES), F32),
            pltpu.SemaphoreType.DMA((1 + lagged,)),
        ],
        compiler_params=PARAMS,
        name="combine",
    )(mine, forecast, *from_partners(forecast), *lagged_parts)
    return out.reshape(members, 1 + lagged, fields, height, width)


def solution(mesh):
    return jax.shard_map(
        shards,
        mesh=mesh,
        in_specs=(
            P("mem", None, "slab", None),
            P("mem", None, None, "slab", None),
            P("slab", None),
            P(None, "slab", None),
            P(),
            P(),
            P(),
            P(),
            P(),
            P(),
        ),
        out_specs=P("mem", None, None, "slab", None),
        check_vma=False,
    )
```

```python
import functools

import jax
import jax.numpy as jnp
from jax import lax
from jax.experimental import pallas as pl
from jax.experimental.pallas import tpu as pltpu
from jax.sharding import PartitionSpec as P

LANES = 128
F32 = jnp.float32
BF16 = jnp.bfloat16
HIGHEST = lax.Precision.HIGHEST
PARAMS = pltpu.CompilerParams(vmem_limit_bytes=48 * 1024 * 1024)


SELECT_FLOPS = 1
OWN_FLOPS, SUM_FLOPS, GATHER_FLOPS, SOLVE_FLOPS = 1, (7*10**8,7*10**8,1), 10**8, 5*10**8


def estimate(flops):
    return pl.CostEstimate(flops=flops, transcendentals=0, bytes_accessed=0)


def rows_of(array):
    return array.reshape(-1, LANES)


def in_hbm(arrays):
    return [pltpu.with_memory_space_constraint(array, pltpu.HBM) for array in arrays]


def shape_of(shape, dtype=F32):
    return jax.ShapeDtypeStruct(shape, dtype)


def split_two(x):
    high = x.astype(BF16)
    low = (x - high.astype(F32)).astype(BF16)
    return high, low


def split_three(x):
    high = x.astype(BF16)
    rest = x - high.astype(F32)
    middle = rest.astype(BF16)
    low = (rest - middle.astype(F32)).astype(BF16)
    return high, middle, low


def line(ref, start, chunks):
    return jnp.concatenate([ref[start + c : start + c + 1, :] for c in range(chunks)], axis=1)


def stacked_planes(ref, members, fields, chunks):
    return jnp.concatenate(
        [
            jnp.concatenate(
                [
                    ref[pl.ds(f * chunks + c, members, stride=fields * chunks), :]
                    for c in range(chunks)
                ],
                axis=1,
            )
            for f in range(fields)
        ],
        axis=0,
    )


def at_once(sources, targets, sems):
    copies = [
        pltpu.make_async_copy(source, target, sems.at[i])
        for i, (source, target) in enumerate(zip(sources, targets))
    ]
    for copy in copies:
        copy.start()
    return copies


def picked_values(planes, taps):
    high, middle, low = (
        jnp.dot(part, taps, preferred_element_type=F32) for part in split_three(planes)
    )
    return low + middle + high


def load_kernel(chunks, *refs):
    count = (len(refs) - 1) // 2
    sources, packed_ref, held, sems = refs[:count], refs[count], refs[count + 1 : -1], refs[-1]
    rows = sources[0].shape[0]
    copies = at_once(sources, (packed_ref.at[:rows], *held), sems)
    copies[1].wait()
    copies[2].wait()
    spread = held[0][...]
    half = held[1][:chunks, :] * 0.5
    packed_ref[rows : rows + chunks, :] = spread + half
    packed_ref[rows + chunks : rows + 2 * chunks, :] = spread - half
    for copy in (copies[0], *copies[3:]):
        copy.wait()


def keeps_first(parts):
    rest = lax.axis_index("slab")
    ones = lax.axis_index("mem") if parts == 2 else 0
    for _ in range(lax.axis_size("slab").bit_length() - 1):
        ones = ones + lax.rem(rest, 2)
        rest = rest // 2
    return lax.rem(ones, 2) == 0


def weights(packed_ref, chunks):
    rows = packed_ref.shape[0] - 2 * chunks
    return line(packed_ref, rows, chunks), line(packed_ref, rows + chunks, chunks)


def selector_kernel(row_ref, col_ref, field_ref, taps_ref, kinds_ref):
    batches, count = row_ref.shape
    shape = taps_ref.shape
    flat = lambda ref: jnp.concatenate([ref[b : b + 1, :] for b in range(batches)], axis=1)
    rows, cols, kinds = flat(row_ref), flat(col_ref), flat(field_ref)
    own_row = lax.axis_index("slab")
    for k, row in enumerate((own_row, own_row + 1)):
        kinds_ref[k : k + 1, :] = jnp.where(rows == row, kinds, -1)
    at = lax.broadcasted_iota(jnp.int32, shape, 0).astype(F32) * 0.25
    taps_ref[...] = jnp.maximum(0.5 - jnp.abs(at - cols.astype(F32) * 0.25), 0.0).astype(BF16)


def own_row_kernel(
    members,
    fields,
    chunks,
    packed_ref,
    spread_ref,
    ratio_ref,
    taps_ref,
    kinds_ref,
    part_ref,
    here_ref,
    obs_ref,
):
    width = chunks * LANES
    spread = line(spread_ref, 0, chunks)
    along_columns = line(ratio_ref, chunks, chunks)
    here = stacked_planes(packed_ref, members, fields, chunks)
    here_ref[...] = here
    lane = lax.broadcasted_iota(jnp.int32, here.shape, 1)
    left = jnp.where(lane == 0, 0.0, pltpu.roll(here, 1, 1))
    right = jnp.where(lane == width - 1, 0.0, pltpu.roll(here, width - 1, 1))
    part = (
        here
        + spread * (right + left - 4.0 * here)
        - along_columns * (right - left) * 0.5
    )
    part_ref[...] = part
    picked = picked_values(part, taps_ref[...])
    observed = jnp.zeros(obs_ref.shape, F32)
    for f in range(fields):
        observed += jnp.where(
            kinds_ref[0:1, :] == f, picked[f * members : (f + 1) * members], 0.0
        )
    obs_ref[...] = observed


def observe_kernel(
    parts,
    members,
    fields,
    chunks,
    packed_ref,
    next_ref,
    part_ref,
    part_obs_ref,
    here_ref,
    taps_ref,
    kinds_ref,
    keep_ref,
    send_ref,
    partial_ref,
):
    _, below = weights(packed_ref, chunks)
    above_of_below, _ = weights(next_ref, chunks)
    taken = below * stacked_planes(next_ref, members, fields, chunks)
    given = above_of_below * here_ref[...]
    partial_ref[...] = part_ref[...] + taken
    picked = sum(
        jnp.dot(part, taps_ref[...], preferred_element_type=F32)
        for part in reversed(split_two(jnp.concatenate([taken, given], axis=0)))
    )
    observed = part_obs_ref[...]
    for side in range(2):
        kinds = kinds_ref[side : side + 1, :]
        for f in range(fields):
            start = (side * fields + f) * members
            observed += jnp.where(kinds == f, picked[start : start + members], 0.0)
    first_here = keeps_first(parts)
    half = observed.shape[1] // 2
    first, second = observed[:, :half], observed[:, half:]
    keep_ref[...] = jnp.where(first_here, first, second)
    send_ref[...] = jnp.where(first_here, second, first)


def sum_kernel(terms_ref, other_ref, *refs):
    refs[-1][...] = terms_ref[...] + other_ref[...]


def complete_kernel(members, fields, chunks, partial_ref, previous_ref, packed_ref, forecast_ref):
    above, _ = weights(packed_ref, chunks)
    forecast_ref[...] = partial_ref[...] + above * stacked_planes(
        previous_ref, members, fields, chunks
    )


def gather_kernel(*refs):
    local = refs[2].shape[0]
    for d, ref in enumerate(refs[2:-1]):
        refs[-1][d * local : (d + 1) * local, :] = ref[...]


def identity(rows, columns):
    return (
        lax.broadcasted_iota(jnp.int32, (rows, columns), 0)
        == lax.broadcasted_iota(jnp.int32, (rows, columns), 1)
    ).astype(F32)


def precise(x, y):
    return jnp.dot(x, y, precision=HIGHEST, preferred_element_type=F32)


def three_pass(x, y):
    x_high, x_low = split_two(x)
    y_high, y_low = split_two(y)
    dot = functools.partial(jnp.dot, preferred_element_type=F32)
    return dot(x_low, y_high) + dot(x_high, y_low) + dot(x_high, y_high)


def solve_transposed(system, right_t, floor):
    size = system.shape[0]
    eye = identity(size, size)
    sums = jnp.sum(jnp.abs(system), axis=0, keepdims=True)
    top = jnp.max(sums, axis=1, keepdims=True) + 1.0
    scale = 2.0 / (top + floor)
    start = (1.0 - floor * scale, eye - scale * system, scale * right_t)

    def double(product, carry):
        eps, residual, answer = carry
        both = product(jnp.concatenate([residual, answer], axis=0), residual)
        square = eps * eps
        share = 1.0 / (2.0 - square)
        return (
            square * share,
            (2.0 * both[:size] - square * eye) * share,
            (answer + both[size:]) * (2.0 * share),
        )

    def steps(count):
        carry = start
        for _ in range(count):
            carry = double(three_pass, carry)
        return carry[2]

    def loop():
        return lax.while_loop(
            lambda carry: jnp.max(carry[0]) > 1e-6, functools.partial(double, precise), start
        )[2]

    condition = jnp.max(top) / floor
    return lax.cond(
        condition < 20.0,
        lambda: steps(5),
        lambda: lax.cond(condition < 78.0, lambda: steps(6), loop),
    )


def precise_nt(x, y):
    return lax.dot_general(
        x, y, (((1,), (1,)), ((), ())), precision=HIGHEST, preferred_element_type=F32
    )


def solve_kernel(parts, value_ref, error_ref, noise_ref, kept_ref, received_ref, mine_ref):
    batches, members, count = noise_ref.shape
    local = members // parts
    own = lax.axis_index("mem")
    first_here = keeps_first(parts)
    halves = [
        jnp.where(first_here, kept_ref[...], received_ref[...]),
        jnp.where(first_here, received_ref[...], kept_ref[...]),
    ]
    prior = jnp.concatenate(halves, axis=1)
    grams = []
    for b in range(batches):
        wanted = local if b == batches - 1 else members
        observed = prior[:, b * count : (b + 1) * count]
        share = 1.0 / error_ref[b : b + 1, :]
        mean = jnp.mean(observed, axis=0, keepdims=True)
        anomalies = (observed - mean) * share
        blocks = []
        for d in range(wanted // local):
            owner = lax.rem(own + d, parts)
            blocks.append(
                noise_ref[b, pl.ds(pl.multiple_of(owner * local, local), local), :]
            )
        innovation = (value_ref[b : b + 1, :] - mean) * share + jnp.concatenate(blocks, axis=0)
        both = precise_nt(jnp.concatenate([anomalies, innovation], axis=0), anomalies)
        grams.append((both[:members], both[members:]))
    diagonal = (members - 1.0) * identity(members, members)
    product_t = None
    for b, (gram, cross) in enumerate(grams):
        wanted = cross.shape[0]
        if product_t is None:
            system, right_t = gram, cross - gram[:wanted]
        else:
            centred = product_t - jnp.mean(product_t, axis=0, keepdims=True)
            both = precise(jnp.concatenate([centred, product_t[:wanted]], axis=0), gram)
            both = precise_nt(
                jnp.concatenate([both[:members], cross - both[members:]], axis=0), centred
            )
            system, right_t = both[:members], both[members:]
        weights_t = solve_transposed(system + diagonal, right_t, members - 1.0)
        matrix_t = (
            identity(wanted, members) + weights_t - jnp.mean(weights_t, axis=1, keepdims=True)
        )
        product_t = matrix_t if product_t is None else precise(matrix_t, product_t)
    mine_ref[...] = product_t


def prepare_kernel(parts, *refs):
    sources, high_ref, low_ref = refs[:parts], refs[parts], refs[parts + 1]
    lagged = high_ref.shape[1] // LANES
    local = high_ref.shape[0] // parts
    for k in range(lagged):
        held = jnp.concatenate(
            [ref[pl.ds(k, local, stride=lagged), :] for ref in sources], axis=0
        )
        high, low = split_two(held)
        high_ref[:, k * LANES : (k + 1) * LANES] = high
        low_ref[:, k * LANES : (k + 1) * LANES] = low


def combine_kernel(parts, fields, mine_ref, *refs):
    forecast_refs = refs[:parts]
    lagged_high_ref, lagged_low_ref, out_ref, done_ref, sems = refs[parts:]
    local = mine_ref.shape[0]
    high, low = split_two(mine_ref[...])
    left = jnp.concatenate([high, high, low], axis=1)
    width = forecast_refs[0].shape[1]
    chunks = width // LANES
    level = fields * chunks
    planes = level + lagged_high_ref.shape[1] // LANES
    copies = []
    for first in [*range(level, planes, level), 0]:
        for f in range(fields):
            start = first + f * chunks
            if first == 0:
                held_high, held_low = split_two(
                    jnp.concatenate(
                        [ref[f * local : (f + 1) * local, :] for ref in forecast_refs], axis=0
                    )
                )
            else:
                lanes = slice((start - level) * LANES, (start - level) * LANES + width)
                held_high, held_low = lagged_high_ref[:, lanes], lagged_low_ref[:, lanes]
            result = jnp.dot(
                left,
                jnp.concatenate([held_high, held_low, held_high], axis=0),
                preferred_element_type=F32,
            )
            for c in range(chunks):
                done_ref[pl.ds(start + c, local, stride=planes), :] = result[
                    :, c * LANES : (c + 1) * LANES
                ]
        copies.append(
            pltpu.make_async_copy(
                done_ref.reshape(local, planes, LANES).at[:, first : first + level, :],
                out_ref.at[:, first : first + level, :],
                sems.at[len(copies)],
            )
        )
        copies[-1].start()
    for copy in copies:
        copy.wait()


def shards(
    present_ensemble,
    delayed_ensemble,
    spreading_coefficient,
    transport_ratios,
    obs_value,
    obs_error,
    obs_noise,
    obs_row,
    obs_col,
    obs_field,
):
    members, fields, height, width = present_ensemble.shape
    assert height == 1 and width % LANES == 0
    chunks = width // LANES
    lagged = delayed_ensemble.shape[1]
    slabs, parts = lax.axis_size("slab"), lax.axis_size("mem")
    assert slabs & (slabs - 1) == 0 and slabs >= 8
    batches, all_members, count = obs_noise.shape
    total = batches * count
    planes = (1 + lagged) * fields * chunks
    stacked = (fields * members, width)
    hbm = pl.BlockSpec(memory_space=pltpu.HBM)
    sizes = (members, fields, chunks)

    def from_slab(array, bit):
        return lax.ppermute(array, "slab", [(i, i ^ bit) for i in range(slabs)])

    def from_other_pair(array, bit):
        return from_slab(array, bit ^ 1)

    def from_other_mem(array):
        if parts != 2:
            return from_partners(array)
        return [
            lax.ppermute(
                array, ("slab", "mem"), [(i ^ 3, i) for i in range(slabs * parts)]
            )
        ]

    def from_partners(array):
        return [
            lax.ppermute(array, "mem", [((i + d) % parts, i) for i in range(parts)])
            for d in range(1, parts)
        ]

    present, delayed = rows_of(present_ensemble), rows_of(delayed_ensemble)
    spread, ratios = rows_of(spreading_coefficient), rows_of(transport_ratios)
    sources = in_hbm((present, spread, ratios))
    packed, *held = pl.pallas_call(
        functools.partial(load_kernel, chunks),
        out_shape=[shape_of((present.shape[0] + 2 * chunks, LANES))]
        + [shape_of(x.shape, x.dtype) for x in sources[1:]],
        in_specs=[hbm] * len(sources),
        scratch_shapes=[pltpu.SemaphoreType.DMA((len(sources),))],
        compiler_params=PARAMS,
        name="load",
    )(*sources)
    up = [(i, i + 1) for i in range(slabs - 1)]
    from_below = lax.ppermute(packed, "slab", [(j, i) for i, j in up])
    others_delayed = from_partners(
        lax.optimization_barrier((delayed, packed))[0]
    )
    taps, kinds = pl.pallas_call(
        selector_kernel,
        out_shape=(shape_of((width, total), BF16), shape_of((2, total), jnp.int32)),
        compiler_params=PARAMS,
        cost_estimate=estimate(SELECT_FLOPS),
        name="selector",
    )(obs_row, obs_col, obs_field)
    part, here, part_obs = pl.pallas_call(
        functools.partial(own_row_kernel, *sizes),
        out_shape=(shape_of(stacked), shape_of(stacked), shape_of((members, total))),
        compiler_params=PARAMS,
        cost_estimate=estimate(OWN_FLOPS),
        name="own_row",
    )(packed, *held, taps, kinds)
    from_above = lax.ppermute(lax.optimization_barrier((packed, part))[0], "slab", up)
    keep, send, partial = pl.pallas_call(
        functools.partial(observe_kernel, parts, *sizes),
        out_shape=(
            shape_of((members, total // 2)),
            shape_of((members, total // 2)),
            shape_of(stacked),
        ),
        compiler_params=PARAMS,
        name="observe",
    )(packed, from_below, part, part_obs, here, taps, kinds)
    def summed(terms, other, flops, *arrived):
        return pl.pallas_call(
            sum_kernel,
            out_shape=shape_of(terms.shape),
            cost_estimate=estimate(flops),
            compiler_params=PARAMS,
            name="sum",
        )(terms, other, *arrived)

    terms = keep + from_slab(send, 1)
    for bit in [1 << k for k in reversed(range(1, slabs.bit_length() - 1))]:
        terms = summed(
            terms,
            from_other_pair(terms, bit),
            SUM_FLOPS[min(slabs // 2 // bit, 4) // 2],
            *([others_delayed[0]] if bit == 2 else []),
        )
        if bit == slabs // 2:
            after_far = terms
    forecast = pl.pallas_call(
        functools.partial(complete_kernel, *sizes),
        out_shape=shape_of(stacked),
        compiler_params=PARAMS,
        name="complete",
    )(
        lax.optimization_barrier((partial, after_far))[0], from_above, packed
    )

    lagged_parts = pl.pallas_call(
        functools.partial(prepare_kernel, parts),
        out_shape=[shape_of((all_members, delayed.size // members), BF16)] * 2,
        compiler_params=PARAMS,
        name="prepare",
    )(delayed, *others_delayed)
    prior = pl.pallas_call(
        gather_kernel,
        out_shape=shape_of((all_members, total // 2)),
        cost_estimate=estimate(GATHER_FLOPS),
        compiler_params=PARAMS,
        name="gather",
    )(*lagged_parts, terms, *from_other_mem(terms))
    mine = pl.pallas_call(
        functools.partial(solve_kernel, parts),
        out_shape=shape_of((members, all_members)),
        compiler_params=PARAMS,
        cost_estimate=estimate(SOLVE_FLOPS),
        name="solve",
    )(obs_value, obs_error, obs_noise, prior, from_slab(prior, 1))
    out = pl.pallas_call(
        functools.partial(combine_kernel, parts, fields),
        out_shape=shape_of((members, planes, LANES)),
        out_specs=hbm,
        scratch_shapes=[
            pltpu.VMEM((members * planes, LANES), F32),
            pltpu.SemaphoreType.DMA((1 + lagged,)),
        ],
        compiler_params=PARAMS,
        name="combine",
    )(mine, forecast, *from_partners(forecast), *lagged_parts)
    return out.reshape(members, 1 + lagged, fields, height, width)


def solution(mesh):
    return jax.shard_map(
        shards,
        mesh=mesh,
        in_specs=(
            P("mem", None, "slab", None),
            P("mem", None, None, "slab", None),
            P("slab", None),
            P(None, "slab", None),
            P(),
            P(),
            P(),
            P(),
            P(),
            P(),
        ),
        out_specs=P("mem", None, None, "slab", None),
        check_vma=False,
    )
```

```python
import functools

import jax
import jax.numpy as jnp
from jax import lax
from jax.experimental import pallas as pl
from jax.experimental.pallas import tpu as pltpu
from jax.sharding import PartitionSpec as P

LANES = 128
F32 = jnp.float32
BF16 = jnp.bfloat16
HIGHEST = lax.Precision.HIGHEST
PARAMS = pltpu.CompilerParams(vmem_limit_bytes=48 * 1024 * 1024)


SELECT_FLOPS = 1
OWN_FLOPS, SUM_FLOPS, GATHER_FLOPS, SOLVE_FLOPS = 1, (2*10**9,1,8*10**8), 10**8, 7*10**8


def estimate(flops):
    return pl.CostEstimate(flops=flops, transcendentals=0, bytes_accessed=0)


def rows_of(array):
    return array.reshape(-1, LANES)


def in_hbm(arrays):
    return [pltpu.with_memory_space_constraint(array, pltpu.HBM) for array in arrays]


def shape_of(shape, dtype=F32):
    return jax.ShapeDtypeStruct(shape, dtype)


def split_two(x):
    high = x.astype(BF16)
    low = (x - high.astype(F32)).astype(BF16)
    return high, low


def split_three(x):
    high = x.astype(BF16)
    rest = x - high.astype(F32)
    middle = rest.astype(BF16)
    low = (rest - middle.astype(F32)).astype(BF16)
    return high, middle, low


def line(ref, start, chunks):
    return jnp.concatenate([ref[start + c : start + c + 1, :] for c in range(chunks)], axis=1)


def stacked_planes(ref, members, fields, chunks):
    return jnp.concatenate(
        [
            jnp.concatenate(
                [
                    ref[pl.ds(f * chunks + c, members, stride=fields * chunks), :]
                    for c in range(chunks)
                ],
                axis=1,
            )
            for f in range(fields)
        ],
        axis=0,
    )


def at_once(sources, targets, sems):
    copies = [
        pltpu.make_async_copy(source, target, sems.at[i])
        for i, (source, target) in enumerate(zip(sources, targets))
    ]
    for copy in copies:
        copy.start()
    return copies


def picked_values(planes, taps):
    high, middle, low = (
        jnp.dot(part, taps, preferred_element_type=F32) for part in split_three(planes)
    )
    return low + middle + high


def load_kernel(chunks, *refs):
    count = (len(refs) - 1) // 2
    sources, packed_ref, held, sems = refs[:count], refs[count], refs[count + 1 : -1], refs[-1]
    rows = sources[0].shape[0]
    copies = at_once(sources, (packed_ref.at[:rows], *held), sems)
    copies[1].wait()
    copies[2].wait()
    spread = held[0][...]
    half = held[1][:chunks, :] * 0.5
    packed_ref[rows : rows + chunks, :] = spread + half
    packed_ref[rows + chunks : rows + 2 * chunks, :] = spread - half
    for copy in (copies[0], *copies[3:]):
        copy.wait()


def keeps_first(parts):
    rest = lax.axis_index("slab")
    ones = lax.axis_index("mem") if parts == 2 else 0
    for _ in range(lax.axis_size("slab").bit_length() - 1):
        ones = ones + lax.rem(rest, 2)
        rest = rest // 2
    return lax.rem(ones, 2) == 0


def weights(packed_ref, chunks):
    rows = packed_ref.shape[0] - 2 * chunks
    return line(packed_ref, rows, chunks), line(packed_ref, rows + chunks, chunks)


def selector_kernel(row_ref, col_ref, field_ref, taps_ref, kinds_ref):
    batches, count = row_ref.shape
    shape = taps_ref.shape
    flat = lambda ref: jnp.concatenate([ref[b : b + 1, :] for b in range(batches)], axis=1)
    rows, cols, kinds = flat(row_ref), flat(col_ref), flat(field_ref)
    own_row = lax.axis_index("slab")
    for k, row in enumerate((own_row, own_row + 1)):
        kinds_ref[k : k + 1, :] = jnp.where(rows == row, kinds, -1)
    at = lax.broadcasted_iota(jnp.int32, shape, 0).astype(F32) * 0.25
    taps_ref[...] = jnp.maximum(0.5 - jnp.abs(at - cols.astype(F32) * 0.25), 0.0).astype(BF16)


def own_row_kernel(
    members,
    fields,
    chunks,
    packed_ref,
    spread_ref,
    ratio_ref,
    taps_ref,
    kinds_ref,
    part_ref,
    here_ref,
    obs_ref,
):
    width = chunks * LANES
    spread = line(spread_ref, 0, chunks)
    along_columns = line(ratio_ref, chunks, chunks)
    here = stacked_planes(packed_ref, members, fields, chunks)
    here_ref[...] = here
    lane = lax.broadcasted_iota(jnp.int32, here.shape, 1)
    left = jnp.where(lane == 0, 0.0, pltpu.roll(here, 1, 1))
    right = jnp.where(lane == width - 1, 0.0, pltpu.roll(here, width - 1, 1))
    part = (
        here
        + spread * (right + left - 4.0 * here)
        - along_columns * (right - left) * 0.5
    )
    part_ref[...] = part
    picked = picked_values(part, taps_ref[...])
    observed = jnp.zeros(obs_ref.shape, F32)
    for f in range(fields):
        observed += jnp.where(
            kinds_ref[0:1, :] == f, picked[f * members : (f + 1) * members], 0.0
        )
    obs_ref[...] = observed


def observe_kernel(
    parts,
    members,
    fields,
    chunks,
    packed_ref,
    next_ref,
    part_ref,
    part_obs_ref,
    here_ref,
    taps_ref,
    kinds_ref,
    keep_ref,
    send_ref,
    partial_ref,
):
    _, below = weights(packed_ref, chunks)
    above_of_below, _ = weights(next_ref, chunks)
    taken = below * stacked_planes(next_ref, members, fields, chunks)
    given = above_of_below * here_ref[...]
    partial_ref[...] = part_ref[...] + taken
    picked = sum(
        jnp.dot(part, taps_ref[...], preferred_element_type=F32)
        for part in reversed(split_two(jnp.concatenate([taken, given], axis=0)))
    )
    observed = part_obs_ref[...]
    for side in range(2):
        kinds = kinds_ref[side : side + 1, :]
        for f in range(fields):
            start = (side * fields + f) * members
            observed += jnp.where(kinds == f, picked[start : start + members], 0.0)
    first_here = keeps_first(parts)
    half = observed.shape[1] // 2
    first, second = observed[:, :half], observed[:, half:]
    keep_ref[...] = jnp.where(first_here, first, second)
    send_ref[...] = jnp.where(first_here, second, first)


def sum_kernel(terms_ref, other_ref, *refs):
    refs[-1][...] = terms_ref[...] + other_ref[...]


def complete_kernel(members, fields, chunks, partial_ref, previous_ref, packed_ref, forecast_ref):
    above, _ = weights(packed_ref, chunks)
    forecast_ref[...] = partial_ref[...] + above * stacked_planes(
        previous_ref, members, fields, chunks
    )


def gather_kernel(*refs):
    local = refs[0].shape[0]
    for d, ref in enumerate(refs[:-1]):
        refs[-1][d * local : (d + 1) * local, :] = ref[...]


def identity(rows, columns):
    return (
        lax.broadcasted_iota(jnp.int32, (rows, columns), 0)
        == lax.broadcasted_iota(jnp.int32, (rows, columns), 1)
    ).astype(F32)


def precise(x, y):
    return jnp.dot(x, y, precision=HIGHEST, preferred_element_type=F32)


def three_pass(x, y):
    x_high, x_low = split_two(x)
    y_high, y_low = split_two(y)
    dot = functools.partial(jnp.dot, preferred_element_type=F32)
    return dot(x_low, y_high) + dot(x_high, y_low) + dot(x_high, y_high)


def solve_transposed(system, right_t, floor):
    size = system.shape[0]
    eye = identity(size, size)
    sums = jnp.sum(jnp.abs(system), axis=0, keepdims=True)
    top = jnp.max(sums, axis=1, keepdims=True) + 1.0
    scale = 2.0 / (top + floor)
    start = (1.0 - floor * scale, eye - scale * system, scale * right_t)

    def double(product, carry):
        eps, residual, answer = carry
        both = product(jnp.concatenate([residual, answer], axis=0), residual)
        square = eps * eps
        share = 1.0 / (2.0 - square)
        return (
            square * share,
            (2.0 * both[:size] - square * eye) * share,
            (answer + both[size:]) * (2.0 * share),
        )

    def steps(count):
        carry = start
        for _ in range(count):
            carry = double(three_pass, carry)
        return carry[2]

    def loop():
        return lax.while_loop(
            lambda carry: jnp.max(carry[0]) > 1e-6, functools.partial(double, precise), start
        )[2]

    condition = jnp.max(top) / floor
    return lax.cond(
        condition < 20.0,
        lambda: steps(5),
        lambda: lax.cond(condition < 78.0, lambda: steps(6), loop),
    )


def precise_nt(x, y):
    return lax.dot_general(
        x, y, (((1,), (1,)), ((), ())), precision=HIGHEST, preferred_element_type=F32
    )


def solve_kernel(parts, value_ref, error_ref, noise_ref, kept_ref, received_ref, mine_ref):
    batches, members, count = noise_ref.shape
    local = members // parts
    own = lax.axis_index("mem")
    first_here = keeps_first(parts)
    halves = [
        jnp.where(first_here, kept_ref[...], received_ref[...]),
        jnp.where(first_here, received_ref[...], kept_ref[...]),
    ]
    prior = jnp.concatenate(halves, axis=1)
    grams = []
    for b in range(batches):
        wanted = local if b == batches - 1 else members
        observed = prior[:, b * count : (b + 1) * count]
        share = 1.0 / error_ref[b : b + 1, :]
        mean = jnp.mean(observed, axis=0, keepdims=True)
        anomalies = (observed - mean) * share
        blocks = []
        for d in range(wanted // local):
            owner = lax.rem(own + d, parts)
            blocks.append(
                noise_ref[b, pl.ds(pl.multiple_of(owner * local, local), local), :]
            )
        innovation = (value_ref[b : b + 1, :] - mean) * share + jnp.concatenate(blocks, axis=0)
        both = precise_nt(jnp.concatenate([anomalies, innovation], axis=0), anomalies)
        grams.append((both[:members], both[members:]))
    diagonal = (members - 1.0) * identity(members, members)
    product_t = None
    for b, (gram, cross) in enumerate(grams):
        wanted = cross.shape[0]
        if product_t is None:
            system, right_t = gram, cross - gram[:wanted]
        else:
            centred = product_t - jnp.mean(product_t, axis=0, keepdims=True)
            both = precise(jnp.concatenate([centred, product_t[:wanted]], axis=0), gram)
            both = precise_nt(
                jnp.concatenate([both[:members], cross - both[members:]], axis=0), centred
            )
            system, right_t = both[:members], both[members:]
        weights_t = solve_transposed(system + diagonal, right_t, members - 1.0)
        matrix_t = (
            identity(wanted, members) + weights_t - jnp.mean(weights_t, axis=1, keepdims=True)
        )
        product_t = matrix_t if product_t is None else precise(matrix_t, product_t)
    mine_ref[...] = product_t


def prepare_kernel(parts, *refs):
    sources, high_ref, low_ref = refs[:parts], refs[parts], refs[parts + 1]
    lagged = high_ref.shape[1] // LANES
    local = high_ref.shape[0] // parts
    for k in range(lagged):
        held = jnp.concatenate(
            [ref[pl.ds(k, local, stride=lagged), :] for ref in sources], axis=0
        )
        high, low = split_two(held)
        high_ref[:, k * LANES : (k + 1) * LANES] = high
        low_ref[:, k * LANES : (k + 1) * LANES] = low


def combine_kernel(parts, fields, mine_ref, *refs):
    forecast_refs = refs[:parts]
    lagged_high_ref, lagged_low_ref, out_ref, done_ref, sems = refs[parts:]
    local = mine_ref.shape[0]
    high, low = split_two(mine_ref[...])
    left = jnp.concatenate([high, high, low], axis=1)
    width = forecast_refs[0].shape[1]
    chunks = width // LANES
    level = fields * chunks
    planes = level + lagged_high_ref.shape[1] // LANES
    copies = []
    for first in [*range(level, planes, level), 0]:
        for f in range(fields):
            start = first + f * chunks
            if first == 0:
                held_high, held_low = split_two(
                    jnp.concatenate(
                        [ref[f * local : (f + 1) * local, :] for ref in forecast_refs], axis=0
                    )
                )
            else:
                lanes = slice((start - level) * LANES, (start - level) * LANES + width)
                held_high, held_low = lagged_high_ref[:, lanes], lagged_low_ref[:, lanes]
            result = jnp.dot(
                left,
                jnp.concatenate([held_high, held_low, held_high], axis=0),
                preferred_element_type=F32,
            )
            for c in range(chunks):
                done_ref[pl.ds(start + c, local, stride=planes), :] = result[
                    :, c * LANES : (c + 1) * LANES
                ]
        copies.append(
            pltpu.make_async_copy(
                done_ref.reshape(local, planes, LANES).at[:, first : first + level, :],
                out_ref.at[:, first : first + level, :],
                sems.at[len(copies)],
            )
        )
        copies[-1].start()
    for copy in copies:
        copy.wait()


def shards(
    present_ensemble,
    delayed_ensemble,
    spreading_coefficient,
    transport_ratios,
    obs_value,
    obs_error,
    obs_noise,
    obs_row,
    obs_col,
    obs_field,
):
    members, fields, height, width = present_ensemble.shape
    assert height == 1 and width % LANES == 0
    chunks = width // LANES
    lagged = delayed_ensemble.shape[1]
    slabs, parts = lax.axis_size("slab"), lax.axis_size("mem")
    assert slabs & (slabs - 1) == 0 and slabs >= 8
    batches, all_members, count = obs_noise.shape
    total = batches * count
    planes = (1 + lagged) * fields * chunks
    stacked = (fields * members, width)
    hbm = pl.BlockSpec(memory_space=pltpu.HBM)
    sizes = (members, fields, chunks)

    def from_slab(array, bit):
        return lax.ppermute(array, "slab", [(i, i ^ bit) for i in range(slabs)])

    def from_other_pair(array, bit):
        return from_slab(array, bit ^ 1)

    def from_other_mem(array):
        if parts != 2:
            return from_partners(array)
        return [
            lax.ppermute(
                array, ("slab", "mem"), [(i ^ 3, i) for i in range(slabs * parts)]
            )
        ]

    def from_partners(array):
        return [
            lax.ppermute(array, "mem", [((i + d) % parts, i) for i in range(parts)])
            for d in range(1, parts)
        ]

    present, delayed = rows_of(present_ensemble), rows_of(delayed_ensemble)
    spread, ratios = rows_of(spreading_coefficient), rows_of(transport_ratios)
    sources = in_hbm((present, spread, ratios, obs_row, obs_col, obs_field))
    packed, *held = pl.pallas_call(
        functools.partial(load_kernel, chunks),
        out_shape=[shape_of((present.shape[0] + 2 * chunks, LANES))]
        + [shape_of(x.shape, x.dtype) for x in sources[1:]],
        in_specs=[hbm] * len(sources),
        scratch_shapes=[pltpu.SemaphoreType.DMA((len(sources),))],
        compiler_params=PARAMS,
        name="load",
    )(*sources)
    up = [(i, i + 1) for i in range(slabs - 1)]
    from_below = lax.ppermute(packed, "slab", [(j, i) for i, j in up])
    others_delayed = from_partners(
        lax.optimization_barrier((delayed, packed))[0]
    )
    taps, kinds = pl.pallas_call(
        selector_kernel,
        out_shape=(shape_of((width, total), BF16), shape_of((2, total), jnp.int32)),
        compiler_params=PARAMS,
        cost_estimate=estimate(SELECT_FLOPS),
        name="selector",
    )(*held[2:])
    part, here, part_obs = pl.pallas_call(
        functools.partial(own_row_kernel, *sizes),
        out_shape=(shape_of(stacked), shape_of(stacked), shape_of((members, total))),
        compiler_params=PARAMS,
        cost_estimate=estimate(OWN_FLOPS),
        name="own_row",
    )(packed, *held[:2], taps, kinds)
    keep, send, partial = pl.pallas_call(
        functools.partial(observe_kernel, parts, *sizes),
        out_shape=(
            shape_of((members, total // 2)),
            shape_of((members, total // 2)),
            shape_of(stacked),
        ),
        compiler_params=PARAMS,
        name="observe",
    )(packed, from_below, part, part_obs, here, taps, kinds)
    def summed(terms, other, flops, *arrived):
        return pl.pallas_call(
            sum_kernel,
            out_shape=shape_of(terms.shape),
            cost_estimate=estimate(flops),
            compiler_params=PARAMS,
            name="sum",
        )(terms, other, *arrived)

    terms = keep + from_slab(send, 1)
    from_above = lax.ppermute(lax.optimization_barrier((packed, terms))[0], "slab", up)
    for bit in [1 << k for k in reversed(range(1, slabs.bit_length() - 1))]:
        terms = summed(
            terms,
            from_other_pair(terms, bit),
            SUM_FLOPS[min(slabs // 2 // bit, 4) // 2],
            *([others_delayed[0]] if bit == 2 else []),
        )
        if bit == 4:
            before_last = terms
    forecast = pl.pallas_call(
        functools.partial(complete_kernel, *sizes),
        out_shape=shape_of(stacked),
        compiler_params=PARAMS,
        name="complete",
    )(
        lax.optimization_barrier((partial, before_last))[0], from_above, packed
    )

    prior = pl.pallas_call(
        gather_kernel,
        out_shape=shape_of((all_members, total // 2)),
        cost_estimate=estimate(GATHER_FLOPS),
        compiler_params=PARAMS,
        name="gather",
    )(terms, *from_other_mem(terms))
    mine = pl.pallas_call(
        functools.partial(solve_kernel, parts),
        out_shape=shape_of((members, all_members)),
        compiler_params=PARAMS,
        cost_estimate=estimate(SOLVE_FLOPS),
        name="solve",
    )(obs_value, obs_error, obs_noise, prior, from_slab(prior, 1))
    lagged_parts = pl.pallas_call(
        functools.partial(prepare_kernel, parts),
        out_shape=[shape_of((all_members, delayed.size // members), BF16)] * 2,
        compiler_params=PARAMS,
        name="prepare",
    )(delayed, *others_delayed)
    out = pl.pallas_call(
        functools.partial(combine_kernel, parts, fields),
        out_shape=shape_of((members, planes, LANES)),
        out_specs=hbm,
        scratch_shapes=[
            pltpu.VMEM((members * planes, LANES), F32),
            pltpu.SemaphoreType.DMA((1 + lagged,)),
        ],
        compiler_params=PARAMS,
        name="combine",
    )(mine, forecast, *from_partners(forecast), *lagged_parts)
    return out.reshape(members, 1 + lagged, fields, height, width)


def solution(mesh):
    return jax.shard_map(
        shards,
        mesh=mesh,
        in_specs=(
            P("mem", None, "slab", None),
            P("mem", None, None, "slab", None),
            P("slab", None),
            P(None, "slab", None),
            P(),
            P(),
            P(),
            P(),
            P(),
            P(),
        ),
        out_specs=P("mem", None, None, "slab", None),
        check_vma=False,
    )
```

```python
import functools

import jax
import jax.numpy as jnp
from jax import lax
from jax.experimental import pallas as pl
from jax.experimental.pallas import tpu as pltpu
from jax.sharding import PartitionSpec as P

LANES = 128
F32 = jnp.float32
BF16 = jnp.bfloat16
HIGHEST = lax.Precision.HIGHEST
PARAMS = pltpu.CompilerParams(vmem_limit_bytes=48 * 1024 * 1024)


SELECT_FLOPS = 1
PIECES = 4
OWN_FLOPS, SUM_FLOPS, GATHER_FLOPS, SOLVE_FLOPS = 1, (7*10**8,7*10**8,1), 10**8, 5*10**8


def estimate(flops):
    return pl.CostEstimate(flops=flops, transcendentals=0, bytes_accessed=0)


def rows_of(array):
    return array.reshape(-1, LANES)


def in_hbm(arrays):
    return [pltpu.with_memory_space_constraint(array, pltpu.HBM) for array in arrays]


def shape_of(shape, dtype=F32):
    return jax.ShapeDtypeStruct(shape, dtype)


def split_two(x):
    high = x.astype(BF16)
    low = (x - high.astype(F32)).astype(BF16)
    return high, low


def split_three(x):
    high = x.astype(BF16)
    rest = x - high.astype(F32)
    middle = rest.astype(BF16)
    low = (rest - middle.astype(F32)).astype(BF16)
    return high, middle, low


def line(ref, start, chunks):
    return jnp.concatenate([ref[start + c : start + c + 1, :] for c in range(chunks)], axis=1)


def stacked_planes(ref, members, fields, chunks):
    return jnp.concatenate(
        [
            jnp.concatenate(
                [
                    ref[pl.ds(f * chunks + c, members, stride=fields * chunks), :]
                    for c in range(chunks)
                ],
                axis=1,
            )
            for f in range(fields)
        ],
        axis=0,
    )


def at_once(sources, targets, sems):
    copies = [
        pltpu.make_async_copy(source, target, sems.at[i])
        for i, (source, target) in enumerate(zip(sources, targets))
    ]
    for copy in copies:
        copy.start()
    return copies


def picked_values(planes, taps):
    high, middle, low = (
        jnp.dot(part, taps, preferred_element_type=F32) for part in split_three(planes)
    )
    return low + middle + high


def load_kernel(chunks, *refs):
    count = (len(refs) - 1) // 2
    (present, *others), packed_ref, held, sems = (
        refs[:count],
        refs[count],
        refs[count + 1 : -1],
        refs[-1],
    )
    rows = present.shape[0]
    piece = rows // PIECES
    pieces = [pl.ds(k * piece, piece) for k in range(PIECES)]
    copies = at_once(
        [*(present.at[p] for p in pieces), *others],
        [*(packed_ref.at[p] for p in pieces), *held],
        sems,
    )
    copies[PIECES].wait()
    copies[PIECES + 1].wait()
    spread = held[0][...]
    half = held[1][:chunks, :] * 0.5
    packed_ref[rows : rows + chunks, :] = spread + half
    packed_ref[rows + chunks : rows + 2 * chunks, :] = spread - half
    for copy in (*copies[:PIECES], *copies[PIECES + 2 :]):
        copy.wait()


def keeps_first(parts):
    rest = lax.axis_index("slab")
    ones = lax.axis_index("mem") if parts == 2 else 0
    for _ in range(lax.axis_size("slab").bit_length() - 1):
        ones = ones + lax.rem(rest, 2)
        rest = rest // 2
    return lax.rem(ones, 2) == 0


def weights(packed_ref, chunks):
    rows = packed_ref.shape[0] - 2 * chunks
    return line(packed_ref, rows, chunks), line(packed_ref, rows + chunks, chunks)


def selector_kernel(row_ref, col_ref, field_ref, taps_ref, kinds_ref):
    batches, count = row_ref.shape
    shape = taps_ref.shape
    flat = lambda ref: jnp.concatenate([ref[b : b + 1, :] for b in range(batches)], axis=1)
    rows, cols, kinds = flat(row_ref), flat(col_ref), flat(field_ref)
    own_row = lax.axis_index("slab")
    for k, row in enumerate((own_row, own_row + 1)):
        kinds_ref[k : k + 1, :] = jnp.where(rows == row, kinds, -1)
    at = lax.broadcasted_iota(jnp.int32, shape, 0).astype(F32) * 0.25
    taps_ref[...] = jnp.maximum(0.5 - jnp.abs(at - cols.astype(F32) * 0.25), 0.0).astype(BF16)


def own_row_kernel(
    members,
    fields,
    chunks,
    packed_ref,
    spread_ref,
    ratio_ref,
    taps_ref,
    kinds_ref,
    part_ref,
    here_ref,
    obs_ref,
):
    width = chunks * LANES
    spread = line(spread_ref, 0, chunks)
    along_columns = line(ratio_ref, chunks, chunks)
    here = stacked_planes(packed_ref, members, fields, chunks)
    here_ref[...] = here
    lane = lax.broadcasted_iota(jnp.int32, here.shape, 1)
    left = jnp.where(lane == 0, 0.0, pltpu.roll(here, 1, 1))
    right = jnp.where(lane == width - 1, 0.0, pltpu.roll(here, width - 1, 1))
    part = (
        here
        + spread * (right + left - 4.0 * here)
        - along_columns * (right - left) * 0.5
    )
    part_ref[...] = part
    picked = picked_values(part, taps_ref[...])
    observed = jnp.zeros(obs_ref.shape, F32)
    for f in range(fields):
        observed += jnp.where(
            kinds_ref[0:1, :] == f, picked[f * members : (f + 1) * members], 0.0
        )
    obs_ref[...] = observed


def observe_kernel(
    parts,
    members,
    fields,
    chunks,
    packed_ref,
    next_ref,
    part_ref,
    part_obs_ref,
    here_ref,
    taps_ref,
    kinds_ref,
    keep_ref,
    send_ref,
    partial_ref,
):
    _, below = weights(packed_ref, chunks)
    above_of_below, _ = weights(next_ref, chunks)
    taken = below * stacked_planes(next_ref, members, fields, chunks)
    given = above_of_below * here_ref[...]
    partial_ref[...] = part_ref[...] + taken
    picked = sum(
        jnp.dot(part, taps_ref[...], preferred_element_type=F32)
        for part in reversed(split_two(jnp.concatenate([taken, given], axis=0)))
    )
    observed = part_obs_ref[...]
    for side in range(2):
        kinds = kinds_ref[side : side + 1, :]
        for f in range(fields):
            start = (side * fields + f) * members
            observed += jnp.where(kinds == f, picked[start : start + members], 0.0)
    first_here = keeps_first(parts)
    half = observed.shape[1] // 2
    first, second = observed[:, :half], observed[:, half:]
    keep_ref[...] = jnp.where(first_here, first, second)
    send_ref[...] = jnp.where(first_here, second, first)


def sum_kernel(terms_ref, other_ref, *refs):
    refs[-1][...] = terms_ref[...] + other_ref[...]


def complete_kernel(members, fields, chunks, partial_ref, previous_ref, packed_ref, forecast_ref):
    above, _ = weights(packed_ref, chunks)
    forecast_ref[...] = partial_ref[...] + above * stacked_planes(
        previous_ref, members, fields, chunks
    )


def gather_kernel(*refs):
    local = refs[0].shape[0]
    for d, ref in enumerate(refs[:-1]):
        refs[-1][d * local : (d + 1) * local, :] = ref[...]


def identity(rows, columns):
    return (
        lax.broadcasted_iota(jnp.int32, (rows, columns), 0)
        == lax.broadcasted_iota(jnp.int32, (rows, columns), 1)
    ).astype(F32)


def precise(x, y):
    return jnp.dot(x, y, precision=HIGHEST, preferred_element_type=F32)


def three_pass(x, y):
    x_high, x_low = split_two(x)
    y_high, y_low = split_two(y)
    dot = functools.partial(jnp.dot, preferred_element_type=F32)
    return dot(x_low, y_high) + dot(x_high, y_low) + dot(x_high, y_high)


def solve_transposed(system, right_t, floor):
    size = system.shape[0]
    eye = identity(size, size)
    sums = jnp.sum(jnp.abs(system), axis=0, keepdims=True)
    top = jnp.max(sums, axis=1, keepdims=True) + 1.0
    scale = 2.0 / (top + floor)
    start = (1.0 - floor * scale, eye - scale * system, scale * right_t)

    def double(product, carry):
        eps, residual, answer = carry
        both = product(jnp.concatenate([residual, answer], axis=0), residual)
        square = eps * eps
        share = 1.0 / (2.0 - square)
        return (
            square * share,
            (2.0 * both[:size] - square * eye) * share,
            (answer + both[size:]) * (2.0 * share),
        )

    def steps(count):
        carry = start
        for _ in range(count):
            carry = double(three_pass, carry)
        return carry[2]

    def loop():
        return lax.while_loop(
            lambda carry: jnp.max(carry[0]) > 1e-6, functools.partial(double, precise), start
        )[2]

    condition = jnp.max(top) / floor
    return lax.cond(
        condition < 20.0,
        lambda: steps(5),
        lambda: lax.cond(condition < 78.0, lambda: steps(6), loop),
    )


def precise_nt(x, y):
    return lax.dot_general(
        x, y, (((1,), (1,)), ((), ())), precision=HIGHEST, preferred_element_type=F32
    )


def solve_kernel(parts, value_ref, error_ref, noise_ref, kept_ref, received_ref, mine_ref):
    batches, members, count = noise_ref.shape
    local = members // parts
    own = lax.axis_index("mem")
    first_here = keeps_first(parts)
    halves = [
        jnp.where(first_here, kept_ref[...], received_ref[...]),
        jnp.where(first_here, received_ref[...], kept_ref[...]),
    ]
    prior = jnp.concatenate(halves, axis=1)
    grams = []
    for b in range(batches):
        wanted = local if b == batches - 1 else members
        observed = prior[:, b * count : (b + 1) * count]
        share = 1.0 / error_ref[b : b + 1, :]
        mean = jnp.mean(observed, axis=0, keepdims=True)
        anomalies = (observed - mean) * share
        blocks = []
        for d in range(wanted // local):
            owner = lax.rem(own + d, parts)
            blocks.append(
                noise_ref[b, pl.ds(pl.multiple_of(owner * local, local), local), :]
            )
        innovation = (value_ref[b : b + 1, :] - mean) * share + jnp.concatenate(blocks, axis=0)
        both = precise_nt(jnp.concatenate([anomalies, innovation], axis=0), anomalies)
        grams.append((both[:members], both[members:]))
    diagonal = (members - 1.0) * identity(members, members)
    product_t = None
    for b, (gram, cross) in enumerate(grams):
        wanted = cross.shape[0]
        if product_t is None:
            system, right_t = gram, cross - gram[:wanted]
        else:
            centred = product_t - jnp.mean(product_t, axis=0, keepdims=True)
            both = precise(jnp.concatenate([centred, product_t[:wanted]], axis=0), gram)
            both = precise_nt(
                jnp.concatenate([both[:members], cross - both[members:]], axis=0), centred
            )
            system, right_t = both[:members], both[members:]
        weights_t = solve_transposed(system + diagonal, right_t, members - 1.0)
        matrix_t = (
            identity(wanted, members) + weights_t - jnp.mean(weights_t, axis=1, keepdims=True)
        )
        product_t = matrix_t if product_t is None else precise(matrix_t, product_t)
    mine_ref[...] = product_t


def prepare_kernel(parts, *refs):
    sources, high_ref, low_ref = refs[:parts], refs[parts], refs[parts + 1]
    lagged = high_ref.shape[1] // LANES
    local = high_ref.shape[0] // parts
    for k in range(lagged):
        held = jnp.concatenate(
            [ref[pl.ds(k, local, stride=lagged), :] for ref in sources], axis=0
        )
        high, low = split_two(held)
        high_ref[:, k * LANES : (k + 1) * LANES] = high
        low_ref[:, k * LANES : (k + 1) * LANES] = low


def combine_kernel(parts, fields, mine_ref, *refs):
    forecast_refs = refs[:parts]
    lagged_high_ref, lagged_low_ref, out_ref, done_ref, sems = refs[parts:]
    local = mine_ref.shape[0]
    high, low = split_two(mine_ref[...])
    left = jnp.concatenate([high, high, low], axis=1)
    width = forecast_refs[0].shape[1]
    chunks = width // LANES
    level = fields * chunks
    planes = level + lagged_high_ref.shape[1] // LANES
    copies = []
    for first in [*range(level, planes, level), 0]:
        for f in range(fields):
            start = first + f * chunks
            if first == 0:
                held_high, held_low = split_two(
                    jnp.concatenate(
                        [ref[f * local : (f + 1) * local, :] for ref in forecast_refs], axis=0
                    )
                )
            else:
                lanes = slice((start - level) * LANES, (start - level) * LANES + width)
                held_high, held_low = lagged_high_ref[:, lanes], lagged_low_ref[:, lanes]
            result = jnp.dot(
                left,
                jnp.concatenate([held_high, held_low, held_high], axis=0),
                preferred_element_type=F32,
            )
            for c in range(chunks):
                done_ref[pl.ds(start + c, local, stride=planes), :] = result[
                    :, c * LANES : (c + 1) * LANES
                ]
            if f == fields // 2 - 1 or f == fields - 1:
                count = fields // 2 * chunks
                out_planes = slice(start + chunks - count, start + chunks)
                copies.append(
                    pltpu.make_async_copy(
                        done_ref.reshape(local, planes, LANES).at[:, out_planes, :],
                        out_ref.at[:, out_planes, :],
                        sems.at[len(copies)],
                    )
                )
                copies[-1].start()
    for copy in copies:
        copy.wait()


def shards(
    present_ensemble,
    delayed_ensemble,
    spreading_coefficient,
    transport_ratios,
    obs_value,
    obs_error,
    obs_noise,
    obs_row,
    obs_col,
    obs_field,
):
    members, fields, height, width = present_ensemble.shape
    assert height == 1 and width % LANES == 0
    chunks = width // LANES
    lagged = delayed_ensemble.shape[1]
    slabs, parts = lax.axis_size("slab"), lax.axis_size("mem")
    assert slabs & (slabs - 1) == 0 and slabs >= 8
    batches, all_members, count = obs_noise.shape
    total = batches * count
    planes = (1 + lagged) * fields * chunks
    stacked = (fields * members, width)
    hbm = pl.BlockSpec(memory_space=pltpu.HBM)
    sizes = (members, fields, chunks)

    def from_slab(array, bit):
        return lax.ppermute(array, "slab", [(i, i ^ bit) for i in range(slabs)])

    def from_other_pair(array, bit):
        return from_slab(array, bit ^ 1)

    def from_other_mem(array):
        if parts != 2:
            return from_partners(array)
        return [
            lax.ppermute(
                array, ("slab", "mem"), [(i ^ 3, i) for i in range(slabs * parts)]
            )
        ]

    def from_partners(array):
        return [
            lax.ppermute(array, "mem", [((i + d) % parts, i) for i in range(parts)])
            for d in range(1, parts)
        ]

    present, delayed = rows_of(present_ensemble), rows_of(delayed_ensemble)
    spread, ratios = rows_of(spreading_coefficient), rows_of(transport_ratios)
    sources = in_hbm((present, spread, ratios, obs_row, obs_col, obs_field))
    packed, *held = pl.pallas_call(
        functools.partial(load_kernel, chunks),
        out_shape=[shape_of((present.shape[0] + 2 * chunks, LANES))]
        + [shape_of(x.shape, x.dtype) for x in sources[1:]],
        in_specs=[hbm] * len(sources),
        scratch_shapes=[pltpu.SemaphoreType.DMA((len(sources) - 1 + PIECES,))],
        compiler_params=PARAMS,
        name="load",
    )(*sources)
    up = [(i, i + 1) for i in range(slabs - 1)]
    from_below = lax.ppermute(packed, "slab", [(j, i) for i, j in up])
    others_delayed = from_partners(
        lax.optimization_barrier((delayed, packed))[0]
    )
    taps, kinds = pl.pallas_call(
        selector_kernel,
        out_shape=(shape_of((width, total), BF16), shape_of((2, total), jnp.int32)),
        compiler_params=PARAMS,
        cost_estimate=estimate(SELECT_FLOPS),
        name="selector",
    )(*held[2:])
    part, here, part_obs = pl.pallas_call(
        functools.partial(own_row_kernel, *sizes),
        out_shape=(shape_of(stacked), shape_of(stacked), shape_of((members, total))),
        compiler_params=PARAMS,
        cost_estimate=estimate(OWN_FLOPS),
        name="own_row",
    )(packed, *held[:2], taps, kinds)
    from_above = lax.ppermute(lax.optimization_barrier((packed, part))[0], "slab", up)
    keep, send, partial = pl.pallas_call(
        functools.partial(observe_kernel, parts, *sizes),
        out_shape=(
            shape_of((members, total // 2)),
            shape_of((members, total // 2)),
            shape_of(stacked),
        ),
        compiler_params=PARAMS,
        name="observe",
    )(packed, from_below, part, part_obs, here, taps, kinds)
    def summed(terms, other, flops, *arrived):
        return pl.pallas_call(
            sum_kernel,
            out_shape=shape_of(terms.shape),
            cost_estimate=estimate(flops),
            compiler_params=PARAMS,
            name="sum",
        )(terms, other, *arrived)

    terms = keep + from_slab(send, 1)
    for bit in [1 << k for k in reversed(range(1, slabs.bit_length() - 1))]:
        terms = summed(
            terms,
            from_other_pair(terms, bit),
            SUM_FLOPS[min(slabs // 2 // bit, 4) // 2],
            *([others_delayed[0]] if bit == 2 else []),
        )
        if bit == slabs // 2:
            after_far = terms
    forecast = pl.pallas_call(
        functools.partial(complete_kernel, *sizes),
        out_shape=shape_of(stacked),
        compiler_params=PARAMS,
        name="complete",
    )(
        lax.optimization_barrier((partial, after_far))[0], from_above, packed
    )

    prior = pl.pallas_call(
        gather_kernel,
        out_shape=shape_of((all_members, total // 2)),
        cost_estimate=estimate(GATHER_FLOPS),
        compiler_params=PARAMS,
        name="gather",
    )(terms, *from_other_mem(terms))
    mine = pl.pallas_call(
        functools.partial(solve_kernel, parts),
        out_shape=shape_of((members, all_members)),
        compiler_params=PARAMS,
        cost_estimate=estimate(SOLVE_FLOPS),
        name="solve",
    )(obs_value, obs_error, obs_noise, prior, from_slab(prior, 1))
    lagged_parts = pl.pallas_call(
        functools.partial(prepare_kernel, parts),
        out_shape=[shape_of((all_members, delayed.size // members), BF16)] * 2,
        compiler_params=PARAMS,
        name="prepare",
    )(delayed, *others_delayed)
    out = pl.pallas_call(
        functools.partial(combine_kernel, parts, fields),
        out_shape=shape_of((members, planes, LANES)),
        out_specs=hbm,
        scratch_shapes=[
            pltpu.VMEM((members * planes, LANES), F32),
            pltpu.SemaphoreType.DMA((2 * (1 + lagged),)),
        ],
        compiler_params=PARAMS,
        name="combine",
    )(mine, forecast, *from_partners(forecast), *lagged_parts)
    return out.reshape(members, 1 + lagged, fields, height, width)


def solution(mesh):
    return jax.shard_map(
        shards,
        mesh=mesh,
        in_specs=(
            P("mem", None, "slab", None),
            P("mem", None, None, "slab", None),
            P("slab", None),
            P(None, "slab", None),
            P(),
            P(),
            P(),
            P(),
            P(),
            P(),
        ),
        out_specs=P("mem", None, None, "slab", None),
        check_vma=False,
    )
```

```python
import functools

import jax
import jax.numpy as jnp
from jax import lax
from jax.experimental import pallas as pl
from jax.experimental.pallas import tpu as pltpu
from jax.sharding import PartitionSpec as P

LANES = 128
F32 = jnp.float32
BF16 = jnp.bfloat16
HIGHEST = lax.Precision.HIGHEST
PARAMS = pltpu.CompilerParams(vmem_limit_bytes=48 * 1024 * 1024)


SELECT_FLOPS = 1
OWN_FLOPS, SUM_FLOPS, GATHER_FLOPS, SOLVE_FLOPS = 1, (7*10**8,7*10**8,1), 10**8, 5*10**8


def estimate(flops):
    return pl.CostEstimate(flops=flops, transcendentals=0, bytes_accessed=0)


def rows_of(array):
    return array.reshape(-1, LANES)


def in_hbm(arrays):
    return [pltpu.with_memory_space_constraint(array, pltpu.HBM) for array in arrays]


def shape_of(shape, dtype=F32):
    return jax.ShapeDtypeStruct(shape, dtype)


def split_two(x):
    high = x.astype(BF16)
    low = (x - high.astype(F32)).astype(BF16)
    return high, low


def split_three(x):
    high = x.astype(BF16)
    rest = x - high.astype(F32)
    middle = rest.astype(BF16)
    low = (rest - middle.astype(F32)).astype(BF16)
    return high, middle, low


def line(ref, start, chunks):
    return jnp.concatenate([ref[start + c : start + c + 1, :] for c in range(chunks)], axis=1)


def stacked_planes(ref, members, fields, chunks):
    return jnp.concatenate(
        [
            jnp.concatenate(
                [
                    ref[pl.ds(f * chunks + c, members, stride=fields * chunks), :]
                    for c in range(chunks)
                ],
                axis=1,
            )
            for f in range(fields)
        ],
        axis=0,
    )


def at_once(sources, targets, sems):
    copies = [
        pltpu.make_async_copy(source, target, sems.at[i])
        for i, (source, target) in enumerate(zip(sources, targets))
    ]
    for copy in copies:
        copy.start()
    return copies


def picked_values(planes, taps):
    high, middle, low = (
        jnp.dot(part, taps, preferred_element_type=F32) for part in split_three(planes)
    )
    return low + middle + high


def load_kernel(chunks, *refs):
    count = (len(refs) - 1) // 2
    sources, packed_ref, held, sems = refs[:count], refs[count], refs[count + 1 : -1], refs[-1]
    rows = sources[0].shape[0]
    copies = at_once(sources, (packed_ref.at[:rows], *held), sems)
    copies[1].wait()
    copies[2].wait()
    spread = held[0][...]
    half = held[1][:chunks, :] * 0.5
    packed_ref[rows : rows + chunks, :] = spread + half
    packed_ref[rows + chunks : rows + 2 * chunks, :] = spread - half
    for copy in (copies[0], *copies[3:]):
        copy.wait()


def keeps_first(parts):
    rest = lax.axis_index("slab")
    ones = lax.axis_index("mem") if parts == 2 else 0
    for _ in range(lax.axis_size("slab").bit_length() - 1):
        ones = ones + lax.rem(rest, 2)
        rest = rest // 2
    return lax.rem(ones, 2) == 0


def weights(packed_ref, chunks):
    rows = packed_ref.shape[0] - 2 * chunks
    return line(packed_ref, rows, chunks), line(packed_ref, rows + chunks, chunks)


def selector_kernel(row_ref, col_ref, field_ref, taps_ref, kinds_ref):
    batches, count = row_ref.shape
    width, total = taps_ref.shape[0] // 2, taps_ref.shape[1]
    flat = lambda ref: jnp.concatenate([ref[b : b + 1, :] for b in range(batches)], axis=1)
    rows, cols = flat(row_ref), flat(col_ref)
    kinds_ref[...] = flat(field_ref)
    at = lax.broadcasted_iota(jnp.int32, (width, total), 0).astype(F32) * 0.25
    taps = jnp.maximum(0.5 - jnp.abs(at - cols.astype(F32) * 0.25), 0.0)
    own_row = lax.axis_index("slab")
    for k in range(2):
        taps_ref[k * width : (k + 1) * width, :] = jnp.where(
            rows == own_row + k, taps, 0.0
        ).astype(BF16)


def own_row_kernel(
    members,
    fields,
    chunks,
    packed_ref,
    spread_ref,
    ratio_ref,
    taps_ref,
    kinds_ref,
    part_ref,
    here_ref,
    obs_ref,
):
    width = chunks * LANES
    spread = line(spread_ref, 0, chunks)
    along_columns = line(ratio_ref, chunks, chunks)
    here = stacked_planes(packed_ref, members, fields, chunks)
    here_ref[...] = here
    lane = lax.broadcasted_iota(jnp.int32, here.shape, 1)
    left = jnp.where(lane == 0, 0.0, pltpu.roll(here, 1, 1))
    right = jnp.where(lane == width - 1, 0.0, pltpu.roll(here, width - 1, 1))
    part = (
        here
        + spread * (right + left - 4.0 * here)
        - along_columns * (right - left) * 0.5
    )
    part_ref[...] = part
    picked = picked_values(part, taps_ref[:width, :])
    observed = jnp.zeros(obs_ref.shape, F32)
    for f in range(fields):
        observed += jnp.where(
            kinds_ref[0:1, :] == f, picked[f * members : (f + 1) * members], 0.0
        )
    obs_ref[...] = observed


def observe_kernel(
    parts,
    members,
    fields,
    chunks,
    packed_ref,
    next_ref,
    part_ref,
    part_obs_ref,
    here_ref,
    taps_ref,
    kinds_ref,
    keep_ref,
    send_ref,
    partial_ref,
):
    _, below = weights(packed_ref, chunks)
    above_of_below, _ = weights(next_ref, chunks)
    taken = below * stacked_planes(next_ref, members, fields, chunks)
    given = above_of_below * here_ref[...]
    partial_ref[...] = part_ref[...] + taken
    picked = sum(
        jnp.dot(part, taps_ref[...], preferred_element_type=F32)
        for part in reversed(split_two(jnp.concatenate([taken, given], axis=1)))
    )
    observed = part_obs_ref[...]
    for f in range(fields):
        observed += jnp.where(
            kinds_ref[...] == f, picked[f * members : (f + 1) * members], 0.0
        )
    first_here = keeps_first(parts)
    half = observed.shape[1] // 2
    first, second = observed[:, :half], observed[:, half:]
    keep_ref[...] = jnp.where(first_here, first, second)
    send_ref[...] = jnp.where(first_here, second, first)


def sum_kernel(terms_ref, other_ref, *refs):
    refs[-1][...] = terms_ref[...] + other_ref[...]


def complete_kernel(members, fields, chunks, partial_ref, previous_ref, packed_ref, forecast_ref):
    above, _ = weights(packed_ref, chunks)
    forecast_ref[...] = partial_ref[...] + above * stacked_planes(
        previous_ref, members, fields, chunks
    )


def gather_kernel(*refs):
    local = refs[0].shape[0]
    for d, ref in enumerate(refs[:-1]):
        refs[-1][d * local : (d + 1) * local, :] = ref[...]


def identity(rows, columns):
    return (
        lax.broadcasted_iota(jnp.int32, (rows, columns), 0)
        == lax.broadcasted_iota(jnp.int32, (rows, columns), 1)
    ).astype(F32)


def precise(x, y):
    return jnp.dot(x, y, precision=HIGHEST, preferred_element_type=F32)


def three_pass(x, y):
    x_high, x_low = split_two(x)
    y_high, y_low = split_two(y)
    dot = functools.partial(jnp.dot, preferred_element_type=F32)
    return dot(x_low, y_high) + dot(x_high, y_low) + dot(x_high, y_high)


def solve_transposed(system, right_t, floor):
    size = system.shape[0]
    eye = identity(size, size)
    sums = jnp.sum(jnp.abs(system), axis=0, keepdims=True)
    top = jnp.max(sums, axis=1, keepdims=True) + 1.0
    scale = 2.0 / (top + floor)
    start = (1.0 - floor * scale, eye - scale * system, scale * right_t)

    def double(product, carry):
        eps, residual, answer = carry
        both = product(jnp.concatenate([residual, answer], axis=0), residual)
        square = eps * eps
        share = 1.0 / (2.0 - square)
        return (
            square * share,
            (2.0 * both[:size] - square * eye) * share,
            (answer + both[size:]) * (2.0 * share),
        )

    def steps(count):
        carry = start
        for _ in range(count):
            carry = double(three_pass, carry)
        return carry[2]

    def loop():
        return lax.while_loop(
            lambda carry: jnp.max(carry[0]) > 1e-6, functools.partial(double, precise), start
        )[2]

    condition = jnp.max(top) / floor
    return lax.cond(
        condition < 20.0,
        lambda: steps(5),
        lambda: lax.cond(condition < 78.0, lambda: steps(6), loop),
    )


def precise_nt(x, y):
    return lax.dot_general(
        x, y, (((1,), (1,)), ((), ())), precision=HIGHEST, preferred_element_type=F32
    )


def solve_kernel(parts, value_ref, error_ref, noise_ref, kept_ref, received_ref, mine_ref):
    batches, members, count = noise_ref.shape
    local = members // parts
    own = lax.axis_index("mem")
    first_here = keeps_first(parts)
    halves = [
        jnp.where(first_here, kept_ref[...], received_ref[...]),
        jnp.where(first_here, received_ref[...], kept_ref[...]),
    ]
    prior = jnp.concatenate(halves, axis=1)
    grams = []
    for b in range(batches):
        wanted = local if b == batches - 1 else members
        observed = prior[:, b * count : (b + 1) * count]
        share = 1.0 / error_ref[b : b + 1, :]
        mean = jnp.mean(observed, axis=0, keepdims=True)
        anomalies = (observed - mean) * share
        blocks = []
        for d in range(wanted // local):
            owner = lax.rem(own + d, parts)
            blocks.append(
                noise_ref[b, pl.ds(pl.multiple_of(owner * local, local), local), :]
            )
        innovation = (value_ref[b : b + 1, :] - mean) * share + jnp.concatenate(blocks, axis=0)
        both = precise_nt(jnp.concatenate([anomalies, innovation], axis=0), anomalies)
        grams.append((both[:members], both[members:]))
    diagonal = (members - 1.0) * identity(members, members)
    product_t = None
    for b, (gram, cross) in enumerate(grams):
        wanted = cross.shape[0]
        if product_t is None:
            system, right_t = gram, cross - gram[:wanted]
        else:
            centred = product_t - jnp.mean(product_t, axis=0, keepdims=True)
            both = precise(jnp.concatenate([centred, product_t[:wanted]], axis=0), gram)
            both = precise_nt(
                jnp.concatenate([both[:members], cross - both[members:]], axis=0), centred
            )
            system, right_t = both[:members], both[members:]
        weights_t = solve_transposed(system + diagonal, right_t, members - 1.0)
        matrix_t = (
            identity(wanted, members) + weights_t - jnp.mean(weights_t, axis=1, keepdims=True)
        )
        product_t = matrix_t if product_t is None else precise(matrix_t, product_t)
    mine_ref[...] = product_t


def prepare_kernel(parts, *refs):
    sources, high_ref, low_ref = refs[:parts], refs[parts], refs[parts + 1]
    lagged = high_ref.shape[1] // LANES
    local = high_ref.shape[0] // parts
    for k in range(lagged):
        held = jnp.concatenate(
            [ref[pl.ds(k, local, stride=lagged), :] for ref in sources], axis=0
        )
        high, low = split_two(held)
        high_ref[:, k * LANES : (k + 1) * LANES] = high
        low_ref[:, k * LANES : (k + 1) * LANES] = low


def combine_kernel(parts, fields, mine_ref, *refs):
    forecast_refs = refs[:parts]
    lagged_high_ref, lagged_low_ref, out_ref, done_ref, sems = refs[parts:]
    local = mine_ref.shape[0]
    high, low = split_two(mine_ref[...])
    left = jnp.concatenate([high, high, low], axis=1)
    width = forecast_refs[0].shape[1]
    chunks = width // LANES
    level = fields * chunks
    planes = level + lagged_high_ref.shape[1] // LANES
    copies = []
    for first in [*range(level, planes, level), 0]:
        for f in range(fields):
            start = first + f * chunks
            if first == 0:
                held_high, held_low = split_two(
                    jnp.concatenate(
                        [ref[f * local : (f + 1) * local, :] for ref in forecast_refs], axis=0
                    )
                )
            else:
                lanes = slice((start - level) * LANES, (start - level) * LANES + width)
                held_high, held_low = lagged_high_ref[:, lanes], lagged_low_ref[:, lanes]
            result = jnp.dot(
                left,
                jnp.concatenate([held_high, held_low, held_high], axis=0),
                preferred_element_type=F32,
            )
            for c in range(chunks):
                done_ref[pl.ds(start + c, local, stride=planes), :] = result[
                    :, c * LANES : (c + 1) * LANES
                ]
        copies.append(
            pltpu.make_async_copy(
                done_ref.reshape(local, planes, LANES).at[:, first : first + level, :],
                out_ref.at[:, first : first + level, :],
                sems.at[len(copies)],
            )
        )
        copies[-1].start()
    for copy in copies:
        copy.wait()


def shards(
    present_ensemble,
    delayed_ensemble,
    spreading_coefficient,
    transport_ratios,
    obs_value,
    obs_error,
    obs_noise,
    obs_row,
    obs_col,
    obs_field,
):
    members, fields, height, width = present_ensemble.shape
    assert height == 1 and width % LANES == 0
    chunks = width // LANES
    lagged = delayed_ensemble.shape[1]
    slabs, parts = lax.axis_size("slab"), lax.axis_size("mem")
    assert slabs & (slabs - 1) == 0 and slabs >= 8
    batches, all_members, count = obs_noise.shape
    total = batches * count
    planes = (1 + lagged) * fields * chunks
    stacked = (fields * members, width)
    hbm = pl.BlockSpec(memory_space=pltpu.HBM)
    sizes = (members, fields, chunks)

    def from_slab(array, bit):
        return lax.ppermute(array, "slab", [(i, i ^ bit) for i in range(slabs)])

    def from_other_pair(array, bit):
        return from_slab(array, bit ^ 1)

    def from_other_mem(array):
        if parts != 2:
            return from_partners(array)
        return [
            lax.ppermute(
                array, ("slab", "mem"), [(i ^ 3, i) for i in range(slabs * parts)]
            )
        ]

    def from_partners(array):
        return [
            lax.ppermute(array, "mem", [((i + d) % parts, i) for i in range(parts)])
            for d in range(1, parts)
        ]

    present, delayed = rows_of(present_ensemble), rows_of(delayed_ensemble)
    spread, ratios = rows_of(spreading_coefficient), rows_of(transport_ratios)
    sources = in_hbm((present, spread, ratios, obs_row, obs_col, obs_field))
    packed, *held = pl.pallas_call(
        functools.partial(load_kernel, chunks),
        out_shape=[shape_of((present.shape[0] + 2 * chunks, LANES))]
        + [shape_of(x.shape, x.dtype) for x in sources[1:]],
        in_specs=[hbm] * len(sources),
        scratch_shapes=[pltpu.SemaphoreType.DMA((len(sources),))],
        compiler_params=PARAMS,
        name="load",
    )(*sources)
    up = [(i, i + 1) for i in range(slabs - 1)]
    from_below = lax.ppermute(packed, "slab", [(j, i) for i, j in up])
    others_delayed = from_partners(
        lax.optimization_barrier((delayed, packed))[0]
    )
    taps, kinds = pl.pallas_call(
        selector_kernel,
        out_shape=(shape_of((2 * width, total), BF16), shape_of((1, total), jnp.int32)),
        compiler_params=PARAMS,
        cost_estimate=estimate(SELECT_FLOPS),
        name="selector",
    )(*held[2:])
    part, here, part_obs = pl.pallas_call(
        functools.partial(own_row_kernel, *sizes),
        out_shape=(shape_of(stacked), shape_of(stacked), shape_of((members, total))),
        compiler_params=PARAMS,
        cost_estimate=estimate(OWN_FLOPS),
        name="own_row",
    )(packed, *held[:2], taps, kinds)
    from_above = lax.ppermute(lax.optimization_barrier((packed, part))[0], "slab", up)
    keep, send, partial = pl.pallas_call(
        functools.partial(observe_kernel, parts, *sizes),
        out_shape=(
            shape_of((members, total // 2)),
            shape_of((members, total // 2)),
            shape_of(stacked),
        ),
        compiler_params=PARAMS,
        name="observe",
    )(packed, from_below, part, part_obs, here, taps, kinds)
    def summed(terms, other, flops, *arrived):
        return pl.pallas_call(
            sum_kernel,
            out_shape=shape_of(terms.shape),
            cost_estimate=estimate(flops),
            compiler_params=PARAMS,
            name="sum",
        )(terms, other, *arrived)

    terms = keep + from_slab(send, 1)
    for bit in [1 << k for k in reversed(range(1, slabs.bit_length() - 1))]:
        terms = summed(
            terms,
            from_other_pair(terms, bit),
            SUM_FLOPS[min(slabs // 2 // bit, 4) // 2],
            *([others_delayed[0]] if bit == 2 else []),
        )
        if bit == slabs // 2:
            after_far = terms
    forecast = pl.pallas_call(
        functools.partial(complete_kernel, *sizes),
        out_shape=shape_of(stacked),
        compiler_params=PARAMS,
        name="complete",
    )(
        lax.optimization_barrier((partial, after_far))[0], from_above, packed
    )

    prior = pl.pallas_call(
        gather_kernel,
        out_shape=shape_of((all_members, total // 2)),
        cost_estimate=estimate(GATHER_FLOPS),
        compiler_params=PARAMS,
        name="gather",
    )(terms, *from_other_mem(terms))
    mine = pl.pallas_call(
        functools.partial(solve_kernel, parts),
        out_shape=shape_of((members, all_members)),
        compiler_params=PARAMS,
        cost_estimate=estimate(SOLVE_FLOPS),
        name="solve",
    )(obs_value, obs_error, obs_noise, prior, from_slab(prior, 1))
    lagged_parts = pl.pallas_call(
        functools.partial(prepare_kernel, parts),
        out_shape=[shape_of((all_members, delayed.size // members), BF16)] * 2,
        compiler_params=PARAMS,
        name="prepare",
    )(delayed, *others_delayed)
    out = pl.pallas_call(
        functools.partial(combine_kernel, parts, fields),
        out_shape=shape_of((members, planes, LANES)),
        out_specs=hbm,
        scratch_shapes=[
            pltpu.VMEM((members * planes, LANES), F32),
            pltpu.SemaphoreType.DMA((1 + lagged,)),
        ],
        compiler_params=PARAMS,
        name="combine",
    )(mine, forecast, *from_partners(forecast), *lagged_parts)
    return out.reshape(members, 1 + lagged, fields, height, width)


def solution(mesh):
    return jax.shard_map(
        shards,
        mesh=mesh,
        in_specs=(
            P("mem", None, "slab", None),
            P("mem", None, None, "slab", None),
            P("slab", None),
            P(None, "slab", None),
            P(),
            P(),
            P(),
            P(),
            P(),
            P(),
        ),
        out_specs=P("mem", None, None, "slab", None),
        check_vma=False,
    )
```

```python
import functools

import jax
import jax.numpy as jnp
from jax import lax
from jax.experimental import pallas as pl
from jax.experimental.pallas import tpu as pltpu
from jax.sharding import PartitionSpec as P

LANES = 128
F32 = jnp.float32
BF16 = jnp.bfloat16
HIGHEST = lax.Precision.HIGHEST
PARAMS = pltpu.CompilerParams(vmem_limit_bytes=48 * 1024 * 1024)


SELECT_FLOPS = 1
PIECES = 4
OWN_FLOPS, SUM_FLOPS, GATHER_FLOPS, SOLVE_FLOPS = 1, (7*10**8,7*10**8,1), 10**8, 8*10**8


def estimate(flops):
    return pl.CostEstimate(flops=flops, transcendentals=0, bytes_accessed=0)


def rows_of(array):
    return array.reshape(-1, LANES)


def in_hbm(arrays):
    return [pltpu.with_memory_space_constraint(array, pltpu.HBM) for array in arrays]


def shape_of(shape, dtype=F32):
    return jax.ShapeDtypeStruct(shape, dtype)


def split_two(x):
    high = x.astype(BF16)
    low = (x - high.astype(F32)).astype(BF16)
    return high, low


def split_three(x):
    high = x.astype(BF16)
    rest = x - high.astype(F32)
    middle = rest.astype(BF16)
    low = (rest - middle.astype(F32)).astype(BF16)
    return high, middle, low


def line(ref, start, chunks):
    return jnp.concatenate([ref[start + c : start + c + 1, :] for c in range(chunks)], axis=1)


def stacked_planes(ref, members, fields, chunks):
    return jnp.concatenate(
        [
            jnp.concatenate(
                [
                    ref[pl.ds(f * chunks + c, members, stride=fields * chunks), :]
                    for c in range(chunks)
                ],
                axis=1,
            )
            for f in range(fields)
        ],
        axis=0,
    )


def at_once(sources, targets, sems):
    copies = [
        pltpu.make_async_copy(source, target, sems.at[i])
        for i, (source, target) in enumerate(zip(sources, targets))
    ]
    for copy in copies:
        copy.start()
    return copies


def picked_values(planes, taps):
    high, middle, low = (
        jnp.dot(part, taps, preferred_element_type=F32) for part in split_three(planes)
    )
    return low + middle + high


def load_kernel(chunks, *refs):
    count = (len(refs) - 1) // 2
    (present, *others), packed_ref, held, sems = (
        refs[:count],
        refs[count],
        refs[count + 1 : -1],
        refs[-1],
    )
    rows = present.shape[0]
    piece = rows // PIECES
    pieces = [pl.ds(k * piece, piece) for k in range(PIECES)]
    copies = at_once(
        [*(present.at[p] for p in pieces), *others],
        [*(packed_ref.at[p] for p in pieces), *held],
        sems,
    )
    copies[PIECES].wait()
    copies[PIECES + 1].wait()
    spread = held[0][...]
    half = held[1][:chunks, :] * 0.5
    packed_ref[rows : rows + chunks, :] = spread + half
    packed_ref[rows + chunks : rows + 2 * chunks, :] = spread - half
    for copy in (*copies[:PIECES], *copies[PIECES + 2 :]):
        copy.wait()


def keeps_first(parts):
    rest = lax.axis_index("slab")
    ones = lax.axis_index("mem") if parts == 2 else 0
    for _ in range(lax.axis_size("slab").bit_length() - 1):
        ones = ones + lax.rem(rest, 2)
        rest = rest // 2
    return lax.rem(ones, 2) == 0


def weights(packed_ref, chunks):
    rows = packed_ref.shape[0] - 2 * chunks
    return line(packed_ref, rows, chunks), line(packed_ref, rows + chunks, chunks)


def selector_kernel(row_ref, col_ref, field_ref, taps_ref, kinds_ref):
    batches, count = row_ref.shape
    shape = taps_ref.shape
    flat = lambda ref: jnp.concatenate([ref[b : b + 1, :] for b in range(batches)], axis=1)
    rows, cols, kinds = flat(row_ref), flat(col_ref), flat(field_ref)
    own_row = lax.axis_index("slab")
    for k, row in enumerate((own_row, own_row + 1)):
        kinds_ref[k : k + 1, :] = jnp.where(rows == row, kinds, -1)
    at = lax.broadcasted_iota(jnp.int32, shape, 0).astype(F32) * 0.25
    taps_ref[...] = jnp.maximum(0.5 - jnp.abs(at - cols.astype(F32) * 0.25), 0.0).astype(BF16)


def own_row_kernel(
    members,
    fields,
    chunks,
    packed_ref,
    spread_ref,
    ratio_ref,
    taps_ref,
    kinds_ref,
    part_ref,
    here_ref,
    obs_ref,
):
    width = chunks * LANES
    spread = line(spread_ref, 0, chunks)
    along_columns = line(ratio_ref, chunks, chunks)
    here = stacked_planes(packed_ref, members, fields, chunks)
    here_ref[...] = here
    lane = lax.broadcasted_iota(jnp.int32, here.shape, 1)
    left = jnp.where(lane == 0, 0.0, pltpu.roll(here, 1, 1))
    right = jnp.where(lane == width - 1, 0.0, pltpu.roll(here, width - 1, 1))
    part = (
        here
        + spread * (right + left - 4.0 * here)
        - along_columns * (right - left) * 0.5
    )
    part_ref[...] = part
    picked = picked_values(part, taps_ref[...])
    observed = jnp.zeros(obs_ref.shape, F32)
    for f in range(fields):
        observed += jnp.where(
            kinds_ref[0:1, :] == f, picked[f * members : (f + 1) * members], 0.0
        )
    obs_ref[...] = observed


def observe_kernel(
    parts,
    members,
    fields,
    chunks,
    packed_ref,
    next_ref,
    part_ref,
    part_obs_ref,
    here_ref,
    taps_ref,
    kinds_ref,
    keep_ref,
    send_ref,
    partial_ref,
):
    _, below = weights(packed_ref, chunks)
    above_of_below, _ = weights(next_ref, chunks)
    taken = below * stacked_planes(next_ref, members, fields, chunks)
    given = above_of_below * here_ref[...]
    partial_ref[...] = part_ref[...] + taken
    picked = sum(
        jnp.dot(part, taps_ref[...], preferred_element_type=F32)
        for part in reversed(split_two(jnp.concatenate([taken, given], axis=0)))
    )
    observed = part_obs_ref[...]
    for side in range(2):
        kinds = kinds_ref[side : side + 1, :]
        for f in range(fields):
            start = (side * fields + f) * members
            observed += jnp.where(kinds == f, picked[start : start + members], 0.0)
    first_here = keeps_first(parts)
    half = observed.shape[1] // 2
    first, second = observed[:, :half], observed[:, half:]
    keep_ref[...] = jnp.where(first_here, first, second)
    send_ref[...] = jnp.where(first_here, second, first)


def sum_kernel(terms_ref, other_ref, *refs):
    refs[-1][...] = terms_ref[...] + other_ref[...]


def complete_kernel(members, fields, chunks, partial_ref, previous_ref, packed_ref, forecast_ref):
    above, _ = weights(packed_ref, chunks)
    forecast_ref[...] = partial_ref[...] + above * stacked_planes(
        previous_ref, members, fields, chunks
    )


def identity(rows, columns):
    return (
        lax.broadcasted_iota(jnp.int32, (rows, columns), 0)
        == lax.broadcasted_iota(jnp.int32, (rows, columns), 1)
    ).astype(F32)


def precise(x, y):
    return jnp.dot(x, y, precision=HIGHEST, preferred_element_type=F32)


def three_pass(x, y):
    x_high, x_low = split_two(x)
    y_high, y_low = split_two(y)
    dot = functools.partial(jnp.dot, preferred_element_type=F32)
    return dot(x_low, y_high) + dot(x_high, y_low) + dot(x_high, y_high)


def precise_nt(x, y):
    return lax.dot_general(
        x, y, (((1,), (1,)), ((), ())), precision=HIGHEST, preferred_element_type=F32
    )


def gram_kernel(parts, value_ref, error_ref, noise_ref, _high, _low, *refs):
    term_refs, grams_ref = refs[:parts], refs[parts]
    members, count = noise_ref.shape[1:]
    local = members // parts
    own = lax.axis_index("mem")
    batch = 1 - keeps_first(parts).astype(jnp.int32)
    observed = jnp.concatenate([ref[...] for ref in term_refs], axis=0)
    share = 1.0 / error_ref[pl.ds(batch, 1), :]
    mean = jnp.mean(observed, axis=0, keepdims=True)
    anomalies = (observed - mean) * share
    noise = jnp.concatenate(
        [
            noise_ref[batch, pl.ds(pl.multiple_of(lax.rem(own + d, parts) * local, local), local), :]
            for d in range(parts)
        ],
        axis=0,
    )
    innovation = (value_ref[pl.ds(batch, 1), :] - mean) * share + noise
    grams_ref[...] = precise_nt(jnp.concatenate([anomalies, innovation], axis=0), anomalies)


def solve_transposed(system, right_t, floor):
    size = system.shape[0]
    eye = identity(size, size)
    sums = jnp.sum(jnp.abs(system), axis=0, keepdims=True)
    top = jnp.max(sums, axis=1, keepdims=True) + 1.0
    scale = 2.0 / (top + floor)
    start = (1.0 - floor * scale, eye - scale * system, scale * right_t)

    def double(product, carry):
        eps, residual, answer = carry
        both = product(jnp.concatenate([residual, answer], axis=0), residual)
        square = eps * eps
        share = 1.0 / (2.0 - square)
        return (
            square * share,
            (2.0 * both[:size] - square * eye) * share,
            (answer + both[size:]) * (2.0 * share),
        )

    def steps(count):
        carry = start
        for _ in range(count):
            carry = double(three_pass, carry)
        return carry[2]

    def loop():
        return lax.while_loop(
            lambda carry: jnp.max(carry[0]) > 1e-6, functools.partial(double, precise), start
        )[2]

    condition = jnp.max(top) / floor
    return lax.cond(
        condition < 20.0,
        lambda: steps(5),
        lambda: lax.cond(condition < 78.0, lambda: steps(6), loop),
    )


def solve_kernel(parts, batches, kept_ref, received_ref, mine_ref):
    members = kept_ref.shape[1]
    local = members // parts
    first_here = keeps_first(parts)
    kept, received = kept_ref[...], received_ref[...]
    grams = [
        jnp.where(first_here, kept, received),
        jnp.where(first_here, received, kept),
    ]
    diagonal = (members - 1.0) * identity(members, members)
    product_t = None
    for b, both in enumerate(grams):
        wanted = local if b == batches - 1 else members
        gram, cross = both[:members], both[members : members + wanted]
        if product_t is None:
            system, right_t = gram, cross - gram[:wanted]
        else:
            centred = product_t - jnp.mean(product_t, axis=0, keepdims=True)
            both = precise(jnp.concatenate([centred, product_t[:wanted]], axis=0), gram)
            both = precise_nt(
                jnp.concatenate([both[:members], cross - both[members:]], axis=0), centred
            )
            system, right_t = both[:members], both[members:]
        weights_t = solve_transposed(system + diagonal, right_t, members - 1.0)
        matrix_t = (
            identity(wanted, members) + weights_t - jnp.mean(weights_t, axis=1, keepdims=True)
        )
        product_t = matrix_t if product_t is None else precise(matrix_t, product_t)
    mine_ref[...] = product_t


def prepare_kernel(parts, *refs):
    sources, high_ref, low_ref = refs[:parts], refs[parts], refs[parts + 1]
    lagged = high_ref.shape[1] // LANES
    local = high_ref.shape[0] // parts
    for k in range(lagged):
        held = jnp.concatenate(
            [ref[pl.ds(k, local, stride=lagged), :] for ref in sources], axis=0
        )
        high, low = split_two(held)
        high_ref[:, k * LANES : (k + 1) * LANES] = high
        low_ref[:, k * LANES : (k + 1) * LANES] = low


def combine_kernel(parts, fields, mine_ref, *refs):
    forecast_refs = refs[:parts]
    lagged_high_ref, lagged_low_ref, out_ref, done_ref, sems = refs[parts:]
    local = mine_ref.shape[0]
    high, low = split_two(mine_ref[...])
    left = jnp.concatenate([high, high, low], axis=1)
    width = forecast_refs[0].shape[1]
    chunks = width // LANES
    level = fields * chunks
    planes = level + lagged_high_ref.shape[1] // LANES
    copies = []
    for first in [*range(level, planes, level), 0]:
        for f in range(fields):
            start = first + f * chunks
            if first == 0:
                held_high, held_low = split_two(
                    jnp.concatenate(
                        [ref[f * local : (f + 1) * local, :] for ref in forecast_refs], axis=0
                    )
                )
            else:
                lanes = slice((start - level) * LANES, (start - level) * LANES + width)
                held_high, held_low = lagged_high_ref[:, lanes], lagged_low_ref[:, lanes]
            result = jnp.dot(
                left,
                jnp.concatenate([held_high, held_low, held_high], axis=0),
                preferred_element_type=F32,
            )
            for c in range(chunks):
                done_ref[pl.ds(start + c, local, stride=planes), :] = result[
                    :, c * LANES : (c + 1) * LANES
                ]
            if f == fields // 2 - 1 or f == fields - 1:
                count = fields // 2 * chunks
                out_planes = slice(start + chunks - count, start + chunks)
                copies.append(
                    pltpu.make_async_copy(
                        done_ref.reshape(local, planes, LANES).at[:, out_planes, :],
                        out_ref.at[:, out_planes, :],
                        sems.at[len(copies)],
                    )
                )
                copies[-1].start()
    for copy in copies:
        copy.wait()


def shards(
    present_ensemble,
    delayed_ensemble,
    spreading_coefficient,
    transport_ratios,
    obs_value,
    obs_error,
    obs_noise,
    obs_row,
    obs_col,
    obs_field,
):
    members, fields, height, width = present_ensemble.shape
    assert height == 1 and width % LANES == 0
    chunks = width // LANES
    lagged = delayed_ensemble.shape[1]
    slabs, parts = lax.axis_size("slab"), lax.axis_size("mem")
    assert slabs & (slabs - 1) == 0 and slabs >= 8
    batches, all_members, count = obs_noise.shape
    total = batches * count
    planes = (1 + lagged) * fields * chunks
    stacked = (fields * members, width)
    hbm = pl.BlockSpec(memory_space=pltpu.HBM)
    sizes = (members, fields, chunks)

    def from_slab(array, bit):
        return lax.ppermute(array, "slab", [(i, i ^ bit) for i in range(slabs)])

    def from_other_pair(array, bit):
        return from_slab(array, bit ^ 1)

    def from_other_mem(array):
        if parts != 2:
            return from_partners(array)
        return [
            lax.ppermute(
                array, ("slab", "mem"), [(i ^ 3, i) for i in range(slabs * parts)]
            )
        ]

    def from_partners(array):
        return [
            lax.ppermute(array, "mem", [((i + d) % parts, i) for i in range(parts)])
            for d in range(1, parts)
        ]

    present, delayed = rows_of(present_ensemble), rows_of(delayed_ensemble)
    spread, ratios = rows_of(spreading_coefficient), rows_of(transport_ratios)
    sources = in_hbm((present, spread, ratios, obs_row, obs_col, obs_field))
    packed, *held = pl.pallas_call(
        functools.partial(load_kernel, chunks),
        out_shape=[shape_of((present.shape[0] + 2 * chunks, LANES))]
        + [shape_of(x.shape, x.dtype) for x in sources[1:]],
        in_specs=[hbm] * len(sources),
        scratch_shapes=[pltpu.SemaphoreType.DMA((len(sources) - 1 + PIECES,))],
        compiler_params=PARAMS,
        name="load",
    )(*sources)
    up = [(i, i + 1) for i in range(slabs - 1)]
    from_below = lax.ppermute(packed, "slab", [(j, i) for i, j in up])
    others_delayed = from_partners(
        lax.optimization_barrier((delayed, packed))[0]
    )
    taps, kinds = pl.pallas_call(
        selector_kernel,
        out_shape=(shape_of((width, total), BF16), shape_of((2, total), jnp.int32)),
        compiler_params=PARAMS,
        cost_estimate=estimate(SELECT_FLOPS),
        name="selector",
    )(*held[2:])
    part, here, part_obs = pl.pallas_call(
        functools.partial(own_row_kernel, *sizes),
        out_shape=(shape_of(stacked), shape_of(stacked), shape_of((members, total))),
        compiler_params=PARAMS,
        cost_estimate=estimate(OWN_FLOPS),
        name="own_row",
    )(packed, *held[:2], taps, kinds)
    from_above = lax.ppermute(lax.optimization_barrier((packed, part))[0], "slab", up)
    keep, send, partial = pl.pallas_call(
        functools.partial(observe_kernel, parts, *sizes),
        out_shape=(
            shape_of((members, total // 2)),
            shape_of((members, total // 2)),
            shape_of(stacked),
        ),
        compiler_params=PARAMS,
        name="observe",
    )(packed, from_below, part, part_obs, here, taps, kinds)
    def summed(terms, other, flops, *arrived):
        return pl.pallas_call(
            sum_kernel,
            out_shape=shape_of(terms.shape),
            cost_estimate=estimate(flops),
            compiler_params=PARAMS,
            name="sum",
        )(terms, other, *arrived)

    terms = keep + from_slab(send, 1)
    for bit in [1 << k for k in reversed(range(1, slabs.bit_length() - 1))]:
        terms = summed(
            terms,
            from_other_pair(terms, bit),
            SUM_FLOPS[min(slabs // 2 // bit, 4) // 2],
            *([others_delayed[0]] if bit == 2 else []),
        )
        if bit == slabs // 2:
            after_far = terms
    forecast = pl.pallas_call(
        functools.partial(complete_kernel, *sizes),
        out_shape=shape_of(stacked),
        compiler_params=PARAMS,
        name="complete",
    )(
        lax.optimization_barrier((partial, after_far))[0], from_above, packed
    )

    assert batches == 2
    lagged_parts = pl.pallas_call(
        functools.partial(prepare_kernel, parts),
        out_shape=[shape_of((all_members, delayed.size // members), BF16)] * 2,
        compiler_params=PARAMS,
        name="prepare",
    )(delayed, *others_delayed)
    grams = pl.pallas_call(
        functools.partial(gram_kernel, parts),
        out_shape=shape_of((2 * all_members, all_members)),
        cost_estimate=estimate(GATHER_FLOPS),
        compiler_params=PARAMS,
        name="gram",
    )(obs_value, obs_error, obs_noise, *lagged_parts, terms, *from_other_mem(terms))
    mine = pl.pallas_call(
        functools.partial(solve_kernel, parts, batches),
        out_shape=shape_of((members, all_members)),
        compiler_params=PARAMS,
        cost_estimate=estimate(SOLVE_FLOPS),
        name="solve",
    )(grams, from_slab(grams, 1))
    out = pl.pallas_call(
        functools.partial(combine_kernel, parts, fields),
        out_shape=shape_of((members, planes, LANES)),
        out_specs=hbm,
        scratch_shapes=[
            pltpu.VMEM((members * planes, LANES), F32),
            pltpu.SemaphoreType.DMA((2 * (1 + lagged),)),
        ],
        compiler_params=PARAMS,
        name="combine",
    )(mine, forecast, *from_partners(forecast), *lagged_parts)
    return out.reshape(members, 1 + lagged, fields, height, width)


def solution(mesh):
    return jax.shard_map(
        shards,
        mesh=mesh,
        in_specs=(
            P("mem", None, "slab", None),
            P("mem", None, None, "slab", None),
            P("slab", None),
            P(None, "slab", None),
            P(),
            P(),
            P(),
            P(),
            P(),
            P(),
        ),
        out_specs=P("mem", None, None, "slab", None),
        check_vma=False,
    )
```

```python
import functools

import jax
import jax.numpy as jnp
from jax import lax
from jax.experimental import pallas as pl
from jax.experimental.pallas import tpu as pltpu
from jax.sharding import PartitionSpec as P

LANES = 128
F32 = jnp.float32
BF16 = jnp.bfloat16
HIGHEST = lax.Precision.HIGHEST
PARAMS = pltpu.CompilerParams(vmem_limit_bytes=48 * 1024 * 1024)


SELECT_FLOPS = 1
OWN_FLOPS, SUM_FLOPS, GATHER_FLOPS, SOLVE_FLOPS = 1, (7*10**8,7*10**8,1), 10**8, 5*10**8


def estimate(flops):
    return pl.CostEstimate(flops=flops, transcendentals=0, bytes_accessed=0)


def rows_of(array):
    return array.reshape(-1, LANES)


def in_hbm(arrays):
    return [pltpu.with_memory_space_constraint(array, pltpu.HBM) for array in arrays]


def shape_of(shape, dtype=F32):
    return jax.ShapeDtypeStruct(shape, dtype)


def split_two(x):
    high = x.astype(BF16)
    low = (x - high.astype(F32)).astype(BF16)
    return high, low


def split_three(x):
    high = x.astype(BF16)
    rest = x - high.astype(F32)
    middle = rest.astype(BF16)
    low = (rest - middle.astype(F32)).astype(BF16)
    return high, middle, low


def line(ref, start, chunks):
    return jnp.concatenate([ref[start + c : start + c + 1, :] for c in range(chunks)], axis=1)


def stacked_planes(ref, members, fields, chunks):
    return jnp.concatenate(
        [
            jnp.concatenate(
                [
                    ref[pl.ds(f * chunks + c, members, stride=fields * chunks), :]
                    for c in range(chunks)
                ],
                axis=1,
            )
            for f in range(fields)
        ],
        axis=0,
    )


def at_once(sources, targets, sems):
    copies = [
        pltpu.make_async_copy(source, target, sems.at[i])
        for i, (source, target) in enumerate(zip(sources, targets))
    ]
    for copy in copies:
        copy.start()
    return copies


def picked_values(planes, taps):
    high, middle, low = (
        jnp.dot(part, taps, preferred_element_type=F32) for part in split_three(planes)
    )
    return low + middle + high


def load_kernel(chunks, *refs):
    count = (len(refs) - 1) // 2
    sources, packed_ref, held, sems = refs[:count], refs[count], refs[count + 1 : -1], refs[-1]
    rows = sources[0].shape[0]
    copies = at_once(sources, (packed_ref.at[:rows], *held), sems)
    copies[1].wait()
    copies[2].wait()
    spread = held[0][...]
    half = held[1][:chunks, :] * 0.5
    packed_ref[rows : rows + chunks, :] = spread + half
    packed_ref[rows + chunks : rows + 2 * chunks, :] = spread - half
    for copy in (copies[0], *copies[3:]):
        copy.wait()


def keeps_first(parts):
    rest = lax.axis_index("slab")
    ones = lax.axis_index("mem") if parts == 2 else 0
    for _ in range(lax.axis_size("slab").bit_length() - 1):
        ones = ones + lax.rem(rest, 2)
        rest = rest // 2
    return lax.rem(ones, 2) == 0


def weights(packed_ref, chunks):
    rows = packed_ref.shape[0] - 2 * chunks
    return line(packed_ref, rows, chunks), line(packed_ref, rows + chunks, chunks)


def selector_kernel(row_ref, col_ref, field_ref, taps_ref, kinds_ref):
    batches, count = row_ref.shape
    shape = taps_ref.shape
    flat = lambda ref: jnp.concatenate([ref[b : b + 1, :] for b in range(batches)], axis=1)
    rows, cols, kinds = flat(row_ref), flat(col_ref), flat(field_ref)
    own_row = lax.axis_index("slab")
    for k, row in enumerate((own_row, own_row + 1)):
        kinds_ref[k : k + 1, :] = jnp.where(rows == row, kinds, -1)
    at = lax.broadcasted_iota(jnp.int32, shape, 0).astype(F32) * 0.25
    taps_ref[...] = jnp.maximum(0.5 - jnp.abs(at - cols.astype(F32) * 0.25), 0.0).astype(BF16)


def own_row_kernel(
    members,
    fields,
    chunks,
    packed_ref,
    spread_ref,
    ratio_ref,
    taps_ref,
    kinds_ref,
    part_ref,
    here_ref,
    obs_ref,
):
    width = chunks * LANES
    spread = line(spread_ref, 0, chunks)
    along_columns = line(ratio_ref, chunks, chunks)
    here = stacked_planes(packed_ref, members, fields, chunks)
    here_ref[...] = here
    lane = lax.broadcasted_iota(jnp.int32, here.shape, 1)
    left = jnp.where(lane == 0, 0.0, pltpu.roll(here, 1, 1))
    right = jnp.where(lane == width - 1, 0.0, pltpu.roll(here, width - 1, 1))
    part = (
        here
        + spread * (right + left - 4.0 * here)
        - along_columns * (right - left) * 0.5
    )
    part_ref[...] = part
    picked = picked_values(part, taps_ref[...])
    observed = jnp.zeros(obs_ref.shape, F32)
    for f in range(fields):
        observed += jnp.where(
            kinds_ref[0:1, :] == f, picked[f * members : (f + 1) * members], 0.0
        )
    obs_ref[...] = observed


def observe_kernel(
    parts,
    members,
    fields,
    chunks,
    packed_ref,
    next_ref,
    part_ref,
    part_obs_ref,
    here_ref,
    taps_ref,
    kinds_ref,
    keep_ref,
    send_ref,
    partial_ref,
):
    _, below = weights(packed_ref, chunks)
    above_of_below, _ = weights(next_ref, chunks)
    taken = below * stacked_planes(next_ref, members, fields, chunks)
    given = above_of_below * here_ref[...]
    partial_ref[...] = part_ref[...] + taken
    picked = sum(
        jnp.dot(part, taps_ref[...], preferred_element_type=F32)
        for part in reversed(split_two(jnp.concatenate([taken, given], axis=0)))
    )
    observed = part_obs_ref[...]
    for side in range(2):
        kinds = kinds_ref[side : side + 1, :]
        for f in range(fields):
            start = (side * fields + f) * members
            observed += jnp.where(kinds == f, picked[start : start + members], 0.0)
    first_here = keeps_first(parts)
    half = observed.shape[1] // 2
    first, second = observed[:, :half], observed[:, half:]
    keep_ref[...] = jnp.where(first_here, first, second)
    send_ref[...] = jnp.where(first_here, second, first)


def sum_kernel(terms_ref, other_ref, *refs):
    refs[-1][...] = terms_ref[...] + other_ref[...]


def complete_kernel(members, fields, chunks, partial_ref, previous_ref, packed_ref, forecast_ref):
    above, _ = weights(packed_ref, chunks)
    forecast_ref[...] = partial_ref[...] + above * stacked_planes(
        previous_ref, members, fields, chunks
    )


def gather_kernel(*refs):
    local = refs[0].shape[0]
    for d, ref in enumerate(refs[:-1]):
        refs[-1][d * local : (d + 1) * local, :] = ref[...]


def identity(rows, columns):
    return (
        lax.broadcasted_iota(jnp.int32, (rows, columns), 0)
        == lax.broadcasted_iota(jnp.int32, (rows, columns), 1)
    ).astype(F32)


def precise(x, y):
    return jnp.dot(x, y, precision=HIGHEST, preferred_element_type=F32)


def three_pass(x, y):
    x_high, x_low = split_two(x)
    y_high, y_low = split_two(y)
    return jnp.dot(
        jnp.concatenate([x_high, x_high, x_low], axis=1),
        jnp.concatenate([y_high, y_low, y_high], axis=0),
        preferred_element_type=F32,
    )


def solve_transposed(system, right_t, floor):
    size = system.shape[0]
    eye = identity(size, size)
    sums = jnp.sum(jnp.abs(system), axis=0, keepdims=True)
    top = jnp.max(sums, axis=1, keepdims=True) + 1.0
    scale = 2.0 / (top + floor)
    start = (1.0 - floor * scale, eye - scale * system, scale * right_t)

    def double(product, carry):
        eps, residual, answer = carry
        both = product(jnp.concatenate([residual, answer], axis=0), residual)
        square = eps * eps
        share = 1.0 / (2.0 - square)
        return (
            square * share,
            (2.0 * both[:size] - square * eye) * share,
            (answer + both[size:]) * (2.0 * share),
        )

    def steps(count):
        carry = start
        for _ in range(count):
            carry = double(three_pass, carry)
        return carry[2]

    def loop():
        return lax.while_loop(
            lambda carry: jnp.max(carry[0]) > 1e-6, functools.partial(double, precise), start
        )[2]

    condition = jnp.max(top) / floor
    return lax.cond(
        condition < 20.0,
        lambda: steps(5),
        lambda: lax.cond(condition < 78.0, lambda: steps(6), loop),
    )


def precise_nt(x, y):
    return lax.dot_general(
        x, y, (((1,), (1,)), ((), ())), precision=HIGHEST, preferred_element_type=F32
    )


def solve_kernel(parts, value_ref, error_ref, noise_ref, kept_ref, received_ref, mine_ref):
    batches, members, count = noise_ref.shape
    local = members // parts
    own = lax.axis_index("mem")
    first_here = keeps_first(parts)
    halves = [
        jnp.where(first_here, kept_ref[...], received_ref[...]),
        jnp.where(first_here, received_ref[...], kept_ref[...]),
    ]
    prior = jnp.concatenate(halves, axis=1)
    grams = []
    for b in range(batches):
        wanted = local if b == batches - 1 else members
        observed = prior[:, b * count : (b + 1) * count]
        share = 1.0 / error_ref[b : b + 1, :]
        mean = jnp.mean(observed, axis=0, keepdims=True)
        anomalies = (observed - mean) * share
        blocks = []
        for d in range(wanted // local):
            owner = lax.rem(own + d, parts)
            blocks.append(
                noise_ref[b, pl.ds(pl.multiple_of(owner * local, local), local), :]
            )
        innovation = (value_ref[b : b + 1, :] - mean) * share + jnp.concatenate(blocks, axis=0)
        both = precise_nt(jnp.concatenate([anomalies, innovation], axis=0), anomalies)
        grams.append((both[:members], both[members:]))
    diagonal = (members - 1.0) * identity(members, members)
    product_t = None
    for b, (gram, cross) in enumerate(grams):
        wanted = cross.shape[0]
        if product_t is None:
            system, right_t = gram, cross - gram[:wanted]
        else:
            centred = product_t - jnp.mean(product_t, axis=0, keepdims=True)
            both = precise(jnp.concatenate([centred, product_t[:wanted]], axis=0), gram)
            both = precise_nt(
                jnp.concatenate([both[:members], cross - both[members:]], axis=0), centred
            )
            system, right_t = both[:members], both[members:]
        weights_t = solve_transposed(system + diagonal, right_t, members - 1.0)
        matrix_t = (
            identity(wanted, members) + weights_t - jnp.mean(weights_t, axis=1, keepdims=True)
        )
        product_t = matrix_t if product_t is None else precise(matrix_t, product_t)
    mine_ref[...] = product_t


def prepare_kernel(parts, *refs):
    sources, high_ref, low_ref = refs[:parts], refs[parts], refs[parts + 1]
    lagged = high_ref.shape[1] // LANES
    local = high_ref.shape[0] // parts
    for k in range(lagged):
        held = jnp.concatenate(
            [ref[pl.ds(k, local, stride=lagged), :] for ref in sources], axis=0
        )
        high, low = split_two(held)
        high_ref[:, k * LANES : (k + 1) * LANES] = high
        low_ref[:, k * LANES : (k + 1) * LANES] = low


def combine_kernel(parts, fields, mine_ref, *refs):
    forecast_refs = refs[:parts]
    lagged_high_ref, lagged_low_ref, out_ref, done_ref, sems = refs[parts:]
    local = mine_ref.shape[0]
    high, low = split_two(mine_ref[...])
    left = jnp.concatenate([high, high, low], axis=1)
    width = forecast_refs[0].shape[1]
    chunks = width // LANES
    level = fields * chunks
    planes = level + lagged_high_ref.shape[1] // LANES
    copies = []
    for first in [*range(level, planes, level), 0]:
        for f in range(fields):
            start = first + f * chunks
            if first == 0:
                held_high, held_low = split_two(
                    jnp.concatenate(
                        [ref[f * local : (f + 1) * local, :] for ref in forecast_refs], axis=0
                    )
                )
            else:
                lanes = slice((start - level) * LANES, (start - level) * LANES + width)
                held_high, held_low = lagged_high_ref[:, lanes], lagged_low_ref[:, lanes]
            result = jnp.dot(
                left,
                jnp.concatenate([held_high, held_low, held_high], axis=0),
                preferred_element_type=F32,
            )
            for c in range(chunks):
                done_ref[pl.ds(start + c, local, stride=planes), :] = result[
                    :, c * LANES : (c + 1) * LANES
                ]
        copies.append(
            pltpu.make_async_copy(
                done_ref.reshape(local, planes, LANES).at[:, first : first + level, :],
                out_ref.at[:, first : first + level, :],
                sems.at[len(copies)],
            )
        )
        copies[-1].start()
    for copy in copies:
        copy.wait()


def shards(
    present_ensemble,
    delayed_ensemble,
    spreading_coefficient,
    transport_ratios,
    obs_value,
    obs_error,
    obs_noise,
    obs_row,
    obs_col,
    obs_field,
):
    members, fields, height, width = present_ensemble.shape
    assert height == 1 and width % LANES == 0
    chunks = width // LANES
    lagged = delayed_ensemble.shape[1]
    slabs, parts = lax.axis_size("slab"), lax.axis_size("mem")
    assert slabs & (slabs - 1) == 0 and slabs >= 8
    batches, all_members, count = obs_noise.shape
    total = batches * count
    planes = (1 + lagged) * fields * chunks
    stacked = (fields * members, width)
    hbm = pl.BlockSpec(memory_space=pltpu.HBM)
    sizes = (members, fields, chunks)

    def from_slab(array, bit):
        return lax.ppermute(array, "slab", [(i, i ^ bit) for i in range(slabs)])

    def from_other_pair(array, bit):
        return from_slab(array, bit ^ 1)

    def from_other_mem(array):
        if parts != 2:
            return from_partners(array)
        return [
            lax.ppermute(
                array, ("slab", "mem"), [(i ^ 3, i) for i in range(slabs * parts)]
            )
        ]

    def from_partners(array):
        return [
            lax.ppermute(array, "mem", [((i + d) % parts, i) for i in range(parts)])
            for d in range(1, parts)
        ]

    present, delayed = rows_of(present_ensemble), rows_of(delayed_ensemble)
    spread, ratios = rows_of(spreading_coefficient), rows_of(transport_ratios)
    sources = in_hbm((present, spread, ratios, obs_row, obs_col, obs_field))
    packed, *held = pl.pallas_call(
        functools.partial(load_kernel, chunks),
        out_shape=[shape_of((present.shape[0] + 2 * chunks, LANES))]
        + [shape_of(x.shape, x.dtype) for x in sources[1:]],
        in_specs=[hbm] * len(sources),
        scratch_shapes=[pltpu.SemaphoreType.DMA((len(sources),))],
        compiler_params=PARAMS,
        name="load",
    )(*sources)
    up = [(i, i + 1) for i in range(slabs - 1)]
    from_below = lax.ppermute(packed, "slab", [(j, i) for i, j in up])
    others_delayed = from_partners(
        lax.optimization_barrier((delayed, packed))[0]
    )
    taps, kinds = pl.pallas_call(
        selector_kernel,
        out_shape=(shape_of((width, total), BF16), shape_of((2, total), jnp.int32)),
        compiler_params=PARAMS,
        cost_estimate=estimate(SELECT_FLOPS),
        name="selector",
    )(*held[2:])
    part, here, part_obs = pl.pallas_call(
        functools.partial(own_row_kernel, *sizes),
        out_shape=(shape_of(stacked), shape_of(stacked), shape_of((members, total))),
        compiler_params=PARAMS,
        cost_estimate=estimate(OWN_FLOPS),
        name="own_row",
    )(packed, *held[:2], taps, kinds)
    from_above = lax.ppermute(lax.optimization_barrier((packed, part))[0], "slab", up)
    keep, send, partial = pl.pallas_call(
        functools.partial(observe_kernel, parts, *sizes),
        out_shape=(
            shape_of((members, total // 2)),
            shape_of((members, total // 2)),
            shape_of(stacked),
        ),
        compiler_params=PARAMS,
        name="observe",
    )(packed, from_below, part, part_obs, here, taps, kinds)
    def summed(terms, other, flops, *arrived):
        return pl.pallas_call(
            sum_kernel,
            out_shape=shape_of(terms.shape),
            cost_estimate=estimate(flops),
            compiler_params=PARAMS,
            name="sum",
        )(terms, other, *arrived)

    terms = keep + from_slab(send, 1)
    for bit in [1 << k for k in reversed(range(1, slabs.bit_length() - 1))]:
        terms = summed(
            terms,
            from_other_pair(terms, bit),
            SUM_FLOPS[min(slabs // 2 // bit, 4) // 2],
            *([others_delayed[0]] if bit == 2 else []),
        )
        if bit == slabs // 2:
            after_far = terms
    forecast = pl.pallas_call(
        functools.partial(complete_kernel, *sizes),
        out_shape=shape_of(stacked),
        compiler_params=PARAMS,
        name="complete",
    )(
        lax.optimization_barrier((partial, after_far))[0], from_above, packed
    )

    prior = pl.pallas_call(
        gather_kernel,
        out_shape=shape_of((all_members, total // 2)),
        cost_estimate=estimate(GATHER_FLOPS),
        compiler_params=PARAMS,
        name="gather",
    )(terms, *from_other_mem(terms))
    mine = pl.pallas_call(
        functools.partial(solve_kernel, parts),
        out_shape=shape_of((members, all_members)),
        compiler_params=PARAMS,
        cost_estimate=estimate(SOLVE_FLOPS),
        name="solve",
    )(obs_value, obs_error, obs_noise, prior, from_slab(prior, 1))
    lagged_parts = pl.pallas_call(
        functools.partial(prepare_kernel, parts),
        out_shape=[shape_of((all_members, delayed.size // members), BF16)] * 2,
        compiler_params=PARAMS,
        name="prepare",
    )(delayed, *others_delayed)
    out = pl.pallas_call(
        functools.partial(combine_kernel, parts, fields),
        out_shape=shape_of((members, planes, LANES)),
        out_specs=hbm,
        scratch_shapes=[
            pltpu.VMEM((members * planes, LANES), F32),
            pltpu.SemaphoreType.DMA((1 + lagged,)),
        ],
        compiler_params=PARAMS,
        name="combine",
    )(mine, forecast, *from_partners(forecast), *lagged_parts)
    return out.reshape(members, 1 + lagged, fields, height, width)


def solution(mesh):
    return jax.shard_map(
        shards,
        mesh=mesh,
        in_specs=(
            P("mem", None, "slab", None),
            P("mem", None, None, "slab", None),
            P("slab", None),
            P(None, "slab", None),
            P(),
            P(),
            P(),
            P(),
            P(),
            P(),
        ),
        out_specs=P("mem", None, None, "slab", None),
        check_vma=False,
    )
```
